32 devices in a mesh: dp: 8 (over y, x, core), expert: 4 (over z).
Axes of the slice: x: 2, y: 2, z: 4, core: 2. Of those that a mesh axis runs over, the one named last changes fastest.
Arguments:
- tokens: bfloat16 [2, 2048, 2048], P(None, ('dp', 'expert')), may hold values from -6 to 6
- cotangent: bfloat16 [2, 2048, 2048], P(None, ('dp', 'expert')), may hold values from -6 to 6
- seq_lengths: int32 [2, 8, 2], replicated, may hold values from 16 to 240, as said below
- dealing: int32 [2, 2048], P(None, ('dp', 'expert')), may hold values from 0 to 63, as said below
- attn_routes: int32 [2, 2048, 2], P(None, 'dp'), may hold values from 0 to 3, all different within a row; in each aligned block of 64 rows (0 to 63, 64 to 127, ..., all dimensions but the last counted through in order) at most 48 rows name the same one
- ffn_routes: int32 [2, 2048, 2], P(None, 'dp'), may hold values from 0 to 3, all different within a row; in each aligned block of 64 rows (0 to 63, 64 to 127, ..., all dimensions but the last counted through in order) at most 48 rows name the same one
- expert_table: int32 [4], replicated, may hold values from 0 to 3, each once
- clip_limit: int32 [1], replicated, may hold values from 5 to 10
- attn_gain: bfloat16 [2048], replicated, may hold values from 0.5 to 1.5
- ffn_gain: bfloat16 [2048], replicated, may hold values from 0.5 to 1.5
- attn_router: bfloat16 [2048, 4], replicated, may hold values from -0.125 to 0.125
- ffn_router: bfloat16 [2048, 4], replicated, may hold values from -0.125 to 0.125
- query_weight: bfloat16 [4, 2048, 2048], P('expert', 'dp')
- attn_out_weight: bfloat16 [4, 2048, 2048], P('expert', 'dp'), may hold values from -0.375 to 0.375
- kv_weight: bfloat16 [2048, 4096], P('dp', 'expert'), may hold values from -0.125 to 0.125
- gate_up_weight: bfloat16 [4, 2048, 11264], P('expert', 'dp'), may hold values from -0.125 to 0.125
- down_weight: bfloat16 [4, 2048, 5632], P('expert', 'dp'), may hold values from -0.078125 to 0.078125
Outputs:
- block_output: bfloat16 [2, 2048, 2048], P(None, ('dp', 'expert'))
- tokens_grad: bfloat16 [2, 2048, 2048], P(None, ('dp', 'expert'))
- attn_gain_grad: float32 [2048], replicated
- ffn_gain_grad: float32 [2048], replicated
- attn_router_grad: float32 [2048, 4], replicated
- ffn_router_grad: float32 [2048, 4], replicated
- query_grad: float32 [4, 2048, 2048], P('expert', 'dp')
- attn_out_grad: float32 [4, 2048, 2048], P('expert', 'dp')
- kv_grad: float32 [2048, 4096], P('dp', 'expert')
- gate_up_grad: float32 [4, 2048, 11264], P('expert', 'dp')
- down_grad: float32 [4, 2048, 5632], P('expert', 'dp')
- query_clipped: bfloat16 [4, 2048, 2048], P('expert', 'dp')
- kv_clipped: bfloat16 [2048, 4096], P('dp', 'expert')
The draws below stay inside these ranges and needn't reach their ends.
Inputs may be any that keep to these rules, and one draw needn't show every extreme that they name: `seq_lengths`: the two lengths of a group sum to 256; the shorter one is under 64, and which one comes first varies. `dealing`: for each micro-batch, the entries of one device's 64 rows are a permutation of 0 to 63. `attn_routes`: each row names 2 different experts; in each aligned block of 64 rows (the rows of one device) no expert is named by more than 48 rows. `ffn_routes`: each row names 2 different experts; in each aligned block of 64 rows (the rows of one device) no expert is named by more than 48 rows. `expert_table`: A permutation of the experts.
All inputs are finite; a program needn't handle non-finite values.
Results may differ from the reference program's by a relative error of at most 0.02.
Values may be sent and summed in bfloat16 or wider, within the bound.
No kernel may reach another device: no remote copies, remote signals or barrier semaphores. Data moves between devices by JAX's collectives and lax.ppermute only.
A program may use at most 448 MiB of HBM per device.

```python
import math
import jax
import jax.numpy as jnp
import numpy as np
from jax import lax

D = 2048
HEADS = 16
HDIM = 128
FF = 5632
TOP = 2
QW = 2048
EXPERTS = 4
TOK_DEV = 64
MICRO = 2
CAP = 48
GRP = 256
TOKENS = 2048
N_DP = 8
N_EXPERT = 4


def draw_seq_lengths(key, part):
    key = jax.random.fold_in(key, 11)
    group_count = MICRO * N_DP
    least_len = TOK_DEV // 4
    shorter = jax.random.randint(jax.random.fold_in(key, 1), (group_count,), least_len, TOK_DEV)
    chosen = jax.random.permutation(jax.random.fold_in(key, 2), group_count)
    shorter = shorter.at[chosen[0]].set(least_len)
    shorter = shorter.at[chosen[1]].set(TOK_DEV - 1)
    short_first = jax.random.randint(jax.random.fold_in(key, 3), (group_count,), 0, 2)
    longer = TOK_DEV * N_EXPERT - shorter
    lead_len = jnp.where(short_first == 1, shorter, longer)
    tail_len = jnp.where(short_first == 1, longer, shorter)
    return jnp.stack([lead_len, tail_len], axis=-1).reshape(MICRO, N_DP, 2).astype(jnp.int32)


def draw_dealing(key, part):
    key = jax.random.fold_in(key, 12)
    block_count = MICRO * TOKENS // TOK_DEV
    block_keys = jax.random.split(key, block_count)

    def shuffle_block(sub_key):
        return jax.random.permutation(sub_key, TOK_DEV)
    shuffled = jax.vmap(shuffle_block)(block_keys)
    return shuffled.reshape(MICRO, TOKENS).astype(jnp.int32)


def draw_query_weight(key, part):
    key = jax.random.fold_in(key, 13)
    head_scale = jnp.exp(jax.random.uniform(jax.random.fold_in(key, 1), (EXPERTS, 1, HEADS, 1), minval=0.0, maxval=1.0986123))
    base = jax.random.normal(jax.random.fold_in(key, 2), (EXPERTS, D, HEADS, HDIM))
    values = base * head_scale * D ** (-0.5)
    return values.reshape(EXPERTS, D, HEADS * HDIM).astype(jnp.float32).astype(jnp.bfloat16)


def steps_of(key, extent, shards, least, high):
    loudness, own = 1.0, jax.random.fold_in(key, 6)
    for axis_at, blocks in shards:
        heights = jnp.exp(jax.random.uniform(jax.random.fold_in(own, axis_at), (blocks,), jnp.float32, least / len(shards), high / len(shards)))
        loudness = loudness * jnp.repeat(heights, extent[axis_at] // blocks).reshape([-1 if axis == axis_at else 1 for axis in range(len(extent))])
    return loudness


def routed_block(key, own, number, rows, amount, top, most, lean):
    sequence = jax.random.permutation(key, amount)
    heavy_load, common = shares(amount, rows * top, most, lean, True), shares(amount, rows * top, most, lean, False)
    places = jnp.arange(amount)

    def named(sizes, rotation):
        used = int((sizes > 0).sum())
        fixed = max(1, used // 4)
        shifted = fixed + (places - fixed + rotation * (used - fixed)) % max(1, amount - fixed)
        return jnp.zeros((amount,), jnp.int32).at[sequence[jnp.where(places < fixed, places, shifted)]].set(jnp.asarray(sizes, jnp.int32))

    sizes = jnp.where(number % 4 == 0, named(heavy_load, number // 4), named(common, number - number // 4 - 1))
    mixed = jax.random.permutation(jax.random.fold_in(own, 3), amount)
    donor, sink = mixed[0:amount // 2 * 2:2], mixed[1:amount // 2 * 2:2]
    room = jnp.minimum(sizes[donor] - 1, most - sizes[sink]) // 2
    room = jnp.where((donor == sequence[0]) | (sink == sequence[0]) | (sizes[sink] == 0), 0, jnp.maximum(room, 0))
    shifted = jax.random.randint(jax.random.fold_in(own, 4), (amount // 2,), 0, 1 << 20) % (room + 1)
    sizes = sizes.at[donor].add(-shifted).at[sink].add(shifted)
    items = jnp.searchsorted(jnp.cumsum(sizes), jnp.arange(rows * top), side="right").astype(jnp.int32)
    table = items.reshape(top, rows).T
    table = table[jax.random.permutation(jax.random.fold_in(own, 1), rows)]
    rotation = jax.random.randint(jax.random.fold_in(own, 2), (rows, 1), 0, top)
    return jnp.take_along_axis(table, (jnp.arange(top)[None, :] + rotation) % top, axis=1)


def shares(amount, total, reach, lean, full):
    weights = [(1 << 20) // math.isqrt(rank ** lean) + 1 for rank in range(1, amount + 1)]
    largest = reach if full else min(reach, max(-(-total // amount), total * weights[0] // sum(weights)))
    least = 1 if total - largest >= amount - 1 else 0
    counts, surplus = [largest] + [least] * (amount - 1), total - largest - least * (amount - 1)
    while surplus > 0:
        free = [i for i in range(1, amount) if counts[i] < largest] or [i for i in range(1, amount) if counts[i] < reach]
        pool, remaining = sum([weights[i] for i in free]), surplus
        for i in free:
            extra = min(reach - counts[i], max(1, remaining * weights[i] // pool), surplus)
            counts[i] = counts[i] + extra
            surplus = surplus - extra
    return np.array(counts)


def noise(stream_key, dims, width, most, cuts=(), kind=jnp.bfloat16):
    values = width * jax.random.normal(stream_key, dims, jnp.float32)
    if cuts:
        values = values * steps_of(stream_key, dims, cuts, -0.22, 0.18)
    return jnp.clip(values, -most, most).astype(kind)


def setup_inputs(seed: int = 0) -> dict:
    splits = jax.random.split(jax.random.key(seed), 18)
    tokens = noise(splits[0], (MICRO, TOKENS, D), 1.0, 6.0, ((1, 32),))
    cotangent = noise(splits[1], (MICRO, TOKENS, D), 1.0, 6.0, ((1, 32),))
    seq_lengths = draw_seq_lengths(jax.random.fold_in(splits[17], 71), 0)
    dealing = draw_dealing(jax.random.fold_in(splits[17], 71), 0)
    attn_routes_keys = jax.random.split(jax.random.fold_in(splits[4], 1), MICRO * TOKENS // TOK_DEV)
    attn_routes_turns = jax.random.permutation(jax.random.fold_in(splits[4], 3), MICRO * TOKENS // TOK_DEV)
    attn_routes = jax.vmap(lambda own, number: routed_block(jax.random.fold_in(splits[4], 2), own, number, TOK_DEV, EXPERTS, TOP, CAP, 1))(attn_routes_keys, attn_routes_turns).reshape((MICRO, TOKENS, TOP))
    ffn_routes_keys = jax.random.split(jax.random.fold_in(splits[5], 1), MICRO * TOKENS // TOK_DEV)
    ffn_routes_turns = jax.random.permutation(jax.random.fold_in(splits[5], 3), MICRO * TOKENS // TOK_DEV)
    ffn_routes = jax.vmap(lambda own, number: routed_block(jax.random.fold_in(splits[5], 2), own, number, TOK_DEV, EXPERTS, TOP, CAP, 1))(ffn_routes_keys, ffn_routes_turns).reshape((MICRO, TOKENS, TOP))
    expert_table = jax.random.permutation(splits[6], EXPERTS).astype(jnp.int32)
    clip_limit = jax.random.randint(splits[7], (1,), 5, 11).astype(jnp.int32)
    attn_gain = jnp.clip(1.0 + 0.1 * jax.random.normal(splits[8], (D,), jnp.float32), 0.5, 1.5).astype(jnp.bfloat16)
    ffn_gain = jnp.clip(1.0 + 0.1 * jax.random.normal(splits[9], (D,), jnp.float32), 0.5, 1.5).astype(jnp.bfloat16)
    attn_router = noise(splits[10], (D, EXPERTS), D ** -0.5, 0.125)
    ffn_router = noise(splits[11], (D, EXPERTS), D ** -0.5, 0.125)
    query_weight = draw_query_weight(jax.random.fold_in(splits[17], 71), 0)
    attn_out_weight = noise(splits[13], (EXPERTS, D, QW), (QW // 8) ** -0.5, 0.375, ((0, 4), (1, 8)))
    kv_weight = noise(splits[14], (D, 2 * QW), D ** -0.5, 0.125, ((0, 8), (1, 4)))
    gate_up_weight = noise(splits[15], (EXPERTS, D, 2 * FF), D ** -0.5, 0.125, ((0, 4), (1, 8)))
    down_weight = noise(splits[16], (EXPERTS, D, FF), FF ** -0.5, 0.078125, ((0, 4), (1, 8)))
    return {"tokens": tokens, "cotangent": cotangent, "seq_lengths": seq_lengths, "dealing": dealing, "attn_routes": attn_routes, "ffn_routes": ffn_routes, "expert_table": expert_table, "clip_limit": clip_limit, "attn_gain": attn_gain, "ffn_gain": ffn_gain, "attn_router": attn_router, "ffn_router": ffn_router, "query_weight": query_weight, "attn_out_weight": attn_out_weight, "kv_weight": kv_weight, "gate_up_weight": gate_up_weight, "down_weight": down_weight}


eps_norm = 1e-06
rope_base = 10000.0
very_low = -1e+30

@jax.custom_vjp
def low(v):
    return lax.optimization_barrier(v.astype(jnp.bfloat16)).astype(jnp.float32)

@jax.custom_vjp
def low_back(v):
    return v

def low_keep(v):
    return (low(v), None)

def low_pass(kept, grad):
    return (grad,)

def back_keep(v):
    return (v, None)

def back_low(kept, grad):
    return (low(grad),)
low.defvjp(low_keep, low_pass)
low_back.defvjp(back_keep, back_low)

def matmul(left, right):
    return jnp.dot(left, right, precision=lax.Precision.HIGHEST, preferred_element_type=jnp.float32)

def normalize(values):
    return values * lax.rsqrt(lax.optimization_barrier(jnp.mean(values * values, axis=-1, keepdims=True)) + eps_norm)

def rotate(values, places):
    half_dim = HDIM // 2
    frequency = rope_base ** (-jnp.arange(half_dim, dtype=jnp.float32) * 2.0 / HDIM)
    angles = places.astype(jnp.float32)[:, None] * frequency[None, :]
    cosine = jnp.cos(angles)[:, None, :]
    sine = jnp.sin(angles)[:, None, :]
    shaped = values.reshape(values.shape[0], HEADS, HDIM)
    first_half = shaped[..., :half_dim]
    second_half = shaped[..., half_dim:]
    rotated = jnp.concatenate([first_half * cosine - second_half * sine, second_half * cosine + first_half * sine], axis=-1)
    return rotated.reshape(values.shape)

def slot_gates(hidden, router, routes, expert_table):
    logits = low_back(matmul(hidden, router))
    picked = jnp.take_along_axis(logits, routes, axis=1)
    gate_vals = jax.nn.softmax(picked, axis=-1)
    slot_ids = expert_table[routes]
    onehot = slot_ids[:, :, None] == jnp.arange(EXPERTS, dtype=jnp.int32)[None, None, :]
    gates = lax.optimization_barrier(jnp.sum(jnp.where(onehot, gate_vals[:, :, None], 0.0), axis=1))
    return (gates, jnp.any(onehot, axis=1))

def group_forward(params, group_x, lengths, routes_attn, routes_ffn, expert_table):
    attn_gain, ffn_gain, attn_router, ffn_router, query_weight, attn_out_weight, kv_weight, gate_up_weight, down_weight = params
    group_rows = group_x.shape[0]
    query_width = HEADS * HDIM
    positions = jnp.arange(group_rows, dtype=jnp.int32)
    in_second = positions >= lengths[0]
    places = positions - jnp.where(in_second, lengths[0], 0)
    allowed = (positions[None, :] <= positions[:, None]) & (in_second[None, :] == in_second[:, None])
    hidden_one = low(normalize(group_x) * attn_gain)
    gates_one, hits_one = slot_gates(hidden_one, attn_router, routes_attn, expert_table)
    joint_kv = low(low_back(matmul(hidden_one, kv_weight)))
    key_rot = low(rotate(joint_kv[:, :query_width], places))
    key_heads = key_rot.reshape(group_rows, HEADS, HDIM)
    value_heads = joint_kv[:, query_width:].reshape(group_rows, HEADS, HDIM)
    attn_total = jnp.zeros_like(group_x)
    peaks = []
    for slot_index in range(EXPERTS):
        query_rot = low(rotate(low_back(matmul(hidden_one, query_weight[slot_index])), places))
        query_heads = query_rot.reshape(group_rows, HEADS, HDIM)
        raw = low_back(jnp.einsum('rhd,khd->hrk', query_heads, key_heads, precision=lax.Precision.HIGHEST))
        scores = jnp.where(allowed[None], raw * HDIM ** (-0.5), very_low)
        peaks.append(lax.optimization_barrier(jnp.max(jnp.where(hits_one[None, :, slot_index, None], scores, very_low), axis=(1, 2))))
        probs = jax.nn.softmax(scores, axis=-1)
        mixed = jnp.einsum('hrk,khd->rhd', low(probs), value_heads, precision=lax.Precision.HIGHEST)
        mixed = low(low_back(mixed.reshape(group_rows, query_width)))
        branch = low_back(matmul(mixed, attn_out_weight[slot_index].T))
        attn_total = attn_total + gates_one[:, slot_index:slot_index + 1] * branch
    resid = group_x + attn_total
    hidden_two = low(normalize(resid) * ffn_gain)
    gates_two, hits_two = slot_gates(hidden_two, ffn_router, routes_ffn, expert_table)
    ffn_total = jnp.zeros_like(group_x)
    for slot_index in range(EXPERTS):
        joint = low_back(matmul(hidden_two, gate_up_weight[slot_index]))
        active = low(jax.nn.silu(joint[:, :FF]) * joint[:, FF:])
        branch = low_back(matmul(active, down_weight[slot_index].T))
        ffn_total = ffn_total + gates_two[:, slot_index:slot_index + 1] * branch
    return (resid + ffn_total, jnp.stack(peaks))

def reference(tokens, cotangent, seq_lengths, dealing, attn_routes, ffn_routes, expert_table, clip_limit, attn_gain, ffn_gain, attn_router, ffn_router, query_weight, attn_out_weight, kv_weight, gate_up_weight, down_weight):
    piece_rows = TOK_DEV // N_DP
    row_ids = jnp.arange(TOKENS, dtype=jnp.int32)
    group_of = row_ids // GRP
    column_of = row_ids // TOK_DEV % EXPERTS
    source = (dealing // piece_rows * EXPERTS + column_of[None, :]) * TOK_DEV + group_of[None, :] * piece_rows + dealing % piece_rows
    source = source.astype(jnp.int32)
    work_x = jnp.take_along_axis(tokens.astype(jnp.float32), source[:, :, None], axis=1)
    work_grad = jnp.take_along_axis(cotangent.astype(jnp.float32), source[:, :, None], axis=1)
    params = tuple([weight_array.astype(jnp.float32) for weight_array in (attn_gain, ffn_gain, attn_router, ffn_router, query_weight, attn_out_weight, kv_weight, gate_up_weight, down_weight)])
    group_count = MICRO * N_DP

    def one_group(params_in, group_x, lengths, routes_attn, routes_ffn):
        return group_forward(params_in, group_x, lengths, routes_attn, routes_ffn, expert_table)
    checked = jax.checkpoint(one_group)

    def forward(params_in, rows_in):
        inputs = (rows_in.reshape(group_count, GRP, D), seq_lengths.reshape(group_count, 2), attn_routes.reshape(group_count, GRP, TOP), ffn_routes.reshape(group_count, GRP, TOP))

        def scan_step(carry, pieces):
            result_rows, peaks = checked(params_in, pieces[0], pieces[1], pieces[2], pieces[3])
            return (carry, (result_rows, peaks))
        carry_end, (results, peaks) = lax.scan(scan_step, jnp.zeros((), jnp.float32), inputs)
        return (results.reshape(MICRO, TOKENS, D), lax.optimization_barrier(jnp.max(peaks, axis=0)))
    result, pullback, head_peak = jax.vjp(forward, params, work_x, has_aux=True)
    param_grads, input_grad = pullback(work_grad)
    batch_ids = jnp.arange(MICRO, dtype=jnp.int32)[:, None]
    block_output = jnp.zeros((MICRO, TOKENS, D), jnp.float32).at[batch_ids, source].set(result).astype(jnp.bfloat16)
    tokens_grad = jnp.zeros((MICRO, TOKENS, D), jnp.float32).at[batch_ids, source].set(input_grad).astype(jnp.bfloat16)
    limit = clip_limit[0].astype(jnp.float32)
    factor = limit / jnp.maximum(head_peak, limit)
    query_scale = jnp.repeat(jnp.sqrt(factor), HDIM, axis=1)
    query_clipped = (params[4] * query_scale[:, None, :]).astype(jnp.bfloat16)
    key_scale = jnp.concatenate([jnp.repeat(jnp.sqrt(lax.optimization_barrier(jnp.min(factor, axis=0))), HDIM), jnp.ones((HEADS * HDIM,), jnp.float32)])
    kv_clipped = (params[6] * key_scale[None, :]).astype(jnp.bfloat16)
    return (block_output, tokens_grad, param_grads[0], param_grads[1], param_grads[2], param_grads[3], param_grads[4], param_grads[5], param_grads[6], param_grads[7], param_grads[8], query_clipped, kv_clipped)
```

```python
import jax
import jax.numpy as jnp
from jax import lax
from jax.sharding import PartitionSpec as P

HEADS = 16
HDIM = 128
FF = 5632
TOP = 2

eps_norm = 1e-06
rope_base = 10000.0
very_low = -1e30

f32 = jnp.float32
bf16 = jnp.bfloat16


def dot(left, right):
    return jnp.dot(left, right, preferred_element_type=f32)


def dot_t(left, right):
    return lax.dot_general(left, right, (((1,), (1,)), ((), ())), preferred_element_type=f32)


def t_dot(left, right):
    return lax.dot_general(left, right, (((0,), (0,)), ((), ())), preferred_element_type=f32)


def swap(value, axis, step):
    count = lax.axis_size(axis)
    return lax.ppermute(value, axis, [(i, i ^ step) for i in range(count)])


def take(stacked, index):
    return lax.dynamic_index_in_dim(stacked, index, 0, keepdims=False)


def place(parts, positions):
    out = jnp.zeros((len(parts),) + parts[0].shape, parts[0].dtype)
    for part, position in zip(parts, positions):
        out = lax.dynamic_update_index_in_dim(out, part, position, 0)
    return out


def rotation_tables(places):
    half_dim = HDIM // 2
    frequency = rope_base ** (-jnp.arange(half_dim, dtype=f32) * 2.0 / HDIM)
    angles = places.astype(f32)[..., None] * frequency
    return jnp.cos(angles), jnp.sin(angles)


def rotate(values, tables, inverse):
    cosine, sine = tables
    if inverse:
        sine = -sine
    rows = values.shape[0]
    half_dim = HDIM // 2
    shaped = values.reshape(rows, -1, HDIM)
    first_half = shaped[..., :half_dim]
    second_half = shaped[..., half_dim:]
    cosine, sine = cosine[:, None, :], sine[:, None, :]
    rotated = jnp.concatenate(
        [first_half * cosine - second_half * sine, second_half * cosine + first_half * sine],
        axis=-1,
    )
    return rotated.reshape(rows, -1)


def normalize(values):
    row_scale = lax.rsqrt(jnp.mean(values * values, axis=-1, keepdims=True) + eps_norm)
    return values * row_scale, row_scale


def norm_back(grad_hat, normed, row_scale):
    return row_scale * (grad_hat - normed * jnp.mean(grad_hat * normed, axis=-1, keepdims=True))


def route_gates(logits, routes, expert_table):
    expert_ids = jnp.arange(expert_table.shape[0], dtype=jnp.int32)
    matches = routes[:, :, None] == expert_ids[None, None, :]
    picked = jnp.sum(jnp.where(matches, logits[:, None, :], 0.0), axis=-1)
    gate_vals = jax.nn.softmax(picked, axis=-1)
    slot_ids = route_slots(routes, expert_table)
    chosen = slot_ids[:, :, None] == expert_ids[None, None, :]
    gates = jnp.sum(jnp.where(chosen, gate_vals[:, :, None], 0.0), axis=1)
    return gates, matches, chosen, gate_vals


def route_slots(routes, expert_table):
    expert_ids = jnp.arange(expert_table.shape[0], dtype=jnp.int32)
    matches = routes[..., None] == expert_ids
    return jnp.sum(jnp.where(matches, expert_table, 0), axis=-1)


def gate_back(slot_grad, gate_vals, matches, chosen):
    picked = jnp.sum(jnp.where(chosen, slot_grad[:, None, :], 0.0), axis=-1)
    inner_sum = jnp.sum(gate_vals * picked, axis=-1, keepdims=True)
    picked_grad = gate_vals * (picked - inner_sum)
    return jnp.sum(jnp.where(matches, picked_grad[:, :, None], 0.0), axis=1)


def local(
    tokens,
    cotangent,
    seq_lengths,
    dealing,
    attn_routes,
    ffn_routes,
    expert_table,
    clip_limit,
    attn_gain,
    ffn_gain,
    attn_router,
    ffn_router,
    query_weight,
    attn_out_weight,
    kv_weight,
    gate_up_weight,
    down_weight,
):
    micro, tok_rows, width = tokens.shape
    dp_count = lax.axis_size("dp")
    slots = lax.axis_size("expert")
    col = lax.axis_index("expert")
    group = lax.axis_index("dp")
    piece_rows = tok_rows // dp_count
    cap = tok_rows * TOP * 3 // (2 * slots)
    group_rows = tok_rows * slots
    all_rows = micro * group_rows
    home_rows = micro * tok_rows
    query_width = HEADS * HDIM
    own_heads = HEADS // slots
    own_width = own_heads * HDIM
    shard_rows = query_weight.shape[1]
    score_scale = HDIM ** (-0.5)
    core = group % 2
    chip = group // 2
    side = chip % 2
    chips = dp_count // 2
    lines = chips // 2
    quarter = FF // 4
    chip_rows = 2 * shard_rows

    both = jnp.stack([tokens, cotangent]).reshape(2 * micro, dp_count, piece_rows, width)
    both = lax.all_to_all(both.transpose(1, 0, 2, 3), "dp", split_axis=0, concat_axis=0, tiled=True)
    both = both.transpose(1, 0, 2, 3).reshape(2, micro, tok_rows, width)
    deal = (dealing[:, :, None] == jnp.arange(tok_rows, dtype=jnp.int32)).astype(bf16)
    work = jnp.einsum("mtr,bmrd->bmtd", deal, both, preferred_element_type=f32)
    x_home = work[0].reshape(home_rows, width)
    dy_home = work[1].reshape(home_rows, width)

    def columns_of(shard):
        pieces = shard.reshape(shard_rows, slots, own_width)
        parts = [
            swap(lax.dynamic_index_in_dim(pieces, col ^ k, 1, keepdims=False), "expert", k)
            if k
            else lax.dynamic_index_in_dim(pieces, col, 1, keepdims=False)
            for k in range(slots)
        ]
        out = jnp.zeros((shard_rows, query_width), shard.dtype)
        for k, part in enumerate(parts):
            out = lax.dynamic_update_slice_in_dim(out, part, (col ^ k) * own_width, 1)
        return out

    def slots_of(columns):
        pieces = columns.reshape(shard_rows, slots, own_width)
        out = jnp.zeros((shard_rows, query_width), columns.dtype)
        for k in range(slots):
            part = lax.dynamic_index_in_dim(pieces, col ^ k, 1, keepdims=False)
            part = swap(part, "expert", k) if k else part
            out = lax.dynamic_update_slice_in_dim(out, part, (col ^ k) * own_width, 1)
        return out

    half_slots = slots // 2
    first_pairs = [(c, 2 * c) for c in range(half_slots)]
    first_pairs += [(c, 2 * (c - half_slots) + 1) for c in range(half_slots, slots)]
    second_pairs = [(c, 2 * c + 1) for c in range(half_slots)]
    second_pairs += [(c, 2 * (c - half_slots)) for c in range(half_slots, slots)]
    holds_keys = col < half_slots
    even_col = col % 2 == 0
    low_kv, high_kv = kv_weight[:, :own_width], kv_weight[:, own_width:]
    first_got = lax.ppermute(jnp.where(holds_keys, low_kv, high_kv), "expert", first_pairs)
    second_got = lax.ppermute(jnp.where(holds_keys, high_kv, low_kv), "expert", second_pairs)
    own_kv = jnp.concatenate(
        [
            jnp.where(even_col, first_got, second_got),
            jnp.where(even_col, second_got, first_got),
        ],
        axis=1,
    )
    kv_full = lax.all_gather(own_kv, "dp", axis=0, tiled=True)
    query_full = lax.all_gather(columns_of(query_weight[0]), "dp", axis=0, tiled=True)
    out_full = lax.all_gather(columns_of(attn_out_weight[0]), "dp", axis=0, tiled=True)

    def quarter_of(half, part):
        start = (2 * half + part) * quarter
        return jnp.concatenate(
            [
                lax.dynamic_slice_in_dim(gate_up_weight[0], start, quarter, 1),
                lax.dynamic_slice_in_dim(gate_up_weight[0], FF + start, quarter, 1),
                lax.dynamic_slice_in_dim(down_weight[0], start, quarter, 1),
            ],
            axis=1,
        )

    def pair_rows(own, other):
        return jnp.concatenate(
            [jnp.where(core == 0, own, other), jnp.where(core == 0, other, own)], axis=0
        )

    keep_side = pair_rows(quarter_of(side, core), swap(quarter_of(side, 1 - core), "dp", 1))
    send_side = pair_rows(quarter_of(1 - side, core), swap(quarter_of(1 - side, 1 - core), "dp", 1))
    from_side = swap(send_side, "dp", 2)
    chunk_parts = [keep_side, from_side]
    for line in range(1, lines):
        chunk_parts.append(swap(keep_side, "dp", 4 * line))
        chunk_parts.append(swap(from_side, "dp", 4 * line))
    chunk_at = [chip ^ k for k in range(chips)]
    ffn_full = place(chunk_parts, chunk_at).reshape(width, 3 * quarter)
    gate_up_full = ffn_full[:, : 2 * quarter]
    down_full = ffn_full[:, 2 * quarter :]

    positions = jnp.arange(group_rows, dtype=jnp.int32)
    first_len = lax.dynamic_index_in_dim(seq_lengths[:, :, 0], group, 1, keepdims=True)
    in_second = positions[None, :] >= first_len
    places = positions[None, :] - jnp.where(in_second, first_len, 0)
    allowed = (positions[None, None, :] <= positions[None, :, None]) & (
        in_second[:, None, :] == in_second[:, :, None]
    )
    tables = rotation_tables(places.reshape(all_rows))

    def gather_rows(value):
        shaped = value.reshape(micro, tok_rows, -1)
        out = jnp.zeros((micro, group_rows, shaped.shape[-1]), value.dtype)
        for k in range(slots):
            part = swap(shaped, "expert", k) if k else shaped
            out = lax.dynamic_update_slice_in_dim(out, part, (col ^ k) * tok_rows, 1)
        return out.reshape(all_rows, -1)

    def scatter_rows(value):
        shaped = value.reshape(micro, group_rows, -1)
        total = None
        for k in range(slots):
            part = lax.dynamic_slice_in_dim(shaped, (col ^ k) * tok_rows, tok_rows, 1)
            if k:
                part = swap(part.astype(bf16), "expert", k)
            part = part.astype(f32)
            total = part if total is None else total + part
        return total.reshape(home_rows, -1)

    home_routes = lax.dynamic_slice_in_dim(ffn_routes, col * tok_rows, tok_rows, 1)
    home_slots = route_slots(home_routes, expert_table)
    packs = []
    before = jnp.tril(jnp.ones((tok_rows, tok_rows), bf16), -1)
    for k in range(slots):
        hits = jnp.any(home_slots == (col ^ k), axis=-1)
        rank = jnp.einsum("ts,ms->mt", before, hits.astype(bf16), preferred_element_type=f32)
        packs.append(
            hits[:, None, :]
            & (rank[:, None, :] == jnp.arange(cap, dtype=jnp.int32).astype(f32)[None, :, None])
        )
    packs = jnp.stack(packs)
    packs_low = packs.astype(bf16)
    pack_rows = micro * cap
    sent_rows = slots * pack_rows

    def send_packed(value):
        packed = jnp.einsum(
            "kmct,mtd->kmcd", packs_low, value.reshape(micro, tok_rows, -1), preferred_element_type=f32
        ).astype(bf16)
        parts = [swap(packed[k], "expert", k) if k else packed[k] for k in range(slots)]
        return jnp.stack(parts).reshape(sent_rows, -1)

    def quad_rows(value):
        near = swap(value, "dp", 1)
        far = swap(value, "dp", 2)
        across = swap(far, "dp", 1)
        return jnp.concatenate([value, near, far, across], axis=0)

    def quad_sum(value):
        own, near, far, across = jnp.split(value, 4, axis=0)
        far_sum = far.astype(f32) + swap(across.astype(bf16), "dp", 1).astype(f32)
        own_sum = own.astype(f32) + swap(near.astype(bf16), "dp", 1).astype(f32)
        return own_sum + swap(far_sum.astype(bf16), "dp", 2).astype(f32)

    def return_packed(value):
        shaped = value.astype(bf16).reshape(slots, micro, cap, -1)
        parts = [swap(shaped[k], "expert", k) if k else shaped[k] for k in range(slots)]
        return jnp.stack(parts)

    def unpack(packed, scale):
        total = None
        for k in range(slots):
            rows = jnp.einsum("mct,mcd->mtd", packs_low[k], packed[k], preferred_element_type=f32)
            rows = rows.reshape(home_rows, -1) * take(scale.T, col ^ k)[:, None]
            total = rows if total is None else total + rows
        return total

    grad_rows = quad_rows(send_packed(dy_home.astype(bf16)))

    gain_one = attn_gain.astype(f32)
    gain_two = ffn_gain.astype(f32)
    normed_one, scale_one = normalize(x_home)
    hidden_one_home = (normed_one * gain_one).astype(bf16)
    hidden_one = gather_rows(hidden_one_home)
    logits_one = dot(hidden_one, attn_router)
    gates_one, matches_one, chosen_one, gate_vals_one = route_gates(
        logits_one, attn_routes.reshape(all_rows, TOP), expert_table
    )
    hits_one = jnp.any(chosen_one, axis=1)
    kv_part = dot(hidden_one, kv_full).astype(bf16)
    key_rot = rotate(kv_part[:, :own_width].astype(f32), tables, False).astype(bf16)
    query_rot = rotate(dot(hidden_one, query_full), tables, False).astype(bf16)
    keys = key_rot.reshape(micro, group_rows, own_heads, HDIM)
    values = kv_part[:, own_width:].reshape(micro, group_rows, own_heads, HDIM)
    queries = query_rot.reshape(micro, group_rows, slots, own_heads, HDIM)
    raw = jnp.einsum("mrshd,mkhd->mshrk", queries, keys, preferred_element_type=f32)
    scores = jnp.where(allowed[:, None, None], raw * score_scale, very_low)
    hits_grid = hits_one.reshape(micro, group_rows, slots).transpose(0, 2, 1)
    row_peak = jnp.max(scores, axis=-1, keepdims=True)
    own_peak = jnp.max(
        jnp.where(hits_grid[:, :, None, :], row_peak[..., 0], very_low), axis=(0, 3)
    )
    expo = jnp.exp(scores - row_peak)
    probs = expo / jnp.sum(expo, axis=-1, keepdims=True)
    probs_low = probs.astype(bf16)
    attn_vals = jnp.einsum("mshrk,mkhd->mrshd", probs_low, values, preferred_element_type=f32)
    attn_vals = attn_vals.astype(bf16).reshape(all_rows, slots, own_width)
    gated_vals = (gates_one[:, :, None] * attn_vals.astype(f32)).astype(bf16)
    gated_vals = gated_vals.reshape(all_rows, query_width)
    attn_home = scatter_rows(dot_t(gated_vals, out_full))

    resid = x_home + attn_home
    normed_two, scale_two = normalize(resid)
    hidden_two = (normed_two * gain_two).astype(bf16)
    logits_two = dot(hidden_two, ffn_router)
    gates_two, matches_two, chosen_two, gate_vals_two = route_gates(
        logits_two, home_routes.reshape(home_rows, TOP), expert_table
    )
    hidden_rows = quad_rows(send_packed(hidden_two))
    gates_by_slot = gates_two.reshape(micro, tok_rows, slots)
    gate_parts = []
    for k in range(slots):
        gate_col = lax.dynamic_index_in_dim(gates_by_slot, col ^ k, 2, keepdims=False)
        part = jnp.sum(jnp.where(packs[k], gate_col[:, None, :], 0.0), axis=-1).reshape(pack_rows)
        gate_parts.append(swap(part, "expert", k) if k else part)
    gate_rows = quad_rows(jnp.concatenate(gate_parts))

    joint = dot(hidden_rows, gate_up_full)
    gate_pre, up_pre = joint[:, :quarter], joint[:, quarter:]
    sigma = jax.nn.sigmoid(gate_pre)
    silu_vals = gate_pre * sigma
    active = (silu_vals * up_pre).astype(bf16)
    active_grad = dot(grad_rows, down_full)
    gate_grad = active_grad * up_pre * sigma * (1.0 + gate_pre * (1.0 - sigma))
    joint_grad = jnp.concatenate([gate_grad, active_grad * silu_vals], axis=1).astype(bf16)
    slot_part_two = jnp.sum(active.astype(f32) * active_grad, axis=-1, keepdims=True)
    slot_part_two = jnp.pad(slot_part_two, ((0, 0), (0, HDIM - 1))).astype(bf16)
    hidden_part = jnp.concatenate(
        [dot_t(joint_grad, gate_up_full).astype(bf16), slot_part_two], axis=1
    )
    back_packed = return_packed(quad_sum(hidden_part))
    slot_two_grad = jnp.zeros((slots, home_rows), f32)
    for k in range(slots):
        rows = jnp.sum(
            jnp.where(packs[k], back_packed[k][:, :, width].astype(f32)[:, :, None], 0.0), axis=1
        )
        slot_two_grad = lax.dynamic_update_index_in_dim(
            slot_two_grad, rows.reshape(home_rows), col ^ k, 0
        )
    hidden_two_grad = unpack(back_packed[..., :width], gates_two)
    logit_two_grad = gate_back(slot_two_grad.T, gate_vals_two, matches_two, chosen_two).astype(bf16)
    hidden_two_grad = hidden_two_grad + dot_t(logit_two_grad, ffn_router)
    router_two_grad = t_dot(logit_two_grad, hidden_two)
    gain_two_grad = jnp.sum(hidden_two_grad * normed_two, axis=0)
    resid_grad = dy_home + norm_back(hidden_two_grad * gain_two, normed_two, scale_two)

    ffn_packed = return_packed(quad_sum(dot_t(active, down_full)))
    out_home = (resid + unpack(ffn_packed, gates_two)).astype(bf16)

    resid_grad_all = gather_rows(resid_grad.astype(bf16))
    vals_grad = dot(resid_grad_all, out_full).reshape(all_rows, slots, own_width)
    slot_part_one = jnp.sum(attn_vals.astype(f32) * vals_grad, axis=-1)
    vals_grad = (gates_one[:, :, None] * vals_grad).astype(bf16)
    vals_grad = vals_grad.reshape(micro, group_rows, slots, own_heads, HDIM)
    prob_grad = jnp.einsum("mrshd,mkhd->mshrk", vals_grad, values, preferred_element_type=f32)
    inner_sum = jnp.sum(probs * prob_grad, axis=-1, keepdims=True)
    score_grad = (probs * (prob_grad - inner_sum) * score_scale).astype(bf16)
    query_rot_grad = jnp.einsum("mshrk,mkhd->mrshd", score_grad, keys, preferred_element_type=f32)
    query_grad = rotate(query_rot_grad.reshape(all_rows, query_width), tables, True).astype(bf16)
    key_rot_grad = jnp.einsum("mshrk,mrshd->mkhd", score_grad, queries, preferred_element_type=f32)
    value_grad = jnp.einsum("mshrk,mrshd->mkhd", probs_low, vals_grad, preferred_element_type=f32)
    key_grad = rotate(key_rot_grad.reshape(all_rows, own_width), tables, True)
    kv_grad = jnp.concatenate([key_grad, value_grad.reshape(all_rows, own_width)], axis=1)
    kv_grad = kv_grad.astype(bf16)
    hidden_one_part = dot_t(query_grad, query_full) + dot_t(kv_grad, kv_full)
    slot_part_one = jnp.pad(slot_part_one, ((0, 0), (0, HDIM - slots)))
    back_one = scatter_rows(
        jnp.concatenate([hidden_one_part.astype(bf16), slot_part_one.astype(bf16)], axis=1)
    )
    hidden_one_grad, slot_one_grad = back_one[:, :width], back_one[:, width : width + slots]

    def own(value):
        shaped = value.reshape((micro, group_rows) + value.shape[1:])
        part = lax.dynamic_slice_in_dim(shaped, col * tok_rows, tok_rows, 1)
        return part.reshape((home_rows,) + value.shape[1:])

    logit_one_grad = gate_back(
        slot_one_grad, own(gate_vals_one), own(matches_one), own(chosen_one)
    ).astype(bf16)
    hidden_one_grad = hidden_one_grad + dot_t(logit_one_grad, attn_router)
    router_one_grad = t_dot(logit_one_grad, hidden_one_home)
    gain_one_grad = jnp.sum(hidden_one_grad * normed_one, axis=0)
    in_home = resid_grad + norm_back(hidden_one_grad * gain_one, normed_one, scale_one)

    results = jnp.stack([out_home, in_home.astype(bf16)]).reshape(2, micro, tok_rows, width)
    results = jnp.einsum("mtr,bmtd->bmrd", deal, results, preferred_element_type=f32).astype(bf16)
    results = results.reshape(2 * micro, dp_count, piece_rows, width).transpose(1, 0, 2, 3)
    results = lax.all_to_all(results, "dp", split_axis=0, concat_axis=0, tiled=True)
    results = results.transpose(1, 0, 2, 3).reshape(2, micro, tok_rows, width)

    scaled_hidden = (hidden_rows.astype(f32) * gate_rows[:, None]).astype(bf16)
    scaled_grad = (grad_rows.astype(f32) * gate_rows[:, None]).astype(bf16)

    def chunk_grad(k):
        start = (chip ^ k) * chip_rows
        left = lax.dynamic_slice_in_dim(scaled_hidden, start, chip_rows, 1)
        right = lax.dynamic_slice_in_dim(scaled_grad, start, chip_rows, 1)
        return jnp.concatenate([t_dot(left, joint_grad), t_dot(right, active)], axis=1)

    side_grad, keep_grad = chunk_grad(1), chunk_grad(0)
    for line in range(1, lines):
        side_grad = side_grad + swap(chunk_grad(2 * line + 1).astype(bf16), "dp", 4 * line).astype(f32)
        keep_grad = keep_grad + swap(chunk_grad(2 * line).astype(bf16), "dp", 4 * line).astype(f32)
    other_grad = swap(side_grad.astype(bf16), "dp", 2)
    pair = jnp.stack([keep_grad.astype(bf16), other_grad]).reshape(2, 2, shard_rows, 3 * quarter)
    own_pair = lax.dynamic_index_in_dim(pair, core, 1, keepdims=False)
    near_pair = swap(lax.dynamic_index_in_dim(pair, 1 - core, 1, keepdims=False), "dp", 1)
    by_core = [jnp.where(core == 0, own_pair, near_pair), jnp.where(core == 0, near_pair, own_pair)]
    by_side = [[jnp.where(side == s, part[0], part[1]) for part in by_core] for s in range(2)]
    blocks = [part for row in by_side for part in row]
    gate_up_grad = jnp.concatenate(
        [b[:, :quarter] for b in blocks] + [b[:, quarter : 2 * quarter] for b in blocks], axis=1
    ).astype(f32)
    down_grad = jnp.concatenate([b[:, 2 * quarter :] for b in blocks], axis=1).astype(f32)

    def reduced(value):
        return lax.psum_scatter(value.astype(bf16), "dp", scatter_dimension=0, tiled=True)

    out_grad = slots_of(reduced(t_dot(resid_grad_all, gated_vals))).astype(f32)
    query_out = slots_of(reduced(t_dot(hidden_one, query_grad))).astype(f32)
    kv_own = reduced(t_dot(hidden_one, kv_grad))
    key_part, value_part = kv_own[:, :own_width], kv_own[:, own_width:]
    first_back = lax.ppermute(
        jnp.where(even_col, key_part, value_part), "expert", [(b, a) for a, b in first_pairs]
    )
    second_back = lax.ppermute(
        jnp.where(even_col, value_part, key_part), "expert", [(b, a) for a, b in second_pairs]
    )
    kv_out = jnp.concatenate(
        [
            jnp.where(holds_keys, first_back, second_back),
            jnp.where(holds_keys, second_back, first_back),
        ],
        axis=1,
    ).astype(f32)

    sums = lax.psum(
        jnp.concatenate(
            [gain_one_grad[None], gain_two_grad[None], router_one_grad, router_two_grad], axis=0
        ),
        ("dp", "expert"),
    )
    peaks = lax.all_gather(own_peak, "dp", axis=0)
    peaks = jnp.max(peaks, axis=0)
    peaks_all = lax.all_gather(peaks, "expert", axis=1, tiled=True)
    limit = clip_limit[0].astype(f32)
    factor = limit / jnp.maximum(peaks_all, limit)
    query_scale = jnp.repeat(jnp.sqrt(take(factor, col)), HDIM)
    query_clipped = (query_weight.astype(f32) * query_scale[None, None, :]).astype(bf16)
    full_scale = jnp.concatenate(
        [jnp.repeat(jnp.sqrt(jnp.min(factor, axis=0)), HDIM), jnp.ones((query_width,), f32)]
    )
    piece_width = kv_weight.shape[1]
    piece_scale = lax.dynamic_slice_in_dim(full_scale, col * piece_width, piece_width)
    kv_clipped = (kv_weight.astype(f32) * piece_scale[None, :]).astype(bf16)
    return (
        results[0],
        results[1],
        sums[0],
        sums[1],
        sums[2 : 2 + slots].T,
        sums[2 + slots :].T,
        query_out[None],
        out_grad[None],
        kv_out,
        gate_up_grad[None],
        down_grad[None],
        query_clipped,
        kv_clipped,
    )


def solution(mesh):
    placed = (
        P(None, ("dp", "expert"), None),
        P(None, ("dp", "expert"), None),
        P(),
        P(None, ("dp", "expert")),
        P(None, "dp", None),
        P(None, "dp", None),
        P(),
        P(),
        P(),
        P(),
        P(),
        P(),
        P("expert", "dp", None),
        P("expert", "dp", None),
        P("dp", "expert"),
        P("expert", "dp", None),
        P("expert", "dp", None),
    )
    return jax.shard_map(
        local,
        mesh=mesh,
        in_specs=placed,
        out_specs=(
            P(None, ("dp", "expert"), None),
            P(None, ("dp", "expert"), None),
            P(),
            P(),
            P(),
            P(),
            P("expert", "dp", None),
            P("expert", "dp", None),
            P("dp", "expert"),
            P("expert", "dp", None),
            P("expert", "dp", None),
            P("expert", "dp", None),
            P("dp", "expert"),
        ),
        check_vma=False,
    )
```

```python
import jax
import jax.numpy as jnp
from jax import lax
from jax.experimental import pallas as pl
from jax.experimental.pallas import tpu as pltpu
from jax.sharding import PartitionSpec as P

HEADS = 16
HDIM = 128
FF = 5632
TOP = 2

eps_norm = 1e-06
rope_base = 10000.0
very_low = -1e30

f32 = jnp.float32
bf16 = jnp.bfloat16


def dot(left, right):
    return jnp.dot(left, right, preferred_element_type=f32)


def dot_t(left, right):
    return lax.dot_general(left, right, (((1,), (1,)), ((), ())), preferred_element_type=f32)


def t_dot(left, right):
    return lax.dot_general(left, right, (((0,), (0,)), ((), ())), preferred_element_type=f32)


def swap(value, axis, step):
    count = lax.axis_size(axis)
    return lax.ppermute(value, axis, [(i, i ^ step) for i in range(count)])


def take(stacked, index):
    return lax.dynamic_index_in_dim(stacked, index, 0, keepdims=False)


def place(parts, positions):
    out = jnp.zeros((len(parts),) + parts[0].shape, parts[0].dtype)
    for part, position in zip(parts, positions):
        out = lax.dynamic_update_index_in_dim(out, part, position, 0)
    return out


def after(value, *others):
    return lax.optimization_barrier((value, *others))[0]


def spread(value, combine):
    for axis in ("expert", "dp"):
        step = 1
        while step < lax.axis_size(axis):
            value = combine(value, swap(value, axis, step))
            step *= 2
    return value


def rotation_tables(places):
    half_dim = HDIM // 2
    frequency = rope_base ** (-jnp.arange(half_dim, dtype=f32) * 2.0 / HDIM)
    angles = places.astype(f32)[:, None] * frequency[None, :]
    cosine, sine = jnp.cos(angles), jnp.sin(angles)
    return (
        jnp.concatenate([cosine, cosine], axis=1),
        jnp.concatenate([-sine, sine], axis=1),
    )


def turn(values, cosine, sine):
    return values * cosine + pltpu.roll(values, HDIM // 2, 1) * sine


def lane_value(table, lane):
    lanes = lax.broadcasted_iota(jnp.int32, table.shape, 1)
    return jnp.sum(jnp.where(lanes == lane, table, 0.0), axis=1, keepdims=True)


def allowed_pairs(rows, first_len):
    query_at = lax.broadcasted_iota(jnp.int32, (rows, rows), 0)
    key_at = lax.broadcasted_iota(jnp.int32, (rows, rows), 1)
    return (key_at <= query_at) & ((key_at >= first_len) | (query_at < first_len))


def forward_kernel(
    lens, query, key, value, cosine, sine, gates, hits,
    vals_out, gated_out, query_out, key_out, total_out, peak_out,
):
    m, h, s = pl.program_id(0), pl.program_id(1), pl.program_id(2)
    slot_count = pl.num_programs(2)
    rows = query.shape[0]
    lane = h * slot_count + s

    @pl.when(lane == 0)
    def _():
        total_out[...] = jnp.zeros_like(total_out)
        peak_out[...] = jnp.full_like(peak_out, very_low)

    @pl.when(s == 0)
    def _():
        key_out[...] = turn(key[...].astype(f32), cosine[...], sine[...]).astype(bf16)

    turned = turn(query[...], cosine[...], sine[...]).astype(bf16)
    query_out[...] = turned
    raw = dot_t(turned, key_out[...])
    scores = jnp.where(allowed_pairs(rows, lens[m]), raw * HDIM ** (-0.5), very_low)
    row_peak = jnp.max(scores, axis=1, keepdims=True)
    expo = jnp.exp(scores - row_peak)
    denom = jnp.sum(expo, axis=1, keepdims=True)
    probs = expo / denom
    vals = dot(probs.astype(bf16), value[...]).astype(bf16)
    vals_out[...] = vals
    gated_out[...] = (lane_value(gates[...], s) * vals.astype(f32)).astype(bf16)
    lanes = lax.broadcasted_iota(jnp.int32, total_out.shape, 1)
    total_out[...] = jnp.where(lanes == lane, row_peak + jnp.log(denom), total_out[...])
    seen = jnp.where(lane_value(hits[...], s) > 0.0, row_peak, very_low)
    peak_lanes = lax.broadcasted_iota(jnp.int32, peak_out.shape, 1)
    peak_out[...] = jnp.where(
        peak_lanes == lane, jnp.max(seen, axis=0, keepdims=True), peak_out[...]
    )


def backward_kernel(
    lens, query, key, value, vals, vals_grad, cosine, sine, gates, total,
    query_grad, key_grad, value_grad, gate_grad, key_sum, value_sum,
):
    m, h, s = pl.program_id(0), pl.program_id(1), pl.program_id(2)
    slot_count = pl.num_programs(2)
    rows = query.shape[0]
    lane = h * slot_count + s

    @pl.when(lane == 0)
    def _():
        gate_grad[...] = jnp.zeros_like(gate_grad)

    @pl.when(s == 0)
    def _():
        key_sum[...] = jnp.zeros_like(key_sum)
        value_sum[...] = jnp.zeros_like(value_sum)

    full_grad = vals_grad[...]
    lanes = lax.broadcasted_iota(jnp.int32, gate_grad.shape, 1)
    slot_sum = jnp.sum(vals[...].astype(f32) * full_grad, axis=1, keepdims=True)
    gate_grad[...] += jnp.where(lanes == s, slot_sum, 0.0)
    gated_grad = (lane_value(gates[...], s) * full_grad).astype(bf16)
    raw = dot_t(query[...], key[...])
    scores = jnp.where(allowed_pairs(rows, lens[m]), raw * HDIM ** (-0.5), very_low)
    probs = jnp.exp(scores - lane_value(total[...], lane))
    prob_grad = dot_t(gated_grad, value[...])
    inner = jnp.sum(probs * prob_grad, axis=1, keepdims=True)
    score_grad = (probs * (prob_grad - inner) * HDIM ** (-0.5)).astype(bf16)
    back_sine = -sine[...]
    turned = dot(score_grad, key[...])
    query_grad[...] = turn(turned, cosine[...], back_sine).astype(bf16)
    key_sum[...] += t_dot(score_grad, query[...])
    value_sum[...] += t_dot(probs.astype(bf16), gated_grad)

    @pl.when(s == slot_count - 1)
    def _():
        key_grad[...] = turn(key_sum[...], cosine[...], back_sine).astype(bf16)
        value_grad[...] = value_sum[...].astype(bf16)


def attention_specs(own_heads, rows):
    def block(index):
        return pl.BlockSpec((rows, HDIM), index)

    return {
        "query": block(lambda m, h, s, lens: (m, s * own_heads + h)),
        "key": block(lambda m, h, s, lens: (m, h)),
        "value": block(lambda m, h, s, lens: (m, own_heads + h)),
        "rows": block(lambda m, h, s, lens: (m, 0)),
        "peak": pl.BlockSpec((8, HDIM), lambda m, h, s, lens: (m, 0)),
    }


def attention_forward(lens, query, joint_kv, tables, gates, hits, own_heads, rows):
    micro = lens.shape[0]
    slots = query.shape[1] // (own_heads * HDIM)
    at = attention_specs(own_heads, rows)
    shape = jax.ShapeDtypeStruct
    total_rows = micro * rows
    return pl.pallas_call(
        forward_kernel,
        grid_spec=pltpu.PrefetchScalarGridSpec(
            num_scalar_prefetch=1,
            grid=(micro, own_heads, slots),
            in_specs=[at["query"], at["key"], at["value"]] + [at["rows"]] * 4,
            out_specs=[at["query"]] * 3 + [at["key"], at["rows"], at["peak"]],
        ),
        out_shape=[shape(query.shape, bf16)] * 3
        + [
            shape((total_rows, own_heads * HDIM), bf16),
            shape((total_rows, HDIM), f32),
            shape((micro * 8, HDIM), f32),
        ],
        cost_estimate=pl.CostEstimate(
            flops=4 * rows * rows * HDIM * micro * HEADS,
            bytes_accessed=14 * query.size,
            transcendentals=rows * rows * micro * HEADS,
        ),
        name="attention_forward",
    )(lens, query, joint_kv, joint_kv, tables[0], tables[1], gates, hits)


def attention_backward(
    lens, query, key, joint_kv, vals, vals_grad, tables, gates, total, own_heads, rows
):
    micro = lens.shape[0]
    slots = query.shape[1] // (own_heads * HDIM)
    at = attention_specs(own_heads, rows)
    shape = jax.ShapeDtypeStruct
    total_rows = micro * rows
    return pl.pallas_call(
        backward_kernel,
        grid_spec=pltpu.PrefetchScalarGridSpec(
            num_scalar_prefetch=1,
            grid=(micro, own_heads, slots),
            in_specs=[at["query"], at["key"], at["value"], at["query"], at["query"]]
            + [at["rows"]] * 4,
            out_specs=[at["query"], at["key"], at["key"], at["rows"]],
            scratch_shapes=[pltpu.VMEM((rows, HDIM), f32)] * 2,
        ),
        out_shape=[shape(query.shape, bf16)]
        + [shape((total_rows, own_heads * HDIM), bf16)] * 2
        + [shape((total_rows, HDIM), f32)],
        cost_estimate=pl.CostEstimate(
            flops=10 * rows * rows * HDIM * micro * HEADS,
            bytes_accessed=14 * query.size,
            transcendentals=rows * rows * micro * HEADS,
        ),
        name="attention_backward",
    )(lens, query, key, joint_kv, vals, vals_grad, tables[0], tables[1], gates, total)


def normalize(values):
    row_scale = lax.rsqrt(jnp.mean(values * values, axis=-1, keepdims=True) + eps_norm)
    return values * row_scale, row_scale


def norm_back(grad_hat, normed, row_scale):
    return row_scale * (grad_hat - normed * jnp.mean(grad_hat * normed, axis=-1, keepdims=True))


def route_gates(logits, routes, expert_table):
    expert_ids = jnp.arange(expert_table.shape[0], dtype=jnp.int32)
    matches = routes[:, :, None] == expert_ids[None, None, :]
    picked = jnp.sum(jnp.where(matches, logits[:, None, :], 0.0), axis=-1)
    gate_vals = jax.nn.softmax(picked, axis=-1)
    slot_ids = route_slots(routes, expert_table)
    chosen = slot_ids[:, :, None] == expert_ids[None, None, :]
    gates = jnp.sum(jnp.where(chosen, gate_vals[:, :, None], 0.0), axis=1)
    return gates, matches, chosen, gate_vals


def route_slots(routes, expert_table):
    expert_ids = jnp.arange(expert_table.shape[0], dtype=jnp.int32)
    matches = routes[..., None] == expert_ids
    return jnp.sum(jnp.where(matches, expert_table, 0), axis=-1)


def gate_back(slot_grad, gate_vals, matches, chosen):
    picked = jnp.sum(jnp.where(chosen, slot_grad[:, None, :], 0.0), axis=-1)
    inner_sum = jnp.sum(gate_vals * picked, axis=-1, keepdims=True)
    picked_grad = gate_vals * (picked - inner_sum)
    return jnp.sum(jnp.where(matches, picked_grad[:, :, None], 0.0), axis=1)


def local(
    tokens,
    cotangent,
    seq_lengths,
    dealing,
    attn_routes,
    ffn_routes,
    expert_table,
    clip_limit,
    attn_gain,
    ffn_gain,
    attn_router,
    ffn_router,
    query_weight,
    attn_out_weight,
    kv_weight,
    gate_up_weight,
    down_weight,
):
    micro, tok_rows, width = tokens.shape
    dp_count = lax.axis_size("dp")
    slots = lax.axis_size("expert")
    col = lax.axis_index("expert")
    group = lax.axis_index("dp")
    piece_rows = tok_rows // dp_count
    cap = tok_rows * TOP * 3 // (2 * slots)
    group_rows = tok_rows * slots
    all_rows = micro * group_rows
    home_rows = micro * tok_rows
    query_width = HEADS * HDIM
    own_heads = HEADS // slots
    own_width = own_heads * HDIM
    shard_rows = query_weight.shape[1]
    score_scale = HDIM ** (-0.5)
    core = group % 2
    chip = group // 2
    side = chip % 2
    chips = dp_count // 2
    lines = chips // 2
    quarter = FF // 4
    chip_rows = 2 * shard_rows

    both = jnp.stack([tokens, cotangent]).reshape(2 * micro, dp_count, piece_rows, width)
    both = lax.all_to_all(both.transpose(1, 0, 2, 3), "dp", split_axis=0, concat_axis=0, tiled=True)
    both = both.transpose(1, 0, 2, 3).reshape(2, micro, tok_rows, width)
    deal = (dealing[:, :, None] == jnp.arange(tok_rows, dtype=jnp.int32)).astype(bf16)
    work = jnp.einsum("mtr,bmrd->bmtd", deal, both, preferred_element_type=f32)
    x_home = work[0].reshape(home_rows, width)
    dy_home = work[1].reshape(home_rows, width)

    def columns_of(shard):
        pieces = shard.reshape(shard_rows, slots, own_width)
        parts = [
            swap(lax.dynamic_index_in_dim(pieces, col ^ k, 1, keepdims=False), "expert", k)
            if k
            else lax.dynamic_index_in_dim(pieces, col, 1, keepdims=False)
            for k in range(slots)
        ]
        out = jnp.zeros((shard_rows, query_width), shard.dtype)
        for k, part in enumerate(parts):
            out = lax.dynamic_update_slice_in_dim(out, part, (col ^ k) * own_width, 1)
        return out

    def slots_of(columns):
        pieces = columns.reshape(shard_rows, slots, own_width)
        out = jnp.zeros((shard_rows, query_width), columns.dtype)
        for k in range(slots):
            part = lax.dynamic_index_in_dim(pieces, col ^ k, 1, keepdims=False)
            part = swap(part, "expert", k) if k else part
            out = lax.dynamic_update_slice_in_dim(out, part, (col ^ k) * own_width, 1)
        return out

    half_slots = slots // 2
    first_pairs = [(c, 2 * c) for c in range(half_slots)]
    first_pairs += [(c, 2 * (c - half_slots) + 1) for c in range(half_slots, slots)]
    second_pairs = [(c, 2 * c + 1) for c in range(half_slots)]
    second_pairs += [(c, 2 * (c - half_slots)) for c in range(half_slots, slots)]
    holds_keys = col < half_slots
    even_col = col % 2 == 0
    low_kv, high_kv = kv_weight[:, :own_width], kv_weight[:, own_width:]
    first_got = lax.ppermute(jnp.where(holds_keys, low_kv, high_kv), "expert", first_pairs)
    second_got = lax.ppermute(jnp.where(holds_keys, high_kv, low_kv), "expert", second_pairs)
    own_kv = jnp.concatenate(
        [
            jnp.where(even_col, first_got, second_got),
            jnp.where(even_col, second_got, first_got),
        ],
        axis=1,
    )
    kv_full = lax.all_gather(own_kv, "dp", axis=0, tiled=True)
    query_full = lax.all_gather(columns_of(query_weight[0]), "dp", axis=0, tiled=True)
    out_full = lax.all_gather(columns_of(attn_out_weight[0]), "dp", axis=0, tiled=True)

    def quarter_of(half, part):
        start = (2 * half + part) * quarter
        return [
            lax.dynamic_slice_in_dim(gate_up_weight[0], start, quarter, 1),
            lax.dynamic_slice_in_dim(gate_up_weight[0], FF + start, quarter, 1),
            lax.dynamic_slice_in_dim(down_weight[0], start, quarter, 1),
        ]

    def half_of(half):
        return jnp.concatenate(quarter_of(half, 0) + quarter_of(half, 1), axis=1)

    def part_of(piece, part):
        return lax.dynamic_slice_in_dim(piece, part * 3 * quarter, 3 * quarter, 1)

    keep_side = half_of(side)
    from_side = swap(half_of(1 - side), "dp", 2)
    keep_lines = [swap(keep_side, "dp", 4 * line) for line in range(1, lines)]
    from_lines = []
    for line in range(1, lines):
        other_part = swap(part_of(from_side, 1 - core), "dp", 4 * line)
        from_lines.append((swap(part_of(from_side, core), "dp", 4 * line), other_part))

    def pair_rows(own, other):
        near = swap(other, "dp", 1)
        return jnp.concatenate(
            [jnp.where(core == 0, own, near), jnp.where(core == 0, near, own)], axis=0
        )

    chunk_parts = [
        pair_rows(part_of(piece, core), part_of(piece, 1 - core)) for piece in (keep_side, from_side)
    ]
    for line in range(1, lines):
        piece = keep_lines[line - 1]
        chunk_parts.append(pair_rows(part_of(piece, core), part_of(piece, 1 - core)))
        chunk_parts.append(pair_rows(*from_lines[line - 1]))
    chunk_at = [chip ^ k for k in range(chips)]
    ffn_full = place(chunk_parts, chunk_at).reshape(width, 3 * quarter)
    gate_up_full = ffn_full[:, : 2 * quarter]
    down_full = ffn_full[:, 2 * quarter :]

    positions = jnp.arange(group_rows, dtype=jnp.int32)
    first_len = lax.dynamic_index_in_dim(seq_lengths[:, :, 0], group, 1, keepdims=True)
    in_second = positions[None, :] >= first_len
    places = positions[None, :] - jnp.where(in_second, first_len, 0)
    tables = rotation_tables(places.reshape(all_rows))

    def gather_rows(value):
        shaped = value.reshape(micro, tok_rows, -1)
        out = jnp.zeros((micro, group_rows, shaped.shape[-1]), value.dtype)
        for k in range(slots):
            part = swap(shaped, "expert", k) if k else shaped
            out = lax.dynamic_update_slice_in_dim(out, part, (col ^ k) * tok_rows, 1)
        return out.reshape(all_rows, -1)

    def scatter_rows(value):
        shaped = value.reshape(micro, group_rows, -1)
        total = None
        for k in range(slots):
            part = lax.dynamic_slice_in_dim(shaped, (col ^ k) * tok_rows, tok_rows, 1)
            if k:
                part = swap(part.astype(bf16), "expert", k)
            part = part.astype(f32)
            total = part if total is None else total + part
        return total.reshape(home_rows, -1)

    home_routes = lax.dynamic_slice_in_dim(ffn_routes, col * tok_rows, tok_rows, 1)
    home_slots = route_slots(home_routes, expert_table)
    packs = []
    before = jnp.tril(jnp.ones((tok_rows, tok_rows), bf16), -1)
    for k in range(slots):
        hits = jnp.any(home_slots == (col ^ k), axis=-1)
        rank = jnp.einsum("ts,ms->mt", before, hits.astype(bf16), preferred_element_type=f32)
        packs.append(
            hits[:, None, :]
            & (rank[:, None, :] == jnp.arange(cap, dtype=jnp.int32).astype(f32)[None, :, None])
        )
    packs = jnp.stack(packs)
    packs_low = packs.astype(bf16)
    pack_rows = micro * cap
    sent_rows = slots * pack_rows

    def send_packed(value):
        packed = jnp.einsum(
            "kmct,mtd->kmcd", packs_low, value.reshape(micro, tok_rows, -1), preferred_element_type=f32
        ).astype(bf16)
        parts = [swap(packed[k], "expert", k) if k else packed[k] for k in range(slots)]
        return jnp.stack(parts).reshape(sent_rows, -1)

    def quad_rows(value):
        near = swap(value, "dp", 1)
        far = swap(value, "dp", 2)
        across = swap(far, "dp", 1)
        return jnp.concatenate([value, near, far, across], axis=0)

    def quad_sum(value):
        own, near, far, across = jnp.split(value, 4, axis=0)
        far_sum = far.astype(f32) + swap(across.astype(bf16), "dp", 1).astype(f32)
        own_sum = own.astype(f32) + swap(near.astype(bf16), "dp", 1).astype(f32)
        return own_sum + swap(far_sum.astype(bf16), "dp", 2).astype(f32)

    def return_packed(value):
        shaped = value.astype(bf16).reshape(slots, micro, cap, -1)
        parts = [swap(shaped[k], "expert", k) if k else shaped[k] for k in range(slots)]
        return jnp.stack(parts)

    def unpack(packed, scale):
        total = None
        for k in range(slots):
            rows = jnp.einsum("mct,mcd->mtd", packs_low[k], packed[k], preferred_element_type=f32)
            rows = rows.reshape(home_rows, -1) * take(scale.T, col ^ k)[:, None]
            total = rows if total is None else total + rows
        return total

    grad_sent = send_packed(dy_home.astype(bf16))
    grad_rows = quad_rows(grad_sent)

    gain_one = attn_gain.astype(f32)
    gain_two = ffn_gain.astype(f32)
    normed_one, scale_one = normalize(x_home)
    hidden_one_home = (normed_one * gain_one).astype(bf16)
    hidden_one = gather_rows(hidden_one_home)
    logits_one = dot(hidden_one, attn_router)
    gates_one, matches_one, chosen_one, gate_vals_one = route_gates(
        logits_one, attn_routes.reshape(all_rows, TOP), expert_table
    )
    hits_one = jnp.any(chosen_one, axis=1).astype(f32)

    def wide(value):
        return jnp.pad(value, ((0, 0), (0, HDIM - value.shape[1])))

    kv_part = dot(hidden_one, kv_full).astype(bf16)
    query_part = dot(after(hidden_one, from_side, *keep_lines), query_full)
    lens = first_len[:, 0].astype(jnp.int32)
    gates_wide = wide(gates_one)
    attn_vals, gated_vals, query_rot, key_rot, log_total, peaks = attention_forward(
        lens, query_part, kv_part, tables, gates_wide, wide(hits_one), own_heads, group_rows
    )
    peaks = jnp.max(peaks, axis=0)[: own_heads * slots].reshape(own_heads, slots).T
    peak_table = lax.dynamic_update_slice_in_dim(
        jnp.full((slots, HEADS), very_low, f32), peaks, col * own_heads, 1
    )
    peaks_all = spread(peak_table, jnp.maximum)
    gated_vals = after(gated_vals, grad_sent, *[pair[1] for pair in from_lines])
    attn_home = scatter_rows(dot_t(gated_vals, out_full))

    resid = x_home + attn_home
    normed_two, scale_two = normalize(resid)
    hidden_two = (normed_two * gain_two).astype(bf16)
    logits_two = dot(hidden_two, ffn_router)
    gates_two, matches_two, chosen_two, gate_vals_two = route_gates(
        logits_two, home_routes.reshape(home_rows, TOP), expert_table
    )
    hidden_rows = quad_rows(send_packed(after(hidden_two, grad_rows)))
    gates_by_slot = gates_two.reshape(micro, tok_rows, slots)
    gate_parts = []
    for k in range(slots):
        gate_col = lax.dynamic_index_in_dim(gates_by_slot, col ^ k, 2, keepdims=False)
        part = jnp.sum(jnp.where(packs[k], gate_col[:, None, :], 0.0), axis=-1).reshape(pack_rows)
        gate_parts.append(swap(part, "expert", k) if k else part)
    gate_rows = quad_rows(jnp.concatenate(gate_parts))

    joint = dot(hidden_rows, gate_up_full)
    gate_pre, up_pre = joint[:, :quarter], joint[:, quarter:]
    sigma = jax.nn.sigmoid(gate_pre)
    silu_vals = gate_pre * sigma
    active = (silu_vals * up_pre).astype(bf16)
    active_grad = dot(grad_rows, down_full)
    gate_grad = active_grad * up_pre * sigma * (1.0 + gate_pre * (1.0 - sigma))
    joint_grad = jnp.concatenate([gate_grad, active_grad * silu_vals], axis=1).astype(bf16)
    slot_part_two = jnp.sum(active.astype(f32) * active_grad, axis=-1, keepdims=True)
    slot_part_two = jnp.pad(slot_part_two, ((0, 0), (0, HDIM - 1))).astype(bf16)
    hidden_part = jnp.concatenate(
        [dot_t(joint_grad, gate_up_full).astype(bf16), slot_part_two], axis=1
    )
    back_packed = return_packed(quad_sum(hidden_part))
    slot_two_grad = jnp.zeros((slots, home_rows), f32)
    for k in range(slots):
        rows = jnp.sum(
            jnp.where(packs[k], back_packed[k][:, :, width].astype(f32)[:, :, None], 0.0), axis=1
        )
        slot_two_grad = lax.dynamic_update_index_in_dim(
            slot_two_grad, rows.reshape(home_rows), col ^ k, 0
        )
    hidden_two_grad = unpack(back_packed[..., :width], gates_two)
    logit_two_grad = gate_back(slot_two_grad.T, gate_vals_two, matches_two, chosen_two).astype(bf16)
    hidden_two_grad = hidden_two_grad + dot_t(logit_two_grad, ffn_router)
    router_two_grad = t_dot(logit_two_grad, hidden_two)
    gain_two_grad = jnp.sum(hidden_two_grad * normed_two, axis=0)
    resid_grad = dy_home + norm_back(hidden_two_grad * gain_two, normed_two, scale_two)

    ffn_packed = return_packed(quad_sum(dot_t(active, down_full)))
    out_home = (resid + unpack(ffn_packed, gates_two)).astype(bf16)

    scaled_hidden = (hidden_rows.astype(f32) * gate_rows[:, None]).astype(bf16)
    scaled_grad = (grad_rows.astype(f32) * gate_rows[:, None]).astype(bf16)

    def chunk_grad(k):
        start = (chip ^ k) * chip_rows
        left = lax.dynamic_slice_in_dim(scaled_hidden, start, chip_rows, 1)
        right = lax.dynamic_slice_in_dim(scaled_grad, start, chip_rows, 1)
        return jnp.concatenate(
            [t_dot(left, joint_grad).astype(bf16), t_dot(right, active).astype(bf16)], axis=1
        )

    chunk_grads = [chunk_grad(k) for k in range(chips)]
    side_lines = [swap(chunk_grads[2 * line + 1], "dp", 4 * line) for line in range(1, lines)]
    keep_lines_grad = [swap(chunk_grads[2 * line], "dp", 4 * line) for line in range(1, lines)]

    resid_grad_low = after(resid_grad.astype(bf16), *chunk_grads[2:])
    resid_grad_all = gather_rows(resid_grad_low)
    out_part = t_dot(resid_grad_all, gated_vals).astype(bf16)
    vals_grad = dot(resid_grad_all, out_full)
    vals_grad = after(vals_grad, out_part, *chunk_grads[:2], *side_lines)
    query_grad, key_grad, value_grad, slot_part_one = attention_backward(
        lens, query_rot, key_rot, kv_part, attn_vals, vals_grad, tables, gates_wide, log_total,
        own_heads, group_rows,
    )
    kv_grad = jnp.concatenate([key_grad, value_grad], axis=1)
    hidden_one_part = dot_t(query_grad, query_full) + dot_t(kv_grad, kv_full)
    back_one = scatter_rows(
        jnp.concatenate([hidden_one_part.astype(bf16), slot_part_one.astype(bf16)], axis=1)
    )
    hidden_one_grad, slot_one_grad = back_one[:, :width], back_one[:, width : width + slots]

    def own(value):
        shaped = value.reshape((micro, group_rows) + value.shape[1:])
        part = lax.dynamic_slice_in_dim(shaped, col * tok_rows, tok_rows, 1)
        return part.reshape((home_rows,) + value.shape[1:])

    logit_one_grad = gate_back(
        slot_one_grad, own(gate_vals_one), own(matches_one), own(chosen_one)
    ).astype(bf16)
    hidden_one_grad = hidden_one_grad + dot_t(logit_one_grad, attn_router)
    router_one_grad = t_dot(logit_one_grad, hidden_one_home)
    gain_one_grad = jnp.sum(hidden_one_grad * normed_one, axis=0)
    in_home = resid_grad + norm_back(hidden_one_grad * gain_one, normed_one, scale_one)

    results = jnp.stack([out_home, in_home.astype(bf16)]).reshape(2, micro, tok_rows, width)
    results = jnp.einsum("mtr,bmtd->bmrd", deal, results, preferred_element_type=f32).astype(bf16)
    results = results.reshape(2 * micro, dp_count, piece_rows, width).transpose(1, 0, 2, 3)
    results = lax.all_to_all(results, "dp", split_axis=0, concat_axis=0, tiled=True)
    results = results.transpose(1, 0, 2, 3).reshape(2, micro, tok_rows, width)

    side_grad, keep_grad = chunk_grads[1].astype(f32), chunk_grads[0].astype(f32)
    for line in range(lines - 1):
        side_grad = side_grad + side_lines[line].astype(f32)
        keep_grad = keep_grad + keep_lines_grad[line].astype(f32)
    other_grad = swap(side_grad.astype(bf16), "dp", 2)
    pair = jnp.stack([keep_grad.astype(bf16), other_grad]).reshape(2, 2, shard_rows, 3 * quarter)
    own_pair = lax.dynamic_index_in_dim(pair, core, 1, keepdims=False)
    near_pair = swap(lax.dynamic_index_in_dim(pair, 1 - core, 1, keepdims=False), "dp", 1)
    by_core = [jnp.where(core == 0, own_pair, near_pair), jnp.where(core == 0, near_pair, own_pair)]
    by_side = [[jnp.where(side == s, part[0], part[1]) for part in by_core] for s in range(2)]
    blocks = [part for row in by_side for part in row]
    gate_up_grad = jnp.concatenate(
        [b[:, :quarter] for b in blocks] + [b[:, quarter : 2 * quarter] for b in blocks], axis=1
    ).astype(f32)
    down_grad = jnp.concatenate([b[:, 2 * quarter :] for b in blocks], axis=1).astype(f32)

    def reduced(value):
        return lax.psum_scatter(value.astype(bf16), "dp", scatter_dimension=0, tiled=True)

    out_grad = slots_of(reduced(out_part)).astype(f32)
    query_out = slots_of(reduced(t_dot(hidden_one, query_grad))).astype(f32)
    kv_own = reduced(t_dot(hidden_one, kv_grad))
    key_part, value_part = kv_own[:, :own_width], kv_own[:, own_width:]
    first_back = lax.ppermute(
        jnp.where(even_col, key_part, value_part), "expert", [(b, a) for a, b in first_pairs]
    )
    second_back = lax.ppermute(
        jnp.where(even_col, value_part, key_part), "expert", [(b, a) for a, b in second_pairs]
    )
    kv_out = jnp.concatenate(
        [
            jnp.where(holds_keys, first_back, second_back),
            jnp.where(holds_keys, second_back, first_back),
        ],
        axis=1,
    ).astype(f32)

    sums = spread(
        jnp.concatenate(
            [gain_one_grad[None], gain_two_grad[None], router_one_grad, router_two_grad], axis=0
        ),
        jnp.add,
    )
    limit = clip_limit[0].astype(f32)
    factor = limit / jnp.maximum(peaks_all, limit)
    query_scale = jnp.repeat(jnp.sqrt(take(factor, col)), HDIM)
    query_clipped = (query_weight.astype(f32) * query_scale[None, None, :]).astype(bf16)
    full_scale = jnp.concatenate(
        [jnp.repeat(jnp.sqrt(jnp.min(factor, axis=0)), HDIM), jnp.ones((query_width,), f32)]
    )
    piece_width = kv_weight.shape[1]
    piece_scale = lax.dynamic_slice_in_dim(full_scale, col * piece_width, piece_width)
    kv_clipped = (kv_weight.astype(f32) * piece_scale[None, :]).astype(bf16)
    return (
        results[0],
        results[1],
        sums[0],
        sums[1],
        sums[2 : 2 + slots].T,
        sums[2 + slots :].T,
        query_out[None],
        out_grad[None],
        kv_out,
        gate_up_grad[None],
        down_grad[None],
        query_clipped,
        kv_clipped,
    )


def solution(mesh):
    placed = (
        P(None, ("dp", "expert"), None),
        P(None, ("dp", "expert"), None),
        P(),
        P(None, ("dp", "expert")),
        P(None, "dp", None),
        P(None, "dp", None),
        P(),
        P(),
        P(),
        P(),
        P(),
        P(),
        P("expert", "dp", None),
        P("expert", "dp", None),
        P("dp", "expert"),
        P("expert", "dp", None),
        P("expert", "dp", None),
    )
    return jax.shard_map(
        local,
        mesh=mesh,
        in_specs=placed,
        out_specs=(
            P(None, ("dp", "expert"), None),
            P(None, ("dp", "expert"), None),
            P(),
            P(),
            P(),
            P(),
            P("expert", "dp", None),
            P("expert", "dp", None),
            P("dp", "expert"),
            P("expert", "dp", None),
            P("expert", "dp", None),
            P("expert", "dp", None),
            P("dp", "expert"),
        ),
        check_vma=False,
    )
```

```python
import jax
import jax.numpy as jnp
from jax import lax
from jax.experimental import pallas as pl
from jax.experimental.pallas import tpu as pltpu
from jax.sharding import PartitionSpec as P

HEADS = 16
HDIM = 128
FF = 5632
TOP = 2

eps_norm = 1e-06
rope_base = 10000.0
very_low = -1e30

f32 = jnp.float32
bf16 = jnp.bfloat16


def dot(left, right):
    return jnp.dot(left, right, preferred_element_type=f32)


def dot_t(left, right):
    return lax.dot_general(left, right, (((1,), (1,)), ((), ())), preferred_element_type=f32)


def t_dot(left, right):
    return lax.dot_general(left, right, (((0,), (0,)), ((), ())), preferred_element_type=f32)


def swap(value, axis, step):
    count = lax.axis_size(axis)
    return lax.ppermute(value, axis, [(i, i ^ step) for i in range(count)])


def take(stacked, index):
    return lax.dynamic_index_in_dim(stacked, index, 0, keepdims=False)


def place(parts, positions):
    out = jnp.zeros((len(parts),) + parts[0].shape, parts[0].dtype)
    for part, position in zip(parts, positions):
        out = lax.dynamic_update_index_in_dim(out, part, position, 0)
    return out


def after(value, *others):
    return lax.optimization_barrier((value, *others))[0]


def spread(value, combine):
    for axis in ("expert", "dp"):
        step = 1
        while step < lax.axis_size(axis):
            value = combine(value, swap(value, axis, step))
            step *= 2
    return value


def rotation_tables(places):
    half_dim = HDIM // 2
    frequency = rope_base ** (-jnp.arange(half_dim, dtype=f32) * 2.0 / HDIM)
    angles = places.astype(f32)[:, None] * frequency[None, :]
    cosine, sine = jnp.cos(angles), jnp.sin(angles)
    return (
        jnp.concatenate([cosine, cosine], axis=1),
        jnp.concatenate([-sine, sine], axis=1),
    )


def turn(values, cosine, sine):
    return values * cosine + pltpu.roll(values, HDIM // 2, 1) * sine


def lane_value(table, lane):
    lanes = lax.broadcasted_iota(jnp.int32, table.shape, 1)
    return jnp.sum(jnp.where(lanes == lane, table, 0.0), axis=1, keepdims=True)


def allowed_pairs(rows, first_len):
    query_at = lax.broadcasted_iota(jnp.int32, (rows, rows), 0)
    key_at = lax.broadcasted_iota(jnp.int32, (rows, rows), 1)
    return (key_at <= query_at) & ((key_at >= first_len) | (query_at < first_len))


def forward_kernel(
    lens, query, key, value, cosine, sine, gates, hits,
    vals_out, gated_out, query_out, key_out, total_out, peak_out,
):
    m, h, s = pl.program_id(0), pl.program_id(1), pl.program_id(2)
    slot_count = pl.num_programs(2)
    rows = query.shape[0]
    lane = h * slot_count + s

    @pl.when(lane == 0)
    def _():
        total_out[...] = jnp.zeros_like(total_out)
        peak_out[...] = jnp.full_like(peak_out, very_low)

    @pl.when(s == 0)
    def _():
        key_out[...] = turn(key[...].astype(f32), cosine[...], sine[...]).astype(bf16)

    turned = turn(query[...], cosine[...], sine[...]).astype(bf16)
    query_out[...] = turned
    raw = dot_t(turned, key_out[...])
    scores = jnp.where(allowed_pairs(rows, lens[m]), raw * HDIM ** (-0.5), very_low)
    row_peak = jnp.max(scores, axis=1, keepdims=True)
    expo = jnp.exp(scores - row_peak)
    denom = jnp.sum(expo, axis=1, keepdims=True)
    probs = expo / denom
    vals = dot(probs.astype(bf16), value[...]).astype(bf16)
    vals_out[...] = vals
    gated_out[...] = (lane_value(gates[...], s) * vals.astype(f32)).astype(bf16)
    lanes = lax.broadcasted_iota(jnp.int32, total_out.shape, 1)
    total_out[...] = jnp.where(lanes == lane, row_peak + jnp.log(denom), total_out[...])
    seen = jnp.where(lane_value(hits[...], s) > 0.0, row_peak, very_low)
    peak_lanes = lax.broadcasted_iota(jnp.int32, peak_out.shape, 1)
    peak_out[...] = jnp.where(
        peak_lanes == lane, jnp.max(seen, axis=0, keepdims=True), peak_out[...]
    )


def backward_kernel(
    lens, query, key, value, vals, vals_grad, cosine, sine, gates, total,
    query_grad, key_grad, value_grad, gate_grad, key_sum, value_sum,
):
    m, h, s = pl.program_id(0), pl.program_id(1), pl.program_id(2)
    slot_count = pl.num_programs(2)
    rows = query.shape[0]
    lane = h * slot_count + s

    @pl.when(lane == 0)
    def _():
        gate_grad[...] = jnp.zeros_like(gate_grad)

    @pl.when(s == 0)
    def _():
        key_sum[...] = jnp.zeros_like(key_sum)
        value_sum[...] = jnp.zeros_like(value_sum)

    full_grad = vals_grad[...]
    lanes = lax.broadcasted_iota(jnp.int32, gate_grad.shape, 1)
    slot_sum = jnp.sum(vals[...].astype(f32) * full_grad, axis=1, keepdims=True)
    gate_grad[...] += jnp.where(lanes == s, slot_sum, 0.0)
    gated_grad = (lane_value(gates[...], s) * full_grad).astype(bf16)
    raw = dot_t(query[...], key[...])
    scores = jnp.where(allowed_pairs(rows, lens[m]), raw * HDIM ** (-0.5), very_low)
    probs = jnp.exp(scores - lane_value(total[...], lane))
    prob_grad = dot_t(gated_grad, value[...])
    inner = jnp.sum(probs * prob_grad, axis=1, keepdims=True)
    score_grad = (probs * (prob_grad - inner) * HDIM ** (-0.5)).astype(bf16)
    back_sine = -sine[...]
    turned = dot(score_grad, key[...])
    query_grad[...] = turn(turned, cosine[...], back_sine).astype(bf16)
    key_sum[...] += t_dot(score_grad, query[...])
    value_sum[...] += t_dot(probs.astype(bf16), gated_grad)

    @pl.when(s == slot_count - 1)
    def _():
        key_grad[...] = turn(key_sum[...], cosine[...], back_sine).astype(bf16)
        value_grad[...] = value_sum[...].astype(bf16)


def attention_specs(own_heads, rows):
    def block(index):
        return pl.BlockSpec((rows, HDIM), index)

    return {
        "query": block(lambda m, h, s, lens: (m, s * own_heads + h)),
        "key": block(lambda m, h, s, lens: (m, h)),
        "value": block(lambda m, h, s, lens: (m, own_heads + h)),
        "rows": block(lambda m, h, s, lens: (m, 0)),
        "peak": pl.BlockSpec((8, HDIM), lambda m, h, s, lens: (m, 0)),
    }


def attention_forward(lens, query, joint_kv, tables, gates, hits, own_heads, rows):
    micro = lens.shape[0]
    slots = query.shape[1] // (own_heads * HDIM)
    at = attention_specs(own_heads, rows)
    shape = jax.ShapeDtypeStruct
    total_rows = micro * rows
    return pl.pallas_call(
        forward_kernel,
        grid_spec=pltpu.PrefetchScalarGridSpec(
            num_scalar_prefetch=1,
            grid=(micro, own_heads, slots),
            in_specs=[at["query"], at["key"], at["value"]] + [at["rows"]] * 4,
            out_specs=[at["query"]] * 3 + [at["key"], at["rows"], at["peak"]],
        ),
        out_shape=[shape(query.shape, bf16)] * 3
        + [
            shape((total_rows, own_heads * HDIM), bf16),
            shape((total_rows, HDIM), f32),
            shape((micro * 8, HDIM), f32),
        ],
        cost_estimate=pl.CostEstimate(
            flops=4 * rows * rows * HDIM * micro * HEADS,
            bytes_accessed=14 * query.size,
            transcendentals=rows * rows * micro * HEADS,
        ),
        name="attention_forward",
    )(lens, query, joint_kv, joint_kv, tables[0], tables[1], gates, hits)


def attention_backward(
    lens, query, key, joint_kv, vals, vals_grad, tables, gates, total, own_heads, rows
):
    micro = lens.shape[0]
    slots = query.shape[1] // (own_heads * HDIM)
    at = attention_specs(own_heads, rows)
    shape = jax.ShapeDtypeStruct
    total_rows = micro * rows
    return pl.pallas_call(
        backward_kernel,
        grid_spec=pltpu.PrefetchScalarGridSpec(
            num_scalar_prefetch=1,
            grid=(micro, own_heads, slots),
            in_specs=[at["query"], at["key"], at["value"], at["query"], at["query"]]
            + [at["rows"]] * 4,
            out_specs=[at["query"], at["key"], at["key"], at["rows"]],
            scratch_shapes=[pltpu.VMEM((rows, HDIM), f32)] * 2,
        ),
        out_shape=[shape(query.shape, bf16)]
        + [shape((total_rows, own_heads * HDIM), bf16)] * 2
        + [shape((total_rows, HDIM), f32)],
        cost_estimate=pl.CostEstimate(
            flops=10 * rows * rows * HDIM * micro * HEADS,
            bytes_accessed=14 * query.size,
            transcendentals=rows * rows * micro * HEADS,
        ),
        name="attention_backward",
    )(lens, query, key, joint_kv, vals, vals_grad, tables[0], tables[1], gates, total)


def normalize(values):
    row_scale = lax.rsqrt(jnp.mean(values * values, axis=-1, keepdims=True) + eps_norm)
    return values * row_scale, row_scale


def norm_back(grad_hat, normed, row_scale):
    return row_scale * (grad_hat - normed * jnp.mean(grad_hat * normed, axis=-1, keepdims=True))


def route_gates(logits, routes, expert_table):
    expert_ids = jnp.arange(expert_table.shape[0], dtype=jnp.int32)
    matches = routes[:, :, None] == expert_ids[None, None, :]
    picked = jnp.sum(jnp.where(matches, logits[:, None, :], 0.0), axis=-1)
    gate_vals = jax.nn.softmax(picked, axis=-1)
    slot_ids = route_slots(routes, expert_table)
    chosen = slot_ids[:, :, None] == expert_ids[None, None, :]
    gates = jnp.sum(jnp.where(chosen, gate_vals[:, :, None], 0.0), axis=1)
    return gates, matches, chosen, gate_vals


def route_slots(routes, expert_table):
    expert_ids = jnp.arange(expert_table.shape[0], dtype=jnp.int32)
    matches = routes[..., None] == expert_ids
    return jnp.sum(jnp.where(matches, expert_table, 0), axis=-1)


def gate_back(slot_grad, gate_vals, matches, chosen):
    picked = jnp.sum(jnp.where(chosen, slot_grad[:, None, :], 0.0), axis=-1)
    inner_sum = jnp.sum(gate_vals * picked, axis=-1, keepdims=True)
    picked_grad = gate_vals * (picked - inner_sum)
    return jnp.sum(jnp.where(matches, picked_grad[:, :, None], 0.0), axis=1)


def unit_blocks(count):
    return [(start, min(512, count - start)) for start in range(0, count, 512)]


def expert_kernel(place_ref, hidden, grad, *refs):
    piece_count = (len(refs) - 6) // 2
    own_pieces, near_pieces = refs[:piece_count], refs[piece_count : 2 * piece_count]
    out, hidden_out, act_out, joint_out, weights, sems = refs[2 * piece_count :]
    core, chip = place_ref[0], place_ref[1]
    rows, columns = near_pieces[0].shape
    units = columns // 3
    width = hidden.shape[1]

    @pl.when(pl.program_id(0) == 0)
    def _():
        copies = []
        for k in range(piece_count):
            base = (chip ^ k) * (2 * rows)
            own, near = own_pieces[k], near_pieces[k]
            if own.shape[1] != columns:
                own = own.at[:, pl.ds(pl.multiple_of(core * columns, HDIM), columns)]
            for number, (piece, part) in enumerate(((own, core), (near, 1 - core))):
                start = pl.multiple_of(base + part * rows, 16)
                copies.append(
                    pltpu.make_async_copy(
                        piece, weights.at[pl.ds(start, rows)], sems.at[2 * k + number]
                    )
                )
        for copy in copies:
            copy.start()
        for copy in copies:
            copy.wait()

    slot_sum = jnp.zeros((hidden.shape[0], 1), f32)
    for start, size in unit_blocks(units):
        gate_pre = dot(hidden[...], weights[:, start : start + size])
        up_pre = dot(hidden[...], weights[:, units + start : units + start + size])
        act_grad = dot(grad[...], weights[:, 2 * units + start : 2 * units + start + size])
        sigma = 1.0 / (1.0 + jnp.exp(-gate_pre))
        silu_vals = gate_pre * sigma
        active = (silu_vals * up_pre).astype(bf16)
        act_out[:, start : start + size] = active
        slot_sum += jnp.sum(active.astype(f32) * act_grad, axis=1, keepdims=True)
        gate_grad = act_grad * up_pre * sigma * (1.0 + gate_pre * (1.0 - sigma))
        joint_out[:, start : start + size] = gate_grad.astype(bf16)
        joint_out[:, units + start : units + start + size] = (act_grad * silu_vals).astype(bf16)
    for start in range(0, width, 512):
        block = weights[start : start + 512, : 2 * units]
        hidden_out[:, start : start + 512] = dot_t(joint_out[...], block).astype(bf16)
        block = weights[start : start + 512, 2 * units :]
        out[:, start : start + 512] = dot_t(act_out[...], block).astype(bf16)
    lanes = lax.broadcasted_iota(jnp.int32, (hidden.shape[0], HDIM), 1)
    hidden_out[:, width:] = jnp.where(lanes == 0, slot_sum, 0.0).astype(bf16)


def expert_rows(position, hidden, grad, own_pieces, near_pieces):
    rows, width = hidden.shape
    columns = near_pieces[0].shape[1]
    units = columns // 3
    tile = 256
    shape = jax.ShapeDtypeStruct
    count = len(own_pieces)

    def tiled(size):
        return pl.BlockSpec((tile, size), lambda i, at: (i, 0))

    return pl.pallas_call(
        expert_kernel,
        grid_spec=pltpu.PrefetchScalarGridSpec(
            num_scalar_prefetch=1,
            grid=(rows // tile,),
            in_specs=[tiled(width)] * 2 + [pl.BlockSpec(memory_space=pl.ANY)] * (2 * count),
            out_specs=[tiled(width), tiled(width + HDIM), tiled(units), tiled(2 * units)],
            scratch_shapes=[
                pltpu.VMEM((width, columns), bf16),
                pltpu.SemaphoreType.DMA((2 * count,)),
            ],
        ),
        out_shape=[
            shape((rows, width), bf16),
            shape((rows, width + HDIM), bf16),
            shape((rows, units), bf16),
            shape((rows, 2 * units), bf16),
        ],
        compiler_params=pltpu.CompilerParams(vmem_limit_bytes=56 * 2**20),
        cost_estimate=pl.CostEstimate(
            flops=4 * rows * width * columns,
            bytes_accessed=2 * (width * columns + 6 * rows * width),
            transcendentals=rows * units,
        ),
        name="expert_rows",
    )(position, hidden, grad, *own_pieces, *near_pieces)


def expert_grad_kernel(order, hidden, grad, gates, joint, active, *outs):
    gate = gates[...]
    left = (hidden[...].astype(f32) * gate).astype(bf16)
    right = (grad[...].astype(f32) * gate).astype(bf16)
    units = active.shape[1]
    step = pl.program_id(0)
    for number, out in enumerate(outs):

        @pl.when(step // 2 == number)
        def _():
            for start, size in unit_blocks(2 * units):
                out[:, start : start + size] = t_dot(left, joint[:, start : start + size]).astype(bf16)
            for start, size in unit_blocks(units):
                out[:, 2 * units + start : 2 * units + start + size] = t_dot(
                    right, active[:, start : start + size]
                ).astype(bf16)


def expert_grads(chunks, chunk_rows, hidden, grad, gates, joint, active):
    rows, units = active.shape
    half = chunk_rows // 2
    count = len(chunks)
    order = jnp.stack([2 * chunk + part for chunk in chunks for part in range(2)]).astype(jnp.int32)

    def whole(size):
        return pl.BlockSpec((rows, size), lambda i, at: (0, 0), pipeline_mode=pl.Buffered(1))

    column = pl.BlockSpec((rows, half), lambda i, at: (0, at[i]))
    return pl.pallas_call(
        expert_grad_kernel,
        grid_spec=pltpu.PrefetchScalarGridSpec(
            num_scalar_prefetch=1,
            grid=(2 * count,),
            in_specs=[column, column, whole(1), whole(2 * units), whole(units)],
            out_specs=[
                pl.BlockSpec((half, 3 * units), lambda i, at, n=n: (jnp.clip(i - 2 * n, 0, 1), 0))
                for n in range(count)
            ],
        ),
        out_shape=[jax.ShapeDtypeStruct((chunk_rows, 3 * units), bf16)] * count,
        compiler_params=pltpu.CompilerParams(vmem_limit_bytes=48 * 2**20),
        cost_estimate=pl.CostEstimate(
            flops=2 * count * chunk_rows * rows * 3 * units,
            bytes_accessed=2 * (rows * 3 * units + count * chunk_rows * (2 * rows + 3 * units)),
            transcendentals=0,
        ),
        name="expert_grads",
    )(order, hidden, grad, gates, joint, active)


def local(
    tokens,
    cotangent,
    seq_lengths,
    dealing,
    attn_routes,
    ffn_routes,
    expert_table,
    clip_limit,
    attn_gain,
    ffn_gain,
    attn_router,
    ffn_router,
    query_weight,
    attn_out_weight,
    kv_weight,
    gate_up_weight,
    down_weight,
):
    micro, tok_rows, width = tokens.shape
    dp_count = lax.axis_size("dp")
    slots = lax.axis_size("expert")
    col = lax.axis_index("expert")
    group = lax.axis_index("dp")
    piece_rows = tok_rows // dp_count
    cap = tok_rows * TOP * 3 // (2 * slots)
    group_rows = tok_rows * slots
    all_rows = micro * group_rows
    home_rows = micro * tok_rows
    query_width = HEADS * HDIM
    own_heads = HEADS // slots
    own_width = own_heads * HDIM
    shard_rows = query_weight.shape[1]
    score_scale = HDIM ** (-0.5)
    core = group % 2
    chip = group // 2
    side = chip % 2
    chips = dp_count // 2
    lines = chips // 2
    quarter = FF // 4
    chip_rows = 2 * shard_rows

    both = jnp.stack([tokens, cotangent]).reshape(2 * micro, dp_count, piece_rows, width)
    both = lax.all_to_all(both.transpose(1, 0, 2, 3), "dp", split_axis=0, concat_axis=0, tiled=True)
    both = both.transpose(1, 0, 2, 3).reshape(2, micro, tok_rows, width)
    deal = (dealing[:, :, None] == jnp.arange(tok_rows, dtype=jnp.int32)).astype(bf16)
    work = jnp.einsum("mtr,bmrd->bmtd", deal, both, preferred_element_type=f32)
    x_home = work[0].reshape(home_rows, width)
    dy_home = work[1].reshape(home_rows, width)

    def columns_of(shard):
        pieces = shard.reshape(shard_rows, slots, own_width)
        parts = [
            swap(lax.dynamic_index_in_dim(pieces, col ^ k, 1, keepdims=False), "expert", k)
            if k
            else lax.dynamic_index_in_dim(pieces, col, 1, keepdims=False)
            for k in range(slots)
        ]
        out = jnp.zeros((shard_rows, query_width), shard.dtype)
        for k, part in enumerate(parts):
            out = lax.dynamic_update_slice_in_dim(out, part, (col ^ k) * own_width, 1)
        return out

    def slots_of(columns):
        pieces = columns.reshape(shard_rows, slots, own_width)
        out = jnp.zeros((shard_rows, query_width), columns.dtype)
        for k in range(slots):
            part = lax.dynamic_index_in_dim(pieces, col ^ k, 1, keepdims=False)
            part = swap(part, "expert", k) if k else part
            out = lax.dynamic_update_slice_in_dim(out, part, (col ^ k) * own_width, 1)
        return out

    half_slots = slots // 2
    first_pairs = [(c, 2 * c) for c in range(half_slots)]
    first_pairs += [(c, 2 * (c - half_slots) + 1) for c in range(half_slots, slots)]
    second_pairs = [(c, 2 * c + 1) for c in range(half_slots)]
    second_pairs += [(c, 2 * (c - half_slots)) for c in range(half_slots, slots)]
    holds_keys = col < half_slots
    even_col = col % 2 == 0
    low_kv, high_kv = kv_weight[:, :own_width], kv_weight[:, own_width:]
    first_got = lax.ppermute(jnp.where(holds_keys, low_kv, high_kv), "expert", first_pairs)
    second_got = lax.ppermute(jnp.where(holds_keys, high_kv, low_kv), "expert", second_pairs)
    own_kv = jnp.concatenate(
        [
            jnp.where(even_col, first_got, second_got),
            jnp.where(even_col, second_got, first_got),
        ],
        axis=1,
    )
    kv_full = lax.all_gather(own_kv, "dp", axis=0, tiled=True)
    query_full = lax.all_gather(columns_of(query_weight[0]), "dp", axis=0, tiled=True)

    def quarter_of(half, part):
        start = (2 * half + part) * quarter
        return [
            lax.dynamic_slice_in_dim(gate_up_weight[0], start, quarter, 1),
            lax.dynamic_slice_in_dim(gate_up_weight[0], FF + start, quarter, 1),
            lax.dynamic_slice_in_dim(down_weight[0], start, quarter, 1),
        ]

    def half_of(half):
        return jnp.concatenate(quarter_of(half, 0) + quarter_of(half, 1), axis=1)

    def part_of(piece, part):
        return lax.dynamic_slice_in_dim(piece, part * 3 * quarter, 3 * quarter, 1)

    keep_side = half_of(side)
    from_side = swap(half_of(1 - side), "dp", 2)
    keep_lines = [swap(keep_side, "dp", 4 * line) for line in range(1, lines)]
    from_lines = []
    for line in range(1, lines):
        other_part = swap(part_of(from_side, 1 - core), "dp", 4 * line)
        from_lines.append((swap(part_of(from_side, core), "dp", 4 * line), other_part))

    own_pieces = [keep_side, from_side]
    near_pieces = [swap(part_of(piece, 1 - core), "dp", 1) for piece in own_pieces]
    for line in range(lines - 1):
        own_pieces += [keep_lines[line], from_lines[line][0]]
        near_pieces += [
            swap(part_of(keep_lines[line], 1 - core), "dp", 1),
            swap(from_lines[line][1], "dp", 1),
        ]

    positions = jnp.arange(group_rows, dtype=jnp.int32)
    first_len = lax.dynamic_index_in_dim(seq_lengths[:, :, 0], group, 1, keepdims=True)
    in_second = positions[None, :] >= first_len
    places = positions[None, :] - jnp.where(in_second, first_len, 0)
    tables = rotation_tables(places.reshape(all_rows))

    def gather_rows(value):
        shaped = value.reshape(micro, tok_rows, -1)
        out = jnp.zeros((micro, group_rows, shaped.shape[-1]), value.dtype)
        for k in range(slots):
            part = swap(shaped, "expert", k) if k else shaped
            out = lax.dynamic_update_slice_in_dim(out, part, (col ^ k) * tok_rows, 1)
        return out.reshape(all_rows, -1)

    def scatter_rows(value):
        shaped = value.reshape(micro, group_rows, -1)
        total = None
        for k in range(slots):
            part = lax.dynamic_slice_in_dim(shaped, (col ^ k) * tok_rows, tok_rows, 1)
            if k:
                part = swap(part.astype(bf16), "expert", k)
            part = part.astype(f32)
            total = part if total is None else total + part
        return total.reshape(home_rows, -1)

    home_routes = lax.dynamic_slice_in_dim(ffn_routes, col * tok_rows, tok_rows, 1)
    home_slots = route_slots(home_routes, expert_table)
    packs = []
    before = jnp.tril(jnp.ones((tok_rows, tok_rows), bf16), -1)
    for k in range(slots):
        hits = jnp.any(home_slots == (col ^ k), axis=-1)
        rank = jnp.einsum("ts,ms->mt", before, hits.astype(bf16), preferred_element_type=f32)
        packs.append(
            hits[:, None, :]
            & (rank[:, None, :] == jnp.arange(cap, dtype=jnp.int32).astype(f32)[None, :, None])
        )
    packs = jnp.stack(packs)
    packs_low = packs.astype(bf16)
    pack_rows = micro * cap
    sent_rows = slots * pack_rows

    def send_packed(value):
        packed = jnp.einsum(
            "kmct,mtd->kmcd", packs_low, value.reshape(micro, tok_rows, -1), preferred_element_type=f32
        ).astype(bf16)
        parts = [swap(packed[k], "expert", k) if k else packed[k] for k in range(slots)]
        return jnp.stack(parts).reshape(sent_rows, -1)

    def quad_rows(value):
        near = swap(value, "dp", 1)
        far = swap(value, "dp", 2)
        across = swap(far, "dp", 1)
        return jnp.concatenate([value, near, far, across], axis=0)

    def quad_sum(value, *others):
        own, near, far, across = jnp.split(value, 4, axis=0)
        far_sum = far.astype(f32) + swap(across, "dp", 1).astype(f32)
        own_sum = own.astype(f32) + swap(near, "dp", 1).astype(f32)
        return own_sum + after(swap(far_sum.astype(bf16), "dp", 2), *others).astype(f32)

    def return_packed(value, *others):
        shaped = value.astype(bf16).reshape(slots, micro, cap, -1)
        parts = [swap(shaped[k], "expert", k) if k else shaped[k] for k in range(slots)]
        return after(parts, *others)

    def unpack(packed, scale):
        total = None
        for k in range(slots):
            rows = jnp.einsum("mct,mcd->mtd", packs_low[k], packed[k], preferred_element_type=f32)
            rows = rows.reshape(home_rows, -1) * take(scale.T, col ^ k)[:, None]
            total = rows if total is None else total + rows
        return total

    gain_one = attn_gain.astype(f32)
    gain_two = ffn_gain.astype(f32)
    normed_one, scale_one = normalize(x_home)
    hidden_one_home = (normed_one * gain_one).astype(bf16)
    hidden_one_raw = gather_rows(hidden_one_home)
    out_weight, dy_low = lax.optimization_barrier(
        (attn_out_weight[0], dy_home.astype(bf16), hidden_one_raw)
    )[:2]
    out_full = lax.all_gather(columns_of(out_weight), "dp", axis=0, tiled=True)
    grad_sent = send_packed(dy_low)
    grad_rows = quad_rows(grad_sent)
    hidden_one = after(hidden_one_raw, from_side, *keep_lines)
    logits_one = dot(hidden_one, attn_router)
    gates_one, matches_one, chosen_one, gate_vals_one = route_gates(
        logits_one, attn_routes.reshape(all_rows, TOP), expert_table
    )
    hits_one = jnp.any(chosen_one, axis=1).astype(f32)

    def wide(value):
        return jnp.pad(value, ((0, 0), (0, HDIM - value.shape[1])))

    kv_part = dot(hidden_one, kv_full).astype(bf16)
    query_part = dot(hidden_one, query_full)
    lens = first_len[:, 0].astype(jnp.int32)
    gates_wide = wide(gates_one)
    attn_vals, gated_vals, query_rot, key_rot, log_total, peaks = attention_forward(
        lens, query_part, kv_part, tables, gates_wide, wide(hits_one), own_heads, group_rows
    )
    peaks = jnp.max(peaks, axis=0)[: own_heads * slots].reshape(own_heads, slots).T
    peak_table = lax.dynamic_update_slice_in_dim(
        jnp.full((slots, HEADS), very_low, f32), peaks, col * own_heads, 1
    )
    peaks_all = spread(peak_table, jnp.maximum)
    gated_vals = after(gated_vals, grad_sent, *[pair[1] for pair in from_lines])
    attn_home = scatter_rows(dot_t(gated_vals, out_full))

    resid = x_home + attn_home
    normed_two, scale_two = normalize(resid)
    hidden_two = (normed_two * gain_two).astype(bf16)
    logits_two = dot(hidden_two, ffn_router)
    gates_two, matches_two, chosen_two, gate_vals_two = route_gates(
        logits_two, home_routes.reshape(home_rows, TOP), expert_table
    )
    hidden_rows = quad_rows(send_packed(after(hidden_two, grad_rows)))
    gates_by_slot = gates_two.reshape(micro, tok_rows, slots)
    gate_parts = []
    for k in range(slots):
        gate_col = lax.dynamic_index_in_dim(gates_by_slot, col ^ k, 2, keepdims=False)
        part = jnp.sum(jnp.where(packs[k], gate_col[:, None, :], 0.0), axis=-1).reshape(pack_rows)
        gate_parts.append(swap(part, "expert", k) if k else part)
    gate_rows = quad_rows(jnp.concatenate(gate_parts))

    hidden_rows = after(hidden_rows, gate_rows)
    position = jnp.stack([core, chip]).astype(jnp.int32)
    ffn_part, hidden_part, active, joint_grad = expert_rows(
        position, hidden_rows, grad_rows, own_pieces, near_pieces
    )

    def block_grads(steps):
        return expert_grads(
            [chip ^ k for k in steps], chip_rows, hidden_rows, grad_rows, gate_rows[:, None],
            joint_grad, active,
        )

    line_grads = block_grads([k ^ 1 for k in range(2, chips)])
    side_lines = [swap(line_grads[2 * line], "dp", 4 * line + 4) for line in range(lines - 1)]
    keep_lines_grad = [swap(line_grads[2 * line + 1], "dp", 4 * line + 4) for line in range(lines - 1)]
    hidden_sum = quad_sum(hidden_part, *line_grads)
    side_own, keep_own = block_grads([1, 0])
    back_packed = return_packed(hidden_sum, side_own, keep_own)
    slot_two_grad = jnp.zeros((slots, home_rows), f32)
    for k in range(slots):
        rows = jnp.sum(
            jnp.where(packs[k], back_packed[k][:, :, width].astype(f32)[:, :, None], 0.0), axis=1
        )
        slot_two_grad = lax.dynamic_update_index_in_dim(
            slot_two_grad, rows.reshape(home_rows), col ^ k, 0
        )
    hidden_two_grad = unpack([part[..., :width] for part in back_packed], gates_two)
    logit_two_grad = gate_back(slot_two_grad.T, gate_vals_two, matches_two, chosen_two).astype(bf16)
    hidden_two_grad = hidden_two_grad + dot_t(logit_two_grad, ffn_router)
    router_two_grad = t_dot(logit_two_grad, hidden_two)
    gain_two_grad = jnp.sum(hidden_two_grad * normed_two, axis=0)
    resid_grad = dy_home + norm_back(hidden_two_grad * gain_two, normed_two, scale_two)

    ffn_sum = quad_sum(after(ffn_part, *back_packed))

    resid_grad_all = gather_rows(resid_grad.astype(bf16))
    ffn_packed = return_packed(after(ffn_sum, resid_grad_all))
    out_home = (resid + unpack(ffn_packed, gates_two)).astype(bf16)
    out_part = t_dot(resid_grad_all, gated_vals).astype(bf16)
    vals_grad = after(dot(resid_grad_all, out_full), out_part, *side_lines)
    query_grad, key_grad, value_grad, slot_part_one = attention_backward(
        lens, query_rot, key_rot, kv_part, attn_vals, vals_grad, tables, gates_wide, log_total,
        own_heads, group_rows,
    )
    kv_grad = jnp.concatenate([key_grad, value_grad], axis=1)
    hidden_one_part = dot_t(query_grad, query_full) + dot_t(kv_grad, kv_full)
    hidden_one_part = after(hidden_one_part.astype(bf16), *ffn_packed)
    query_part_grad = t_dot(after(hidden_one, hidden_one_part), query_grad).astype(bf16)
    kv_part_grad = t_dot(hidden_one, kv_grad).astype(bf16)
    back_one = scatter_rows(
        jnp.concatenate([hidden_one_part, slot_part_one.astype(bf16)], axis=1)
    )
    back_one = after(back_one, query_part_grad, kv_part_grad)
    hidden_one_grad, slot_one_grad = back_one[:, :width], back_one[:, width : width + slots]

    def own(value):
        shaped = value.reshape((micro, group_rows) + value.shape[1:])
        part = lax.dynamic_slice_in_dim(shaped, col * tok_rows, tok_rows, 1)
        return part.reshape((home_rows,) + value.shape[1:])

    logit_one_grad = gate_back(
        slot_one_grad, own(gate_vals_one), own(matches_one), own(chosen_one)
    ).astype(bf16)
    hidden_one_grad = hidden_one_grad + dot_t(logit_one_grad, attn_router)
    router_one_grad = t_dot(logit_one_grad, hidden_one_home)
    gain_one_grad = jnp.sum(hidden_one_grad * normed_one, axis=0)
    in_home = resid_grad + norm_back(hidden_one_grad * gain_one, normed_one, scale_one)

    results = jnp.stack([out_home, in_home.astype(bf16)]).reshape(2, micro, tok_rows, width)
    results = jnp.einsum("mtr,bmtd->bmrd", deal, results, preferred_element_type=f32).astype(bf16)
    results = results.reshape(2 * micro, dp_count, piece_rows, width).transpose(1, 0, 2, 3)
    results = lax.all_to_all(results, "dp", split_axis=0, concat_axis=0, tiled=True)
    results = results.transpose(1, 0, 2, 3).reshape(2, micro, tok_rows, width)

    side_grad, keep_grad = side_own.astype(f32), keep_own.astype(f32)
    for line in range(lines - 1):
        side_grad = side_grad + side_lines[line].astype(f32)
        keep_grad = keep_grad + keep_lines_grad[line].astype(f32)
    other_grad = swap(side_grad.astype(bf16), "dp", 2)
    pair = jnp.stack([keep_grad.astype(bf16), other_grad]).reshape(2, 2, shard_rows, 3 * quarter)
    own_pair = lax.dynamic_index_in_dim(pair, core, 1, keepdims=False)
    near_pair = swap(lax.dynamic_index_in_dim(pair, 1 - core, 1, keepdims=False), "dp", 1)
    by_core = [jnp.where(core == 0, own_pair, near_pair), jnp.where(core == 0, near_pair, own_pair)]
    by_side = [[jnp.where(side == s, part[0], part[1]) for part in by_core] for s in range(2)]
    blocks = [part for row in by_side for part in row]
    gate_up_grad = jnp.concatenate(
        [b[:, :quarter] for b in blocks] + [b[:, quarter : 2 * quarter] for b in blocks], axis=1
    ).astype(f32)
    down_grad = jnp.concatenate([b[:, 2 * quarter :] for b in blocks], axis=1).astype(f32)

    def reduced(value):
        return lax.psum_scatter(value, "dp", scatter_dimension=0, tiled=True)

    out_grad = slots_of(reduced(out_part)).astype(f32)
    query_out = slots_of(reduced(query_part_grad)).astype(f32)
    kv_own = reduced(kv_part_grad)
    key_part, value_part = kv_own[:, :own_width], kv_own[:, own_width:]
    first_back = lax.ppermute(
        jnp.where(even_col, key_part, value_part), "expert", [(b, a) for a, b in first_pairs]
    )
    second_back = lax.ppermute(
        jnp.where(even_col, value_part, key_part), "expert", [(b, a) for a, b in second_pairs]
    )
    kv_out = jnp.concatenate(
        [
            jnp.where(holds_keys, first_back, second_back),
            jnp.where(holds_keys, second_back, first_back),
        ],
        axis=1,
    ).astype(f32)

    sums = spread(
        jnp.concatenate(
            [gain_one_grad[None], gain_two_grad[None], router_one_grad, router_two_grad], axis=0
        ),
        jnp.add,
    )
    limit = clip_limit[0].astype(f32)
    factor = limit / jnp.maximum(peaks_all, limit)
    query_scale = jnp.repeat(jnp.sqrt(take(factor, col)), HDIM)
    query_clipped = (query_weight.astype(f32) * query_scale[None, None, :]).astype(bf16)
    full_scale = jnp.concatenate(
        [jnp.repeat(jnp.sqrt(jnp.min(factor, axis=0)), HDIM), jnp.ones((query_width,), f32)]
    )
    piece_width = kv_weight.shape[1]
    piece_scale = lax.dynamic_slice_in_dim(full_scale, col * piece_width, piece_width)
    kv_clipped = (kv_weight.astype(f32) * piece_scale[None, :]).astype(bf16)
    return (
        results[0],
        results[1],
        sums[0],
        sums[1],
        sums[2 : 2 + slots].T,
        sums[2 + slots :].T,
        query_out[None],
        out_grad[None],
        kv_out,
        gate_up_grad[None],
        down_grad[None],
        query_clipped,
        kv_clipped,
    )


def solution(mesh):
    placed = (
        P(None, ("dp", "expert"), None),
        P(None, ("dp", "expert"), None),
        P(),
        P(None, ("dp", "expert")),
        P(None, "dp", None),
        P(None, "dp", None),
        P(),
        P(),
        P(),
        P(),
        P(),
        P(),
        P("expert", "dp", None),
        P("expert", "dp", None),
        P("dp", "expert"),
        P("expert", "dp", None),
        P("expert", "dp", None),
    )
    return jax.shard_map(
        local,
        mesh=mesh,
        in_specs=placed,
        out_specs=(
            P(None, ("dp", "expert"), None),
            P(None, ("dp", "expert"), None),
            P(),
            P(),
            P(),
            P(),
            P("expert", "dp", None),
            P("expert", "dp", None),
            P("dp", "expert"),
            P("expert", "dp", None),
            P("expert", "dp", None),
            P("expert", "dp", None),
            P("dp", "expert"),
        ),
        check_vma=False,
    )
```

```python
import functools

import jax
import jax.numpy as jnp
from jax import lax
from jax.experimental import pallas as pl
from jax.experimental.pallas import tpu as pltpu
from jax.sharding import PartitionSpec as P

HEADS = 16
HDIM = 128
FF = 5632
TOP = 2

eps_norm = 1e-06
rope_base = 10000.0
very_low = -1e30

f32 = jnp.float32
bf16 = jnp.bfloat16


def dot(left, right):
    return jnp.dot(left, right, preferred_element_type=f32)


def dot_t(left, right):
    return lax.dot_general(left, right, (((1,), (1,)), ((), ())), preferred_element_type=f32)


def t_dot(left, right):
    return lax.dot_general(left, right, (((0,), (0,)), ((), ())), preferred_element_type=f32)


def swap(value, axis, step):
    count = lax.axis_size(axis)
    return lax.ppermute(value, axis, [(i, i ^ step) for i in range(count)])


def take(stacked, index):
    return lax.dynamic_index_in_dim(stacked, index, 0, keepdims=False)


def place(parts, positions):
    out = jnp.zeros((len(parts),) + parts[0].shape, parts[0].dtype)
    for part, position in zip(parts, positions):
        out = lax.dynamic_update_index_in_dim(out, part, position, 0)
    return out


def after(value, *others):
    return lax.optimization_barrier((value, *others))[0]


def spread(value, combine):
    for axis in ("expert", "dp"):
        step = 1
        while step < lax.axis_size(axis):
            value = combine(value, swap(value, axis, step))
            step *= 2
    return value


def rotation_tables(places):
    half_dim = HDIM // 2
    frequency = rope_base ** (-jnp.arange(half_dim, dtype=f32) * 2.0 / HDIM)
    angles = places.astype(f32)[:, None] * frequency[None, :]
    cosine, sine = jnp.cos(angles), jnp.sin(angles)
    return (
        jnp.concatenate([cosine, cosine], axis=1),
        jnp.concatenate([-sine, sine], axis=1),
    )


def turn(values, cosine, sine):
    return values * cosine + pltpu.roll(values, HDIM // 2, 1) * sine


def lane_value(table, lane):
    lanes = lax.broadcasted_iota(jnp.int32, table.shape, 1)
    return jnp.sum(jnp.where(lanes == lane, table, 0.0), axis=1, keepdims=True)


def allowed_pairs(rows, first_len):
    query_at = lax.broadcasted_iota(jnp.int32, (rows, rows), 0)
    key_at = lax.broadcasted_iota(jnp.int32, (rows, rows), 1)
    return (key_at <= query_at) & ((key_at >= first_len) | (query_at < first_len))


def forward_kernel(
    lens, query, key, value, cosine, sine, gates, hits,
    vals_out, gated_out, query_out, key_out, total_out, peak_out,
):
    m, h, s = pl.program_id(0), pl.program_id(1), pl.program_id(2)
    slot_count = pl.num_programs(2)
    rows = query.shape[0]
    lane = h * slot_count + s

    @pl.when(lane == 0)
    def _():
        total_out[...] = jnp.zeros_like(total_out)
        peak_out[...] = jnp.full_like(peak_out, very_low)

    @pl.when(s == 0)
    def _():
        key_out[...] = turn(key[...].astype(f32), cosine[...], sine[...]).astype(bf16)

    turned = turn(query[...], cosine[...], sine[...]).astype(bf16)
    query_out[...] = turned
    raw = dot_t(turned, key_out[...])
    scores = jnp.where(allowed_pairs(rows, lens[m]), raw * HDIM ** (-0.5), very_low)
    row_peak = jnp.max(scores, axis=1, keepdims=True)
    expo = jnp.exp(scores - row_peak)
    denom = jnp.sum(expo, axis=1, keepdims=True)
    probs = expo / denom
    vals = dot(probs.astype(bf16), value[...]).astype(bf16)
    vals_out[...] = vals
    gated_out[...] = (lane_value(gates[...], s) * vals.astype(f32)).astype(bf16)
    lanes = lax.broadcasted_iota(jnp.int32, total_out.shape, 1)
    total_out[...] = jnp.where(lanes == lane, row_peak + jnp.log(denom), total_out[...])
    seen = jnp.where(lane_value(hits[...], s) > 0.0, row_peak, very_low)
    peak_lanes = lax.broadcasted_iota(jnp.int32, peak_out.shape, 1)
    peak_out[...] = jnp.where(
        peak_lanes == lane, jnp.max(seen, axis=0, keepdims=True), peak_out[...]
    )


def backward_kernel(
    lens, query, key, value, vals, vals_grad, cosine, sine, gates, total,
    query_grad, key_grad, value_grad, gate_grad, key_sum, value_sum,
):
    m, h, s = pl.program_id(0), pl.program_id(1), pl.program_id(2)
    slot_count = pl.num_programs(2)
    rows = query.shape[0]
    lane = h * slot_count + s

    @pl.when(lane == 0)
    def _():
        gate_grad[...] = jnp.zeros_like(gate_grad)

    @pl.when(s == 0)
    def _():
        key_sum[...] = jnp.zeros_like(key_sum)
        value_sum[...] = jnp.zeros_like(value_sum)

    full_grad = vals_grad[...]
    lanes = lax.broadcasted_iota(jnp.int32, gate_grad.shape, 1)
    slot_sum = jnp.sum(vals[...].astype(f32) * full_grad, axis=1, keepdims=True)
    gate_grad[...] += jnp.where(lanes == s, slot_sum, 0.0)
    gated_grad = (lane_value(gates[...], s) * full_grad).astype(bf16)
    raw = dot_t(query[...], key[...])
    scores = jnp.where(allowed_pairs(rows, lens[m]), raw * HDIM ** (-0.5), very_low)
    probs = jnp.exp(scores - lane_value(total[...], lane))
    prob_grad = dot_t(gated_grad, value[...])
    inner = jnp.sum(probs * prob_grad, axis=1, keepdims=True)
    score_grad = (probs * (prob_grad - inner) * HDIM ** (-0.5)).astype(bf16)
    back_sine = -sine[...]
    turned = dot(score_grad, key[...])
    query_grad[...] = turn(turned, cosine[...], back_sine).astype(bf16)
    key_sum[...] += t_dot(score_grad, query[...])
    value_sum[...] += t_dot(probs.astype(bf16), gated_grad)

    @pl.when(s == slot_count - 1)
    def _():
        key_grad[...] = turn(key_sum[...], cosine[...], back_sine).astype(bf16)
        value_grad[...] = value_sum[...].astype(bf16)


def attention_specs(own_heads, rows):
    def block(index):
        return pl.BlockSpec((rows, HDIM), index)

    return {
        "query": block(lambda m, h, s, lens: (m, s * own_heads + h)),
        "key": block(lambda m, h, s, lens: (m, h)),
        "value": block(lambda m, h, s, lens: (m, own_heads + h)),
        "rows": block(lambda m, h, s, lens: (m, 0)),
        "peak": pl.BlockSpec((8, HDIM), lambda m, h, s, lens: (m, 0)),
    }


def attention_forward(lens, query, joint_kv, tables, gates, hits, own_heads, rows):
    micro = lens.shape[0]
    slots = query.shape[1] // (own_heads * HDIM)
    at = attention_specs(own_heads, rows)
    shape = jax.ShapeDtypeStruct
    total_rows = micro * rows
    return pl.pallas_call(
        forward_kernel,
        grid_spec=pltpu.PrefetchScalarGridSpec(
            num_scalar_prefetch=1,
            grid=(micro, own_heads, slots),
            in_specs=[at["query"], at["key"], at["value"]] + [at["rows"]] * 4,
            out_specs=[at["query"]] * 3 + [at["key"], at["rows"], at["peak"]],
        ),
        out_shape=[shape(query.shape, bf16)] * 3
        + [
            shape((total_rows, own_heads * HDIM), bf16),
            shape((total_rows, HDIM), f32),
            shape((micro * 8, HDIM), f32),
        ],
        cost_estimate=pl.CostEstimate(
            flops=4 * rows * rows * HDIM * micro * HEADS,
            bytes_accessed=14 * query.size,
            transcendentals=rows * rows * micro * HEADS,
        ),
        name="attention_forward",
    )(lens, query, joint_kv, joint_kv, tables[0], tables[1], gates, hits)


def attention_backward(
    lens, query, key, joint_kv, vals, vals_grad, tables, gates, total, own_heads, rows
):
    micro = lens.shape[0]
    slots = query.shape[1] // (own_heads * HDIM)
    at = attention_specs(own_heads, rows)
    shape = jax.ShapeDtypeStruct
    total_rows = micro * rows
    return pl.pallas_call(
        backward_kernel,
        grid_spec=pltpu.PrefetchScalarGridSpec(
            num_scalar_prefetch=1,
            grid=(micro, own_heads, slots),
            in_specs=[at["query"], at["key"], at["value"], at["query"], at["query"]]
            + [at["rows"]] * 4,
            out_specs=[at["query"], at["key"], at["key"], at["rows"]],
            scratch_shapes=[pltpu.VMEM((rows, HDIM), f32)] * 2,
        ),
        out_shape=[shape(query.shape, bf16)]
        + [shape((total_rows, own_heads * HDIM), bf16)] * 2
        + [shape((total_rows, HDIM), f32)],
        cost_estimate=pl.CostEstimate(
            flops=10 * rows * rows * HDIM * micro * HEADS,
            bytes_accessed=14 * query.size,
            transcendentals=rows * rows * micro * HEADS,
        ),
        name="attention_backward",
    )(lens, query, key, joint_kv, vals, vals_grad, tables[0], tables[1], gates, total)


def normalize(values):
    row_scale = lax.rsqrt(jnp.mean(values * values, axis=-1, keepdims=True) + eps_norm)
    return values * row_scale, row_scale


def norm_back(grad_hat, normed, row_scale):
    return row_scale * (grad_hat - normed * jnp.mean(grad_hat * normed, axis=-1, keepdims=True))


def route_gates(logits, routes, expert_table):
    expert_ids = jnp.arange(expert_table.shape[0], dtype=jnp.int32)
    matches = routes[:, :, None] == expert_ids[None, None, :]
    picked = jnp.sum(jnp.where(matches, logits[:, None, :], 0.0), axis=-1)
    gate_vals = jax.nn.softmax(picked, axis=-1)
    slot_ids = route_slots(routes, expert_table)
    chosen = slot_ids[:, :, None] == expert_ids[None, None, :]
    gates = jnp.sum(jnp.where(chosen, gate_vals[:, :, None], 0.0), axis=1)
    return gates, matches, chosen, gate_vals


def route_slots(routes, expert_table):
    expert_ids = jnp.arange(expert_table.shape[0], dtype=jnp.int32)
    matches = routes[..., None] == expert_ids
    return jnp.sum(jnp.where(matches, expert_table, 0), axis=-1)


def gate_back(slot_grad, gate_vals, matches, chosen):
    picked = jnp.sum(jnp.where(chosen, slot_grad[:, None, :], 0.0), axis=-1)
    inner_sum = jnp.sum(gate_vals * picked, axis=-1, keepdims=True)
    picked_grad = gate_vals * (picked - inner_sum)
    return jnp.sum(jnp.where(matches, picked_grad[:, :, None], 0.0), axis=1)


def unit_blocks(count):
    return [(start, min(512, count - start)) for start in range(0, count, 512)]


def expert_kernel(place_ref, hidden, grad, *refs):
    piece_count = (len(refs) - 6) // 2
    own_pieces, near_pieces = refs[:piece_count], refs[piece_count : 2 * piece_count]
    out, hidden_out, act_out, joint_out, weights, sems = refs[2 * piece_count :]
    core, chip = place_ref[0], place_ref[1]
    rows, columns = near_pieces[0].shape
    units = columns // 3
    width = hidden.shape[1]

    @pl.when(pl.program_id(0) == 0)
    def _():
        copies = []
        for k in range(piece_count):
            base = (chip ^ k) * (2 * rows)
            for number, (piece, part) in enumerate(
                ((own_pieces[k], core), (near_pieces[k], 1 - core))
            ):
                start = pl.multiple_of(base + part * rows, 16)
                copies.append(
                    pltpu.make_async_copy(
                        piece, weights.at[pl.ds(start, rows)], sems.at[2 * k + number]
                    )
                )
        for copy in copies:
            copy.start()
        for copy in copies:
            copy.wait()

    slot_sum = jnp.zeros((hidden.shape[0], 1), f32)
    for start, size in unit_blocks(units):
        gate_pre = dot(hidden[...], weights[:, start : start + size])
        up_pre = dot(hidden[...], weights[:, units + start : units + start + size])
        act_grad = dot(grad[...], weights[:, 2 * units + start : 2 * units + start + size])
        sigma = 1.0 / (1.0 + jnp.exp(-gate_pre))
        silu_vals = gate_pre * sigma
        active = (silu_vals * up_pre).astype(bf16)
        act_out[:, start : start + size] = active
        slot_sum += jnp.sum(active.astype(f32) * act_grad, axis=1, keepdims=True)
        gate_grad = act_grad * up_pre * sigma * (1.0 + gate_pre * (1.0 - sigma))
        joint_out[:, start : start + size] = gate_grad.astype(bf16)
        joint_out[:, units + start : units + start + size] = (act_grad * silu_vals).astype(bf16)
    for start in range(0, width, 512):
        block = weights[start : start + 512, : 2 * units]
        hidden_out[:, start : start + 512] = dot_t(joint_out[...], block).astype(bf16)
        block = weights[start : start + 512, 2 * units :]
        out[:, start : start + 512] = dot_t(act_out[...], block).astype(bf16)
    lanes = lax.broadcasted_iota(jnp.int32, (hidden.shape[0], HDIM), 1)
    hidden_out[:, width:] = jnp.where(lanes == 0, slot_sum, 0.0).astype(bf16)


def expert_rows(position, hidden, grad, own_pieces, near_pieces):
    rows, width = hidden.shape
    columns = near_pieces[0].shape[1]
    units = columns // 3
    tile = 256
    shape = jax.ShapeDtypeStruct
    count = len(own_pieces)

    def tiled(size):
        return pl.BlockSpec((tile, size), lambda i, at: (i, 0))

    return pl.pallas_call(
        expert_kernel,
        grid_spec=pltpu.PrefetchScalarGridSpec(
            num_scalar_prefetch=1,
            grid=(rows // tile,),
            in_specs=[tiled(width)] * 2 + [pl.BlockSpec(memory_space=pl.ANY)] * (2 * count),
            out_specs=[tiled(width), tiled(width + HDIM), tiled(units), tiled(2 * units)],
            scratch_shapes=[
                pltpu.VMEM((width, columns), bf16),
                pltpu.SemaphoreType.DMA((2 * count,)),
            ],
        ),
        out_shape=[
            shape((rows, width), bf16),
            shape((rows, width + HDIM), bf16),
            shape((rows, units), bf16),
            shape((rows, 2 * units), bf16),
        ],
        compiler_params=pltpu.CompilerParams(vmem_limit_bytes=56 * 2**20),
        cost_estimate=pl.CostEstimate(
            flops=4 * rows * width * columns,
            bytes_accessed=2 * (width * columns + 6 * rows * width),
            transcendentals=rows * units,
        ),
        name="expert_rows",
    )(position, hidden, grad, *own_pieces, *near_pieces)


def expert_grad_kernel(order, hidden, grad, gates, joint, active, *outs):
    gate = gates[...]
    left = (hidden[...].astype(f32) * gate).astype(bf16)
    right = (grad[...].astype(f32) * gate).astype(bf16)
    units = active.shape[1]
    step = pl.program_id(0)
    for number, out in enumerate(outs):

        @pl.when(step == number)
        def _():
            for start, size in unit_blocks(2 * units):
                out[:, start : start + size] = t_dot(left, joint[:, start : start + size]).astype(bf16)
            for start, size in unit_blocks(units):
                out[:, 2 * units + start : 2 * units + start + size] = t_dot(
                    right, active[:, start : start + size]
                ).astype(bf16)


def expert_grads(chunks, chunk_rows, hidden, grad, gates, joint, active):
    rows, units = active.shape
    half = chunk_rows // 2
    count = len(chunks)
    order = jnp.stack([2 * chunk + part for chunk in chunks for part in range(2)]).astype(jnp.int32)

    def whole(size):
        return pl.BlockSpec((rows, size), lambda i, at: (0, 0), pipeline_mode=pl.Buffered(1))

    column = pl.BlockSpec((rows, half), lambda i, at: (0, at[i]))
    return pl.pallas_call(
        expert_grad_kernel,
        grid_spec=pltpu.PrefetchScalarGridSpec(
            num_scalar_prefetch=1,
            grid=(2 * count,),
            in_specs=[column, column, whole(1), whole(2 * units), whole(units)],
            out_specs=[
                pl.BlockSpec((half, 3 * units), lambda i, at: (0, 0)) for _ in range(2 * count)
            ],
        ),
        out_shape=[jax.ShapeDtypeStruct((half, 3 * units), bf16)] * (2 * count),
        compiler_params=pltpu.CompilerParams(vmem_limit_bytes=48 * 2**20),
        cost_estimate=pl.CostEstimate(
            flops=2 * count * chunk_rows * rows * 3 * units,
            bytes_accessed=2 * (rows * 3 * units + count * chunk_rows * (2 * rows + 3 * units)),
            transcendentals=0,
        ),
        name="expert_grads",
    )(order, hidden, grad, gates, joint, active)


def local(
    tokens,
    cotangent,
    seq_lengths,
    dealing,
    attn_routes,
    ffn_routes,
    expert_table,
    clip_limit,
    attn_gain,
    ffn_gain,
    attn_router,
    ffn_router,
    query_weight,
    attn_out_weight,
    kv_weight,
    gate_up_weight,
    down_weight,
):
    micro, tok_rows, width = tokens.shape
    dp_count = lax.axis_size("dp")
    slots = lax.axis_size("expert")
    col = lax.axis_index("expert")
    group = lax.axis_index("dp")
    piece_rows = tok_rows // dp_count
    cap = tok_rows * TOP * 3 // (2 * slots)
    group_rows = tok_rows * slots
    all_rows = micro * group_rows
    home_rows = micro * tok_rows
    query_width = HEADS * HDIM
    own_heads = HEADS // slots
    own_width = own_heads * HDIM
    shard_rows = query_weight.shape[1]
    score_scale = HDIM ** (-0.5)
    core = group % 2
    chip = group // 2
    side = chip % 2
    chips = dp_count // 2
    lines = chips // 2
    quarter = FF // 4
    chip_rows = 2 * shard_rows

    both = jnp.stack([tokens, cotangent]).reshape(2 * micro, dp_count, piece_rows, width)
    both = lax.all_to_all(both.transpose(1, 0, 2, 3), "dp", split_axis=0, concat_axis=0, tiled=True)
    def quarter_of(half, part):
        start = (2 * half + part) * quarter
        return jnp.concatenate(
            [
                lax.dynamic_slice_in_dim(gate_up_weight[0], start, quarter, 1),
                lax.dynamic_slice_in_dim(gate_up_weight[0], FF + start, quarter, 1),
                lax.dynamic_slice_in_dim(down_weight[0], start, quarter, 1),
            ],
            axis=1,
        )

    parts = (1 - core, core)
    keep_pair = [quarter_of(side, part) for part in parts]
    send_pair = [quarter_of(1 - side, part) for part in parts]
    both, keep_pair, send_pair, kv_in, query_in, out_in = lax.optimization_barrier(
        (both, keep_pair, send_pair, kv_weight, query_weight[0], attn_out_weight[0])
    )
    side_pair = [swap(piece, "dp", 2) for piece in send_pair]
    line_steps = [4 * line for line in range(1, lines)]
    keep_lines = [[swap(piece, "dp", step) for step in line_steps] for piece in keep_pair]
    side_lines = [[swap(piece, "dp", step) for step in line_steps] for piece in side_pair]
    pairs = [keep_pair, side_pair]
    for line in range(lines - 1):
        pairs += [[part[line] for part in keep_lines], [part[line] for part in side_lines]]
    near_pieces = [swap(pair[0], "dp", 1) for pair in pairs]
    own_pieces = [pair[1] for pair in pairs]

    both = both.transpose(1, 0, 2, 3).reshape(2, micro, tok_rows, width)
    deal = (dealing[:, :, None] == jnp.arange(tok_rows, dtype=jnp.int32)).astype(bf16)
    work = jnp.einsum("mtr,bmrd->bmtd", deal, both, preferred_element_type=f32)
    x_home = work[0].reshape(home_rows, width)
    dy_home = work[1].reshape(home_rows, width)

    def columns_of(*shards):
        pieces = [shard.reshape(shard_rows, slots, own_width) for shard in shards]
        out = jnp.zeros((shard_rows, len(shards) * query_width), shards[0].dtype)
        for k in range(slots):
            part = jnp.concatenate(
                [lax.dynamic_index_in_dim(piece, col ^ k, 1, keepdims=False) for piece in pieces],
                axis=1,
            )
            part = swap(part, "expert", k) if k else part
            for number in range(len(shards)):
                out = lax.dynamic_update_slice_in_dim(
                    out,
                    part[:, number * own_width : (number + 1) * own_width],
                    number * query_width + (col ^ k) * own_width,
                    1,
                )
        return out

    def slots_of(columns):
        pieces = columns.reshape(shard_rows, slots, own_width)
        out = jnp.zeros((shard_rows, query_width), columns.dtype)
        for k in range(slots):
            part = lax.dynamic_index_in_dim(pieces, col ^ k, 1, keepdims=False)
            part = swap(part, "expert", k) if k else part
            out = lax.dynamic_update_slice_in_dim(out, part, (col ^ k) * own_width, 1)
        return out

    half_slots = slots // 2
    first_pairs = [(c, 2 * c) for c in range(half_slots)]
    first_pairs += [(c, 2 * (c - half_slots) + 1) for c in range(half_slots, slots)]
    second_pairs = [(c, 2 * c + 1) for c in range(half_slots)]
    second_pairs += [(c, 2 * (c - half_slots)) for c in range(half_slots, slots)]
    holds_keys = col < half_slots
    even_col = col % 2 == 0
    low_kv, high_kv = kv_in[:, :own_width], kv_in[:, own_width:]
    first_got = lax.ppermute(jnp.where(holds_keys, low_kv, high_kv), "expert", first_pairs)
    second_got = lax.ppermute(jnp.where(holds_keys, high_kv, low_kv), "expert", second_pairs)
    own_kv = jnp.concatenate(
        [
            jnp.where(even_col, first_got, second_got),
            jnp.where(even_col, second_got, first_got),
        ],
        axis=1,
    )
    kv_full = lax.all_gather(own_kv, "dp", axis=0, tiled=True)
    joint_full = lax.all_gather(
        after(columns_of(query_in, out_in), side_pair[0], *keep_lines[0]), "dp", axis=0, tiled=True
    )
    query_full, out_full = joint_full[:, :query_width], joint_full[:, query_width:]

    positions = jnp.arange(group_rows, dtype=jnp.int32)
    first_len = lax.dynamic_index_in_dim(seq_lengths[:, :, 0], group, 1, keepdims=True)
    in_second = positions[None, :] >= first_len
    places = positions[None, :] - jnp.where(in_second, first_len, 0)
    tables = rotation_tables(places.reshape(all_rows))

    def gather_rows(value):
        shaped = value.reshape(micro, tok_rows, -1)
        out = jnp.zeros((micro, group_rows, shaped.shape[-1]), value.dtype)
        for k in range(slots):
            part = swap(shaped, "expert", k) if k else shaped
            out = lax.dynamic_update_slice_in_dim(out, part, (col ^ k) * tok_rows, 1)
        return out.reshape(all_rows, -1)

    def scatter_rows(value):
        shaped = value.reshape(micro, group_rows, -1)
        total = None
        for k in range(slots):
            part = lax.dynamic_slice_in_dim(shaped, (col ^ k) * tok_rows, tok_rows, 1)
            if k:
                part = swap(part.astype(bf16), "expert", k)
            part = part.astype(f32)
            total = part if total is None else total + part
        return total.reshape(home_rows, -1)

    home_routes = lax.dynamic_slice_in_dim(ffn_routes, col * tok_rows, tok_rows, 1)
    home_slots = route_slots(home_routes, expert_table)
    packs = []
    before = jnp.tril(jnp.ones((tok_rows, tok_rows), bf16), -1)
    for k in range(slots):
        hits = jnp.any(home_slots == (col ^ k), axis=-1)
        rank = jnp.einsum("ts,ms->mt", before, hits.astype(bf16), preferred_element_type=f32)
        packs.append(
            hits[:, None, :]
            & (rank[:, None, :] == jnp.arange(cap, dtype=jnp.int32).astype(f32)[None, :, None])
        )
    packs = jnp.stack(packs)
    packs_low = packs.astype(bf16)
    pack_rows = micro * cap
    sent_rows = slots * pack_rows

    def send_packed(value):
        packed = jnp.einsum(
            "kmct,mtd->kmcd", packs_low, value.reshape(micro, tok_rows, -1), preferred_element_type=f32
        ).astype(bf16)
        parts = [swap(packed[k], "expert", k) if k else packed[k] for k in range(slots)]
        return jnp.stack(parts).reshape(sent_rows, -1)

    def quad_rows(value):
        near = swap(value, "dp", 1)
        far = swap(value, "dp", 2)
        across = swap(far, "dp", 1)
        return jnp.concatenate([value, near, far, across], axis=0)

    def quad_sum(value, *others):
        own, near, far, across = jnp.split(value, 4, axis=0)
        far_sum = far.astype(f32) + swap(across, "dp", 1).astype(f32)
        own_sum = own.astype(f32) + swap(near, "dp", 1).astype(f32)
        return own_sum + after(swap(far_sum.astype(bf16), "dp", 2), *others).astype(f32)

    def return_packed(value, *others):
        shaped = value.astype(bf16).reshape(slots, micro, cap, -1)
        parts = [swap(shaped[k], "expert", k) if k else shaped[k] for k in range(slots)]
        return after(parts, *others)

    def unpack(packed, scale):
        total = None
        for k in range(slots):
            rows = jnp.einsum("mct,mcd->mtd", packs_low[k], packed[k], preferred_element_type=f32)
            rows = rows.reshape(home_rows, -1) * take(scale.T, col ^ k)[:, None]
            total = rows if total is None else total + rows
        return total

    gain_one = attn_gain.astype(f32)
    gain_two = ffn_gain.astype(f32)
    normed_one, scale_one = normalize(x_home)
    hidden_one_home = (normed_one * gain_one).astype(bf16)
    hidden_one_raw = gather_rows(hidden_one_home)
    hidden_one = after(hidden_one_raw, side_pair[1], *keep_lines[1])
    grad_sent = send_packed(after(dy_home.astype(bf16), hidden_one))
    grad_rows = quad_rows(grad_sent)
    logits_one = dot(hidden_one, attn_router)
    gates_one, matches_one, chosen_one, gate_vals_one = route_gates(
        logits_one, attn_routes.reshape(all_rows, TOP), expert_table
    )
    hits_one = jnp.any(chosen_one, axis=1).astype(f32)

    def wide(value):
        return jnp.pad(value, ((0, 0), (0, HDIM - value.shape[1])))

    kv_part = dot(hidden_one, kv_full).astype(bf16)
    query_part = dot(hidden_one, query_full)
    lens = first_len[:, 0].astype(jnp.int32)
    gates_wide = wide(gates_one)
    attn_vals, gated_vals, query_rot, key_rot, log_total, peaks = attention_forward(
        lens, query_part, kv_part, tables, gates_wide, wide(hits_one), own_heads, group_rows
    )
    peaks = jnp.max(peaks, axis=0)[: own_heads * slots].reshape(own_heads, slots).T
    peak_table = lax.dynamic_update_slice_in_dim(
        jnp.full((slots, HEADS), very_low, f32), peaks, col * own_heads, 1
    )
    gated_vals = after(gated_vals, grad_sent, *side_lines[0])
    attn_home = scatter_rows(dot_t(gated_vals, out_full))

    resid = x_home + attn_home
    normed_two, scale_two = normalize(resid)
    hidden_two = (normed_two * gain_two).astype(bf16)
    logits_two = dot(hidden_two, ffn_router)
    gates_two, matches_two, chosen_two, gate_vals_two = route_gates(
        logits_two, home_routes.reshape(home_rows, TOP), expert_table
    )
    hidden_sent = send_packed(after(hidden_two, grad_rows))
    hidden_rows = quad_rows(after(hidden_sent, *side_lines[1], *near_pieces))
    gates_by_slot = gates_two.reshape(micro, tok_rows, slots)
    gate_parts = []
    for k in range(slots):
        gate_col = lax.dynamic_index_in_dim(gates_by_slot, col ^ k, 2, keepdims=False)
        part = jnp.sum(jnp.where(packs[k], gate_col[:, None, :], 0.0), axis=-1).reshape(pack_rows)
        gate_parts.append(swap(part, "expert", k) if k else part)
    gate_rows = quad_rows(jnp.concatenate(gate_parts))

    hidden_rows = after(hidden_rows, gate_rows)
    position = jnp.stack([core, chip]).astype(jnp.int32)
    ffn_part, hidden_part, active, joint_grad = expert_rows(
        position, hidden_rows, grad_rows, own_pieces, near_pieces
    )

    def block_grads(steps):
        return expert_grads(
            [chip ^ k for k in steps], chip_rows, hidden_rows, grad_rows, gate_rows[:, None],
            joint_grad, active,
        )

    line_grads = block_grads([k ^ 1 for k in range(2, chips)])
    side_got, keep_got = [
        [
            [swap(line_grads[4 * line + 2 * which + part], "dp", 4 * line + 4) for line in range(lines - 1)]
            for part in range(2)
        ]
        for which in range(2)
    ]
    hidden_sum = quad_sum(hidden_part, *line_grads)
    own_grads = block_grads([1, 0])
    back_packed = return_packed(hidden_sum, *own_grads)

    def total(own, got):
        return functools.reduce(jnp.add, [part.astype(f32) for part in [own] + got]).astype(bf16)

    other_sums = [swap(total(own_grads[part], side_got[part]), "dp", 2) for part in range(2)]
    slot_two_grad = jnp.zeros((slots, home_rows), f32)
    for k in range(slots):
        rows = jnp.sum(
            jnp.where(packs[k], back_packed[k][:, :, width].astype(f32)[:, :, None], 0.0), axis=1
        )
        slot_two_grad = lax.dynamic_update_index_in_dim(
            slot_two_grad, rows.reshape(home_rows), col ^ k, 0
        )
    hidden_two_grad = unpack([part[..., :width] for part in back_packed], gates_two)
    logit_two_grad = gate_back(slot_two_grad.T, gate_vals_two, matches_two, chosen_two).astype(bf16)
    hidden_two_grad = hidden_two_grad + dot_t(logit_two_grad, ffn_router)
    router_two_grad = t_dot(logit_two_grad, hidden_two)
    gain_two_grad = jnp.sum(hidden_two_grad * normed_two, axis=0)
    resid_grad = dy_home + norm_back(hidden_two_grad * gain_two, normed_two, scale_two)

    ffn_sum = quad_sum(after(ffn_part, hidden_sum))

    resid_grad_low = after(resid_grad.astype(bf16), ffn_sum, *side_got[0])
    resid_grad_all = after(gather_rows(resid_grad_low), *side_got[1])
    ffn_packed = return_packed(after(ffn_sum, resid_grad_all))
    out_home = (resid + unpack(ffn_packed, gates_two)).astype(bf16)
    out_part = t_dot(resid_grad_all, gated_vals).astype(bf16)
    vals_grad = after(dot(resid_grad_all, out_full), out_part, *keep_got[0])
    query_grad, key_grad, value_grad, slot_part_one = attention_backward(
        lens, query_rot, key_rot, kv_part, attn_vals, vals_grad, tables, gates_wide, log_total,
        own_heads, group_rows,
    )
    query_grad, key_grad, value_grad, slot_part_one = lax.optimization_barrier(
        (query_grad, key_grad, value_grad, slot_part_one, ffn_packed, keep_got[1])
    )[:4]
    kv_grad = jnp.concatenate([key_grad, value_grad], axis=1)
    hidden_one_part = dot_t(query_grad, query_full) + dot_t(kv_grad, kv_full)
    hidden_one_part = after(hidden_one_part.astype(bf16), other_sums[0])
    hidden_one_late = after(hidden_one, hidden_one_part)
    query_part_grad = t_dot(hidden_one_late, query_grad).astype(bf16)
    kv_part_grad = t_dot(after(hidden_one_late, query_part_grad), kv_grad).astype(bf16)
    back_one = scatter_rows(
        jnp.concatenate([hidden_one_part, slot_part_one.astype(bf16)], axis=1)
    )
    back_one = after(back_one, query_part_grad, kv_part_grad, other_sums[1])
    hidden_one_grad, slot_one_grad = back_one[:, :width], back_one[:, width : width + slots]

    def own(value):
        shaped = value.reshape((micro, group_rows) + value.shape[1:])
        part = lax.dynamic_slice_in_dim(shaped, col * tok_rows, tok_rows, 1)
        return part.reshape((home_rows,) + value.shape[1:])

    logit_one_grad = gate_back(
        slot_one_grad, own(gate_vals_one), own(matches_one), own(chosen_one)
    ).astype(bf16)
    hidden_one_grad = hidden_one_grad + dot_t(logit_one_grad, attn_router)
    router_one_grad = t_dot(logit_one_grad, hidden_one_home)
    gain_one_grad = jnp.sum(hidden_one_grad * normed_one, axis=0)
    in_home = resid_grad + norm_back(hidden_one_grad * gain_one, normed_one, scale_one)

    keep_sums = [total(own_grads[2 + part], keep_got[part]) for part in range(2)]
    by_rows = [jnp.stack([keep_sums[part], other_sums[part]]) for part in range(2)]
    own_pair = jnp.where(core == 0, by_rows[0], by_rows[1])
    near_pair = swap(jnp.where(core == 0, by_rows[1], by_rows[0]), "dp", 1)
    by_core = [jnp.where(core == 0, own_pair, near_pair), jnp.where(core == 0, near_pair, own_pair)]
    by_side = [[jnp.where(side == s, part[0], part[1]) for part in by_core] for s in range(2)]
    blocks = [part for row in by_side for part in row]
    gate_up_grad = jnp.concatenate(
        [b[:, :quarter] for b in blocks] + [b[:, quarter : 2 * quarter] for b in blocks], axis=1
    ).astype(f32)
    down_grad = jnp.concatenate([b[:, 2 * quarter :] for b in blocks], axis=1).astype(f32)

    results = jnp.stack([out_home, in_home.astype(bf16)]).reshape(2, micro, tok_rows, width)
    results = jnp.einsum("mtr,bmtd->bmrd", deal, results, preferred_element_type=f32).astype(bf16)
    results = results.reshape(2 * micro, dp_count, piece_rows, width).transpose(1, 0, 2, 3)
    results = lax.all_to_all(results, "dp", split_axis=0, concat_axis=0, tiled=True)
    results = results.transpose(1, 0, 2, 3).reshape(2, micro, tok_rows, width)

    def reduced(value):
        return lax.psum_scatter(value, "dp", scatter_dimension=0, tiled=True)

    out_grad = slots_of(reduced(out_part))
    query_own = reduced(query_part_grad)
    kv_own = reduced(kv_part_grad)
    results, out_grad, query_own, kv_own = lax.optimization_barrier(
        (results, out_grad, query_own, kv_own)
    )
    out_grad = out_grad.astype(f32)
    query_out = slots_of(query_own).astype(f32)
    key_part, value_part = kv_own[:, :own_width], kv_own[:, own_width:]
    first_back = lax.ppermute(
        jnp.where(even_col, key_part, value_part), "expert", [(b, a) for a, b in first_pairs]
    )
    second_back = lax.ppermute(
        jnp.where(even_col, value_part, key_part), "expert", [(b, a) for a, b in second_pairs]
    )
    kv_out = jnp.concatenate(
        [
            jnp.where(holds_keys, first_back, second_back),
            jnp.where(holds_keys, second_back, first_back),
        ],
        axis=1,
    ).astype(f32)

    sum_rows = 2 + 2 * slots
    peak_rows = jnp.pad(peak_table, ((0, 0), (0, width - HEADS)))
    sums = spread(
        jnp.concatenate(
            [gain_one_grad[None], gain_two_grad[None], router_one_grad, router_two_grad, peak_rows],
            axis=0,
        ),
        lambda left, right: jnp.where(
            jnp.arange(sum_rows + slots)[:, None] < sum_rows, left + right, jnp.maximum(left, right)
        ),
    )
    peaks_all = sums[sum_rows:, :HEADS]
    limit = clip_limit[0].astype(f32)
    factor = limit / jnp.maximum(peaks_all, limit)
    query_scale = jnp.repeat(jnp.sqrt(take(factor, col)), HDIM)
    query_clipped = (query_weight.astype(f32) * query_scale[None, None, :]).astype(bf16)
    full_scale = jnp.concatenate(
        [jnp.repeat(jnp.sqrt(jnp.min(factor, axis=0)), HDIM), jnp.ones((query_width,), f32)]
    )
    piece_width = kv_weight.shape[1]
    piece_scale = lax.dynamic_slice_in_dim(full_scale, col * piece_width, piece_width)
    kv_clipped = (kv_weight.astype(f32) * piece_scale[None, :]).astype(bf16)
    return (
        results[0],
        results[1],
        sums[0],
        sums[1],
        sums[2 : 2 + slots].T,
        sums[2 + slots : sum_rows].T,
        query_out[None],
        out_grad[None],
        kv_out,
        gate_up_grad[None],
        down_grad[None],
        query_clipped,
        kv_clipped,
    )


def solution(mesh):
    placed = (
        P(None, ("dp", "expert"), None),
        P(None, ("dp", "expert"), None),
        P(),
        P(None, ("dp", "expert")),
        P(None, "dp", None),
        P(None, "dp", None),
        P(),
        P(),
        P(),
        P(),
        P(),
        P(),
        P("expert", "dp", None),
        P("expert", "dp", None),
        P("dp", "expert"),
        P("expert", "dp", None),
        P("expert", "dp", None),
    )
    return jax.shard_map(
        local,
        mesh=mesh,
        in_specs=placed,
        out_specs=(
            P(None, ("dp", "expert"), None),
            P(None, ("dp", "expert"), None),
            P(),
            P(),
            P(),
            P(),
            P("expert", "dp", None),
            P("expert", "dp", None),
            P("dp", "expert"),
            P("expert", "dp", None),
            P("expert", "dp", None),
            P("expert", "dp", None),
            P("dp", "expert"),
        ),
        check_vma=False,
    )
```

```python
import functools

import jax
import jax.numpy as jnp
from jax import lax
from jax.experimental import pallas as pl
from jax.experimental.pallas import tpu as pltpu
from jax.sharding import PartitionSpec as P

HEADS = 16
HDIM = 128
FF = 5632
TOP = 2

eps_norm = 1e-06
rope_base = 10000.0
very_low = -1e30

f32 = jnp.float32
bf16 = jnp.bfloat16


def dot(left, right):
    return jnp.dot(left, right, preferred_element_type=f32)


def dot_t(left, right):
    return lax.dot_general(left, right, (((1,), (1,)), ((), ())), preferred_element_type=f32)


def t_dot(left, right):
    return lax.dot_general(left, right, (((0,), (0,)), ((), ())), preferred_element_type=f32)


def swap(value, axis, step):
    count = lax.axis_size(axis)
    return lax.ppermute(value, axis, [(i, i ^ step) for i in range(count)])


def take(stacked, index):
    return lax.dynamic_index_in_dim(stacked, index, 0, keepdims=False)


def place(parts, positions):
    out = jnp.zeros((len(parts),) + parts[0].shape, parts[0].dtype)
    for part, position in zip(parts, positions):
        out = lax.dynamic_update_index_in_dim(out, part, position, 0)
    return out


def after(value, *others):
    return lax.optimization_barrier((value, others))[0]


def spread(value, combine):
    for axis in ("expert", "dp"):
        step = 1
        while step < lax.axis_size(axis):
            value = combine(value, swap(value, axis, step))
            step *= 2
    return value


def rotation_tables(places):
    half_dim = HDIM // 2
    frequency = rope_base ** (-jnp.arange(half_dim, dtype=f32) * 2.0 / HDIM)
    angles = places.astype(f32)[:, None] * frequency[None, :]
    cosine, sine = jnp.cos(angles), jnp.sin(angles)
    return (
        jnp.concatenate([cosine, cosine], axis=1),
        jnp.concatenate([-sine, sine], axis=1),
    )


def turn(values, cosine, sine):
    return values * cosine + pltpu.roll(values, HDIM // 2, 1) * sine


def lane_value(table, lane):
    lanes = lax.broadcasted_iota(jnp.int32, table.shape, 1)
    return jnp.sum(jnp.where(lanes == lane, table, 0.0), axis=1, keepdims=True)


def allowed_pairs(rows, first_len):
    query_at = lax.broadcasted_iota(jnp.int32, (rows, rows), 0)
    key_at = lax.broadcasted_iota(jnp.int32, (rows, rows), 1)
    return (key_at <= query_at) & ((key_at >= first_len) | (query_at < first_len))


def forward_kernel(
    lens, query, key, value, cosine, sine, gates, hits,
    vals_out, gated_out, query_out, key_out, total_out, peak_out,
):
    m, h, s = pl.program_id(0), pl.program_id(1), pl.program_id(2)
    slot_count = pl.num_programs(2)
    rows = query.shape[0]
    lane = h * slot_count + s

    @pl.when(lane == 0)
    def _():
        total_out[...] = jnp.zeros_like(total_out)
        peak_out[...] = jnp.full_like(peak_out, very_low)

    @pl.when(s == 0)
    def _():
        key_out[...] = turn(key[...].astype(f32), cosine[...], sine[...]).astype(bf16)

    turned = turn(query[...], cosine[...], sine[...]).astype(bf16)
    query_out[...] = turned
    raw = dot_t(turned, key_out[...])
    scores = jnp.where(allowed_pairs(rows, lens[m]), raw * HDIM ** (-0.5), very_low)
    row_peak = jnp.max(scores, axis=1, keepdims=True)
    expo = jnp.exp(scores - row_peak)
    denom = jnp.sum(expo, axis=1, keepdims=True)
    probs = expo / denom
    vals = dot(probs.astype(bf16), value[...]).astype(bf16)
    vals_out[...] = vals
    gated_out[...] = (lane_value(gates[...], s) * vals.astype(f32)).astype(bf16)
    lanes = lax.broadcasted_iota(jnp.int32, total_out.shape, 1)
    total_out[...] = jnp.where(lanes == lane, row_peak + jnp.log(denom), total_out[...])
    seen = jnp.where(lane_value(hits[...], s) > 0.0, row_peak, very_low)
    peak_lanes = lax.broadcasted_iota(jnp.int32, peak_out.shape, 1)
    peak_out[...] = jnp.where(
        peak_lanes == lane, jnp.max(seen, axis=0, keepdims=True), peak_out[...]
    )


def backward_kernel(
    lens, query, key, value, vals, vals_grad, cosine, sine, gates, total,
    query_grad, key_grad, value_grad, gate_grad, key_sum, value_sum,
):
    m, h, s = pl.program_id(0), pl.program_id(1), pl.program_id(2)
    slot_count = pl.num_programs(2)
    rows = query.shape[0]
    lane = h * slot_count + s

    @pl.when(lane == 0)
    def _():
        gate_grad[...] = jnp.zeros_like(gate_grad)

    @pl.when(s == 0)
    def _():
        key_sum[...] = jnp.zeros_like(key_sum)
        value_sum[...] = jnp.zeros_like(value_sum)

    full_grad = vals_grad[...]
    lanes = lax.broadcasted_iota(jnp.int32, gate_grad.shape, 1)
    slot_sum = jnp.sum(vals[...].astype(f32) * full_grad, axis=1, keepdims=True)
    gate_grad[...] += jnp.where(lanes == s, slot_sum, 0.0)
    gated_grad = (lane_value(gates[...], s) * full_grad).astype(bf16)
    raw = dot_t(query[...], key[...])
    scores = jnp.where(allowed_pairs(rows, lens[m]), raw * HDIM ** (-0.5), very_low)
    probs = jnp.exp(scores - lane_value(total[...], lane))
    prob_grad = dot_t(gated_grad, value[...])
    inner = jnp.sum(probs * prob_grad, axis=1, keepdims=True)
    score_grad = (probs * (prob_grad - inner) * HDIM ** (-0.5)).astype(bf16)
    back_sine = -sine[...]
    turned = dot(score_grad, key[...])
    query_grad[...] = turn(turned, cosine[...], back_sine).astype(bf16)
    key_sum[...] += t_dot(score_grad, query[...])
    value_sum[...] += t_dot(probs.astype(bf16), gated_grad)

    @pl.when(s == slot_count - 1)
    def _():
        key_grad[...] = turn(key_sum[...], cosine[...], back_sine).astype(bf16)
        value_grad[...] = value_sum[...].astype(bf16)


def attention_specs(own_heads, rows):
    def block(index):
        return pl.BlockSpec((rows, HDIM), index)

    return {
        "query": block(lambda m, h, s, lens: (m, s * own_heads + h)),
        "key": block(lambda m, h, s, lens: (m, h)),
        "value": block(lambda m, h, s, lens: (m, own_heads + h)),
        "rows": block(lambda m, h, s, lens: (m, 0)),
        "peak": pl.BlockSpec((8, HDIM), lambda m, h, s, lens: (m, 0)),
    }


def attention_forward(lens, query, joint_kv, tables, gates, hits, own_heads, rows):
    micro = lens.shape[0]
    slots = query.shape[1] // (own_heads * HDIM)
    at = attention_specs(own_heads, rows)
    shape = jax.ShapeDtypeStruct
    total_rows = micro * rows
    return pl.pallas_call(
        forward_kernel,
        grid_spec=pltpu.PrefetchScalarGridSpec(
            num_scalar_prefetch=1,
            grid=(micro, own_heads, slots),
            in_specs=[at["query"], at["key"], at["value"]] + [at["rows"]] * 4,
            out_specs=[at["query"]] * 3 + [at["key"], at["rows"], at["peak"]],
        ),
        out_shape=[shape(query.shape, bf16)] * 3
        + [
            shape((total_rows, own_heads * HDIM), bf16),
            shape((total_rows, HDIM), f32),
            shape((micro * 8, HDIM), f32),
        ],
        cost_estimate=pl.CostEstimate(
            flops=4 * rows * rows * HDIM * micro * HEADS,
            bytes_accessed=14 * query.size,
            transcendentals=rows * rows * micro * HEADS,
        ),
        name="attention_forward",
    )(lens, query, joint_kv, joint_kv, tables[0], tables[1], gates, hits)


def attention_backward(
    lens, query, key, joint_kv, vals, vals_grad, tables, gates, total, own_heads, rows
):
    micro = lens.shape[0]
    slots = query.shape[1] // (own_heads * HDIM)
    at = attention_specs(own_heads, rows)
    shape = jax.ShapeDtypeStruct
    total_rows = micro * rows
    return pl.pallas_call(
        backward_kernel,
        grid_spec=pltpu.PrefetchScalarGridSpec(
            num_scalar_prefetch=1,
            grid=(micro, own_heads, slots),
            in_specs=[at["query"], at["key"], at["value"], at["query"], at["query"]]
            + [at["rows"]] * 4,
            out_specs=[at["query"], at["key"], at["key"], at["rows"]],
            scratch_shapes=[pltpu.VMEM((rows, HDIM), f32)] * 2,
        ),
        out_shape=[shape(query.shape, bf16)]
        + [shape((total_rows, own_heads * HDIM), bf16)] * 2
        + [shape((total_rows, HDIM), f32)],
        cost_estimate=pl.CostEstimate(
            flops=10 * rows * rows * HDIM * micro * HEADS,
            bytes_accessed=14 * query.size,
            transcendentals=rows * rows * micro * HEADS,
        ),
        name="attention_backward",
    )(lens, query, key, joint_kv, vals, vals_grad, tables[0], tables[1], gates, total)


def normalize(values):
    row_scale = lax.rsqrt(jnp.mean(values * values, axis=-1, keepdims=True) + eps_norm)
    return values * row_scale, row_scale


def norm_back(grad_hat, normed, row_scale):
    return row_scale * (grad_hat - normed * jnp.mean(grad_hat * normed, axis=-1, keepdims=True))


def route_gates(logits, routes, expert_table):
    expert_ids = jnp.arange(expert_table.shape[0], dtype=jnp.int32)
    matches = routes[:, :, None] == expert_ids[None, None, :]
    picked = jnp.sum(jnp.where(matches, logits[:, None, :], 0.0), axis=-1)
    gate_vals = jax.nn.softmax(picked, axis=-1)
    slot_ids = route_slots(routes, expert_table)
    chosen = slot_ids[:, :, None] == expert_ids[None, None, :]
    gates = jnp.sum(jnp.where(chosen, gate_vals[:, :, None], 0.0), axis=1)
    return gates, matches, chosen, gate_vals


def route_slots(routes, expert_table):
    expert_ids = jnp.arange(expert_table.shape[0], dtype=jnp.int32)
    matches = routes[..., None] == expert_ids
    return jnp.sum(jnp.where(matches, expert_table, 0), axis=-1)


def gate_back(slot_grad, gate_vals, matches, chosen):
    picked = jnp.sum(jnp.where(chosen, slot_grad[:, None, :], 0.0), axis=-1)
    inner_sum = jnp.sum(gate_vals * picked, axis=-1, keepdims=True)
    picked_grad = gate_vals * (picked - inner_sum)
    return jnp.sum(jnp.where(matches, picked_grad[:, :, None], 0.0), axis=1)


def unit_blocks(count):
    return [(start, min(512, count - start)) for start in range(0, count, 512)]


def expert_kernel(place_ref, hidden, grad, *refs):
    piece_count = (len(refs) - 6) // 2
    own_pieces, near_pieces = refs[:piece_count], refs[piece_count : 2 * piece_count]
    out, hidden_out, act_out, joint_out, weights, sems = refs[2 * piece_count :]
    core, chip = place_ref[0], place_ref[1]
    rows, columns = near_pieces[0].shape
    units = columns // 3
    width = grad.shape[1]

    @pl.when(pl.program_id(0) == 0)
    def _():
        copies = []
        for k in range(piece_count):
            base = (chip ^ k) * (2 * rows)
            for number, (piece, part) in enumerate(
                ((own_pieces[k], core), (near_pieces[k], 1 - core))
            ):
                start = pl.multiple_of(base + part * rows, 16)
                copies.append(
                    pltpu.make_async_copy(
                        piece, weights.at[pl.ds(start, rows)], sems.at[2 * k + number]
                    )
                )
        for copy in copies:
            copy.start()
        for copy in copies:
            copy.wait()

    slot_sum = jnp.zeros((hidden.shape[0], 1), f32)
    for start, size in unit_blocks(units):
        gate_pre = dot(hidden[:, :width], weights[:, start : start + size])
        up_pre = dot(hidden[:, :width], weights[:, units + start : units + start + size])
        act_grad = dot(grad[...], weights[:, 2 * units + start : 2 * units + start + size])
        sigma = 1.0 / (1.0 + jnp.exp(-gate_pre))
        silu_vals = gate_pre * sigma
        active = (silu_vals * up_pre).astype(bf16)
        act_out[:, start : start + size] = active
        slot_sum += jnp.sum(active.astype(f32) * act_grad, axis=1, keepdims=True)
        gate_grad = act_grad * up_pre * sigma * (1.0 + gate_pre * (1.0 - sigma))
        joint_out[:, start : start + size] = gate_grad.astype(bf16)
        joint_out[:, units + start : units + start + size] = (act_grad * silu_vals).astype(bf16)
    for start in range(0, width, 512):
        block = weights[start : start + 512, : 2 * units]
        hidden_out[:, start : start + 512] = dot_t(joint_out[...], block).astype(bf16)
        block = weights[start : start + 512, 2 * units :]
        out[:, start : start + 512] = dot_t(act_out[...], block).astype(bf16)
    lanes = lax.broadcasted_iota(jnp.int32, (hidden.shape[0], HDIM), 1)
    hidden_out[:, width:] = jnp.where(lanes == 0, slot_sum, 0.0).astype(bf16)


def expert_rows(position, hidden, grad, own_pieces, near_pieces):
    rows, width = grad.shape
    columns = near_pieces[0].shape[1]
    units = columns // 3
    tile = 256
    shape = jax.ShapeDtypeStruct
    count = len(own_pieces)

    def tiled(size):
        return pl.BlockSpec((tile, size), lambda i, at: (i, 0))

    return pl.pallas_call(
        expert_kernel,
        grid_spec=pltpu.PrefetchScalarGridSpec(
            num_scalar_prefetch=1,
            grid=(rows // tile,),
            in_specs=[tiled(width + HDIM), tiled(width)]
            + [pl.BlockSpec(memory_space=pl.ANY)] * (2 * count),
            out_specs=[tiled(width), tiled(width + HDIM), tiled(units), tiled(2 * units)],
            scratch_shapes=[
                pltpu.VMEM((width, columns), bf16),
                pltpu.SemaphoreType.DMA((2 * count,)),
            ],
        ),
        out_shape=[
            shape((rows, width), bf16),
            shape((rows, width + HDIM), bf16),
            shape((rows, units), bf16),
            shape((rows, 2 * units), bf16),
        ],
        compiler_params=pltpu.CompilerParams(vmem_limit_bytes=56 * 2**20),
        cost_estimate=pl.CostEstimate(
            flops=4 * rows * width * columns,
            bytes_accessed=2 * (width * columns + 6 * rows * width),
            transcendentals=rows * units,
        ),
        name="expert_rows",
    )(position, hidden, grad, *own_pieces, *near_pieces)


def expert_grad_kernel(order, *refs):
    hidden, grad, gates, joint, active = [refs[2 * n : 2 * n + 2] for n in range(5)]
    outs = refs[10:]
    units = active[0].shape[1]

    def scaled(blocks):
        return [
            (block[...].astype(f32) * gate[:, :1].astype(f32)).astype(bf16)
            for block, gate in zip(blocks, gates)
        ]

    left, right = scaled(hidden), scaled(grad)
    step = pl.program_id(0)
    for number, out in enumerate(outs):

        @pl.when(step == number)
        def _():
            for start, size in unit_blocks(2 * units):
                out[:, start : start + size] = sum(
                    t_dot(rows, part[:, start : start + size]) for rows, part in zip(left, joint)
                ).astype(bf16)
            for start, size in unit_blocks(units):
                out[:, 2 * units + start : 2 * units + start + size] = sum(
                    t_dot(rows, part[:, start : start + size]) for rows, part in zip(right, active)
                ).astype(bf16)


def expert_grads(chunks, chunk_rows, rows_of, joints, actives):
    hidden, grad = rows_of[:2], rows_of[2:]
    rows, units = actives[0].shape
    width = grad[0].shape[1]
    half = chunk_rows // 2
    count = len(chunks)
    order = jnp.stack([2 * chunk + part for chunk in chunks for part in range(2)]).astype(jnp.int32)

    def whole(size, column=0):
        return pl.BlockSpec(
            (rows, size), lambda i, at: (0, column), pipeline_mode=pl.Buffered(1)
        )

    column = pl.BlockSpec((rows, half), lambda i, at: (0, at[i]))
    return pl.pallas_call(
        expert_grad_kernel,
        grid_spec=pltpu.PrefetchScalarGridSpec(
            num_scalar_prefetch=1,
            grid=(2 * count,),
            in_specs=[column] * 4
            + [whole(HDIM, width // HDIM)] * 2
            + [whole(2 * units)] * 2
            + [whole(units)] * 2,
            out_specs=[
                pl.BlockSpec((half, 3 * units), lambda i, at: (0, 0)) for _ in range(2 * count)
            ],
        ),
        out_shape=[jax.ShapeDtypeStruct((half, 3 * units), bf16)] * (2 * count),
        compiler_params=pltpu.CompilerParams(vmem_limit_bytes=56 * 2**20),
        cost_estimate=pl.CostEstimate(
            flops=4 * count * chunk_rows * rows * 3 * units,
            bytes_accessed=2 * (rows * 6 * units + count * chunk_rows * (4 * rows + 3 * units)),
            transcendentals=0,
        ),
        name="expert_grads",
    )(order, *hidden, *grad, *hidden, *joints, *actives)


def local(
    tokens,
    cotangent,
    seq_lengths,
    dealing,
    attn_routes,
    ffn_routes,
    expert_table,
    clip_limit,
    attn_gain,
    ffn_gain,
    attn_router,
    ffn_router,
    query_weight,
    attn_out_weight,
    kv_weight,
    gate_up_weight,
    down_weight,
):
    micro, tok_rows, width = tokens.shape
    dp_count = lax.axis_size("dp")
    slots = lax.axis_size("expert")
    col = lax.axis_index("expert")
    group = lax.axis_index("dp")
    piece_rows = tok_rows // dp_count
    cap = tok_rows * TOP * 3 // (2 * slots)
    group_rows = tok_rows * slots
    all_rows = micro * group_rows
    home_rows = micro * tok_rows
    query_width = HEADS * HDIM
    own_heads = HEADS // slots
    own_width = own_heads * HDIM
    shard_rows = query_weight.shape[1]
    score_scale = HDIM ** (-0.5)
    core = group % 2
    chip = group // 2
    side = chip % 2
    chips = dp_count // 2
    lines = chips // 2
    quarter = FF // 4
    chip_rows = 2 * shard_rows

    both = jnp.stack([tokens, cotangent]).reshape(2 * micro, dp_count, piece_rows, width)
    both = lax.all_to_all(both.transpose(1, 0, 2, 3), "dp", split_axis=0, concat_axis=0, tiled=True)
    def quarter_of(half, part):
        start = (2 * half + part) * quarter
        return jnp.concatenate(
            [
                lax.dynamic_slice_in_dim(gate_up_weight[0], start, quarter, 1),
                lax.dynamic_slice_in_dim(gate_up_weight[0], FF + start, quarter, 1),
                lax.dynamic_slice_in_dim(down_weight[0], start, quarter, 1),
            ],
            axis=1,
        )

    parts = (1 - core, core)
    keep_pair = [quarter_of(side, part) for part in parts]
    send_pair = [quarter_of(1 - side, part) for part in parts]
    keep_pair, send_pair, kv_in, query_in, out_in = lax.optimization_barrier(
        (keep_pair, send_pair, kv_weight, query_weight[0], attn_out_weight[0])
    )
    side_pair = [swap(piece, "dp", 2) for piece in send_pair]
    line_steps = [4 * line for line in range(1, lines)]
    keep_lines = [[swap(piece, "dp", step) for step in line_steps] for piece in keep_pair]
    side_lines = [[swap(piece, "dp", step) for step in line_steps] for piece in side_pair]
    pairs = [keep_pair, side_pair]
    for line in range(lines - 1):
        pairs += [[part[line] for part in keep_lines], [part[line] for part in side_lines]]
    near_pieces = [swap(pair[0], "dp", 1) for pair in pairs]
    own_pieces = [pair[1] for pair in pairs]

    both = both.transpose(1, 0, 2, 3).reshape(2, micro, tok_rows, width)
    deal = (dealing[:, :, None] == jnp.arange(tok_rows, dtype=jnp.int32)).astype(bf16)
    work = jnp.einsum("mtr,bmrd->bmtd", deal, both, preferred_element_type=f32)
    x_home = work[0].reshape(home_rows, width)
    dy_home = work[1].reshape(home_rows, width)

    def columns_of(*shards):
        pieces = [shard.reshape(shard_rows, slots, own_width) for shard in shards]
        out = jnp.zeros((shard_rows, len(shards) * query_width), shards[0].dtype)
        for k in range(slots):
            part = jnp.concatenate(
                [lax.dynamic_index_in_dim(piece, col ^ k, 1, keepdims=False) for piece in pieces],
                axis=1,
            )
            part = swap(part, "expert", k) if k else part
            for number in range(len(shards)):
                out = lax.dynamic_update_slice_in_dim(
                    out,
                    part[:, number * own_width : (number + 1) * own_width],
                    number * query_width + (col ^ k) * own_width,
                    1,
                )
        return out

    def slots_of(columns):
        pieces = columns.reshape(shard_rows, slots, own_width)
        out = jnp.zeros((shard_rows, query_width), columns.dtype)
        for k in range(slots):
            part = lax.dynamic_index_in_dim(pieces, col ^ k, 1, keepdims=False)
            part = swap(part, "expert", k) if k else part
            out = lax.dynamic_update_slice_in_dim(out, part, (col ^ k) * own_width, 1)
        return out

    half_slots = slots // 2
    first_pairs = [(c, 2 * c) for c in range(half_slots)]
    first_pairs += [(c, 2 * (c - half_slots) + 1) for c in range(half_slots, slots)]
    second_pairs = [(c, 2 * c + 1) for c in range(half_slots)]
    second_pairs += [(c, 2 * (c - half_slots)) for c in range(half_slots, slots)]
    holds_keys = col < half_slots
    even_col = col % 2 == 0
    low_kv, high_kv = kv_in[:, :own_width], kv_in[:, own_width:]
    first_got = lax.ppermute(jnp.where(holds_keys, low_kv, high_kv), "expert", first_pairs)
    second_got = lax.ppermute(jnp.where(holds_keys, high_kv, low_kv), "expert", second_pairs)
    own_kv = jnp.concatenate(
        [
            jnp.where(even_col, first_got, second_got),
            jnp.where(even_col, second_got, first_got),
        ],
        axis=1,
    )
    kv_full = lax.all_gather(after(own_kv, work), "dp", axis=0, tiled=True)
    joint_full = lax.all_gather(
        after(columns_of(query_in, out_in), side_pair[0], *keep_lines[0]), "dp", axis=0, tiled=True
    )
    query_full, out_full = joint_full[:, :query_width], joint_full[:, query_width:]

    positions = jnp.arange(group_rows, dtype=jnp.int32)
    first_len = lax.dynamic_index_in_dim(seq_lengths[:, :, 0], group, 1, keepdims=True)
    in_second = positions[None, :] >= first_len
    places = positions[None, :] - jnp.where(in_second, first_len, 0)
    tables = rotation_tables(places.reshape(all_rows))

    def gather_rows(value):
        shaped = value.reshape(micro, tok_rows, -1)
        out = jnp.zeros((micro, group_rows, shaped.shape[-1]), value.dtype)
        for k in range(slots):
            part = swap(shaped, "expert", k) if k else shaped
            out = lax.dynamic_update_slice_in_dim(out, part, (col ^ k) * tok_rows, 1)
        return out.reshape(all_rows, -1)

    def scatter_rows(value):
        shaped = value.reshape(micro, group_rows, -1)
        total = None
        for k in range(slots):
            part = lax.dynamic_slice_in_dim(shaped, (col ^ k) * tok_rows, tok_rows, 1)
            if k:
                part = swap(part.astype(bf16), "expert", k)
            part = part.astype(f32)
            total = part if total is None else total + part
        return total.reshape(home_rows, -1)

    home_routes = lax.dynamic_slice_in_dim(ffn_routes, col * tok_rows, tok_rows, 1)
    home_slots = route_slots(home_routes, expert_table)
    packs = []
    before = jnp.tril(jnp.ones((tok_rows, tok_rows), bf16), -1)
    for k in range(slots):
        hits = jnp.any(home_slots == (col ^ k), axis=-1)
        rank = jnp.einsum("ts,ms->mt", before, hits.astype(bf16), preferred_element_type=f32)
        packs.append(
            hits[:, None, :]
            & (rank[:, None, :] == jnp.arange(cap, dtype=jnp.int32).astype(f32)[None, :, None])
        )
    packs = jnp.stack(packs)
    packs_low = packs.astype(bf16)
    pack_rows = micro * cap
    sent_rows = slots * pack_rows

    def send_packed(value, lane=None):
        packed = jnp.einsum(
            "kmct,mtd->kmcd", packs_low, value.reshape(micro, tok_rows, -1), preferred_element_type=f32
        ).astype(bf16)
        if lane is not None:
            lanes = jnp.pad(lane[..., None], ((0, 0), (0, 0), (0, 0), (0, HDIM - 1)))
            packed = jnp.concatenate([packed, lanes.astype(bf16)], axis=-1)
        parts = [swap(packed[k], "expert", k) if k else packed[k] for k in range(slots)]
        return jnp.stack(parts).reshape(sent_rows, -1)

    def near_rows(value):
        return jnp.concatenate([value, swap(value, "dp", 1)], axis=0)

    def quad_sums(value):
        near_half, far_half = value
        own, near = jnp.split(near_half, 2, axis=0)
        far, across = jnp.split(far_half, 2, axis=0)
        far_sum = far.astype(f32) + swap(across, "dp", 1).astype(f32)
        return own.astype(f32) + swap(near, "dp", 1).astype(f32), far_sum.astype(bf16)

    def return_packed(value, *others):
        shaped = value.astype(bf16).reshape(slots, micro, cap, -1)
        parts = [swap(shaped[k], "expert", k) if k else shaped[k] for k in range(slots)]
        return after(parts, *others)

    def unpack(packed, scale):
        total = None
        for k in range(slots):
            rows = jnp.einsum("mct,mcd->mtd", packs_low[k], packed[k], preferred_element_type=f32)
            rows = rows.reshape(home_rows, -1) * take(scale.T, col ^ k)[:, None]
            total = rows if total is None else total + rows
        return total

    gain_one = attn_gain.astype(f32)
    gain_two = ffn_gain.astype(f32)
    normed_one, scale_one = normalize(x_home)
    hidden_one_home = (normed_one * gain_one).astype(bf16)
    hidden_one_raw = gather_rows(hidden_one_home)
    hidden_one = after(hidden_one_raw, side_pair[1], *keep_lines[1])
    grad_sent = send_packed(after(dy_home.astype(bf16), hidden_one))
    logits_one = dot(hidden_one, attn_router)
    gates_one, matches_one, chosen_one, gate_vals_one = route_gates(
        logits_one, attn_routes.reshape(all_rows, TOP), expert_table
    )
    hits_one = jnp.any(chosen_one, axis=1).astype(f32)

    def wide(value):
        return jnp.pad(value, ((0, 0), (0, HDIM - value.shape[1])))

    kv_part = dot(hidden_one, kv_full).astype(bf16)
    query_part = dot(hidden_one, query_full)
    grad_sent = after(grad_sent, kv_part)
    grad_near, grad_far = near_rows(grad_sent), near_rows(swap(grad_sent, "dp", 2))
    lens = first_len[:, 0].astype(jnp.int32)
    gates_wide = wide(gates_one)
    attn_vals, gated_vals, query_rot, key_rot, log_total, peaks = attention_forward(
        lens, query_part, kv_part, tables, gates_wide, wide(hits_one), own_heads, group_rows
    )
    peaks = jnp.max(peaks, axis=0)[: own_heads * slots].reshape(own_heads, slots).T
    peak_table = lax.dynamic_update_slice_in_dim(
        jnp.full((slots, HEADS), very_low, f32), peaks, col * own_heads, 1
    )
    gated_vals = after(gated_vals, grad_sent, *side_lines[0])
    attn_home = after(scatter_rows(dot_t(gated_vals, out_full)), *side_lines[1], *near_pieces)

    resid = x_home + attn_home
    normed_two, scale_two = normalize(resid)
    hidden_two = (normed_two * gain_two).astype(bf16)
    logits_two = dot(hidden_two, ffn_router)
    gates_two, matches_two, chosen_two, gate_vals_two = route_gates(
        logits_two, home_routes.reshape(home_rows, TOP), expert_table
    )
    gates_by_slot = gates_two.reshape(micro, tok_rows, slots)
    gate_parts = []
    for k in range(slots):
        gate_col = lax.dynamic_index_in_dim(gates_by_slot, col ^ k, 2, keepdims=False)
        gate_parts.append(jnp.sum(jnp.where(packs[k], gate_col[:, None, :], 0.0), axis=-1))
    hidden_sent = send_packed(hidden_two, jnp.stack(gate_parts))
    hidden_near, hidden_far = near_rows(hidden_sent), swap(hidden_sent, "dp", 2)
    position = jnp.stack([core, chip]).astype(jnp.int32)
    near_results = expert_rows(
        position, hidden_near, after(grad_near, grad_far), own_pieces, near_pieces
    )
    hidden_far = near_rows(after(hidden_far, near_results))
    far_results = expert_rows(position, hidden_far, grad_far, own_pieces, near_pieces)
    ffn_parts, hidden_parts, actives, joint_grads = zip(near_results, far_results)

    def block_grads(steps, *others):
        rows = after((hidden_near, hidden_far, grad_near, grad_far), *others)
        return expert_grads([chip ^ k for k in steps], chip_rows, rows, joint_grads, actives)

    hidden_sum, hidden_far_sum = quad_sums(hidden_parts)
    ffn_sum, ffn_far_sum = quad_sums(ffn_parts)
    line_grads = block_grads([k ^ 1 for k in range(2, chips)], hidden_far_sum)
    side_got, keep_got = [[], []], [[], []]
    last = ()
    for which, got in enumerate((side_got, keep_got)):
        for part in range(2):
            for line in range(lines - 1):
                block = after(line_grads[4 * line + 2 * which + part], *last)
                got[part].append(swap(block, "dp", 4 * line + 4))
            last = got[part][-1:]
    hidden_got = after(swap(hidden_far_sum, "dp", 2), *line_grads, ffn_far_sum, ffn_sum)
    hidden_sum = hidden_sum + hidden_got.astype(f32)
    own_grads = block_grads([1, 0], hidden_sum)
    back_packed = return_packed(hidden_sum, *own_grads)
    ffn_sum = ffn_sum + swap(after(ffn_far_sum, hidden_got), "dp", 2).astype(f32)

    def total(own, got):
        return functools.reduce(jnp.add, [part.astype(f32) for part in [own] + got]).astype(bf16)

    other_sums = [swap(total(own_grads[part], side_got[part]), "dp", 2) for part in range(2)]
    slot_two_grad = jnp.zeros((slots, home_rows), f32)
    for k in range(slots):
        rows = jnp.sum(
            jnp.where(packs[k], back_packed[k][:, :, width].astype(f32)[:, :, None], 0.0), axis=1
        )
        slot_two_grad = lax.dynamic_update_index_in_dim(
            slot_two_grad, rows.reshape(home_rows), col ^ k, 0
        )
    hidden_two_grad = unpack([part[..., :width] for part in back_packed], gates_two)
    logit_two_grad = gate_back(slot_two_grad.T, gate_vals_two, matches_two, chosen_two).astype(bf16)
    hidden_two_grad = hidden_two_grad + dot_t(logit_two_grad, ffn_router)
    router_two_grad = t_dot(logit_two_grad, hidden_two)
    gain_two_grad = jnp.sum(hidden_two_grad * normed_two, axis=0)
    resid_grad = dy_home + norm_back(hidden_two_grad * gain_two, normed_two, scale_two)

    resid_grad_low = after(resid_grad.astype(bf16), *side_got[0])
    resid_grad_all = after(gather_rows(resid_grad_low), ffn_sum, *side_got[1])
    ffn_packed = return_packed(after(ffn_sum, resid_grad_all))
    out_home = (resid + unpack(ffn_packed, gates_two)).astype(bf16)
    out_part = t_dot(resid_grad_all, gated_vals).astype(bf16)
    vals_grad = after(dot(resid_grad_all, out_full), out_part, *keep_got[0])
    query_grad, key_grad, value_grad, slot_part_one = attention_backward(
        lens, query_rot, key_rot, kv_part, attn_vals, vals_grad, tables, gates_wide, log_total,
        own_heads, group_rows,
    )
    query_grad, key_grad, value_grad, slot_part_one = lax.optimization_barrier(
        (query_grad, key_grad, value_grad, slot_part_one, ffn_packed, keep_got[1])
    )[:4]
    kv_grad = jnp.concatenate([key_grad, value_grad], axis=1)
    hidden_one_part = dot_t(query_grad, query_full) + dot_t(kv_grad, kv_full)
    hidden_one_part = hidden_one_part.astype(bf16)
    hidden_one_late = after(hidden_one, hidden_one_part)
    query_part_grad = t_dot(hidden_one_late, query_grad).astype(bf16)
    kv_part_grad = t_dot(hidden_one_late, kv_grad).astype(bf16)
    back_one = scatter_rows(
        jnp.concatenate([hidden_one_part, slot_part_one.astype(bf16)], axis=1)
    )
    back_one = after(back_one, query_part_grad, kv_part_grad, other_sums[0])
    hidden_one_grad, slot_one_grad = back_one[:, :width], back_one[:, width : width + slots]

    def own(value):
        shaped = value.reshape((micro, group_rows) + value.shape[1:])
        part = lax.dynamic_slice_in_dim(shaped, col * tok_rows, tok_rows, 1)
        return part.reshape((home_rows,) + value.shape[1:])

    logit_one_grad = gate_back(
        slot_one_grad, own(gate_vals_one), own(matches_one), own(chosen_one)
    ).astype(bf16)
    hidden_one_grad = hidden_one_grad + dot_t(logit_one_grad, attn_router)
    router_one_grad = t_dot(logit_one_grad, hidden_one_home)
    gain_one_grad = jnp.sum(hidden_one_grad * normed_one, axis=0)
    in_home = resid_grad + norm_back(hidden_one_grad * gain_one, normed_one, scale_one)

    keep_sums = [total(own_grads[2 + part], keep_got[part]) for part in range(2)]
    by_rows = [jnp.stack([keep_sums[part], other_sums[part]]) for part in range(2)]
    own_pair = jnp.where(core == 0, by_rows[0], by_rows[1])
    near_pair = swap(jnp.where(core == 0, by_rows[1], by_rows[0]), "dp", 1)
    by_core = [jnp.where(core == 0, own_pair, near_pair), jnp.where(core == 0, near_pair, own_pair)]
    by_side = [[jnp.where(side == s, part[0], part[1]) for part in by_core] for s in range(2)]
    blocks = [part for row in by_side for part in row]
    gate_up_grad = jnp.concatenate(
        [b[:, :quarter] for b in blocks] + [b[:, quarter : 2 * quarter] for b in blocks], axis=1
    ).astype(f32)
    down_grad = jnp.concatenate([b[:, 2 * quarter :] for b in blocks], axis=1).astype(f32)

    def reduced(value):
        return lax.psum_scatter(value, "dp", scatter_dimension=0, tiled=True)

    out_grad = slots_of(reduced(out_part))
    joint_own = reduced(jnp.concatenate([query_part_grad, kv_part_grad], axis=1))

    in_low, out_grad, joint_own = lax.optimization_barrier(
        (in_home.astype(bf16), out_grad, joint_own, other_sums[1])
    )[:3]
    query_own, kv_own = joint_own[:, :query_width], joint_own[:, query_width:]
    results = jnp.stack([out_home, in_low]).reshape(2, micro, tok_rows, width)
    results = jnp.einsum("mtr,bmtd->bmrd", deal, results, preferred_element_type=f32).astype(bf16)
    results = results.reshape(2 * micro, dp_count, piece_rows, width).transpose(1, 0, 2, 3)
    results = lax.all_to_all(results, "dp", split_axis=0, concat_axis=0, tiled=True)
    results = results.transpose(1, 0, 2, 3).reshape(2, micro, tok_rows, width)

    out_grad = out_grad.astype(f32)
    query_out = slots_of(query_own).astype(f32)
    key_part, value_part = kv_own[:, :own_width], kv_own[:, own_width:]
    first_back = lax.ppermute(
        jnp.where(even_col, key_part, value_part), "expert", [(b, a) for a, b in first_pairs]
    )
    second_back = lax.ppermute(
        jnp.where(even_col, value_part, key_part), "expert", [(b, a) for a, b in second_pairs]
    )
    kv_out = jnp.concatenate(
        [
            jnp.where(holds_keys, first_back, second_back),
            jnp.where(holds_keys, second_back, first_back),
        ],
        axis=1,
    ).astype(f32)

    sum_rows = 2 + 2 * slots
    peak_rows = jnp.pad(peak_table, ((0, 0), (0, width - HEADS)))
    sums = spread(
        jnp.concatenate(
            [gain_one_grad[None], gain_two_grad[None], router_one_grad, router_two_grad, peak_rows],
            axis=0,
        ),
        lambda left, right: jnp.where(
            jnp.arange(sum_rows + slots)[:, None] < sum_rows, left + right, jnp.maximum(left, right)
        ),
    )
    peaks_all = sums[sum_rows:, :HEADS]
    limit = clip_limit[0].astype(f32)
    factor = limit / jnp.maximum(peaks_all, limit)
    query_scale = jnp.repeat(jnp.sqrt(take(factor, col)), HDIM)
    query_clipped = (query_weight.astype(f32) * query_scale[None, None, :]).astype(bf16)
    full_scale = jnp.concatenate(
        [jnp.repeat(jnp.sqrt(jnp.min(factor, axis=0)), HDIM), jnp.ones((query_width,), f32)]
    )
    piece_width = kv_weight.shape[1]
    piece_scale = lax.dynamic_slice_in_dim(full_scale, col * piece_width, piece_width)
    kv_clipped = (kv_weight.astype(f32) * piece_scale[None, :]).astype(bf16)
    return (
        results[0],
        results[1],
        sums[0],
        sums[1],
        sums[2 : 2 + slots].T,
        sums[2 + slots : sum_rows].T,
        query_out[None],
        out_grad[None],
        kv_out,
        gate_up_grad[None],
        down_grad[None],
        query_clipped,
        kv_clipped,
    )


def solution(mesh):
    placed = (
        P(None, ("dp", "expert"), None),
        P(None, ("dp", "expert"), None),
        P(),
        P(None, ("dp", "expert")),
        P(None, "dp", None),
        P(None, "dp", None),
        P(),
        P(),
        P(),
        P(),
        P(),
        P(),
        P("expert", "dp", None),
        P("expert", "dp", None),
        P("dp", "expert"),
        P("expert", "dp", None),
        P("expert", "dp", None),
    )
    return jax.shard_map(
        local,
        mesh=mesh,
        in_specs=placed,
        out_specs=(
            P(None, ("dp", "expert"), None),
            P(None, ("dp", "expert"), None),
            P(),
            P(),
            P(),
            P(),
            P("expert", "dp", None),
            P("expert", "dp", None),
            P("dp", "expert"),
            P("expert", "dp", None),
            P("expert", "dp", None),
            P("expert", "dp", None),
            P("dp", "expert"),
        ),
        check_vma=False,
    )
```

```python
import functools

import jax
import jax.numpy as jnp
from jax import lax
from jax.experimental import pallas as pl
from jax.experimental.pallas import tpu as pltpu
from jax.sharding import PartitionSpec as P

HEADS = 16
HDIM = 128
FF = 5632
TOP = 2

eps_norm = 1e-06
rope_base = 10000.0
very_low = -1e30

f32 = jnp.float32
bf16 = jnp.bfloat16


def dot(left, right):
    return jnp.dot(left, right, preferred_element_type=f32)


def dot_t(left, right):
    return lax.dot_general(left, right, (((1,), (1,)), ((), ())), preferred_element_type=f32)


def t_dot(left, right):
    return lax.dot_general(left, right, (((0,), (0,)), ((), ())), preferred_element_type=f32)


def swap(value, axis, step):
    count = lax.axis_size(axis)
    return lax.ppermute(value, axis, [(i, i ^ step) for i in range(count)])


def take(stacked, index):
    return lax.dynamic_index_in_dim(stacked, index, 0, keepdims=False)


def place(parts, positions):
    out = jnp.zeros((len(parts),) + parts[0].shape, parts[0].dtype)
    for part, position in zip(parts, positions):
        out = lax.dynamic_update_index_in_dim(out, part, position, 0)
    return out


def after(value, *others):
    return lax.optimization_barrier((value, others))[0]


def rotation_tables(places):
    half_dim = HDIM // 2
    frequency = rope_base ** (-jnp.arange(half_dim, dtype=f32) * 2.0 / HDIM)
    angles = places.astype(f32)[:, None] * frequency[None, :]
    cosine, sine = jnp.cos(angles), jnp.sin(angles)
    return (
        jnp.concatenate([cosine, cosine], axis=1),
        jnp.concatenate([-sine, sine], axis=1),
    )


def turn(values, cosine, sine):
    return values * cosine + pltpu.roll(values, HDIM // 2, 1) * sine


def lane_value(table, lane):
    lanes = lax.broadcasted_iota(jnp.int32, table.shape, 1)
    return jnp.sum(jnp.where(lanes == lane, table, 0.0), axis=1, keepdims=True)


def allowed_pairs(rows, first_len):
    query_at = lax.broadcasted_iota(jnp.int32, (rows, rows), 0)
    key_at = lax.broadcasted_iota(jnp.int32, (rows, rows), 1)
    return (key_at <= query_at) & ((key_at >= first_len) | (query_at < first_len))


def forward_kernel(
    lens, query, key, value, cosine, sine, gates, hits,
    vals_out, gated_out, query_out, key_out, total_out, peak_out,
):
    m, h, s = pl.program_id(0), pl.program_id(1), pl.program_id(2)
    slot_count = pl.num_programs(2)
    rows = query.shape[0]
    lane = h * slot_count + s

    @pl.when(lane == 0)
    def _():
        total_out[...] = jnp.zeros_like(total_out)
        peak_out[...] = jnp.full_like(peak_out, very_low)

    @pl.when(s == 0)
    def _():
        key_out[...] = turn(key[...].astype(f32), cosine[...], sine[...]).astype(bf16)

    turned = turn(query[...], cosine[...], sine[...]).astype(bf16)
    query_out[...] = turned
    raw = dot_t(turned, key_out[...])
    scores = jnp.where(allowed_pairs(rows, lens[m]), raw * HDIM ** (-0.5), very_low)
    row_peak = jnp.max(scores, axis=1, keepdims=True)
    expo = jnp.exp(scores - row_peak)
    denom = jnp.sum(expo, axis=1, keepdims=True)
    probs = expo / denom
    vals = dot(probs.astype(bf16), value[...]).astype(bf16)
    vals_out[...] = vals
    gated_out[...] = (lane_value(gates[...], s) * vals.astype(f32)).astype(bf16)
    lanes = lax.broadcasted_iota(jnp.int32, total_out.shape, 1)
    total_out[...] = jnp.where(lanes == lane, row_peak + jnp.log(denom), total_out[...])
    seen = jnp.where(lane_value(hits[...], s) > 0.0, row_peak, very_low)
    peak_lanes = lax.broadcasted_iota(jnp.int32, peak_out.shape, 1)
    peak_out[...] = jnp.where(
        peak_lanes == lane, jnp.max(seen, axis=0, keepdims=True), peak_out[...]
    )


def backward_kernel(
    lens, query, key, value, vals, vals_grad, cosine, sine, gates, total,
    query_grad, key_grad, value_grad, gate_grad, key_sum, value_sum,
):
    m, h, s = pl.program_id(0), pl.program_id(1), pl.program_id(2)
    slot_count = pl.num_programs(2)
    rows = query.shape[0]
    lane = h * slot_count + s

    @pl.when(lane == 0)
    def _():
        gate_grad[...] = jnp.zeros_like(gate_grad)

    @pl.when(s == 0)
    def _():
        key_sum[...] = jnp.zeros_like(key_sum)
        value_sum[...] = jnp.zeros_like(value_sum)

    full_grad = vals_grad[...]
    lanes = lax.broadcasted_iota(jnp.int32, gate_grad.shape, 1)
    slot_sum = jnp.sum(vals[...].astype(f32) * full_grad, axis=1, keepdims=True)
    gate_grad[...] += jnp.where(lanes == s, slot_sum, 0.0)
    gated_grad = (lane_value(gates[...], s) * full_grad).astype(bf16)
    raw = dot_t(query[...], key[...])
    scores = jnp.where(allowed_pairs(rows, lens[m]), raw * HDIM ** (-0.5), very_low)
    probs = jnp.exp(scores - lane_value(total[...], lane))
    prob_grad = dot_t(gated_grad, value[...])
    inner = jnp.sum(probs * prob_grad, axis=1, keepdims=True)
    score_grad = (probs * (prob_grad - inner) * HDIM ** (-0.5)).astype(bf16)
    back_sine = -sine[...]
    turned = dot(score_grad, key[...])
    query_grad[...] = turn(turned, cosine[...], back_sine).astype(bf16)
    key_sum[...] += t_dot(score_grad, query[...])
    value_sum[...] += t_dot(probs.astype(bf16), gated_grad)

    @pl.when(s == slot_count - 1)
    def _():
        key_grad[...] = turn(key_sum[...], cosine[...], back_sine).astype(bf16)
        value_grad[...] = value_sum[...].astype(bf16)


def attention_specs(own_heads, rows):
    def block(index):
        return pl.BlockSpec((rows, HDIM), index)

    return {
        "query": block(lambda m, h, s, lens: (m, s * own_heads + h)),
        "key": block(lambda m, h, s, lens: (m, h)),
        "value": block(lambda m, h, s, lens: (m, own_heads + h)),
        "rows": block(lambda m, h, s, lens: (m, 0)),
        "peak": pl.BlockSpec((8, HDIM), lambda m, h, s, lens: (m, 0)),
    }


def attention_forward(lens, query, joint_kv, tables, gates, hits, own_heads, rows):
    micro = lens.shape[0]
    slots = query.shape[1] // (own_heads * HDIM)
    at = attention_specs(own_heads, rows)
    shape = jax.ShapeDtypeStruct
    total_rows = micro * rows
    return pl.pallas_call(
        forward_kernel,
        grid_spec=pltpu.PrefetchScalarGridSpec(
            num_scalar_prefetch=1,
            grid=(micro, own_heads, slots),
            in_specs=[at["query"], at["key"], at["value"]] + [at["rows"]] * 4,
            out_specs=[at["query"]] * 3 + [at["key"], at["rows"], at["peak"]],
        ),
        out_shape=[shape(query.shape, bf16)] * 3
        + [
            shape((total_rows, own_heads * HDIM), bf16),
            shape((total_rows, HDIM), f32),
            shape((micro * 8, HDIM), f32),
        ],
        cost_estimate=pl.CostEstimate(
            flops=4 * rows * rows * HDIM * micro * HEADS,
            bytes_accessed=14 * query.size,
            transcendentals=rows * rows * micro * HEADS,
        ),
        name="attention_forward",
    )(lens, query, joint_kv, joint_kv, tables[0], tables[1], gates, hits)


def attention_backward(
    lens, query, key, joint_kv, vals, vals_grad, tables, gates, total, own_heads, rows
):
    micro = lens.shape[0]
    slots = query.shape[1] // (own_heads * HDIM)
    at = attention_specs(own_heads, rows)
    shape = jax.ShapeDtypeStruct
    total_rows = micro * rows
    return pl.pallas_call(
        backward_kernel,
        grid_spec=pltpu.PrefetchScalarGridSpec(
            num_scalar_prefetch=1,
            grid=(micro, own_heads, slots),
            in_specs=[at["query"], at["key"], at["value"], at["query"], at["query"]]
            + [at["rows"]] * 4,
            out_specs=[at["query"], at["key"], at["key"], at["rows"]],
            scratch_shapes=[pltpu.VMEM((rows, HDIM), f32)] * 2,
        ),
        out_shape=[shape(query.shape, bf16)]
        + [shape((total_rows, own_heads * HDIM), bf16)] * 2
        + [shape((total_rows, HDIM), f32)],
        cost_estimate=pl.CostEstimate(
            flops=10 * rows * rows * HDIM * micro * HEADS,
            bytes_accessed=14 * query.size,
            transcendentals=rows * rows * micro * HEADS,
        ),
        name="attention_backward",
    )(lens, query, key, joint_kv, vals, vals_grad, tables[0], tables[1], gates, total)


def normalize(values):
    row_scale = lax.rsqrt(jnp.mean(values * values, axis=-1, keepdims=True) + eps_norm)
    return values * row_scale, row_scale


def norm_back(grad_hat, normed, row_scale):
    return row_scale * (grad_hat - normed * jnp.mean(grad_hat * normed, axis=-1, keepdims=True))


def route_gates(logits, routes, expert_table):
    expert_ids = jnp.arange(expert_table.shape[0], dtype=jnp.int32)
    matches = routes[:, :, None] == expert_ids[None, None, :]
    picked = jnp.sum(jnp.where(matches, logits[:, None, :], 0.0), axis=-1)
    gate_vals = jax.nn.softmax(picked, axis=-1)
    slot_ids = route_slots(routes, expert_table)
    chosen = slot_ids[:, :, None] == expert_ids[None, None, :]
    gates = jnp.sum(jnp.where(chosen, gate_vals[:, :, None], 0.0), axis=1)
    return gates, matches, chosen, gate_vals


def route_slots(routes, expert_table):
    expert_ids = jnp.arange(expert_table.shape[0], dtype=jnp.int32)
    matches = routes[..., None] == expert_ids
    return jnp.sum(jnp.where(matches, expert_table, 0), axis=-1)


def gate_back(slot_grad, gate_vals, matches, chosen):
    picked = jnp.sum(jnp.where(chosen, slot_grad[:, None, :], 0.0), axis=-1)
    inner_sum = jnp.sum(gate_vals * picked, axis=-1, keepdims=True)
    picked_grad = gate_vals * (picked - inner_sum)
    return jnp.sum(jnp.where(matches, picked_grad[:, :, None], 0.0), axis=1)


def unit_blocks(count):
    return [(start, min(512, count - start)) for start in range(0, count, 512)]


def expert_kernel(place_ref, hidden, grad, *refs):
    piece_count = (len(refs) - 6) // 2
    own_pieces, near_pieces = refs[:piece_count], refs[piece_count : 2 * piece_count]
    out, hidden_out, act_out, joint_out, weights, sems = refs[2 * piece_count :]
    core, chip = place_ref[0], place_ref[1]
    rows, columns = near_pieces[0].shape
    units = columns // 3
    width = grad.shape[1]

    @pl.when(pl.program_id(0) == 0)
    def _():
        copies = []
        for k in range(piece_count):
            base = (chip ^ k) * (2 * rows)
            for number, (piece, part) in enumerate(
                ((own_pieces[k], core), (near_pieces[k], 1 - core))
            ):
                start = pl.multiple_of(base + part * rows, 16)
                copies.append(
                    pltpu.make_async_copy(
                        piece, weights.at[pl.ds(start, rows)], sems.at[2 * k + number]
                    )
                )
        for copy in copies:
            copy.start()
        for copy in copies:
            copy.wait()

    slot_sum = jnp.zeros((hidden.shape[0], 1), f32)
    for start, size in unit_blocks(units):
        gate_pre = dot(hidden[:, :width], weights[:, start : start + size])
        up_pre = dot(hidden[:, :width], weights[:, units + start : units + start + size])
        act_grad = dot(grad[...], weights[:, 2 * units + start : 2 * units + start + size])
        sigma = 1.0 / (1.0 + jnp.exp(-gate_pre))
        silu_vals = gate_pre * sigma
        active = (silu_vals * up_pre).astype(bf16)
        act_out[:, start : start + size] = active
        slot_sum += jnp.sum(active.astype(f32) * act_grad, axis=1, keepdims=True)
        gate_grad = act_grad * up_pre * sigma * (1.0 + gate_pre * (1.0 - sigma))
        joint_out[:, start : start + size] = gate_grad.astype(bf16)
        joint_out[:, units + start : units + start + size] = (act_grad * silu_vals).astype(bf16)
    for start in range(0, width, 512):
        block = weights[start : start + 512, : 2 * units]
        hidden_out[:, start : start + 512] = dot_t(joint_out[...], block).astype(bf16)
        block = weights[start : start + 512, 2 * units :]
        out[:, start : start + 512] = dot_t(act_out[...], block).astype(bf16)
    lanes = lax.broadcasted_iota(jnp.int32, (hidden.shape[0], HDIM), 1)
    hidden_out[:, width:] = jnp.where(lanes == 0, slot_sum, 0.0).astype(bf16)


def expert_rows(position, hidden, grad, own_pieces, near_pieces):
    rows, width = grad.shape
    columns = near_pieces[0].shape[1]
    units = columns // 3
    tile = 384 if rows % 384 == 0 else 256
    shape = jax.ShapeDtypeStruct
    count = len(own_pieces)

    def tiled(size):
        return pl.BlockSpec((tile, size), lambda i, at: (i, 0))

    return pl.pallas_call(
        expert_kernel,
        grid_spec=pltpu.PrefetchScalarGridSpec(
            num_scalar_prefetch=1,
            grid=(rows // tile,),
            in_specs=[tiled(width + HDIM), tiled(width)]
            + [pl.BlockSpec(memory_space=pl.ANY)] * (2 * count),
            out_specs=[tiled(width), tiled(width + HDIM), tiled(units), tiled(2 * units)],
            scratch_shapes=[
                pltpu.VMEM((width, columns), bf16),
                pltpu.SemaphoreType.DMA((2 * count,)),
            ],
        ),
        out_shape=[
            shape((rows, width), bf16),
            shape((rows, width + HDIM), bf16),
            shape((rows, units), bf16),
            shape((rows, 2 * units), bf16),
        ],
        compiler_params=pltpu.CompilerParams(vmem_limit_bytes=56 * 2**20),
        cost_estimate=pl.CostEstimate(
            flops=4 * rows * width * columns,
            bytes_accessed=2 * (width * columns + 6 * rows * width),
            transcendentals=rows * units,
        ),
        name="expert_rows",
    )(position, hidden, grad, *own_pieces, *near_pieces)


def expert_grad_kernel(order, *refs):
    hidden, grad, gates, joint, active = [refs[2 * n : 2 * n + 2] for n in range(5)]
    outs = refs[10:]
    units = active[0].shape[1]

    def scaled(blocks):
        return [
            (block[...].astype(f32) * gate[:, :1].astype(f32)).astype(bf16)
            for block, gate in zip(blocks, gates)
        ]

    left, right = scaled(hidden), scaled(grad)
    step = pl.program_id(0)
    for number, out in enumerate(outs):

        @pl.when(step == number)
        def _():
            for start, size in unit_blocks(2 * units):
                out[:, start : start + size] = sum(
                    t_dot(rows, part[:, start : start + size]) for rows, part in zip(left, joint)
                ).astype(bf16)
            for start, size in unit_blocks(units):
                out[:, 2 * units + start : 2 * units + start + size] = sum(
                    t_dot(rows, part[:, start : start + size]) for rows, part in zip(right, active)
                ).astype(bf16)


def expert_grads(chunks, chunk_rows, rows_of, joints, actives):
    hidden, grad = rows_of[:2], rows_of[2:]
    rows, units = actives[0].shape
    width = grad[0].shape[1]
    half = chunk_rows // 2
    count = len(chunks)
    order = jnp.stack([2 * chunk + part for chunk in chunks for part in range(2)]).astype(jnp.int32)

    def whole(size, column=0):
        return pl.BlockSpec(
            (rows, size), lambda i, at: (0, column), pipeline_mode=pl.Buffered(1)
        )

    column = pl.BlockSpec((rows, half), lambda i, at: (0, at[i]))
    return pl.pallas_call(
        expert_grad_kernel,
        grid_spec=pltpu.PrefetchScalarGridSpec(
            num_scalar_prefetch=1,
            grid=(2 * count,),
            in_specs=[column] * 4
            + [whole(HDIM, width // HDIM)] * 2
            + [whole(2 * units)] * 2
            + [whole(units)] * 2,
            out_specs=[
                pl.BlockSpec((half, 3 * units), lambda i, at: (0, 0)) for _ in range(2 * count)
            ],
        ),
        out_shape=[jax.ShapeDtypeStruct((half, 3 * units), bf16)] * (2 * count),
        compiler_params=pltpu.CompilerParams(vmem_limit_bytes=56 * 2**20),
        cost_estimate=pl.CostEstimate(
            flops=4 * count * chunk_rows * rows * 3 * units,
            bytes_accessed=2 * (rows * 6 * units + count * chunk_rows * (4 * rows + 3 * units)),
            transcendentals=0,
        ),
        name="expert_grads",
    )(order, *hidden, *grad, *hidden, *joints, *actives)


def local(
    tokens,
    cotangent,
    seq_lengths,
    dealing,
    attn_routes,
    ffn_routes,
    expert_table,
    clip_limit,
    attn_gain,
    ffn_gain,
    attn_router,
    ffn_router,
    query_weight,
    attn_out_weight,
    kv_weight,
    gate_up_weight,
    down_weight,
):
    micro, tok_rows, width = tokens.shape
    dp_count = lax.axis_size("dp")
    slots = lax.axis_size("expert")
    col = lax.axis_index("expert")
    group = lax.axis_index("dp")
    piece_rows = tok_rows // dp_count
    cap = tok_rows * TOP * 3 // (2 * slots)
    group_rows = tok_rows * slots
    all_rows = micro * group_rows
    home_rows = micro * tok_rows
    query_width = HEADS * HDIM
    own_heads = HEADS // slots
    own_width = own_heads * HDIM
    shard_rows = query_weight.shape[1]
    score_scale = HDIM ** (-0.5)
    core = group % 2
    chip = group // 2
    side = chip % 2
    chips = dp_count // 2
    lines = chips // 2
    quarter = FF // 4
    chip_rows = 2 * shard_rows

    both = jnp.stack([tokens, cotangent]).reshape(2 * micro, dp_count, piece_rows, width)
    both = lax.all_to_all(both.transpose(1, 0, 2, 3), "dp", split_axis=0, concat_axis=0, tiled=True)
    def quarter_of(half, part):
        start = (2 * half + part) * quarter
        return jnp.concatenate(
            [
                lax.dynamic_slice_in_dim(gate_up_weight[0], start, quarter, 1),
                lax.dynamic_slice_in_dim(gate_up_weight[0], FF + start, quarter, 1),
                lax.dynamic_slice_in_dim(down_weight[0], start, quarter, 1),
            ],
            axis=1,
        )

    parts = (1 - core, core)
    keep_pair = [quarter_of(side, part) for part in parts]
    send_pair = [quarter_of(1 - side, part) for part in parts]
    both = both.transpose(1, 0, 2, 3).reshape(2, micro, tok_rows, width)
    deal = (dealing[:, :, None] == jnp.arange(tok_rows, dtype=jnp.int32)).astype(bf16)
    work = jnp.einsum("mtr,bmrd->bmtd", deal, both, preferred_element_type=f32)
    x_home = work[0].reshape(home_rows, width)
    dy_home = work[1].reshape(home_rows, width)

    def columns_of(*shards):
        pieces = [shard.reshape(shard_rows, slots, own_width) for shard in shards]
        out = jnp.zeros((shard_rows, len(shards) * query_width), shards[0].dtype)
        for k in range(slots):
            part = jnp.concatenate(
                [lax.dynamic_index_in_dim(piece, col ^ k, 1, keepdims=False) for piece in pieces],
                axis=1,
            )
            part = swap(part, "expert", k) if k else part
            for number in range(len(shards)):
                out = lax.dynamic_update_slice_in_dim(
                    out,
                    part[:, number * own_width : (number + 1) * own_width],
                    number * query_width + (col ^ k) * own_width,
                    1,
                )
        return out

    def slots_of(columns):
        pieces = columns.reshape(shard_rows, slots, own_width)
        out = jnp.zeros((shard_rows, query_width), columns.dtype)
        for k in range(slots):
            part = lax.dynamic_index_in_dim(pieces, col ^ k, 1, keepdims=False)
            part = swap(part, "expert", k) if k else part
            out = lax.dynamic_update_slice_in_dim(out, part, (col ^ k) * own_width, 1)
        return out

    half_slots = slots // 2
    first_pairs = [(c, 2 * c) for c in range(half_slots)]
    first_pairs += [(c, 2 * (c - half_slots) + 1) for c in range(half_slots, slots)]
    second_pairs = [(c, 2 * c + 1) for c in range(half_slots)]
    second_pairs += [(c, 2 * (c - half_slots)) for c in range(half_slots, slots)]
    holds_keys = col < half_slots
    even_col = col % 2 == 0
    low_kv, high_kv = kv_weight[:, :own_width], kv_weight[:, own_width:]
    first_got = lax.ppermute(jnp.where(holds_keys, low_kv, high_kv), "expert", first_pairs)
    second_got = lax.ppermute(jnp.where(holds_keys, high_kv, low_kv), "expert", second_pairs)
    own_kv = jnp.concatenate(
        [
            jnp.where(even_col, first_got, second_got),
            jnp.where(even_col, second_got, first_got),
        ],
        axis=1,
    )
    kv_full = lax.all_gather(after(own_kv, work), "dp", axis=0, tiled=True)
    line_steps = [4 * line for line in range(1, lines)]
    side_first = swap(send_pair[0], "dp", 2)
    keep_first = [swap(keep_pair[0], "dp", step) for step in line_steps]
    joint_own = columns_of(query_weight[0], attn_out_weight[0])
    joint_full = lax.all_gather(
        after(joint_own, side_first, keep_first), "dp", axis=0, tiled=True
    )
    late_pair = after((keep_pair[1], send_pair[1], side_first), joint_full)
    keep_second = [swap(late_pair[0], "dp", step) for step in line_steps]
    side_second = swap(late_pair[1], "dp", 2)
    first_lines = [swap(late_pair[2], "dp", step) for step in line_steps]
    second_lines = [swap(after(side_second, first_lines), "dp", step) for step in line_steps]
    firsts, seconds = [keep_pair[0], side_first], [keep_pair[1], side_second]
    for line in range(lines - 1):
        firsts += [keep_first[line], first_lines[line]]
        seconds += [keep_second[line], second_lines[line]]
    near_pieces = [swap(piece, "dp", 1) for piece in firsts]
    own_pieces = seconds
    query_full, out_full = joint_full[:, :query_width], joint_full[:, query_width:]

    positions = jnp.arange(group_rows, dtype=jnp.int32)
    first_len = lax.dynamic_index_in_dim(seq_lengths[:, :, 0], group, 1, keepdims=True)
    in_second = positions[None, :] >= first_len
    places = positions[None, :] - jnp.where(in_second, first_len, 0)
    tables = rotation_tables(places.reshape(all_rows))

    def gather_rows(value):
        shaped = value.reshape(micro, tok_rows, -1)
        out = jnp.zeros((micro, group_rows, shaped.shape[-1]), value.dtype)
        for k in range(slots):
            part = swap(shaped, "expert", k) if k else shaped
            out = lax.dynamic_update_slice_in_dim(out, part, (col ^ k) * tok_rows, 1)
        return out.reshape(all_rows, -1)

    def scatter_rows(value):
        shaped = value.reshape(micro, group_rows, -1)
        total = None
        for k in range(slots):
            part = lax.dynamic_slice_in_dim(shaped, (col ^ k) * tok_rows, tok_rows, 1)
            if k:
                part = swap(part.astype(bf16), "expert", k)
            part = part.astype(f32)
            total = part if total is None else total + part
        return total.reshape(home_rows, -1)

    home_routes = lax.dynamic_slice_in_dim(ffn_routes, col * tok_rows, tok_rows, 1)
    home_slots = route_slots(home_routes, expert_table)
    packs = []
    before = jnp.tril(jnp.ones((tok_rows, tok_rows), bf16), -1)
    for k in range(slots):
        hits = jnp.any(home_slots == (col ^ k), axis=-1)
        rank = jnp.einsum("ts,ms->mt", before, hits.astype(bf16), preferred_element_type=f32)
        packs.append(
            hits[:, None, :]
            & (rank[:, None, :] == jnp.arange(cap, dtype=jnp.int32).astype(f32)[None, :, None])
        )
    packs = jnp.stack(packs)
    packs_low = packs.astype(bf16)
    pack_rows = micro * cap
    sent_rows = slots * pack_rows

    def send_packed(value, lane=None):
        packed = jnp.einsum(
            "kmct,mtd->kmcd", packs_low, value.reshape(micro, tok_rows, -1), preferred_element_type=f32
        ).astype(bf16)
        if lane is not None:
            lanes = jnp.pad(lane[..., None], ((0, 0), (0, 0), (0, 0), (0, HDIM - 1)))
            packed = jnp.concatenate([packed, lanes.astype(bf16)], axis=-1)
        parts = [swap(packed[k], "expert", k) if k else packed[k] for k in range(slots)]
        return jnp.stack(parts).reshape(sent_rows, -1)

    def near_rows(value):
        return jnp.concatenate([value, swap(value, "dp", 1)], axis=0)

    def quad_sums(value):
        near_half, far_half = value
        own, near = jnp.split(near_half, 2, axis=0)
        far, across = jnp.split(far_half, 2, axis=0)
        far_sum = far.astype(f32) + swap(across, "dp", 1).astype(f32)
        return own.astype(f32) + swap(near, "dp", 1).astype(f32), far_sum.astype(bf16)

    def return_packed(value, *others):
        shaped = value.astype(bf16).reshape(slots, micro, cap, -1)
        parts = [swap(shaped[k], "expert", k) if k else shaped[k] for k in range(slots)]
        return after(parts, *others)

    def unpack(packed, scale):
        total = None
        for k in range(slots):
            rows = jnp.einsum("mct,mcd->mtd", packs_low[k], packed[k], preferred_element_type=f32)
            rows = rows.reshape(home_rows, -1) * take(scale.T, col ^ k)[:, None]
            total = rows if total is None else total + rows
        return total

    gain_one = attn_gain.astype(f32)
    gain_two = ffn_gain.astype(f32)
    normed_one, scale_one = normalize(x_home)
    hidden_one_home = (normed_one * gain_one).astype(bf16)
    hidden_one_raw = gather_rows(hidden_one_home)
    hidden_one = hidden_one_raw
    grad_sent = send_packed(after(dy_home.astype(bf16), hidden_one))
    logits_one = dot(hidden_one, attn_router)
    gates_one, matches_one, chosen_one, gate_vals_one = route_gates(
        logits_one, attn_routes.reshape(all_rows, TOP), expert_table
    )
    hits_one = jnp.any(chosen_one, axis=1).astype(f32)

    def wide(value):
        return jnp.pad(value, ((0, 0), (0, HDIM - value.shape[1])))

    kv_part = dot(hidden_one, kv_full).astype(bf16)
    query_part = dot(hidden_one, query_full)
    grad_sent = after(grad_sent, kv_part, joint_full)
    grad_near, grad_far = near_rows(grad_sent), near_rows(swap(grad_sent, "dp", 2))
    lens = first_len[:, 0].astype(jnp.int32)
    gates_wide = wide(gates_one)
    attn_vals, gated_vals, query_rot, key_rot, log_total, peaks = attention_forward(
        lens, query_part, kv_part, tables, gates_wide, wide(hits_one), own_heads, group_rows
    )
    peaks = jnp.max(peaks, axis=0)[: own_heads * slots]
    gated_vals = after(gated_vals, keep_second, side_second)
    attn_home = after(scatter_rows(dot_t(gated_vals, out_full)), first_lines, grad_near, grad_far)

    resid = x_home + attn_home
    normed_two, scale_two = normalize(resid)
    hidden_two = (normed_two * gain_two).astype(bf16)
    logits_two = dot(hidden_two, ffn_router)
    gates_two, matches_two, chosen_two, gate_vals_two = route_gates(
        logits_two, home_routes.reshape(home_rows, TOP), expert_table
    )
    gates_by_slot = gates_two.reshape(micro, tok_rows, slots)
    gate_parts = []
    for k in range(slots):
        gate_col = lax.dynamic_index_in_dim(gates_by_slot, col ^ k, 2, keepdims=False)
        gate_parts.append(jnp.sum(jnp.where(packs[k], gate_col[:, None, :], 0.0), axis=-1))
    hidden_sent = send_packed(hidden_two, jnp.stack(gate_parts))
    hidden_near, hidden_far = near_rows(hidden_sent), swap(hidden_sent, "dp", 2)
    hidden_near = after(hidden_near, second_lines, near_pieces)
    position = jnp.stack([core, chip]).astype(jnp.int32)
    near_results = expert_rows(
        position, hidden_near, after(grad_near, grad_far), own_pieces, near_pieces
    )
    hidden_far = near_rows(after(hidden_far, near_results))
    far_results = expert_rows(position, hidden_far, grad_far, own_pieces, near_pieces)
    ffn_parts, hidden_parts, actives, joint_grads = zip(near_results, far_results)

    def block_grads(steps, *others):
        rows = after((hidden_near, hidden_far, grad_near, grad_far), *others)
        return expert_grads([chip ^ k for k in steps], chip_rows, rows, joint_grads, actives)

    hidden_sum, hidden_far_sum = quad_sums(hidden_parts)
    ffn_sum, ffn_far_sum = quad_sums(ffn_parts)
    line_grads = block_grads([k ^ 1 for k in range(2, chips)], hidden_far_sum)
    side_got, keep_got = [[], []], [[], []]
    last = ()
    for which, got in enumerate((side_got, keep_got)):
        for part in range(2):
            for line in range(lines - 1):
                block = after(line_grads[4 * line + 2 * which + part], *last)
                got[part].append(swap(block, "dp", 4 * line + 4))
            last = got[part][-1:]
    hidden_got = after(swap(hidden_far_sum, "dp", 2), *line_grads, ffn_far_sum, ffn_sum)
    hidden_sum = hidden_sum + hidden_got.astype(f32)
    own_grads = block_grads([1, 0], hidden_sum)
    back_packed = return_packed(hidden_sum, *own_grads)
    ffn_sum = ffn_sum + swap(after(ffn_far_sum, hidden_got), "dp", 2).astype(f32)

    def total(own, got):
        return functools.reduce(jnp.add, [part.astype(f32) for part in [own] + got]).astype(bf16)

    other_sums = [swap(total(own_grads[part], side_got[part]), "dp", 2) for part in range(2)]
    slot_two_grad = jnp.zeros((slots, home_rows), f32)
    for k in range(slots):
        rows = jnp.sum(
            jnp.where(packs[k], back_packed[k][:, :, width].astype(f32)[:, :, None], 0.0), axis=1
        )
        slot_two_grad = lax.dynamic_update_index_in_dim(
            slot_two_grad, rows.reshape(home_rows), col ^ k, 0
        )
    hidden_two_grad = unpack([part[..., :width] for part in back_packed], gates_two)
    logit_two_grad = gate_back(slot_two_grad.T, gate_vals_two, matches_two, chosen_two).astype(bf16)
    hidden_two_grad = hidden_two_grad + dot_t(logit_two_grad, ffn_router)
    router_two_grad = t_dot(logit_two_grad, hidden_two)
    gain_two_grad = jnp.sum(hidden_two_grad * normed_two, axis=0)
    resid_grad = dy_home + norm_back(hidden_two_grad * gain_two, normed_two, scale_two)

    resid_grad_low = after(resid_grad.astype(bf16), *side_got[0])
    resid_grad_all = after(gather_rows(resid_grad_low), ffn_sum)
    out_part = t_dot(resid_grad_all, gated_vals).astype(bf16)
    vals_grad = after(dot(resid_grad_all, out_full), out_part, side_got[1])
    ffn_packed = return_packed(after(ffn_sum, vals_grad))
    out_home = (resid + unpack(ffn_packed, gates_two)).astype(bf16)
    query_grad, key_grad, value_grad, slot_part_one = attention_backward(
        lens, query_rot, key_rot, kv_part, attn_vals, vals_grad, tables, gates_wide, log_total,
        own_heads, group_rows,
    )
    query_grad, key_grad, value_grad, slot_part_one = lax.optimization_barrier(
        (query_grad, key_grad, value_grad, slot_part_one, ffn_packed, keep_got[0])
    )[:4]
    kv_grad = jnp.concatenate([key_grad, value_grad], axis=1)
    hidden_one_part = dot_t(query_grad, query_full) + dot_t(kv_grad, kv_full)
    hidden_one_part = hidden_one_part.astype(bf16)
    hidden_one_late = after(hidden_one, hidden_one_part)
    query_part_grad = t_dot(hidden_one_late, query_grad).astype(bf16)
    kv_part_grad = t_dot(hidden_one_late, kv_grad).astype(bf16)
    back_one = scatter_rows(
        jnp.concatenate([hidden_one_part, slot_part_one.astype(bf16)], axis=1)
    )
    back_one = after(back_one, query_part_grad, kv_part_grad, keep_got[1])
    hidden_one_grad, slot_one_grad = back_one[:, :width], back_one[:, width : width + slots]

    def own(value):
        shaped = value.reshape((micro, group_rows) + value.shape[1:])
        part = lax.dynamic_slice_in_dim(shaped, col * tok_rows, tok_rows, 1)
        return part.reshape((home_rows,) + value.shape[1:])

    logit_one_grad = gate_back(
        slot_one_grad, own(gate_vals_one), own(matches_one), own(chosen_one)
    ).astype(bf16)
    hidden_one_grad = hidden_one_grad + dot_t(logit_one_grad, attn_router)
    router_one_grad = t_dot(logit_one_grad, hidden_one_home)
    gain_one_grad = jnp.sum(hidden_one_grad * normed_one, axis=0)
    in_home = resid_grad + norm_back(hidden_one_grad * gain_one, normed_one, scale_one)

    keep_sums = [total(own_grads[2 + part], keep_got[part]) for part in range(2)]
    by_rows = [jnp.stack([keep_sums[part], other_sums[part]]) for part in range(2)]
    own_pair = jnp.where(core == 0, by_rows[0], by_rows[1])
    near_pair = swap(jnp.where(core == 0, by_rows[1], by_rows[0]), "dp", 1)
    by_core = [jnp.where(core == 0, own_pair, near_pair), jnp.where(core == 0, near_pair, own_pair)]
    by_side = [[jnp.where(side == s, part[0], part[1]) for part in by_core] for s in range(2)]
    blocks = [part for row in by_side for part in row]
    gate_up_grad = jnp.concatenate(
        [b[:, :quarter] for b in blocks] + [b[:, quarter : 2 * quarter] for b in blocks], axis=1
    ).astype(f32)
    down_grad = jnp.concatenate([b[:, 2 * quarter :] for b in blocks], axis=1).astype(f32)

    def reduced(value):
        return lax.psum_scatter(value, "dp", scatter_dimension=0, tiled=True)

    out_grad = slots_of(reduced(out_part))
    joint_own = reduced(jnp.concatenate([query_part_grad, kv_part_grad], axis=1))

    query_own, kv_own = joint_own[:, :query_width], joint_own[:, query_width:]
    in_low, out_grad = lax.optimization_barrier(
        (in_home.astype(bf16), out_grad, other_sums[0])
    )[:2]
    results = jnp.stack([out_home, in_low]).reshape(2, micro, tok_rows, width)
    results = jnp.einsum("mtr,bmtd->bmrd", deal, results, preferred_element_type=f32).astype(bf16)
    results = results.reshape(2 * micro, dp_count, piece_rows, width).transpose(1, 0, 2, 3)
    results = results.reshape(dp_count, 2 * micro * piece_rows, width)
    sent_back = results.shape[1]
    small = jnp.concatenate(
        [gain_one_grad[None], gain_two_grad[None], router_one_grad, router_two_grad], axis=0
    ).astype(bf16)
    sum_rows = small.shape[0]
    peak_count = own_heads * slots
    peak_parts, rest = [], peaks
    for _ in range(3):
        peak_parts.append(lax.reduce_precision(rest, 8, 7))
        rest = rest - peak_parts[-1]
    peak_row = jnp.concatenate(peak_parts).astype(bf16)
    small = jnp.pad(small, ((0, -sum_rows % 16 or 16), (0, 0)))
    small = lax.dynamic_update_slice(small, peak_row[None], (sum_rows, 0))
    small = jnp.broadcast_to(small[None], (dp_count,) + small.shape)
    results = jnp.concatenate([results, small], axis=1)
    results = lax.all_to_all(results, "dp", split_axis=0, concat_axis=0, tiled=True)
    small = results[:, sent_back:].astype(f32)
    results = results[:, :sent_back].reshape(dp_count, 2 * micro, piece_rows, width)
    results = results.transpose(1, 0, 2, 3).reshape(2, micro, tok_rows, width)
    peak_row = small[:, sum_rows, : 3 * peak_count].reshape(dp_count, 3, peak_count)
    peak_row = jnp.max((peak_row[:, 0] + peak_row[:, 1]) + peak_row[:, 2], axis=0)
    small = jnp.sum(small, axis=0)
    small = lax.dynamic_update_slice(small, peak_row[None], (sum_rows, 0))
    small = place(
        [swap(small, "expert", k) if k else small for k in range(slots)],
        [col ^ k for k in range(slots)],
    )
    sums = jnp.sum(small[:, :sum_rows], axis=0)
    peaks_all = small[:, sum_rows, :peak_count].reshape(slots, own_heads, slots)
    peaks_all = peaks_all.transpose(2, 0, 1).reshape(slots, HEADS)

    out_grad = out_grad.astype(f32)
    query_out = slots_of(query_own).astype(f32)
    key_part, value_part = kv_own[:, :own_width], kv_own[:, own_width:]
    first_back = lax.ppermute(
        jnp.where(even_col, key_part, value_part), "expert", [(b, a) for a, b in first_pairs]
    )
    second_back = lax.ppermute(
        jnp.where(even_col, value_part, key_part), "expert", [(b, a) for a, b in second_pairs]
    )
    kv_out = jnp.concatenate(
        [
            jnp.where(holds_keys, first_back, second_back),
            jnp.where(holds_keys, second_back, first_back),
        ],
        axis=1,
    ).astype(f32)

    limit = clip_limit[0].astype(f32)
    factor = limit / jnp.maximum(peaks_all, limit)
    query_scale = jnp.repeat(jnp.sqrt(take(factor, col)), HDIM)
    query_clipped = (query_weight.astype(f32) * query_scale[None, None, :]).astype(bf16)
    full_scale = jnp.concatenate(
        [jnp.repeat(jnp.sqrt(jnp.min(factor, axis=0)), HDIM), jnp.ones((query_width,), f32)]
    )
    piece_width = kv_weight.shape[1]
    piece_scale = lax.dynamic_slice_in_dim(full_scale, col * piece_width, piece_width)
    kv_clipped = (kv_weight.astype(f32) * piece_scale[None, :]).astype(bf16)
    return (
        results[0],
        results[1],
        sums[0],
        sums[1],
        sums[2 : 2 + slots].T,
        sums[2 + slots : sum_rows].T,
        query_out[None],
        out_grad[None],
        kv_out,
        gate_up_grad[None],
        down_grad[None],
        query_clipped,
        kv_clipped,
    )


def solution(mesh):
    placed = (
        P(None, ("dp", "expert"), None),
        P(None, ("dp", "expert"), None),
        P(),
        P(None, ("dp", "expert")),
        P(None, "dp", None),
        P(None, "dp", None),
        P(),
        P(),
        P(),
        P(),
        P(),
        P(),
        P("expert", "dp", None),
        P("expert", "dp", None),
        P("dp", "expert"),
        P("expert", "dp", None),
        P("expert", "dp", None),
    )
    return jax.shard_map(
        local,
        mesh=mesh,
        in_specs=placed,
        out_specs=(
            P(None, ("dp", "expert"), None),
            P(None, ("dp", "expert"), None),
            P(),
            P(),
            P(),
            P(),
            P("expert", "dp", None),
            P("expert", "dp", None),
            P("dp", "expert"),
            P("expert", "dp", None),
            P("expert", "dp", None),
            P("expert", "dp", None),
            P("dp", "expert"),
        ),
        check_vma=False,
    )
```

```python
import functools

import jax
import jax.numpy as jnp
from jax import lax
from jax.experimental import pallas as pl
from jax.experimental.pallas import tpu as pltpu
from jax.sharding import PartitionSpec as P

HEADS = 16
HDIM = 128
FF = 5632
TOP = 2

eps_norm = 1e-06
rope_base = 10000.0
very_low = -1e30

f32 = jnp.float32
bf16 = jnp.bfloat16


def dot(left, right):
    return jnp.dot(left, right, preferred_element_type=f32)


def dot_t(left, right):
    return lax.dot_general(left, right, (((1,), (1,)), ((), ())), preferred_element_type=f32)


def t_dot(left, right):
    return lax.dot_general(left, right, (((0,), (0,)), ((), ())), preferred_element_type=f32)


def swap(value, axis, step):
    count = lax.axis_size(axis)
    return lax.ppermute(value, axis, [(i, i ^ step) for i in range(count)])


def take(stacked, index):
    return lax.dynamic_index_in_dim(stacked, index, 0, keepdims=False)


def place(parts, positions):
    out = jnp.zeros((len(parts),) + parts[0].shape, parts[0].dtype)
    for part, position in zip(parts, positions):
        out = lax.dynamic_update_index_in_dim(out, part, position, 0)
    return out


def after(value, *others):
    return lax.optimization_barrier((value, others))[0]


def rotation_tables(places):
    half_dim = HDIM // 2
    frequency = rope_base ** (-jnp.arange(half_dim, dtype=f32) * 2.0 / HDIM)
    angles = places.astype(f32)[:, None] * frequency[None, :]
    cosine, sine = jnp.cos(angles), jnp.sin(angles)
    return (
        jnp.concatenate([cosine, cosine], axis=1),
        jnp.concatenate([-sine, sine], axis=1),
    )


def turn(values, cosine, sine):
    return values * cosine + pltpu.roll(values, HDIM // 2, 1) * sine


def lane_value(table, lane):
    lanes = lax.broadcasted_iota(jnp.int32, table.shape, 1)
    return jnp.sum(jnp.where(lanes == lane, table, 0.0), axis=1, keepdims=True)


def allowed_pairs(rows, first_len):
    query_at = lax.broadcasted_iota(jnp.int32, (rows, rows), 0)
    key_at = lax.broadcasted_iota(jnp.int32, (rows, rows), 1)
    return (key_at <= query_at) & ((key_at >= first_len) | (query_at < first_len))


def forward_kernel(
    lens, query, key, value, cosine, sine, gates, hits,
    vals_out, gated_out, query_out, key_out, total_out, peak_out,
):
    m, h = pl.program_id(0), pl.program_id(1)
    heads = pl.num_programs(1)
    rows = query.shape[0]
    slots = query.shape[1] // (heads * HDIM)

    @pl.when(h == 0)
    def _():
        total_out[...] = jnp.zeros_like(total_out)
        peak_out[...] = jnp.full_like(peak_out, very_low)

    cos_part, sin_part = cosine[...], sine[...]
    allowed = allowed_pairs(rows, lens[m])
    keys = turn(key[...].astype(f32), cos_part, sin_part).astype(bf16)
    key_out[...] = keys
    values = value[...]
    lanes = lax.broadcasted_iota(jnp.int32, total_out.shape, 1)
    peak_lanes = lax.broadcasted_iota(jnp.int32, peak_out.shape, 1)
    totals, peaks = total_out[...], peak_out[...]
    for s in range(slots):
        columns = pl.ds(pl.multiple_of((s * heads + h) * HDIM, HDIM), HDIM)
        turned = turn(query[:, columns], cos_part, sin_part).astype(bf16)
        query_out[:, columns] = turned
        scores = jnp.where(allowed, dot_t(turned, keys) * HDIM ** (-0.5), very_low)
        row_peak = jnp.max(scores, axis=1, keepdims=True)
        expo = jnp.exp(scores - row_peak)
        denom = jnp.sum(expo, axis=1, keepdims=True)
        probs = expo * (1.0 / denom)
        vals = dot(probs.astype(bf16), values).astype(bf16)
        vals_out[:, columns] = vals
        gated_out[:, columns] = (gates[:, s : s + 1] * vals.astype(f32)).astype(bf16)
        lane = h * slots + s
        totals = jnp.where(lanes == lane, row_peak + jnp.log(denom), totals)
        seen = jnp.where(hits[:, s : s + 1] > 0.0, row_peak, very_low)
        peaks = jnp.where(peak_lanes == lane, jnp.max(seen, axis=0, keepdims=True), peaks)
    total_out[...] = totals
    peak_out[...] = peaks


def backward_kernel(
    lens, query, key, value, vals, vals_grad, cosine, sine, gates, total,
    query_grad, key_grad, value_grad, gate_grad,
):
    m, h = pl.program_id(0), pl.program_id(1)
    heads = pl.num_programs(1)
    rows = query.shape[0]
    slots = query.shape[1] // (heads * HDIM)

    @pl.when(h == 0)
    def _():
        gate_grad[...] = jnp.zeros_like(gate_grad)

    allowed = allowed_pairs(rows, lens[m])
    cos_part, back_sine = cosine[...], -sine[...]
    keys, values, totals = key[...], value[...], total[...]
    lanes = lax.broadcasted_iota(jnp.int32, gate_grad.shape, 1)
    slot_sums = gate_grad[...]
    key_sum = jnp.zeros(key.shape, f32)
    value_sum = jnp.zeros(value.shape, f32)
    for s in range(slots):
        columns = pl.ds(pl.multiple_of((s * heads + h) * HDIM, HDIM), HDIM)
        full_grad = vals_grad[:, columns]
        slot_sum = jnp.sum(vals[:, columns].astype(f32) * full_grad, axis=1, keepdims=True)
        slot_sums += jnp.where(lanes == s, slot_sum, 0.0)
        gated_grad = (gates[:, s : s + 1] * full_grad).astype(bf16)
        queries = query[:, columns]
        scores = jnp.where(allowed, dot_t(queries, keys) * HDIM ** (-0.5), very_low)
        probs = jnp.exp(scores - lane_value(totals, h * slots + s))
        prob_grad = dot_t(gated_grad, values)
        inner = jnp.sum(probs * prob_grad, axis=1, keepdims=True)
        score_grad = (probs * (prob_grad - inner) * HDIM ** (-0.5)).astype(bf16)
        query_grad[:, columns] = turn(dot(score_grad, keys), cos_part, back_sine).astype(bf16)
        key_sum += t_dot(score_grad, queries)
        value_sum += t_dot(probs.astype(bf16), gated_grad)
    gate_grad[...] = slot_sums
    key_grad[...] = turn(key_sum, cos_part, back_sine).astype(bf16)
    value_grad[...] = value_sum.astype(bf16)


def attention_specs(own_heads, rows, width):
    def block(columns, index):
        return pl.BlockSpec((rows, columns), index)

    return {
        "query": block(width, lambda m, h, lens: (m, 0)),
        "key": block(HDIM, lambda m, h, lens: (m, h)),
        "value": block(HDIM, lambda m, h, lens: (m, own_heads + h)),
        "rows": block(HDIM, lambda m, h, lens: (m, 0)),
        "peak": pl.BlockSpec((8, HDIM), lambda m, h, lens: (m, 0)),
    }


def attention_forward(lens, query, joint_kv, tables, gates, hits, own_heads, rows):
    micro = lens.shape[0]
    at = attention_specs(own_heads, rows, query.shape[1])
    shape = jax.ShapeDtypeStruct
    total_rows = micro * rows
    return pl.pallas_call(
        forward_kernel,
        grid_spec=pltpu.PrefetchScalarGridSpec(
            num_scalar_prefetch=1,
            grid=(micro, own_heads),
            in_specs=[at["query"], at["key"], at["value"]] + [at["rows"]] * 4,
            out_specs=[at["query"]] * 3 + [at["key"], at["rows"], at["peak"]],
        ),
        out_shape=[shape(query.shape, bf16)] * 3
        + [
            shape((total_rows, own_heads * HDIM), bf16),
            shape((total_rows, HDIM), f32),
            shape((micro * 8, HDIM), f32),
        ],
        compiler_params=pltpu.CompilerParams(vmem_limit_bytes=48 * 2**20),
        cost_estimate=pl.CostEstimate(
            flops=4 * rows * rows * HDIM * micro * HEADS,
            bytes_accessed=14 * query.size,
            transcendentals=rows * rows * micro * HEADS,
        ),
        name="attention_forward",
    )(lens, query, joint_kv, joint_kv, tables[0], tables[1], gates, hits)


def attention_backward(
    lens, query, key, joint_kv, vals, vals_grad, tables, gates, total, own_heads, rows
):
    micro = lens.shape[0]
    at = attention_specs(own_heads, rows, query.shape[1])
    shape = jax.ShapeDtypeStruct
    total_rows = micro * rows
    return pl.pallas_call(
        backward_kernel,
        grid_spec=pltpu.PrefetchScalarGridSpec(
            num_scalar_prefetch=1,
            grid=(micro, own_heads),
            in_specs=[at["query"], at["key"], at["value"], at["query"], at["query"]]
            + [at["rows"]] * 4,
            out_specs=[at["query"], at["key"], at["key"], at["rows"]],
        ),
        out_shape=[shape(query.shape, bf16)]
        + [shape((total_rows, own_heads * HDIM), bf16)] * 2
        + [shape((total_rows, HDIM), f32)],
        compiler_params=pltpu.CompilerParams(vmem_limit_bytes=48 * 2**20),
        cost_estimate=pl.CostEstimate(
            flops=10 * rows * rows * HDIM * micro * HEADS,
            bytes_accessed=14 * query.size,
            transcendentals=rows * rows * micro * HEADS,
        ),
        name="attention_backward",
    )(lens, query, key, joint_kv, vals, vals_grad, tables[0], tables[1], gates, total)


def normalize(values):
    row_scale = lax.rsqrt(jnp.mean(values * values, axis=-1, keepdims=True) + eps_norm)
    return values * row_scale, row_scale


def norm_back(grad_hat, normed, row_scale):
    return row_scale * (grad_hat - normed * jnp.mean(grad_hat * normed, axis=-1, keepdims=True))


def route_gates(logits, routes, expert_table):
    expert_ids = jnp.arange(expert_table.shape[0], dtype=jnp.int32)
    matches = routes[:, :, None] == expert_ids[None, None, :]
    picked = jnp.sum(jnp.where(matches, logits[:, None, :], 0.0), axis=-1)
    gate_vals = jax.nn.softmax(picked, axis=-1)
    slot_ids = route_slots(routes, expert_table)
    chosen = slot_ids[:, :, None] == expert_ids[None, None, :]
    gates = jnp.sum(jnp.where(chosen, gate_vals[:, :, None], 0.0), axis=1)
    return gates, matches, chosen, gate_vals


def route_slots(routes, expert_table):
    expert_ids = jnp.arange(expert_table.shape[0], dtype=jnp.int32)
    matches = routes[..., None] == expert_ids
    return jnp.sum(jnp.where(matches, expert_table, 0), axis=-1)


def gate_back(slot_grad, gate_vals, matches, chosen):
    picked = jnp.sum(jnp.where(chosen, slot_grad[:, None, :], 0.0), axis=-1)
    inner_sum = jnp.sum(gate_vals * picked, axis=-1, keepdims=True)
    picked_grad = gate_vals * (picked - inner_sum)
    return jnp.sum(jnp.where(matches, picked_grad[:, :, None], 0.0), axis=1)


def unit_blocks(count):
    return [(start, min(512, count - start)) for start in range(0, count, 512)]


def expert_kernel(place_ref, hidden, grad, *refs):
    piece_count = (len(refs) - 6) // 2
    own_pieces, near_pieces = refs[:piece_count], refs[piece_count : 2 * piece_count]
    out, hidden_out, act_out, joint_out, weights, sems = refs[2 * piece_count :]
    core, chip = place_ref[0], place_ref[1]
    rows, columns = near_pieces[0].shape
    units = columns // 3
    width = grad.shape[1]

    @pl.when(pl.program_id(0) == 0)
    def _():
        copies = []
        for k in range(piece_count):
            base = (chip ^ k) * (2 * rows)
            for number, (piece, part) in enumerate(
                ((own_pieces[k], core), (near_pieces[k], 1 - core))
            ):
                start = pl.multiple_of(base + part * rows, 16)
                copies.append(
                    pltpu.make_async_copy(
                        piece, weights.at[pl.ds(start, rows)], sems.at[2 * k + number]
                    )
                )
        for copy in copies:
            copy.start()
        for copy in copies:
            copy.wait()

    slot_sum = jnp.zeros((hidden.shape[0], 1), f32)
    for start, size in unit_blocks(units):
        gate_pre = dot(hidden[:, :width], weights[:, start : start + size])
        up_pre = dot(hidden[:, :width], weights[:, units + start : units + start + size])
        act_grad = dot(grad[...], weights[:, 2 * units + start : 2 * units + start + size])
        sigma = 1.0 / (1.0 + jnp.exp(-gate_pre))
        silu_vals = gate_pre * sigma
        active = (silu_vals * up_pre).astype(bf16)
        act_out[:, start : start + size] = active
        slot_sum += jnp.sum(active.astype(f32) * act_grad, axis=1, keepdims=True)
        gate_grad = act_grad * up_pre * sigma * (1.0 + gate_pre * (1.0 - sigma))
        joint_out[:, start : start + size] = gate_grad.astype(bf16)
        joint_out[:, units + start : units + start + size] = (act_grad * silu_vals).astype(bf16)
    for start in range(0, width, 512):
        block = weights[start : start + 512, : 2 * units]
        hidden_out[:, start : start + 512] = dot_t(joint_out[...], block).astype(bf16)
        block = weights[start : start + 512, 2 * units :]
        out[:, start : start + 512] = dot_t(act_out[...], block).astype(bf16)
    lanes = lax.broadcasted_iota(jnp.int32, (hidden.shape[0], HDIM), 1)
    hidden_out[:, width:] = jnp.where(lanes == 0, slot_sum, 0.0).astype(bf16)


def expert_rows(position, hidden, grad, own_pieces, near_pieces):
    rows, width = grad.shape
    columns = near_pieces[0].shape[1]
    units = columns // 3
    tile = 384 if rows % 384 == 0 else 256
    shape = jax.ShapeDtypeStruct
    count = len(own_pieces)

    def tiled(size):
        return pl.BlockSpec((tile, size), lambda i, at: (i, 0))

    return pl.pallas_call(
        expert_kernel,
        grid_spec=pltpu.PrefetchScalarGridSpec(
            num_scalar_prefetch=1,
            grid=(rows // tile,),
            in_specs=[tiled(width + HDIM), tiled(width)]
            + [pl.BlockSpec(memory_space=pl.ANY)] * (2 * count),
            out_specs=[tiled(width), tiled(width + HDIM), tiled(units), tiled(2 * units)],
            scratch_shapes=[
                pltpu.VMEM((width, columns), bf16),
                pltpu.SemaphoreType.DMA((2 * count,)),
            ],
        ),
        out_shape=[
            shape((rows, width), bf16),
            shape((rows, width + HDIM), bf16),
            shape((rows, units), bf16),
            shape((rows, 2 * units), bf16),
        ],
        compiler_params=pltpu.CompilerParams(vmem_limit_bytes=56 * 2**20),
        cost_estimate=pl.CostEstimate(
            flops=4 * rows * width * columns,
            bytes_accessed=2 * (width * columns + 6 * rows * width),
            transcendentals=rows * units,
        ),
        name="expert_rows",
    )(position, hidden, grad, *own_pieces, *near_pieces)


def expert_grad_kernel(order, *refs):
    hidden, grad, gates, joint, active = [refs[2 * n : 2 * n + 2] for n in range(5)]
    outs = refs[10:]
    units = active[0].shape[1]

    def scaled(blocks):
        return [
            (block[...].astype(f32) * gate[:, :1].astype(f32)).astype(bf16)
            for block, gate in zip(blocks, gates)
        ]

    left, right = scaled(hidden), scaled(grad)
    step = pl.program_id(0)
    for number, out in enumerate(outs):

        @pl.when(step == number)
        def _():
            for start, size in unit_blocks(2 * units):
                out[:, start : start + size] = sum(
                    t_dot(rows, part[:, start : start + size]) for rows, part in zip(left, joint)
                ).astype(bf16)
            for start, size in unit_blocks(units):
                out[:, 2 * units + start : 2 * units + start + size] = sum(
                    t_dot(rows, part[:, start : start + size]) for rows, part in zip(right, active)
                ).astype(bf16)


def expert_grads(chunks, chunk_rows, rows_of, joints, actives):
    hidden, grad = rows_of[:2], rows_of[2:]
    rows, units = actives[0].shape
    width = grad[0].shape[1]
    half = chunk_rows // 2
    count = len(chunks)
    order = jnp.stack([2 * chunk + part for chunk in chunks for part in range(2)]).astype(jnp.int32)

    def whole(size, column=0):
        return pl.BlockSpec(
            (rows, size), lambda i, at: (0, column), pipeline_mode=pl.Buffered(1)
        )

    column = pl.BlockSpec((rows, half), lambda i, at: (0, at[i]))
    return pl.pallas_call(
        expert_grad_kernel,
        grid_spec=pltpu.PrefetchScalarGridSpec(
            num_scalar_prefetch=1,
            grid=(2 * count,),
            in_specs=[column] * 4
            + [whole(HDIM, width // HDIM)] * 2
            + [whole(2 * units)] * 2
            + [whole(units)] * 2,
            out_specs=[
                pl.BlockSpec((half, 3 * units), lambda i, at: (0, 0)) for _ in range(2 * count)
            ],
        ),
        out_shape=[jax.ShapeDtypeStruct((half, 3 * units), bf16)] * (2 * count),
        compiler_params=pltpu.CompilerParams(vmem_limit_bytes=56 * 2**20),
        cost_estimate=pl.CostEstimate(
            flops=4 * count * chunk_rows * rows * 3 * units,
            bytes_accessed=2 * (rows * 6 * units + count * chunk_rows * (4 * rows + 3 * units)),
            transcendentals=0,
        ),
        name="expert_grads",
    )(order, *hidden, *grad, *hidden, *joints, *actives)


def local(
    tokens,
    cotangent,
    seq_lengths,
    dealing,
    attn_routes,
    ffn_routes,
    expert_table,
    clip_limit,
    attn_gain,
    ffn_gain,
    attn_router,
    ffn_router,
    query_weight,
    attn_out_weight,
    kv_weight,
    gate_up_weight,
    down_weight,
):
    micro, tok_rows, width = tokens.shape
    dp_count = lax.axis_size("dp")
    slots = lax.axis_size("expert")
    col = lax.axis_index("expert")
    group = lax.axis_index("dp")
    piece_rows = tok_rows // dp_count
    cap = tok_rows * TOP * 3 // (2 * slots)
    group_rows = tok_rows * slots
    all_rows = micro * group_rows
    home_rows = micro * tok_rows
    query_width = HEADS * HDIM
    own_heads = HEADS // slots
    own_width = own_heads * HDIM
    shard_rows = query_weight.shape[1]
    score_scale = HDIM ** (-0.5)
    core = group % 2
    chip = group // 2
    side = chip % 2
    chips = dp_count // 2
    lines = chips // 2
    quarter = FF // 4
    chip_rows = 2 * shard_rows

    both = jnp.stack([tokens, cotangent]).reshape(2 * micro, dp_count, piece_rows, width)
    both = lax.all_to_all(both.transpose(1, 0, 2, 3), "dp", split_axis=0, concat_axis=0, tiled=True)
    def quarter_of(half, part):
        start = (2 * half + part) * quarter
        return jnp.concatenate(
            [
                lax.dynamic_slice_in_dim(gate_up_weight[0], start, quarter, 1),
                lax.dynamic_slice_in_dim(gate_up_weight[0], FF + start, quarter, 1),
                lax.dynamic_slice_in_dim(down_weight[0], start, quarter, 1),
            ],
            axis=1,
        )

    parts = (1 - core, core)
    keep_pair = [quarter_of(side, part) for part in parts]
    send_pair = [quarter_of(1 - side, part) for part in parts]
    both = both.transpose(1, 0, 2, 3).reshape(2, micro, tok_rows, width)
    deal = (dealing[:, :, None] == jnp.arange(tok_rows, dtype=jnp.int32)).astype(bf16)
    work = jnp.einsum("mtr,bmrd->bmtd", deal, both, preferred_element_type=f32)
    x_home = work[0].reshape(home_rows, width)
    dy_home = work[1].reshape(home_rows, width)

    def columns_of(*shards):
        pieces = [shard.reshape(shard_rows, slots, own_width) for shard in shards]
        out = jnp.zeros((shard_rows, len(shards) * query_width), shards[0].dtype)
        for k in range(slots):
            part = jnp.concatenate(
                [lax.dynamic_index_in_dim(piece, col ^ k, 1, keepdims=False) for piece in pieces],
                axis=1,
            )
            part = swap(part, "expert", k) if k else part
            for number in range(len(shards)):
                out = lax.dynamic_update_slice_in_dim(
                    out,
                    part[:, number * own_width : (number + 1) * own_width],
                    number * query_width + (col ^ k) * own_width,
                    1,
                )
        return out

    def slots_of(columns):
        pieces = columns.reshape(shard_rows, slots, own_width)
        out = jnp.zeros((shard_rows, query_width), columns.dtype)
        for k in range(slots):
            part = lax.dynamic_index_in_dim(pieces, col ^ k, 1, keepdims=False)
            part = swap(part, "expert", k) if k else part
            out = lax.dynamic_update_slice_in_dim(out, part, (col ^ k) * own_width, 1)
        return out

    half_slots = slots // 2
    first_pairs = [(c, 2 * c) for c in range(half_slots)]
    first_pairs += [(c, 2 * (c - half_slots) + 1) for c in range(half_slots, slots)]
    second_pairs = [(c, 2 * c + 1) for c in range(half_slots)]
    second_pairs += [(c, 2 * (c - half_slots)) for c in range(half_slots, slots)]
    holds_keys = col < half_slots
    even_col = col % 2 == 0
    low_kv, high_kv = kv_weight[:, :own_width], kv_weight[:, own_width:]
    first_got = lax.ppermute(jnp.where(holds_keys, low_kv, high_kv), "expert", first_pairs)
    second_got = lax.ppermute(jnp.where(holds_keys, high_kv, low_kv), "expert", second_pairs)
    own_kv = jnp.concatenate(
        [
            jnp.where(even_col, first_got, second_got),
            jnp.where(even_col, second_got, first_got),
        ],
        axis=1,
    )
    line_steps = [4 * line for line in range(1, lines)]
    side_first = swap(send_pair[0], "dp", 2)
    keep_first = [swap(keep_pair[0], "dp", step) for step in line_steps]
    joint_own = columns_of(query_weight[0], attn_out_weight[0])
    joint_own = jnp.concatenate([joint_own, own_kv], axis=1)
    joint_full = lax.all_gather(
        after(joint_own, side_first, keep_first), "dp", axis=0, tiled=True
    )
    late_pair = after((keep_pair[1], send_pair[1], side_first), joint_full)
    keep_second = [swap(late_pair[0], "dp", step) for step in line_steps]
    side_second = swap(late_pair[1], "dp", 2)
    first_lines = [swap(late_pair[2], "dp", step) for step in line_steps]
    second_lines = [swap(side_second, "dp", step) for step in line_steps]
    firsts, seconds = [keep_pair[0], side_first], [keep_pair[1], side_second]
    for line in range(lines - 1):
        firsts += [keep_first[line], first_lines[line]]
        seconds += [keep_second[line], second_lines[line]]
    near_pieces = [swap(piece, "dp", 1) for piece in firsts]
    own_pieces = seconds
    query_full = joint_full[:, :query_width]
    out_full = joint_full[:, query_width : 2 * query_width]
    kv_full = joint_full[:, 2 * query_width :]

    positions = jnp.arange(group_rows, dtype=jnp.int32)
    first_len = lax.dynamic_index_in_dim(seq_lengths[:, :, 0], group, 1, keepdims=True)
    in_second = positions[None, :] >= first_len
    places = positions[None, :] - jnp.where(in_second, first_len, 0)
    tables = rotation_tables(places.reshape(all_rows))

    def gather_rows(value):
        shaped = value.reshape(micro, tok_rows, -1)
        out = jnp.zeros((micro, group_rows, shaped.shape[-1]), value.dtype)
        for k in range(slots):
            part = swap(shaped, "expert", k) if k else shaped
            out = lax.dynamic_update_slice_in_dim(out, part, (col ^ k) * tok_rows, 1)
        return out.reshape(all_rows, -1)

    def scatter_rows(value):
        shaped = value.reshape(micro, group_rows, -1)
        total = None
        for k in range(slots):
            part = lax.dynamic_slice_in_dim(shaped, (col ^ k) * tok_rows, tok_rows, 1)
            if k:
                part = swap(part.astype(bf16), "expert", k)
            part = part.astype(f32)
            total = part if total is None else total + part
        return total.reshape(home_rows, -1)

    home_routes = lax.dynamic_slice_in_dim(ffn_routes, col * tok_rows, tok_rows, 1)
    home_slots = route_slots(home_routes, expert_table)
    packs = []
    before = jnp.tril(jnp.ones((tok_rows, tok_rows), bf16), -1)
    for k in range(slots):
        hits = jnp.any(home_slots == (col ^ k), axis=-1)
        rank = jnp.einsum("ts,ms->mt", before, hits.astype(bf16), preferred_element_type=f32)
        packs.append(
            hits[:, None, :]
            & (rank[:, None, :] == jnp.arange(cap, dtype=jnp.int32).astype(f32)[None, :, None])
        )
    packs = jnp.stack(packs)
    packs_low = packs.astype(bf16)
    pack_rows = micro * cap
    sent_rows = slots * pack_rows

    def send_packed(value, lane=None):
        packed = jnp.einsum(
            "kmct,mtd->kmcd", packs_low, value.reshape(micro, tok_rows, -1), preferred_element_type=f32
        ).astype(bf16)
        if lane is not None:
            lanes = jnp.pad(lane[..., None], ((0, 0), (0, 0), (0, 0), (0, HDIM - 1)))
            packed = jnp.concatenate([packed, lanes.astype(bf16)], axis=-1)
        parts = [swap(packed[k], "expert", k) if k else packed[k] for k in range(slots)]
        return jnp.stack(parts).reshape(sent_rows, -1)

    def near_rows(value):
        return jnp.concatenate([value, swap(value, "dp", 1)], axis=0)

    def quad_sums(value):
        near_half, far_half = value
        own, near = jnp.split(near_half, 2, axis=0)
        far, across = jnp.split(far_half, 2, axis=0)
        far_sum = far.astype(f32) + swap(across, "dp", 1).astype(f32)
        return own.astype(f32) + swap(near, "dp", 1).astype(f32), far_sum.astype(bf16)

    def return_packed(value, *others):
        shaped = value.astype(bf16).reshape(slots, micro, cap, -1)
        parts = [swap(shaped[k], "expert", k) if k else shaped[k] for k in range(slots)]
        return after(parts, *others)

    def unpack(packed, scale):
        total = None
        for k in range(slots):
            rows = jnp.einsum("mct,mcd->mtd", packs_low[k], packed[k], preferred_element_type=f32)
            rows = rows.reshape(home_rows, -1) * take(scale.T, col ^ k)[:, None]
            total = rows if total is None else total + rows
        return total

    gain_one = attn_gain.astype(f32)
    gain_two = ffn_gain.astype(f32)
    normed_one, scale_one = normalize(x_home)
    hidden_one_home = (normed_one * gain_one).astype(bf16)
    hidden_one_raw = gather_rows(hidden_one_home)
    hidden_one = hidden_one_raw
    grad_sent = send_packed(after(dy_home.astype(bf16), hidden_one))
    logits_one = dot(hidden_one, attn_router)
    gates_one, matches_one, chosen_one, gate_vals_one = route_gates(
        logits_one, attn_routes.reshape(all_rows, TOP), expert_table
    )
    hits_one = jnp.any(chosen_one, axis=1).astype(f32)

    def wide(value):
        return jnp.pad(value, ((0, 0), (0, HDIM - value.shape[1])))

    kv_part = dot(hidden_one, kv_full).astype(bf16)
    query_part = dot(hidden_one, query_full)
    grad_sent = after(grad_sent, kv_part)
    grad_near, grad_far = near_rows(grad_sent), near_rows(swap(grad_sent, "dp", 2))
    lens = first_len[:, 0].astype(jnp.int32)
    gates_wide = wide(gates_one)
    attn_vals, gated_vals, query_rot, key_rot, log_total, peaks = attention_forward(
        lens, query_part, kv_part, tables, gates_wide, wide(hits_one), own_heads, group_rows
    )
    peaks = jnp.max(peaks, axis=0)[: own_heads * slots]
    gated_vals = after(gated_vals, keep_second, side_second)
    attn_home = after(scatter_rows(dot_t(gated_vals, out_full)), first_lines, second_lines)

    resid = x_home + attn_home
    normed_two, scale_two = normalize(resid)
    hidden_two = (normed_two * gain_two).astype(bf16)
    logits_two = dot(hidden_two, ffn_router)
    gates_two, matches_two, chosen_two, gate_vals_two = route_gates(
        logits_two, home_routes.reshape(home_rows, TOP), expert_table
    )
    gates_by_slot = gates_two.reshape(micro, tok_rows, slots)
    gate_parts = []
    for k in range(slots):
        gate_col = lax.dynamic_index_in_dim(gates_by_slot, col ^ k, 2, keepdims=False)
        gate_parts.append(jnp.sum(jnp.where(packs[k], gate_col[:, None, :], 0.0), axis=-1))
    hidden_sent = send_packed(hidden_two, jnp.stack(gate_parts))
    hidden_near, hidden_far = near_rows(hidden_sent), swap(hidden_sent, "dp", 2)
    hidden_near = after(hidden_near, near_pieces, grad_near, grad_far)
    position = jnp.stack([core, chip]).astype(jnp.int32)
    near_results = expert_rows(
        position, hidden_near, after(grad_near, grad_far), own_pieces, near_pieces
    )
    hidden_far = near_rows(after(hidden_far, near_results))
    far_results = expert_rows(position, hidden_far, grad_far, own_pieces, near_pieces)
    ffn_parts, hidden_parts, actives, joint_grads = zip(near_results, far_results)

    def block_grads(steps, *others):
        rows = after((hidden_near, hidden_far, grad_near, grad_far), *others)
        return expert_grads([chip ^ k for k in steps], chip_rows, rows, joint_grads, actives)

    hidden_sum, hidden_far_sum = quad_sums(hidden_parts)
    ffn_sum, ffn_far_sum = quad_sums(ffn_parts)
    line_grads = block_grads([k ^ 1 for k in range(2, chips)], hidden_far_sum)
    side_got, keep_got = [[], []], [[], []]
    last = ()
    for which, got in enumerate((side_got, keep_got)):
        for part in range(2):
            for line in range(lines - 1):
                block = after(line_grads[4 * line + 2 * which + part], *last)
                got[part].append(swap(block, "dp", 4 * line + 4))
            last = got[part][-1:]
    hidden_got, ffn_far_sum, ffn_sum = lax.optimization_barrier(
        (swap(hidden_far_sum, "dp", 2), ffn_far_sum, ffn_sum, line_grads)
    )[:3]
    hidden_sum = hidden_sum + hidden_got.astype(f32)
    own_grads = block_grads([1, 0], hidden_sum)
    back_packed = return_packed(hidden_sum, *own_grads)
    ffn_sum = ffn_sum + swap(after(ffn_far_sum, hidden_got), "dp", 2).astype(f32)

    def total(own, got):
        return functools.reduce(jnp.add, [part.astype(f32) for part in [own] + got]).astype(bf16)

    other_sums = [swap(total(own_grads[part], side_got[part]), "dp", 2) for part in range(2)]
    slot_two_grad = jnp.zeros((slots, home_rows), f32)
    for k in range(slots):
        rows = jnp.sum(
            jnp.where(packs[k], back_packed[k][:, :, width].astype(f32)[:, :, None], 0.0), axis=1
        )
        slot_two_grad = lax.dynamic_update_index_in_dim(
            slot_two_grad, rows.reshape(home_rows), col ^ k, 0
        )
    hidden_two_grad = unpack([part[..., :width] for part in back_packed], gates_two)
    logit_two_grad = gate_back(slot_two_grad.T, gate_vals_two, matches_two, chosen_two).astype(bf16)
    hidden_two_grad = hidden_two_grad + dot_t(logit_two_grad, ffn_router)
    router_two_grad = t_dot(logit_two_grad, hidden_two)
    gain_two_grad = jnp.sum(hidden_two_grad * normed_two, axis=0)
    resid_grad = dy_home + norm_back(hidden_two_grad * gain_two, normed_two, scale_two)

    resid_grad_low = after(resid_grad.astype(bf16), *side_got[0])
    resid_grad_all = after(gather_rows(resid_grad_low), ffn_sum)
    out_part = t_dot(resid_grad_all, gated_vals).astype(bf16)
    vals_grad = after(dot(resid_grad_all, out_full), out_part, side_got[1])
    ffn_packed = return_packed(after(ffn_sum, vals_grad))
    out_home = (resid + unpack(ffn_packed, gates_two)).astype(bf16)
    query_grad, key_grad, value_grad, slot_part_one = attention_backward(
        lens, query_rot, key_rot, kv_part, attn_vals, vals_grad, tables, gates_wide, log_total,
        own_heads, group_rows,
    )
    query_grad, key_grad, value_grad, slot_part_one = lax.optimization_barrier(
        (query_grad, key_grad, value_grad, slot_part_one, ffn_packed)
    )[:4]
    kv_grad = jnp.concatenate([key_grad, value_grad], axis=1)
    hidden_one_part = dot_t(query_grad, query_full) + dot_t(kv_grad, kv_full)
    hidden_one_part = hidden_one_part.astype(bf16)
    hidden_one_late = after(hidden_one, hidden_one_part, keep_got[0])
    query_part_grad = t_dot(hidden_one_late, query_grad).astype(bf16)
    kv_part_grad = t_dot(hidden_one_late, kv_grad).astype(bf16)
    back_one = scatter_rows(
        jnp.concatenate([hidden_one_part, slot_part_one.astype(bf16)], axis=1)
    )
    back_one, keep_got, other_sums = lax.optimization_barrier(
        (back_one, keep_got, other_sums, query_part_grad, kv_part_grad)
    )[:3]
    hidden_one_grad, slot_one_grad = back_one[:, :width], back_one[:, width : width + slots]

    def own(value):
        shaped = value.reshape((micro, group_rows) + value.shape[1:])
        part = lax.dynamic_slice_in_dim(shaped, col * tok_rows, tok_rows, 1)
        return part.reshape((home_rows,) + value.shape[1:])

    logit_one_grad = gate_back(
        slot_one_grad, own(gate_vals_one), own(matches_one), own(chosen_one)
    ).astype(bf16)
    hidden_one_grad = hidden_one_grad + dot_t(logit_one_grad, attn_router)
    router_one_grad = t_dot(logit_one_grad, hidden_one_home)
    gain_one_grad = jnp.sum(hidden_one_grad * normed_one, axis=0)
    in_home = resid_grad + norm_back(hidden_one_grad * gain_one, normed_one, scale_one)

    keep_sums = [total(own_grads[2 + part], keep_got[part]) for part in range(2)]
    by_rows = [jnp.stack([keep_sums[part], other_sums[part]]) for part in range(2)]
    own_pair = jnp.where(core == 0, by_rows[0], by_rows[1])
    near_pair = swap(jnp.where(core == 0, by_rows[1], by_rows[0]), "dp", 1)
    by_core = [jnp.where(core == 0, own_pair, near_pair), jnp.where(core == 0, near_pair, own_pair)]
    by_side = [[jnp.where(side == s, part[0], part[1]) for part in by_core] for s in range(2)]
    blocks = [part for row in by_side for part in row]
    gate_up_grad = jnp.concatenate(
        [b[:, :quarter] for b in blocks] + [b[:, quarter : 2 * quarter] for b in blocks], axis=1
    ).astype(f32)
    down_grad = jnp.concatenate([b[:, 2 * quarter :] for b in blocks], axis=1).astype(f32)

    def reduced(value):
        return lax.psum_scatter(value, "dp", scatter_dimension=0, tiled=True)

    in_low = in_home.astype(bf16)
    out_grad = slots_of(after(reduced(out_part), in_low))
    joint_own = reduced(jnp.concatenate([query_part_grad, kv_part_grad], axis=1))

    query_own, kv_own = joint_own[:, :query_width], joint_own[:, query_width:]
    results = jnp.stack([out_home, in_low]).reshape(2, micro, tok_rows, width)
    results = jnp.einsum("mtr,bmtd->bmrd", deal, results, preferred_element_type=f32).astype(bf16)
    results = results.reshape(2 * micro, dp_count, piece_rows, width).transpose(1, 0, 2, 3)
    results = results.reshape(dp_count, 2 * micro * piece_rows, width)
    sent_back = results.shape[1]
    small = jnp.concatenate(
        [gain_one_grad[None], gain_two_grad[None], router_one_grad, router_two_grad], axis=0
    ).astype(bf16)
    sum_rows = small.shape[0]
    peak_count = own_heads * slots
    peak_parts, rest = [], peaks
    for _ in range(3):
        peak_parts.append(lax.reduce_precision(rest, 8, 7))
        rest = rest - peak_parts[-1]
    peak_row = jnp.concatenate(peak_parts).astype(bf16)
    small = jnp.pad(small, ((0, -sum_rows % 16 or 16), (0, 0)))
    small = lax.dynamic_update_slice(small, peak_row[None], (sum_rows, 0))
    small = jnp.broadcast_to(small[None], (dp_count,) + small.shape)
    results = jnp.concatenate([results, small], axis=1)
    results = lax.all_to_all(results, "dp", split_axis=0, concat_axis=0, tiled=True)
    small = results[:, sent_back:].astype(f32)
    results = results[:, :sent_back].reshape(dp_count, 2 * micro, piece_rows, width)
    results = results.transpose(1, 0, 2, 3).reshape(2, micro, tok_rows, width)
    peak_row = small[:, sum_rows, : 3 * peak_count].reshape(dp_count, 3, peak_count)
    peak_row = jnp.max((peak_row[:, 0] + peak_row[:, 1]) + peak_row[:, 2], axis=0)
    small = jnp.sum(small, axis=0)
    small = lax.dynamic_update_slice(small, peak_row[None], (sum_rows, 0))
    small = place(
        [swap(small, "expert", k) if k else small for k in range(slots)],
        [col ^ k for k in range(slots)],
    )
    sums = jnp.sum(small[:, :sum_rows], axis=0)
    peaks_all = small[:, sum_rows, :peak_count].reshape(slots, own_heads, slots)
    peaks_all = peaks_all.transpose(2, 0, 1).reshape(slots, HEADS)

    out_grad = out_grad.astype(f32)
    query_out = slots_of(query_own).astype(f32)
    key_part, value_part = kv_own[:, :own_width], kv_own[:, own_width:]
    first_back = lax.ppermute(
        jnp.where(even_col, key_part, value_part), "expert", [(b, a) for a, b in first_pairs]
    )
    second_back = lax.ppermute(
        jnp.where(even_col, value_part, key_part), "expert", [(b, a) for a, b in second_pairs]
    )
    kv_out = jnp.concatenate(
        [
            jnp.where(holds_keys, first_back, second_back),
            jnp.where(holds_keys, second_back, first_back),
        ],
        axis=1,
    ).astype(f32)

    limit = clip_limit[0].astype(f32)
    factor = limit / jnp.maximum(peaks_all, limit)
    query_scale = jnp.repeat(jnp.sqrt(take(factor, col)), HDIM)
    query_clipped = (query_weight.astype(f32) * query_scale[None, None, :]).astype(bf16)
    full_scale = jnp.concatenate(
        [jnp.repeat(jnp.sqrt(jnp.min(factor, axis=0)), HDIM), jnp.ones((query_width,), f32)]
    )
    piece_width = kv_weight.shape[1]
    piece_scale = lax.dynamic_slice_in_dim(full_scale, col * piece_width, piece_width)
    kv_clipped = (kv_weight.astype(f32) * piece_scale[None, :]).astype(bf16)
    return (
        results[0],
        results[1],
        sums[0],
        sums[1],
        sums[2 : 2 + slots].T,
        sums[2 + slots : sum_rows].T,
        query_out[None],
        out_grad[None],
        kv_out,
        gate_up_grad[None],
        down_grad[None],
        query_clipped,
        kv_clipped,
    )


def solution(mesh):
    placed = (
        P(None, ("dp", "expert"), None),
        P(None, ("dp", "expert"), None),
        P(),
        P(None, ("dp", "expert")),
        P(None, "dp", None),
        P(None, "dp", None),
        P(),
        P(),
        P(),
        P(),
        P(),
        P(),
        P("expert", "dp", None),
        P("expert", "dp", None),
        P("dp", "expert"),
        P("expert", "dp", None),
        P("expert", "dp", None),
    )
    return jax.shard_map(
        local,
        mesh=mesh,
        in_specs=placed,
        out_specs=(
            P(None, ("dp", "expert"), None),
            P(None, ("dp", "expert"), None),
            P(),
            P(),
            P(),
            P(),
            P("expert", "dp", None),
            P("expert", "dp", None),
            P("dp", "expert"),
            P("expert", "dp", None),
            P("expert", "dp", None),
            P("expert", "dp", None),
            P("dp", "expert"),
        ),
        check_vma=False,
    )
```

```python
import functools

import jax
import jax.numpy as jnp
from jax import lax
from jax.experimental import pallas as pl
from jax.experimental.pallas import tpu as pltpu
from jax.sharding import PartitionSpec as P

HEADS = 16
HDIM = 128
FF = 5632
TOP = 2

eps_norm = 1e-06
rope_base = 10000.0
very_low = -1e30

f32 = jnp.float32
bf16 = jnp.bfloat16


def dot(left, right):
    return jnp.dot(left, right, preferred_element_type=f32)


def dot_t(left, right):
    return lax.dot_general(left, right, (((1,), (1,)), ((), ())), preferred_element_type=f32)


def t_dot(left, right):
    return lax.dot_general(left, right, (((0,), (0,)), ((), ())), preferred_element_type=f32)


def swap(value, axis, step):
    count = lax.axis_size(axis)
    return lax.ppermute(value, axis, [(i, i ^ step) for i in range(count)])


def take(stacked, index):
    return lax.dynamic_index_in_dim(stacked, index, 0, keepdims=False)


def place(parts, positions):
    out = jnp.zeros((len(parts),) + parts[0].shape, parts[0].dtype)
    for part, position in zip(parts, positions):
        out = lax.dynamic_update_index_in_dim(out, part, position, 0)
    return out


def after(value, *others):
    return lax.optimization_barrier((value, others))[0]


def rotation_tables(places):
    half_dim = HDIM // 2
    frequency = rope_base ** (-jnp.arange(half_dim, dtype=f32) * 2.0 / HDIM)
    angles = places.astype(f32)[:, None] * frequency[None, :]
    cosine, sine = jnp.cos(angles), jnp.sin(angles)
    return (
        jnp.concatenate([cosine, cosine], axis=1),
        jnp.concatenate([-sine, sine], axis=1),
    )


def turn(values, cosine, sine):
    return values * cosine + pltpu.roll(values, HDIM // 2, 1) * sine


def lane_value(table, lane):
    lanes = lax.broadcasted_iota(jnp.int32, table.shape, 1)
    return jnp.sum(jnp.where(lanes == lane, table, 0.0), axis=1, keepdims=True)


def allowed_pairs(rows, first_len):
    query_at = lax.broadcasted_iota(jnp.int32, (rows, rows), 0)
    key_at = lax.broadcasted_iota(jnp.int32, (rows, rows), 1)
    return (key_at <= query_at) & ((key_at >= first_len) | (query_at < first_len))


def forward_kernel(
    lens, query, key, value, cosine, sine, gates, hits,
    vals_out, gated_out, query_out, key_out, total_out, peak_out,
):
    m, h = pl.program_id(0), pl.program_id(1)
    heads = pl.num_programs(1)
    rows = query.shape[0]
    slots = query.shape[1] // (heads * HDIM)

    @pl.when(h == 0)
    def _():
        total_out[...] = jnp.zeros_like(total_out)
        peak_out[...] = jnp.full_like(peak_out, very_low)

    cos_part, sin_part = cosine[...], sine[...]
    allowed = allowed_pairs(rows, lens[m])
    keys = turn(key[...].astype(f32), cos_part, sin_part).astype(bf16)
    key_out[...] = keys
    values = value[...]
    lanes = lax.broadcasted_iota(jnp.int32, total_out.shape, 1)
    peak_lanes = lax.broadcasted_iota(jnp.int32, peak_out.shape, 1)
    totals, peaks = total_out[...], peak_out[...]
    for s in range(slots):
        columns = pl.ds(pl.multiple_of((s * heads + h) * HDIM, HDIM), HDIM)
        turned = turn(query[:, columns], cos_part, sin_part).astype(bf16)
        query_out[:, columns] = turned
        scores = jnp.where(allowed, dot_t(turned, keys) * HDIM ** (-0.5), very_low)
        row_peak = jnp.max(scores, axis=1, keepdims=True)
        expo = jnp.exp(scores - row_peak)
        denom = jnp.sum(expo, axis=1, keepdims=True)
        probs = expo * (1.0 / denom)
        vals = dot(probs.astype(bf16), values).astype(bf16)
        vals_out[:, columns] = vals
        gated_out[:, columns] = (gates[:, s : s + 1] * vals.astype(f32)).astype(bf16)
        lane = h * slots + s
        totals = jnp.where(lanes == lane, row_peak + jnp.log(denom), totals)
        seen = jnp.where(hits[:, s : s + 1] > 0.0, row_peak, very_low)
        peaks = jnp.where(peak_lanes == lane, jnp.max(seen, axis=0, keepdims=True), peaks)
    total_out[...] = totals
    peak_out[...] = peaks


def backward_kernel(
    lens, query, key, value, vals, vals_grad, cosine, sine, gates, total,
    query_grad, key_grad, value_grad, gate_grad,
):
    m, h = pl.program_id(0), pl.program_id(1)
    heads = pl.num_programs(1)
    rows = query.shape[0]
    slots = query.shape[1] // (heads * HDIM)

    @pl.when(h == 0)
    def _():
        gate_grad[...] = jnp.zeros_like(gate_grad)

    allowed = allowed_pairs(rows, lens[m])
    cos_part, back_sine = cosine[...], -sine[...]
    keys, values, totals = key[...], value[...], total[...]
    lanes = lax.broadcasted_iota(jnp.int32, gate_grad.shape, 1)
    slot_sums = gate_grad[...]
    key_sum = jnp.zeros(key.shape, f32)
    value_sum = jnp.zeros(value.shape, f32)
    for s in range(slots):
        columns = pl.ds(pl.multiple_of((s * heads + h) * HDIM, HDIM), HDIM)
        full_grad = vals_grad[:, columns]
        slot_sum = jnp.sum(vals[:, columns].astype(f32) * full_grad, axis=1, keepdims=True)
        slot_sums += jnp.where(lanes == s, slot_sum, 0.0)
        gated_grad = (gates[:, s : s + 1] * full_grad).astype(bf16)
        queries = query[:, columns]
        scores = jnp.where(allowed, dot_t(queries, keys) * HDIM ** (-0.5), very_low)
        probs = jnp.exp(scores - lane_value(totals, h * slots + s))
        prob_grad = dot_t(gated_grad, values)
        inner = jnp.sum(probs * prob_grad, axis=1, keepdims=True)
        score_grad = (probs * (prob_grad - inner) * HDIM ** (-0.5)).astype(bf16)
        query_grad[:, columns] = turn(dot(score_grad, keys), cos_part, back_sine).astype(bf16)
        key_sum += t_dot(score_grad, queries)
        value_sum += t_dot(probs.astype(bf16), gated_grad)
    gate_grad[...] = slot_sums
    key_grad[...] = turn(key_sum, cos_part, back_sine).astype(bf16)
    value_grad[...] = value_sum.astype(bf16)


def attention_specs(own_heads, rows, width):
    def block(columns, index):
        return pl.BlockSpec((rows, columns), index)

    return {
        "query": block(width, lambda m, h, lens: (m, 0)),
        "key": block(HDIM, lambda m, h, lens: (m, h)),
        "value": block(HDIM, lambda m, h, lens: (m, own_heads + h)),
        "rows": block(HDIM, lambda m, h, lens: (m, 0)),
        "peak": pl.BlockSpec((8, HDIM), lambda m, h, lens: (m, 0)),
    }


def attention_forward(lens, query, joint_kv, tables, gates, hits, own_heads, rows):
    micro = lens.shape[0]
    at = attention_specs(own_heads, rows, query.shape[1])
    shape = jax.ShapeDtypeStruct
    total_rows = micro * rows
    return pl.pallas_call(
        forward_kernel,
        grid_spec=pltpu.PrefetchScalarGridSpec(
            num_scalar_prefetch=1,
            grid=(micro, own_heads),
            in_specs=[at["query"], at["key"], at["value"]] + [at["rows"]] * 4,
            out_specs=[at["query"]] * 3 + [at["key"], at["rows"], at["peak"]],
        ),
        out_shape=[shape(query.shape, bf16)] * 3
        + [
            shape((total_rows, own_heads * HDIM), bf16),
            shape((total_rows, HDIM), f32),
            shape((micro * 8, HDIM), f32),
        ],
        compiler_params=pltpu.CompilerParams(vmem_limit_bytes=48 * 2**20),
        cost_estimate=pl.CostEstimate(
            flops=4 * rows * rows * HDIM * micro * HEADS,
            bytes_accessed=14 * query.size,
            transcendentals=rows * rows * micro * HEADS,
        ),
        name="attention_forward",
    )(lens, query, joint_kv, joint_kv, tables[0], tables[1], gates, hits)


def attention_backward(
    lens, query, key, joint_kv, vals, vals_grad, tables, gates, total, own_heads, rows
):
    micro = lens.shape[0]
    at = attention_specs(own_heads, rows, query.shape[1])
    shape = jax.ShapeDtypeStruct
    total_rows = micro * rows
    return pl.pallas_call(
        backward_kernel,
        grid_spec=pltpu.PrefetchScalarGridSpec(
            num_scalar_prefetch=1,
            grid=(micro, own_heads),
            in_specs=[at["query"], at["key"], at["value"], at["query"], at["query"]]
            + [at["rows"]] * 4,
            out_specs=[at["query"], at["key"], at["key"], at["rows"]],
        ),
        out_shape=[shape(query.shape, bf16)]
        + [shape((total_rows, own_heads * HDIM), bf16)] * 2
        + [shape((total_rows, HDIM), f32)],
        compiler_params=pltpu.CompilerParams(vmem_limit_bytes=48 * 2**20),
        cost_estimate=pl.CostEstimate(
            flops=10 * rows * rows * HDIM * micro * HEADS,
            bytes_accessed=14 * query.size,
            transcendentals=rows * rows * micro * HEADS,
        ),
        name="attention_backward",
    )(lens, query, key, joint_kv, vals, vals_grad, tables[0], tables[1], gates, total)


def normalize(values):
    row_scale = lax.rsqrt(jnp.mean(values * values, axis=-1, keepdims=True) + eps_norm)
    return values * row_scale, row_scale


def norm_back(grad_hat, normed, row_scale):
    return row_scale * (grad_hat - normed * jnp.mean(grad_hat * normed, axis=-1, keepdims=True))


def route_gates(logits, routes, expert_table):
    expert_ids = jnp.arange(expert_table.shape[0], dtype=jnp.int32)
    matches = routes[:, :, None] == expert_ids[None, None, :]
    picked = jnp.sum(jnp.where(matches, logits[:, None, :], 0.0), axis=-1)
    gate_vals = jax.nn.softmax(picked, axis=-1)
    slot_ids = route_slots(routes, expert_table)
    chosen = slot_ids[:, :, None] == expert_ids[None, None, :]
    gates = jnp.sum(jnp.where(chosen, gate_vals[:, :, None], 0.0), axis=1)
    return gates, matches, chosen, gate_vals


def route_slots(routes, expert_table):
    expert_ids = jnp.arange(expert_table.shape[0], dtype=jnp.int32)
    matches = routes[..., None] == expert_ids
    return jnp.sum(jnp.where(matches, expert_table, 0), axis=-1)


def gate_back(slot_grad, gate_vals, matches, chosen):
    picked = jnp.sum(jnp.where(chosen, slot_grad[:, None, :], 0.0), axis=-1)
    inner_sum = jnp.sum(gate_vals * picked, axis=-1, keepdims=True)
    picked_grad = gate_vals * (picked - inner_sum)
    return jnp.sum(jnp.where(matches, picked_grad[:, :, None], 0.0), axis=1)


def unit_blocks(count):
    return [(start, min(512, count - start)) for start in range(0, count, 512)]


def expert_kernel(place_ref, hidden, grad, *refs):
    piece_count = (len(refs) - 8) // 2
    own_pieces, near_pieces = refs[:piece_count], refs[piece_count : 2 * piece_count]
    out_pair, hidden_pair = refs[2 * piece_count :][:2], refs[2 * piece_count :][2:4]
    act_out, joint_out, weights, sems = refs[2 * piece_count + 4 :]
    core, chip = place_ref[0], place_ref[1]
    rows, columns = near_pieces[0].shape
    units = columns // 3
    width = grad.shape[1]

    @pl.when(pl.program_id(0) == 0)
    def _():
        copies = []
        for k in range(piece_count):
            base = (chip ^ k) * (2 * rows)
            for number, (piece, part) in enumerate(
                ((own_pieces[k], core), (near_pieces[k], 1 - core))
            ):
                start = pl.multiple_of(base + part * rows, 16)
                copies.append(
                    pltpu.make_async_copy(
                        piece, weights.at[pl.ds(start, rows)], sems.at[2 * k + number]
                    )
                )
        for copy in copies:
            copy.start()
        for copy in copies:
            copy.wait()

    slot_sum = jnp.zeros((hidden.shape[0], 1), f32)
    for start, size in unit_blocks(units):
        gate_pre = dot(hidden[:, :width], weights[:, start : start + size])
        up_pre = dot(hidden[:, :width], weights[:, units + start : units + start + size])
        act_grad = dot(grad[...], weights[:, 2 * units + start : 2 * units + start + size])
        sigma = 1.0 / (1.0 + jnp.exp(-gate_pre))
        silu_vals = gate_pre * sigma
        active = (silu_vals * up_pre).astype(bf16)
        act_out[:, start : start + size] = active
        slot_sum += jnp.sum(active.astype(f32) * act_grad, axis=1, keepdims=True)
        gate_grad = act_grad * up_pre * sigma * (1.0 + gate_pre * (1.0 - sigma))
        joint_out[:, start : start + size] = gate_grad.astype(bf16)
        joint_out[:, units + start : units + start + size] = (act_grad * silu_vals).astype(bf16)
    lanes = lax.broadcasted_iota(jnp.int32, (hidden.shape[0], HDIM), 1)
    last = jnp.where(lanes == 0, slot_sum, 0.0).astype(bf16)
    for number in range(2):

        @pl.when(pl.program_id(0) == number)
        def _():
            out, hidden_out = out_pair[number], hidden_pair[number]
            for start in range(0, width, 512):
                block = weights[start : start + 512, : 2 * units]
                hidden_out[:, start : start + 512] = dot_t(joint_out[...], block).astype(bf16)
                block = weights[start : start + 512, 2 * units :]
                out[:, start : start + 512] = dot_t(act_out[...], block).astype(bf16)
            hidden_out[:, width:] = last


def expert_rows(position, hidden, grad, own_pieces, near_pieces):
    rows, width = grad.shape
    columns = near_pieces[0].shape[1]
    units = columns // 3
    tile = rows // 2
    shape = jax.ShapeDtypeStruct
    count = len(own_pieces)

    def tiled(size):
        return pl.BlockSpec((tile, size), lambda i, at: (i, 0))

    def fixed(size):
        return pl.BlockSpec((tile, size), lambda i, at: (0, 0))

    return pl.pallas_call(
        expert_kernel,
        grid_spec=pltpu.PrefetchScalarGridSpec(
            num_scalar_prefetch=1,
            grid=(rows // tile,),
            in_specs=[tiled(width + HDIM), tiled(width)]
            + [pl.BlockSpec(memory_space=pl.ANY)] * (2 * count),
            out_specs=[fixed(width)] * 2
            + [fixed(width + HDIM)] * 2
            + [tiled(units), tiled(2 * units)],
            scratch_shapes=[
                pltpu.VMEM((width, columns), bf16),
                pltpu.SemaphoreType.DMA((2 * count,)),
            ],
        ),
        out_shape=[
            shape((tile, width), bf16),
            shape((tile, width), bf16),
            shape((tile, width + HDIM), bf16),
            shape((tile, width + HDIM), bf16),
            shape((rows, units), bf16),
            shape((rows, 2 * units), bf16),
        ],
        compiler_params=pltpu.CompilerParams(vmem_limit_bytes=56 * 2**20),
        cost_estimate=pl.CostEstimate(
            flops=4 * rows * width * columns,
            bytes_accessed=2 * (width * columns + 6 * rows * width),
            transcendentals=rows * units,
        ),
        name="expert_rows",
    )(position, hidden, grad, *own_pieces, *near_pieces)


def expert_grad_kernel(order, *refs):
    hidden, grad, gates, joint, active = [refs[2 * n : 2 * n + 2] for n in range(5)]
    outs = refs[10:]
    units = active[0].shape[1]

    def scaled(blocks):
        return [
            (block[...].astype(f32) * gate[:, :1].astype(f32)).astype(bf16)
            for block, gate in zip(blocks, gates)
        ]

    left, right = scaled(hidden), scaled(grad)
    step = pl.program_id(0)
    for number, out in enumerate(outs):

        @pl.when(step == number)
        def _():
            for start, size in unit_blocks(2 * units):
                out[:, start : start + size] = sum(
                    t_dot(rows, part[:, start : start + size]) for rows, part in zip(left, joint)
                ).astype(bf16)
            for start, size in unit_blocks(units):
                out[:, 2 * units + start : 2 * units + start + size] = sum(
                    t_dot(rows, part[:, start : start + size]) for rows, part in zip(right, active)
                ).astype(bf16)


def expert_grads(chunks, chunk_rows, rows_of, joints, actives):
    hidden, grad = rows_of[:2], rows_of[2:]
    rows, units = actives[0].shape
    width = grad[0].shape[1]
    half = chunk_rows // 2
    count = len(chunks)
    order = jnp.stack([2 * chunk + part for chunk in chunks for part in range(2)]).astype(jnp.int32)

    def whole(size, column=0):
        return pl.BlockSpec(
            (rows, size), lambda i, at: (0, column), pipeline_mode=pl.Buffered(1)
        )

    column = pl.BlockSpec((rows, half), lambda i, at: (0, at[i]))
    return pl.pallas_call(
        expert_grad_kernel,
        grid_spec=pltpu.PrefetchScalarGridSpec(
            num_scalar_prefetch=1,
            grid=(2 * count,),
            in_specs=[column] * 4
            + [whole(HDIM, width // HDIM)] * 2
            + [whole(2 * units)] * 2
            + [whole(units)] * 2,
            out_specs=[
                pl.BlockSpec((half, 3 * units), lambda i, at: (0, 0)) for _ in range(2 * count)
            ],
        ),
        out_shape=[jax.ShapeDtypeStruct((half, 3 * units), bf16)] * (2 * count),
        compiler_params=pltpu.CompilerParams(vmem_limit_bytes=56 * 2**20),
        cost_estimate=pl.CostEstimate(
            flops=4 * count * chunk_rows * rows * 3 * units,
            bytes_accessed=2 * (rows * 6 * units + count * chunk_rows * (4 * rows + 3 * units)),
            transcendentals=0,
        ),
        name="expert_grads",
    )(order, *hidden, *grad, *hidden, *joints, *actives)


def local(
    tokens,
    cotangent,
    seq_lengths,
    dealing,
    attn_routes,
    ffn_routes,
    expert_table,
    clip_limit,
    attn_gain,
    ffn_gain,
    attn_router,
    ffn_router,
    query_weight,
    attn_out_weight,
    kv_weight,
    gate_up_weight,
    down_weight,
):
    micro, tok_rows, width = tokens.shape
    dp_count = lax.axis_size("dp")
    slots = lax.axis_size("expert")
    col = lax.axis_index("expert")
    group = lax.axis_index("dp")
    piece_rows = tok_rows // dp_count
    cap = tok_rows * TOP * 3 // (2 * slots)
    group_rows = tok_rows * slots
    all_rows = micro * group_rows
    home_rows = micro * tok_rows
    query_width = HEADS * HDIM
    own_heads = HEADS // slots
    own_width = own_heads * HDIM
    shard_rows = query_weight.shape[1]
    score_scale = HDIM ** (-0.5)
    core = group % 2
    chip = group // 2
    side = chip % 2
    chips = dp_count // 2
    lines = chips // 2
    quarter = FF // 4
    chip_rows = 2 * shard_rows

    both = jnp.stack([tokens, cotangent]).reshape(2 * micro, dp_count, piece_rows, width)
    both = lax.all_to_all(both.transpose(1, 0, 2, 3), "dp", split_axis=0, concat_axis=0, tiled=True)
    def quarter_of(half, part):
        start = (2 * half + part) * quarter
        return jnp.concatenate(
            [
                lax.dynamic_slice_in_dim(gate_up_weight[0], start, quarter, 1),
                lax.dynamic_slice_in_dim(gate_up_weight[0], FF + start, quarter, 1),
                lax.dynamic_slice_in_dim(down_weight[0], start, quarter, 1),
            ],
            axis=1,
        )

    parts = (1 - core, core)
    keep_pair = [quarter_of(side, part) for part in parts]
    send_pair = [quarter_of(1 - side, part) for part in parts]
    both = both.transpose(1, 0, 2, 3).reshape(2, micro, tok_rows, width)
    deal = (dealing[:, :, None] == jnp.arange(tok_rows, dtype=jnp.int32)).astype(bf16)
    work = jnp.einsum("mtr,bmrd->bmtd", deal, both, preferred_element_type=f32)
    x_home = work[0].reshape(home_rows, width)
    dy_home = work[1].reshape(home_rows, width)

    def columns_of(*shards):
        pieces = [shard.reshape(shard_rows, slots, own_width) for shard in shards]
        out = jnp.zeros((shard_rows, len(shards) * query_width), shards[0].dtype)
        for k in range(slots):
            part = jnp.concatenate(
                [lax.dynamic_index_in_dim(piece, col ^ k, 1, keepdims=False) for piece in pieces],
                axis=1,
            )
            part = swap(part, "expert", k) if k else part
            for number in range(len(shards)):
                out = lax.dynamic_update_slice_in_dim(
                    out,
                    part[:, number * own_width : (number + 1) * own_width],
                    number * query_width + (col ^ k) * own_width,
                    1,
                )
        return out

    def slots_of(columns):
        pieces = columns.reshape(shard_rows, slots, own_width)
        out = jnp.zeros((shard_rows, query_width), columns.dtype)
        for k in range(slots):
            part = lax.dynamic_index_in_dim(pieces, col ^ k, 1, keepdims=False)
            part = swap(part, "expert", k) if k else part
            out = lax.dynamic_update_slice_in_dim(out, part, (col ^ k) * own_width, 1)
        return out

    half_slots = slots // 2
    first_pairs = [(c, 2 * c) for c in range(half_slots)]
    first_pairs += [(c, 2 * (c - half_slots) + 1) for c in range(half_slots, slots)]
    second_pairs = [(c, 2 * c + 1) for c in range(half_slots)]
    second_pairs += [(c, 2 * (c - half_slots)) for c in range(half_slots, slots)]
    holds_keys = col < half_slots
    even_col = col % 2 == 0
    low_kv, high_kv = kv_weight[:, :own_width], kv_weight[:, own_width:]
    first_got = lax.ppermute(jnp.where(holds_keys, low_kv, high_kv), "expert", first_pairs)
    second_got = lax.ppermute(jnp.where(holds_keys, high_kv, low_kv), "expert", second_pairs)
    own_kv = jnp.concatenate(
        [
            jnp.where(even_col, first_got, second_got),
            jnp.where(even_col, second_got, first_got),
        ],
        axis=1,
    )
    line_steps = [4 * line for line in range(1, lines)]
    side_first = swap(send_pair[0], "dp", 2)
    keep_first = [swap(keep_pair[0], "dp", step) for step in line_steps]
    joint_own = columns_of(query_weight[0], attn_out_weight[0])
    joint_own = jnp.concatenate([joint_own, own_kv], axis=1)
    joint_full = lax.all_gather(
        after(joint_own, side_first, keep_first), "dp", axis=0, tiled=True
    )
    late_pair = after((keep_pair[1], send_pair[1], side_first), joint_full)
    keep_second = [swap(late_pair[0], "dp", step) for step in line_steps]
    side_second = swap(late_pair[1], "dp", 2)
    first_lines = [swap(late_pair[2], "dp", step) for step in line_steps]
    second_lines = [swap(side_second, "dp", step) for step in line_steps]
    firsts, seconds = [keep_pair[0], side_first], [keep_pair[1], side_second]
    for line in range(lines - 1):
        firsts += [keep_first[line], first_lines[line]]
        seconds += [keep_second[line], second_lines[line]]
    near_pieces = [swap(piece, "dp", 1) for piece in firsts]
    own_pieces = seconds
    query_full = joint_full[:, :query_width]
    out_full = joint_full[:, query_width : 2 * query_width]
    kv_full = joint_full[:, 2 * query_width :]

    positions = jnp.arange(group_rows, dtype=jnp.int32)
    first_len = lax.dynamic_index_in_dim(seq_lengths[:, :, 0], group, 1, keepdims=True)
    in_second = positions[None, :] >= first_len
    places = positions[None, :] - jnp.where(in_second, first_len, 0)
    tables = rotation_tables(places.reshape(all_rows))

    def gather_rows(value):
        shaped = value.reshape(micro, tok_rows, -1)
        out = jnp.zeros((micro, group_rows, shaped.shape[-1]), value.dtype)
        for k in range(slots):
            part = swap(shaped, "expert", k) if k else shaped
            out = lax.dynamic_update_slice_in_dim(out, part, (col ^ k) * tok_rows, 1)
        return out.reshape(all_rows, -1)

    def scatter_rows(value):
        shaped = value.reshape(micro, group_rows, -1)
        total = None
        for k in range(slots):
            part = lax.dynamic_slice_in_dim(shaped, (col ^ k) * tok_rows, tok_rows, 1)
            if k:
                part = swap(part.astype(bf16), "expert", k)
            part = part.astype(f32)
            total = part if total is None else total + part
        return total.reshape(home_rows, -1)

    home_routes = lax.dynamic_slice_in_dim(ffn_routes, col * tok_rows, tok_rows, 1)
    home_slots = route_slots(home_routes, expert_table)
    packs = []
    before = jnp.tril(jnp.ones((tok_rows, tok_rows), bf16), -1)
    for k in range(slots):
        hits = jnp.any(home_slots == (col ^ k), axis=-1)
        rank = jnp.einsum("ts,ms->mt", before, hits.astype(bf16), preferred_element_type=f32)
        packs.append(
            hits[:, None, :]
            & (rank[:, None, :] == jnp.arange(cap, dtype=jnp.int32).astype(f32)[None, :, None])
        )
    packs = jnp.stack(packs)
    packs_low = packs.astype(bf16)
    pack_rows = micro * cap
    sent_rows = slots * pack_rows

    def send_packed(value, lane=None):
        packed = jnp.einsum(
            "kmct,mtd->kmcd", packs_low, value.reshape(micro, tok_rows, -1), preferred_element_type=f32
        ).astype(bf16)
        if lane is not None:
            lanes = jnp.pad(lane[..., None], ((0, 0), (0, 0), (0, 0), (0, HDIM - 1)))
            packed = jnp.concatenate([packed, lanes.astype(bf16)], axis=-1)
        parts = [swap(packed[k], "expert", k) if k else packed[k] for k in range(slots)]
        return jnp.stack(parts).reshape(sent_rows, -1)

    def near_rows(value):
        return jnp.concatenate([value, swap(value, "dp", 1)], axis=0)

    def quad_sums(value):
        (own, near), (far, across) = value
        far_sum = far.astype(f32) + swap(across, "dp", 1).astype(f32)
        return own.astype(f32) + swap(near, "dp", 1).astype(f32), far_sum.astype(bf16)

    def return_packed(value, *others):
        shaped = value.astype(bf16).reshape(slots, micro, cap, -1)
        parts = [swap(shaped[k], "expert", k) if k else shaped[k] for k in range(slots)]
        return after(parts, *others)

    def unpack(packed, scale):
        total = None
        for k in range(slots):
            rows = jnp.einsum("mct,mcd->mtd", packs_low[k], packed[k], preferred_element_type=f32)
            rows = rows.reshape(home_rows, -1) * take(scale.T, col ^ k)[:, None]
            total = rows if total is None else total + rows
        return total

    gain_one = attn_gain.astype(f32)
    gain_two = ffn_gain.astype(f32)
    normed_one, scale_one = normalize(x_home)
    hidden_one_home = (normed_one * gain_one).astype(bf16)
    hidden_one_raw = gather_rows(hidden_one_home)
    hidden_one = after(hidden_one_raw, near_pieces[:3])
    grad_sent = send_packed(after(dy_home.astype(bf16), hidden_one))
    logits_one = dot(hidden_one, attn_router)
    gates_one, matches_one, chosen_one, gate_vals_one = route_gates(
        logits_one, attn_routes.reshape(all_rows, TOP), expert_table
    )
    hits_one = jnp.any(chosen_one, axis=1).astype(f32)

    def wide(value):
        return jnp.pad(value, ((0, 0), (0, HDIM - value.shape[1])))

    kv_part = dot(hidden_one, kv_full).astype(bf16)
    query_part = dot(hidden_one, query_full)
    lens = first_len[:, 0].astype(jnp.int32)
    gates_wide = wide(gates_one)
    attn_vals, gated_vals, query_rot, key_rot, log_total, peaks = attention_forward(
        lens, query_part, kv_part, tables, gates_wide, wide(hits_one), own_heads, group_rows
    )
    peaks = jnp.max(peaks, axis=0)[: own_heads * slots]
    attn_part = after(dot_t(gated_vals, out_full), keep_second, side_second)
    attn_home = after(scatter_rows(attn_part), first_lines)
    grad_sent = after(grad_sent, attn_home)
    grad_near, grad_far = near_rows(grad_sent), near_rows(swap(grad_sent, "dp", 2))

    resid = x_home + attn_home
    normed_two, scale_two = normalize(resid)
    hidden_two = (normed_two * gain_two).astype(bf16)
    logits_two = dot(hidden_two, ffn_router)
    gates_two, matches_two, chosen_two, gate_vals_two = route_gates(
        logits_two, home_routes.reshape(home_rows, TOP), expert_table
    )
    gates_by_slot = gates_two.reshape(micro, tok_rows, slots)
    gate_parts = []
    for k in range(slots):
        gate_col = lax.dynamic_index_in_dim(gates_by_slot, col ^ k, 2, keepdims=False)
        gate_parts.append(jnp.sum(jnp.where(packs[k], gate_col[:, None, :], 0.0), axis=-1))
    hidden_sent = after(
        send_packed(hidden_two, jnp.stack(gate_parts)), second_lines
    )
    hidden_near, hidden_far = near_rows(hidden_sent), swap(hidden_sent, "dp", 2)
    hidden_near = after(hidden_near, near_pieces, grad_near, grad_far)
    position = jnp.stack([core, chip]).astype(jnp.int32)
    near_results = expert_rows(
        position, hidden_near, after(grad_near, grad_far), own_pieces, near_pieces
    )
    hidden_far = near_rows(after(hidden_far, near_results))
    far_results = expert_rows(position, hidden_far, grad_far, own_pieces, near_pieces)
    ffn_parts = near_results[:2], far_results[:2]
    hidden_parts = near_results[2:4], far_results[2:4]
    actives, joint_grads = zip(near_results[4:], far_results[4:])

    def block_grads(steps, *others):
        rows = after((hidden_near, hidden_far, grad_near, grad_far), *others)
        return expert_grads([chip ^ k for k in steps], chip_rows, rows, joint_grads, actives)

    hidden_sum, hidden_far_sum = quad_sums(hidden_parts)
    ffn_sum, ffn_far_sum = quad_sums(ffn_parts)
    line_grads = block_grads([k ^ 1 for k in range(2, chips)], hidden_far_sum)
    side_got, keep_got = [[], []], [[], []]
    last = ()
    for which, got in enumerate((side_got, keep_got)):
        for part in range(2):
            for line in range(lines - 1):
                block = after(line_grads[4 * line + 2 * which + part], *last)
                got[part].append(swap(block, "dp", 4 * line + 4))
            last = got[part][-1:]
    hidden_got, ffn_far_sum, ffn_sum = lax.optimization_barrier(
        (swap(hidden_far_sum, "dp", 2), ffn_far_sum, ffn_sum, line_grads)
    )[:3]
    hidden_sum = hidden_sum + hidden_got.astype(f32)
    own_grads = block_grads([1, 0], hidden_sum)
    back_packed = return_packed(hidden_sum, *own_grads)
    ffn_sum = ffn_sum + swap(after(ffn_far_sum, hidden_got), "dp", 2).astype(f32)

    def total(own, got):
        return functools.reduce(jnp.add, [part.astype(f32) for part in [own] + got]).astype(bf16)

    slot_two_grad = jnp.zeros((slots, home_rows), f32)
    for k in range(slots):
        rows = jnp.sum(
            jnp.where(packs[k], back_packed[k][:, :, width].astype(f32)[:, :, None], 0.0), axis=1
        )
        slot_two_grad = lax.dynamic_update_index_in_dim(
            slot_two_grad, rows.reshape(home_rows), col ^ k, 0
        )
    hidden_two_grad = unpack([part[..., :width] for part in back_packed], gates_two)
    logit_two_grad = gate_back(slot_two_grad.T, gate_vals_two, matches_two, chosen_two).astype(bf16)
    hidden_two_grad = hidden_two_grad + dot_t(logit_two_grad, ffn_router)
    router_two_grad = t_dot(logit_two_grad, hidden_two)
    gain_two_grad = jnp.sum(hidden_two_grad * normed_two, axis=0)
    resid_grad = dy_home + norm_back(hidden_two_grad * gain_two, normed_two, scale_two)

    resid_grad_low = after(resid_grad.astype(bf16), *side_got[0])
    resid_grad_all = after(gather_rows(resid_grad_low), ffn_sum)
    out_part = t_dot(resid_grad_all, gated_vals).astype(bf16)
    vals_grad = after(dot(resid_grad_all, out_full), out_part, side_got[1])
    ffn_packed = return_packed(after(ffn_sum, vals_grad))
    out_home = (resid + unpack(ffn_packed, gates_two)).astype(bf16)
    query_grad, key_grad, value_grad, slot_part_one = attention_backward(
        lens, query_rot, key_rot, kv_part, attn_vals, vals_grad, tables, gates_wide, log_total,
        own_heads, group_rows,
    )
    query_grad, key_grad, value_grad, slot_part_one = lax.optimization_barrier(
        (query_grad, key_grad, value_grad, slot_part_one, ffn_packed)
    )[:4]
    kv_grad = jnp.concatenate([key_grad, value_grad], axis=1)
    side_own = after((own_grads[:2], side_got), query_grad)
    other_sums = [swap(total(*pair), "dp", 2) for pair in zip(*side_own)]
    hidden_one_part = dot_t(query_grad, query_full) + dot_t(kv_grad, kv_full)
    hidden_one_part = hidden_one_part.astype(bf16)
    joint_part_grad = t_dot(
        after(hidden_one, hidden_one_part), jnp.concatenate([query_grad, kv_grad], axis=1)
    ).astype(bf16)
    back_one = scatter_rows(
        jnp.concatenate([hidden_one_part, slot_part_one.astype(bf16)], axis=1)
    )
    back_one, keep_first_got = lax.optimization_barrier((back_one, keep_got[0], joint_part_grad))[:2]
    hidden_one_grad, slot_one_grad = back_one[:, :width], back_one[:, width : width + slots]

    def own(value):
        shaped = value.reshape((micro, group_rows) + value.shape[1:])
        part = lax.dynamic_slice_in_dim(shaped, col * tok_rows, tok_rows, 1)
        return part.reshape((home_rows,) + value.shape[1:])

    logit_one_grad = gate_back(
        slot_one_grad, own(gate_vals_one), own(matches_one), own(chosen_one)
    ).astype(bf16)
    hidden_one_grad = hidden_one_grad + dot_t(logit_one_grad, attn_router)
    router_one_grad = t_dot(logit_one_grad, hidden_one_home)
    gain_one_grad = jnp.sum(hidden_one_grad * normed_one, axis=0)
    in_home = resid_grad + norm_back(hidden_one_grad * gain_one, normed_one, scale_one)

    def reduced(value):
        return lax.psum_scatter(value, "dp", scatter_dimension=0, tiled=True)

    in_low = in_home.astype(bf16)
    out_grad = slots_of(after(reduced(out_part), in_low))
    joint_own = reduced(joint_part_grad)

    query_own, kv_own = joint_own[:, :query_width], joint_own[:, query_width:]
    results = jnp.stack([out_home, in_low]).reshape(2, micro, tok_rows, width)
    results = jnp.einsum("mtr,bmtd->bmrd", deal, results, preferred_element_type=f32).astype(bf16)
    results = results.reshape(2 * micro, dp_count, piece_rows, width).transpose(1, 0, 2, 3)
    results = results.reshape(dp_count, 2 * micro * piece_rows, width)
    sent_back = results.shape[1]
    small = jnp.concatenate(
        [gain_one_grad[None], gain_two_grad[None], router_one_grad, router_two_grad], axis=0
    ).astype(bf16)
    sum_rows = small.shape[0]
    peak_count = own_heads * slots
    peak_parts, rest = [], peaks
    for _ in range(3):
        peak_parts.append(lax.reduce_precision(rest, 8, 7))
        rest = rest - peak_parts[-1]
    peak_row = jnp.concatenate(peak_parts).astype(bf16)
    small = jnp.pad(small, ((0, -sum_rows % 16 or 16), (0, 0)))
    small = lax.dynamic_update_slice(small, peak_row[None], (sum_rows, 0))
    small = jnp.broadcast_to(small[None], (dp_count,) + small.shape)
    results = jnp.concatenate([results, small], axis=1)
    results = lax.all_to_all(results, "dp", split_axis=0, concat_axis=0, tiled=True)
    results, keep_last_got, other_sums, out_grad = lax.optimization_barrier(
        (results, keep_got[1], other_sums, out_grad)
    )
    small = results[:, sent_back:].astype(f32)
    results = results[:, :sent_back].reshape(dp_count, 2 * micro, piece_rows, width)
    results = results.transpose(1, 0, 2, 3).reshape(2, micro, tok_rows, width)
    peak_row = small[:, sum_rows, : 3 * peak_count].reshape(dp_count, 3, peak_count)
    peak_row = jnp.max((peak_row[:, 0] + peak_row[:, 1]) + peak_row[:, 2], axis=0)
    small = jnp.sum(small, axis=0)
    small = lax.dynamic_update_slice(small, peak_row[None], (sum_rows, 0))
    small = place(
        [swap(small, "expert", k) if k else small for k in range(slots)],
        [col ^ k for k in range(slots)],
    )
    sums = jnp.sum(small[:, :sum_rows], axis=0)
    peaks_all = small[:, sum_rows, :peak_count].reshape(slots, own_heads, slots)
    peaks_all = peaks_all.transpose(2, 0, 1).reshape(slots, HEADS)

    keep_parts = keep_first_got, keep_last_got
    keep_sums = [total(own_grads[2 + part], keep_parts[part]) for part in range(2)]
    by_rows = [jnp.stack([keep_sums[part], other_sums[part]]) for part in range(2)]
    own_pair = jnp.where(core == 0, by_rows[0], by_rows[1])
    near_pair = swap(jnp.where(core == 0, by_rows[1], by_rows[0]), "dp", 1)
    by_core = [jnp.where(core == 0, own_pair, near_pair), jnp.where(core == 0, near_pair, own_pair)]
    by_side = [[jnp.where(side == s, part[0], part[1]) for part in by_core] for s in range(2)]
    blocks = [part for row in by_side for part in row]
    gate_up_grad = jnp.concatenate(
        [b[:, :quarter] for b in blocks] + [b[:, quarter : 2 * quarter] for b in blocks], axis=1
    ).astype(f32)
    down_grad = jnp.concatenate([b[:, 2 * quarter :] for b in blocks], axis=1).astype(f32)

    out_grad = out_grad.astype(f32)
    query_out = slots_of(query_own).astype(f32)
    key_part, value_part = kv_own[:, :own_width], kv_own[:, own_width:]
    first_back = lax.ppermute(
        jnp.where(even_col, key_part, value_part), "expert", [(b, a) for a, b in first_pairs]
    )
    second_back = lax.ppermute(
        jnp.where(even_col, value_part, key_part), "expert", [(b, a) for a, b in second_pairs]
    )
    kv_out = jnp.concatenate(
        [
            jnp.where(holds_keys, first_back, second_back),
            jnp.where(holds_keys, second_back, first_back),
        ],
        axis=1,
    ).astype(f32)

    limit = clip_limit[0].astype(f32)
    factor = limit / jnp.maximum(peaks_all, limit)
    query_scale = jnp.repeat(jnp.sqrt(take(factor, col)), HDIM)
    query_clipped = (query_weight.astype(f32) * query_scale[None, None, :]).astype(bf16)
    full_scale = jnp.concatenate(
        [jnp.repeat(jnp.sqrt(jnp.min(factor, axis=0)), HDIM), jnp.ones((query_width,), f32)]
    )
    piece_width = kv_weight.shape[1]
    piece_scale = lax.dynamic_slice_in_dim(full_scale, col * piece_width, piece_width)
    kv_clipped = (kv_weight.astype(f32) * piece_scale[None, :]).astype(bf16)
    return (
        results[0],
        results[1],
        sums[0],
        sums[1],
        sums[2 : 2 + slots].T,
        sums[2 + slots : sum_rows].T,
        query_out[None],
        out_grad[None],
        kv_out,
        gate_up_grad[None],
        down_grad[None],
        query_clipped,
        kv_clipped,
    )


def solution(mesh):
    placed = (
        P(None, ("dp", "expert"), None),
        P(None, ("dp", "expert"), None),
        P(),
        P(None, ("dp", "expert")),
        P(None, "dp", None),
        P(None, "dp", None),
        P(),
        P(),
        P(),
        P(),
        P(),
        P(),
        P("expert", "dp", None),
        P("expert", "dp", None),
        P("dp", "expert"),
        P("expert", "dp", None),
        P("expert", "dp", None),
    )
    return jax.shard_map(
        local,
        mesh=mesh,
        in_specs=placed,
        out_specs=(
            P(None, ("dp", "expert"), None),
            P(None, ("dp", "expert"), None),
            P(),
            P(),
            P(),
            P(),
            P("expert", "dp", None),
            P("expert", "dp", None),
            P("dp", "expert"),
            P("expert", "dp", None),
            P("expert", "dp", None),
            P("expert", "dp", None),
            P("dp", "expert"),
        ),
        check_vma=False,
    )
```

```python
import functools

import jax
import jax.numpy as jnp
from jax import lax
from jax.experimental import pallas as pl
from jax.experimental.pallas import tpu as pltpu
from jax.sharding import PartitionSpec as P

HEADS = 16
HDIM = 128
FF = 5632
TOP = 2

eps_norm = 1e-06
rope_base = 10000.0
very_low = -1e30

f32 = jnp.float32
bf16 = jnp.bfloat16


def dot(left, right):
    return jnp.dot(left, right, preferred_element_type=f32)


def dot_t(left, right):
    return lax.dot_general(left, right, (((1,), (1,)), ((), ())), preferred_element_type=f32)


def t_dot(left, right):
    return lax.dot_general(left, right, (((0,), (0,)), ((), ())), preferred_element_type=f32)


def swap(value, axis, step):
    count = lax.axis_size(axis)
    return lax.ppermute(value, axis, [(i, i ^ step) for i in range(count)])


def take(stacked, index):
    return lax.dynamic_index_in_dim(stacked, index, 0, keepdims=False)


def place(parts, positions):
    out = jnp.zeros((len(parts),) + parts[0].shape, parts[0].dtype)
    for part, position in zip(parts, positions):
        out = lax.dynamic_update_index_in_dim(out, part, position, 0)
    return out


def after(value, *others):
    return lax.optimization_barrier((value, others))[0]


def rotation_tables(places):
    half_dim = HDIM // 2
    frequency = rope_base ** (-jnp.arange(half_dim, dtype=f32) * 2.0 / HDIM)
    angles = places.astype(f32)[:, None] * frequency[None, :]
    cosine, sine = jnp.cos(angles), jnp.sin(angles)
    return (
        jnp.concatenate([cosine, cosine], axis=1),
        jnp.concatenate([-sine, sine], axis=1),
    )


def turn(values, cosine, sine):
    return values * cosine + pltpu.roll(values, HDIM // 2, 1) * sine


def lane_value(table, lane):
    lanes = lax.broadcasted_iota(jnp.int32, table.shape, 1)
    return jnp.sum(jnp.where(lanes == lane, table, 0.0), axis=1, keepdims=True)


def allowed_pairs(rows, first_len):
    query_at = lax.broadcasted_iota(jnp.int32, (rows, rows), 0)
    key_at = lax.broadcasted_iota(jnp.int32, (rows, rows), 1)
    return (key_at <= query_at) & ((key_at >= first_len) | (query_at < first_len))


def forward_kernel(
    lens, query, key, value, cosine, sine, gates, hits,
    vals_out, gated_out, query_out, key_out, total_out, peak_out,
):
    m, h = pl.program_id(0), pl.program_id(1)
    heads = pl.num_programs(1)
    rows = query.shape[0]
    slots = query.shape[1] // (heads * HDIM)

    @pl.when(h == 0)
    def _():
        total_out[...] = jnp.zeros_like(total_out)
        peak_out[...] = jnp.full_like(peak_out, very_low)

    cos_part, sin_part = cosine[...], sine[...]
    allowed = allowed_pairs(rows, lens[m])
    keys = turn(key[...].astype(f32), cos_part, sin_part).astype(bf16)
    key_out[...] = keys
    values = value[...]
    lanes = lax.broadcasted_iota(jnp.int32, total_out.shape, 1)
    peak_lanes = lax.broadcasted_iota(jnp.int32, peak_out.shape, 1)
    totals, peaks = total_out[...], peak_out[...]
    for s in range(slots):
        columns = pl.ds(pl.multiple_of((s * heads + h) * HDIM, HDIM), HDIM)
        turned = turn(query[:, columns], cos_part, sin_part).astype(bf16)
        query_out[:, columns] = turned
        scores = jnp.where(allowed, dot_t(turned, keys) * HDIM ** (-0.5), very_low)
        row_peak = jnp.max(scores, axis=1, keepdims=True)
        expo = jnp.exp(scores - row_peak)
        denom = jnp.sum(expo, axis=1, keepdims=True)
        probs = expo * (1.0 / denom)
        vals = dot(probs.astype(bf16), values).astype(bf16)
        vals_out[:, columns] = vals
        gated_out[:, columns] = (gates[:, s : s + 1] * vals.astype(f32)).astype(bf16)
        lane = h * slots + s
        totals = jnp.where(lanes == lane, row_peak + jnp.log(denom), totals)
        seen = jnp.where(hits[:, s : s + 1] > 0.0, row_peak, very_low)
        peaks = jnp.where(peak_lanes == lane, jnp.max(seen, axis=0, keepdims=True), peaks)
    total_out[...] = totals
    peak_out[...] = peaks


def backward_kernel(
    lens, query, key, value, vals, vals_grad, cosine, sine, gates, total,
    query_grad, key_grad, value_grad, gate_grad,
):
    m, h = pl.program_id(0), pl.program_id(1)
    heads = pl.num_programs(1)
    rows = query.shape[0]
    slots = query.shape[1] // (heads * HDIM)

    @pl.when(h == 0)
    def _():
        gate_grad[...] = jnp.zeros_like(gate_grad)

    allowed = allowed_pairs(rows, lens[m])
    cos_part, back_sine = cosine[...], -sine[...]
    keys, values, totals = key[...], value[...], total[...]
    lanes = lax.broadcasted_iota(jnp.int32, gate_grad.shape, 1)
    slot_sums = gate_grad[...]
    key_sum = jnp.zeros(key.shape, f32)
    value_sum = jnp.zeros(value.shape, f32)
    for s in range(slots):
        columns = pl.ds(pl.multiple_of((s * heads + h) * HDIM, HDIM), HDIM)
        full_grad = vals_grad[:, columns]
        slot_sum = jnp.sum(vals[:, columns].astype(f32) * full_grad, axis=1, keepdims=True)
        slot_sums += jnp.where(lanes == s, slot_sum, 0.0)
        gated_grad = (gates[:, s : s + 1] * full_grad).astype(bf16)
        queries = query[:, columns]
        scores = jnp.where(allowed, dot_t(queries, keys) * HDIM ** (-0.5), very_low)
        probs = jnp.exp(scores - lane_value(totals, h * slots + s))
        prob_grad = dot_t(gated_grad, values)
        inner = jnp.sum(probs * prob_grad, axis=1, keepdims=True)
        score_grad = (probs * (prob_grad - inner) * HDIM ** (-0.5)).astype(bf16)
        query_grad[:, columns] = turn(dot(score_grad, keys), cos_part, back_sine).astype(bf16)
        key_sum += t_dot(score_grad, queries)
        value_sum += t_dot(probs.astype(bf16), gated_grad)
    gate_grad[...] = slot_sums
    key_grad[...] = turn(key_sum, cos_part, back_sine).astype(bf16)
    value_grad[...] = value_sum.astype(bf16)


def attention_specs(own_heads, rows, width):
    def block(columns, index):
        return pl.BlockSpec((rows, columns), index)

    return {
        "query": block(width, lambda m, h, lens: (m, 0)),
        "key": block(HDIM, lambda m, h, lens: (m, h)),
        "value": block(HDIM, lambda m, h, lens: (m, own_heads + h)),
        "rows": block(HDIM, lambda m, h, lens: (m, 0)),
        "peak": pl.BlockSpec((8, HDIM), lambda m, h, lens: (m, 0)),
    }


def attention_forward(lens, query, joint_kv, tables, gates, hits, own_heads, rows):
    micro = lens.shape[0]
    at = attention_specs(own_heads, rows, query.shape[1])
    shape = jax.ShapeDtypeStruct
    total_rows = micro * rows
    return pl.pallas_call(
        forward_kernel,
        grid_spec=pltpu.PrefetchScalarGridSpec(
            num_scalar_prefetch=1,
            grid=(micro, own_heads),
            in_specs=[at["query"], at["key"], at["value"]] + [at["rows"]] * 4,
            out_specs=[at["query"]] * 3 + [at["key"], at["rows"], at["peak"]],
        ),
        out_shape=[shape(query.shape, bf16)] * 3
        + [
            shape((total_rows, own_heads * HDIM), bf16),
            shape((total_rows, HDIM), f32),
            shape((micro * 8, HDIM), f32),
        ],
        compiler_params=pltpu.CompilerParams(vmem_limit_bytes=48 * 2**20),
        cost_estimate=pl.CostEstimate(
            flops=4 * rows * rows * HDIM * micro * HEADS,
            bytes_accessed=14 * query.size,
            transcendentals=rows * rows * micro * HEADS,
        ),
        name="attention_forward",
    )(lens, query, joint_kv, joint_kv, tables[0], tables[1], gates, hits)


def attention_backward(
    lens, query, key, joint_kv, vals, vals_grad, tables, gates, total, own_heads, rows
):
    micro = lens.shape[0]
    at = attention_specs(own_heads, rows, query.shape[1])
    shape = jax.ShapeDtypeStruct
    total_rows = micro * rows
    return pl.pallas_call(
        backward_kernel,
        grid_spec=pltpu.PrefetchScalarGridSpec(
            num_scalar_prefetch=1,
            grid=(micro, own_heads),
            in_specs=[at["query"], at["key"], at["value"], at["query"], at["query"]]
            + [at["rows"]] * 4,
            out_specs=[at["query"], at["key"], at["key"], at["rows"]],
        ),
        out_shape=[shape(query.shape, bf16)]
        + [shape((total_rows, own_heads * HDIM), bf16)] * 2
        + [shape((total_rows, HDIM), f32)],
        compiler_params=pltpu.CompilerParams(vmem_limit_bytes=48 * 2**20),
        cost_estimate=pl.CostEstimate(
            flops=10 * rows * rows * HDIM * micro * HEADS,
            bytes_accessed=14 * query.size,
            transcendentals=rows * rows * micro * HEADS,
        ),
        name="attention_backward",
    )(lens, query, key, joint_kv, vals, vals_grad, tables[0], tables[1], gates, total)


def normalize(values):
    row_scale = lax.rsqrt(jnp.mean(values * values, axis=-1, keepdims=True) + eps_norm)
    return values * row_scale, row_scale


def norm_back(grad_hat, normed, row_scale):
    return row_scale * (grad_hat - normed * jnp.mean(grad_hat * normed, axis=-1, keepdims=True))


def route_gates(logits, routes, expert_table):
    expert_ids = jnp.arange(expert_table.shape[0], dtype=jnp.int32)
    matches = routes[:, :, None] == expert_ids[None, None, :]
    picked = jnp.sum(jnp.where(matches, logits[:, None, :], 0.0), axis=-1)
    gate_vals = jax.nn.softmax(picked, axis=-1)
    slot_ids = route_slots(routes, expert_table)
    chosen = slot_ids[:, :, None] == expert_ids[None, None, :]
    gates = jnp.sum(jnp.where(chosen, gate_vals[:, :, None], 0.0), axis=1)
    return gates, matches, chosen, gate_vals


def route_slots(routes, expert_table):
    expert_ids = jnp.arange(expert_table.shape[0], dtype=jnp.int32)
    matches = routes[..., None] == expert_ids
    return jnp.sum(jnp.where(matches, expert_table, 0), axis=-1)


def gate_back(slot_grad, gate_vals, matches, chosen):
    picked = jnp.sum(jnp.where(chosen, slot_grad[:, None, :], 0.0), axis=-1)
    inner_sum = jnp.sum(gate_vals * picked, axis=-1, keepdims=True)
    picked_grad = gate_vals * (picked - inner_sum)
    return jnp.sum(jnp.where(matches, picked_grad[:, :, None], 0.0), axis=1)


def unit_blocks(count):
    return [(start, min(512, count - start)) for start in range(0, count, 512)]


def expert_kernel(place_ref, hidden, grad, *refs):
    piece_count = (len(refs) - 6) // 2
    own_pieces, near_pieces = refs[:piece_count], refs[piece_count : 2 * piece_count]
    out, hidden_out, act_out, joint_out, weights, sems = refs[2 * piece_count :]
    core, chip = place_ref[0], place_ref[1]
    rows, columns = near_pieces[0].shape
    units = columns // 3
    width = grad.shape[1]

    @pl.when(pl.program_id(0) == 0)
    def _():
        copies = []
        for k in range(piece_count):
            base = (chip ^ k) * (2 * rows)
            for number, (piece, part) in enumerate(
                ((own_pieces[k], core), (near_pieces[k], 1 - core))
            ):
                start = pl.multiple_of(base + part * rows, 16)
                copies.append(
                    pltpu.make_async_copy(
                        piece, weights.at[pl.ds(start, rows)], sems.at[2 * k + number]
                    )
                )
        for copy in copies:
            copy.start()
        for copy in copies:
            copy.wait()

    slot_sum = jnp.zeros((hidden.shape[0], 1), f32)
    for start, size in unit_blocks(units):
        gate_pre = dot(hidden[:, :width], weights[:, start : start + size])
        up_pre = dot(hidden[:, :width], weights[:, units + start : units + start + size])
        act_grad = dot(grad[...], weights[:, 2 * units + start : 2 * units + start + size])
        sigma = 1.0 / (1.0 + jnp.exp(-gate_pre))
        silu_vals = gate_pre * sigma
        active = (silu_vals * up_pre).astype(bf16)
        act_out[:, start : start + size] = active
        slot_sum += jnp.sum(active.astype(f32) * act_grad, axis=1, keepdims=True)
        gate_grad = act_grad * up_pre * sigma * (1.0 + gate_pre * (1.0 - sigma))
        joint_out[:, start : start + size] = gate_grad.astype(bf16)
        joint_out[:, units + start : units + start + size] = (act_grad * silu_vals).astype(bf16)
    for start in range(0, width, 512):
        block = weights[start : start + 512, : 2 * units]
        hidden_out[:, start : start + 512] = dot_t(joint_out[...], block).astype(bf16)
        block = weights[start : start + 512, 2 * units :]
        out[:, start : start + 512] = dot_t(act_out[...], block).astype(bf16)
    lanes = lax.broadcasted_iota(jnp.int32, (hidden.shape[0], HDIM), 1)
    hidden_out[:, width:] = jnp.where(lanes == 0, slot_sum, 0.0).astype(bf16)


def expert_rows(position, hidden, grad, own_pieces, near_pieces):
    rows, width = grad.shape
    columns = near_pieces[0].shape[1]
    units = columns // 3
    tile = rows // 2
    shape = jax.ShapeDtypeStruct
    count = len(own_pieces)

    def tiled(size):
        return pl.BlockSpec((tile, size), lambda i, at: (i, 0))

    return pl.pallas_call(
        expert_kernel,
        grid_spec=pltpu.PrefetchScalarGridSpec(
            num_scalar_prefetch=1,
            grid=(rows // tile,),
            in_specs=[tiled(width + HDIM), tiled(width)]
            + [pl.BlockSpec(memory_space=pl.ANY)] * (2 * count),
            out_specs=[tiled(width), tiled(width + HDIM), tiled(units), tiled(2 * units)],
            scratch_shapes=[
                pltpu.VMEM((width, columns), bf16),
                pltpu.SemaphoreType.DMA((2 * count,)),
            ],
        ),
        out_shape=[
            shape((rows, width), bf16),
            shape((rows, width + HDIM), bf16),
            shape((rows, units), bf16),
            shape((rows, 2 * units), bf16),
        ],
        compiler_params=pltpu.CompilerParams(vmem_limit_bytes=56 * 2**20),
        cost_estimate=pl.CostEstimate(
            flops=4 * rows * width * columns,
            bytes_accessed=2 * (width * columns + 6 * rows * width),
            transcendentals=rows * units,
        ),
        name="expert_rows",
    )(position, hidden, grad, *own_pieces, *near_pieces)


def expert_grad_kernel(cuts, order, *refs):
    hidden, grad, gates, joint, active = [refs[2 * n : 2 * n + 2] for n in range(5)]
    outs = refs[10:]
    units = active[0].shape[1]

    def scaled(blocks):
        return [
            (block[...].astype(f32) * gate[:, :1].astype(f32)).astype(bf16)
            for block, gate in zip(blocks, gates)
        ]

    left, right = scaled(hidden), scaled(grad)
    step = pl.program_id(0)
    first = [0]
    for cut in cuts:
        first.append(first[-1] + cut)
    for out, start, cut in zip(outs, first, cuts):

        @pl.when((step >= start) & (step < start + cut))
        def _():
            for start, size in unit_blocks(2 * units):
                out[:, start : start + size] = sum(
                    t_dot(rows, part[:, start : start + size]) for rows, part in zip(left, joint)
                ).astype(bf16)
            for start, size in unit_blocks(units):
                out[:, 2 * units + start : 2 * units + start + size] = sum(
                    t_dot(rows, part[:, start : start + size]) for rows, part in zip(right, active)
                ).astype(bf16)


def expert_grads(chunks, cuts, chunk_rows, rows_of, joints, actives):
    hidden, grad = rows_of[:2], rows_of[2:]
    rows, units = actives[0].shape
    width = grad[0].shape[1]
    half = chunk_rows // 2
    count = len(chunks)
    order = jnp.stack([2 * chunk + part for chunk in chunks for part in range(2)]).astype(jnp.int32)

    def whole(size, column=0):
        return pl.BlockSpec(
            (rows, size), lambda i, at: (0, column), pipeline_mode=pl.Buffered(1)
        )

    column = pl.BlockSpec((rows, half), lambda i, at: (0, at[i]))
    return pl.pallas_call(
        functools.partial(expert_grad_kernel, cuts),
        grid_spec=pltpu.PrefetchScalarGridSpec(
            num_scalar_prefetch=1,
            grid=(2 * count,),
            in_specs=[column] * 4
            + [whole(HDIM, width // HDIM)] * 2
            + [whole(2 * units)] * 2
            + [whole(units)] * 2,
            out_specs=[
                pl.BlockSpec(
                    (half, 3 * units),
                    lambda i, at, start=sum(cuts[:n]), cut=cut: (jnp.clip(i - start, 0, cut - 1), 0),
                )
                for n, cut in enumerate(cuts)
            ],
        ),
        out_shape=[jax.ShapeDtypeStruct((cut * half, 3 * units), bf16) for cut in cuts],
        compiler_params=pltpu.CompilerParams(vmem_limit_bytes=56 * 2**20),
        cost_estimate=pl.CostEstimate(
            flops=4 * count * chunk_rows * rows * 3 * units,
            bytes_accessed=2 * (rows * 6 * units + count * chunk_rows * (4 * rows + 3 * units)),
            transcendentals=0,
        ),
        name="expert_grads",
    )(order, *hidden, *grad, *hidden, *joints, *actives)


def local(
    tokens,
    cotangent,
    seq_lengths,
    dealing,
    attn_routes,
    ffn_routes,
    expert_table,
    clip_limit,
    attn_gain,
    ffn_gain,
    attn_router,
    ffn_router,
    query_weight,
    attn_out_weight,
    kv_weight,
    gate_up_weight,
    down_weight,
):
    micro, tok_rows, width = tokens.shape
    dp_count = lax.axis_size("dp")
    slots = lax.axis_size("expert")
    col = lax.axis_index("expert")
    group = lax.axis_index("dp")
    piece_rows = tok_rows // dp_count
    cap = tok_rows * TOP * 3 // (2 * slots)
    group_rows = tok_rows * slots
    all_rows = micro * group_rows
    home_rows = micro * tok_rows
    query_width = HEADS * HDIM
    own_heads = HEADS // slots
    own_width = own_heads * HDIM
    shard_rows = query_weight.shape[1]
    score_scale = HDIM ** (-0.5)
    core = group % 2
    chip = group // 2
    side = chip % 2
    chips = dp_count // 2
    lines = chips // 2
    quarter = FF // 4
    chip_rows = 2 * shard_rows

    both = jnp.stack([tokens, cotangent]).reshape(2 * micro, dp_count, piece_rows, width)
    both = lax.all_to_all(both.transpose(1, 0, 2, 3), "dp", split_axis=0, concat_axis=0, tiled=True)
    def quarter_of(half, part):
        start = (2 * half + part) * quarter
        return jnp.concatenate(
            [
                lax.dynamic_slice_in_dim(gate_up_weight[0], start, quarter, 1),
                lax.dynamic_slice_in_dim(gate_up_weight[0], FF + start, quarter, 1),
                lax.dynamic_slice_in_dim(down_weight[0], start, quarter, 1),
            ],
            axis=1,
        )

    parts = (1 - core, core)
    keep_pair = [quarter_of(side, part) for part in parts]
    send_pair = [quarter_of(1 - side, part) for part in parts]
    both = both.transpose(1, 0, 2, 3).reshape(2, micro, tok_rows, width)
    deal = (dealing[:, :, None] == jnp.arange(tok_rows, dtype=jnp.int32)).astype(bf16)
    work = jnp.einsum("mtr,bmrd->bmtd", deal, both, preferred_element_type=f32)
    x_home = work[0].reshape(home_rows, width)
    dy_home = work[1].reshape(home_rows, width)

    def columns_of(*shards):
        pieces = [shard.reshape(shard_rows, slots, own_width) for shard in shards]
        out = jnp.zeros((shard_rows, len(shards) * query_width), shards[0].dtype)
        for k in range(slots):
            part = jnp.concatenate(
                [lax.dynamic_index_in_dim(piece, col ^ k, 1, keepdims=False) for piece in pieces],
                axis=1,
            )
            part = swap(part, "expert", k) if k else part
            for number in range(len(shards)):
                out = lax.dynamic_update_slice_in_dim(
                    out,
                    part[:, number * own_width : (number + 1) * own_width],
                    number * query_width + (col ^ k) * own_width,
                    1,
                )
        return out

    def slots_of(columns):
        pieces = columns.reshape(shard_rows, slots, own_width)
        out = jnp.zeros((shard_rows, query_width), columns.dtype)
        for k in range(slots):
            part = lax.dynamic_index_in_dim(pieces, col ^ k, 1, keepdims=False)
            part = swap(part, "expert", k) if k else part
            out = lax.dynamic_update_slice_in_dim(out, part, (col ^ k) * own_width, 1)
        return out

    half_slots = slots // 2
    first_pairs = [(c, 2 * c) for c in range(half_slots)]
    first_pairs += [(c, 2 * (c - half_slots) + 1) for c in range(half_slots, slots)]
    second_pairs = [(c, 2 * c + 1) for c in range(half_slots)]
    second_pairs += [(c, 2 * (c - half_slots)) for c in range(half_slots, slots)]
    holds_keys = col < half_slots
    even_col = col % 2 == 0
    low_kv, high_kv = kv_weight[:, :own_width], kv_weight[:, own_width:]
    first_got = lax.ppermute(jnp.where(holds_keys, low_kv, high_kv), "expert", first_pairs)
    second_got = lax.ppermute(jnp.where(holds_keys, high_kv, low_kv), "expert", second_pairs)
    own_kv = jnp.concatenate(
        [
            jnp.where(even_col, first_got, second_got),
            jnp.where(even_col, second_got, first_got),
        ],
        axis=1,
    )
    line_steps = [4 * line for line in range(1, lines)]
    side_first = swap(send_pair[0], "dp", 2)
    keep_first = [swap(keep_pair[0], "dp", step) for step in line_steps]
    joint_own = columns_of(query_weight[0], attn_out_weight[0])
    first_own = jnp.concatenate([joint_own[:, :query_width], own_kv], axis=1)
    first_own, second_own = lax.optimization_barrier(
        (first_own, joint_own[:, query_width:], side_first, keep_first)
    )[:2]
    joint_full = lax.all_gather(first_own, "dp", axis=0, tiled=True)
    out_full = lax.all_gather(second_own, "dp", axis=0, tiled=True)
    late_pair = after((keep_pair[1], send_pair[1], side_first), joint_full)
    keep_second = [swap(late_pair[0], "dp", step) for step in line_steps]
    side_second = swap(late_pair[1], "dp", 2)
    first_lines = [swap(after(late_pair[2], out_full), "dp", step) for step in line_steps]
    second_lines = [swap(side_second, "dp", step) for step in line_steps]
    firsts, seconds = [keep_pair[0], side_first], [keep_pair[1], side_second]
    for line in range(lines - 1):
        firsts += [keep_first[line], first_lines[line]]
        seconds += [keep_second[line], second_lines[line]]
    near_pieces = [swap(piece, "dp", 1) for piece in firsts]
    own_pieces = seconds
    query_full = joint_full[:, :query_width]
    kv_full = joint_full[:, query_width:]

    positions = jnp.arange(group_rows, dtype=jnp.int32)
    first_len = lax.dynamic_index_in_dim(seq_lengths[:, :, 0], group, 1, keepdims=True)
    in_second = positions[None, :] >= first_len
    places = positions[None, :] - jnp.where(in_second, first_len, 0)
    tables = rotation_tables(places.reshape(all_rows))

    def gather_rows(value):
        shaped = value.reshape(micro, tok_rows, -1)
        out = jnp.zeros((micro, group_rows, shaped.shape[-1]), value.dtype)
        for k in range(slots):
            part = swap(shaped, "expert", k) if k else shaped
            out = lax.dynamic_update_slice_in_dim(out, part, (col ^ k) * tok_rows, 1)
        return out.reshape(all_rows, -1)

    def scatter_rows(value):
        shaped = value.reshape(micro, group_rows, -1)
        total = None
        for k in range(slots):
            part = lax.dynamic_slice_in_dim(shaped, (col ^ k) * tok_rows, tok_rows, 1)
            if k:
                part = swap(part.astype(bf16), "expert", k)
            part = part.astype(f32)
            total = part if total is None else total + part
        return total.reshape(home_rows, -1)

    home_routes = lax.dynamic_slice_in_dim(ffn_routes, col * tok_rows, tok_rows, 1)
    home_slots = route_slots(home_routes, expert_table)
    packs = []
    before = jnp.tril(jnp.ones((tok_rows, tok_rows), bf16), -1)
    for k in range(slots):
        hits = jnp.any(home_slots == (col ^ k), axis=-1)
        rank = jnp.einsum("ts,ms->mt", before, hits.astype(bf16), preferred_element_type=f32)
        packs.append(
            hits[:, None, :]
            & (rank[:, None, :] == jnp.arange(cap, dtype=jnp.int32).astype(f32)[None, :, None])
        )
    packs = jnp.stack(packs)
    packs_low = packs.astype(bf16)
    pack_rows = micro * cap
    sent_rows = slots * pack_rows

    def send_packed(value, lane=None):
        packed = jnp.einsum(
            "kmct,mtd->kmcd", packs_low, value.reshape(micro, tok_rows, -1), preferred_element_type=f32
        ).astype(bf16)
        if lane is not None:
            lanes = jnp.pad(lane[..., None], ((0, 0), (0, 0), (0, 0), (0, HDIM - 1)))
            packed = jnp.concatenate([packed, lanes.astype(bf16)], axis=-1)
        parts = [swap(packed[k], "expert", k) if k else packed[k] for k in range(slots)]
        return jnp.stack(parts).reshape(sent_rows, -1)

    def near_rows(value):
        return jnp.concatenate([value, swap(value, "dp", 1)], axis=0)

    def quad_sums(value):
        (own, near), (far, across) = [jnp.split(half, 2, axis=0) for half in value]
        far_sum = far.astype(f32) + swap(across, "dp", 1).astype(f32)
        return own.astype(f32) + swap(near, "dp", 1).astype(f32), far_sum.astype(bf16)

    def return_packed(value, *others):
        shaped = value.astype(bf16).reshape(slots, micro, cap, -1)
        parts = [swap(shaped[k], "expert", k) if k else shaped[k] for k in range(slots)]
        return after(parts, *others)

    def unpack(packed, scale):
        total = None
        for k in range(slots):
            rows = jnp.einsum("mct,mcd->mtd", packs_low[k], packed[k], preferred_element_type=f32)
            rows = rows.reshape(home_rows, -1) * take(scale.T, col ^ k)[:, None]
            total = rows if total is None else total + rows
        return total

    gain_one = attn_gain.astype(f32)
    gain_two = ffn_gain.astype(f32)
    normed_one, scale_one = normalize(x_home)
    hidden_one_home = (normed_one * gain_one).astype(bf16)
    hidden_one_raw = gather_rows(after(hidden_one_home, near_pieces[:3]))
    hidden_one = hidden_one_raw
    grad_sent = send_packed(after(dy_home.astype(bf16), hidden_one))
    logits_one = dot(hidden_one, attn_router)
    gates_one, matches_one, chosen_one, gate_vals_one = route_gates(
        logits_one, attn_routes.reshape(all_rows, TOP), expert_table
    )
    hits_one = jnp.any(chosen_one, axis=1).astype(f32)

    def wide(value):
        return jnp.pad(value, ((0, 0), (0, HDIM - value.shape[1])))

    kv_part = dot(hidden_one, kv_full).astype(bf16)
    query_part = dot(hidden_one, query_full)
    lens = first_len[:, 0].astype(jnp.int32)
    gates_wide = wide(gates_one)
    attn_vals, gated_vals, query_rot, key_rot, log_total, peaks = attention_forward(
        lens, query_part, kv_part, tables, gates_wide, wide(hits_one), own_heads, group_rows
    )
    peaks = jnp.max(peaks, axis=0)[: own_heads * slots]
    attn_part = after(dot_t(gated_vals, out_full), keep_second, side_second)
    attn_home = after(scatter_rows(attn_part), first_lines)
    grad_sent = after(grad_sent, attn_home)
    grad_near, grad_far = near_rows(grad_sent), near_rows(swap(grad_sent, "dp", 2))

    resid = x_home + attn_home
    normed_two, scale_two = normalize(resid)
    hidden_two = (normed_two * gain_two).astype(bf16)
    logits_two = dot(hidden_two, ffn_router)
    gates_two, matches_two, chosen_two, gate_vals_two = route_gates(
        logits_two, home_routes.reshape(home_rows, TOP), expert_table
    )
    gates_by_slot = gates_two.reshape(micro, tok_rows, slots)
    gate_parts = []
    for k in range(slots):
        gate_col = lax.dynamic_index_in_dim(gates_by_slot, col ^ k, 2, keepdims=False)
        gate_parts.append(jnp.sum(jnp.where(packs[k], gate_col[:, None, :], 0.0), axis=-1))
    hidden_sent = after(
        send_packed(hidden_two, jnp.stack(gate_parts)), second_lines
    )
    hidden_near, hidden_far = near_rows(hidden_sent), swap(hidden_sent, "dp", 2)
    hidden_near = after(hidden_near, near_pieces, grad_near, grad_far)
    position = jnp.stack([core, chip]).astype(jnp.int32)
    near_results = expert_rows(
        position, hidden_near, after(grad_near, grad_far), own_pieces, near_pieces
    )
    hidden_far = near_rows(after(hidden_far, near_results))
    far_results = expert_rows(position, hidden_far, grad_far, own_pieces, near_pieces)
    ffn_parts, hidden_parts, actives, joint_grads = zip(near_results, far_results)

    def block_grads(steps, *others):
        rows = after((hidden_near, hidden_far, grad_near, grad_far), *others)
        cuts = (2, 1, 1) * (len(steps) // 2)
        return expert_grads([chip ^ k for k in steps], cuts, chip_rows, rows, joint_grads, actives)

    hidden_sum, hidden_far_sum = quad_sums(hidden_parts)
    ffn_sum, ffn_far_sum = quad_sums(ffn_parts)
    line_grads = block_grads([k ^ 1 for k in range(2, chips)], hidden_far_sum)
    side_got = [swap(line_grads[3 * line], "dp", step) for line, step in enumerate(line_steps)]
    keep_got = []
    for part in range(2):
        blocks = after(line_grads[part + 1 :: 3], side_got, keep_got)
        keep_got.append([swap(block, "dp", step) for block, step in zip(blocks, line_steps)])
    hidden_got, ffn_far_sum, ffn_sum = lax.optimization_barrier(
        (swap(hidden_far_sum, "dp", 2), ffn_far_sum, ffn_sum, line_grads)
    )[:3]
    hidden_sum = hidden_sum + hidden_got.astype(f32)
    own_grads = block_grads([1, 0], hidden_sum)
    back_packed = return_packed(hidden_sum, *own_grads)
    ffn_sum = ffn_sum + swap(after(ffn_far_sum, back_packed), "dp", 2).astype(f32)

    def total(own, got):
        return functools.reduce(jnp.add, [part.astype(f32) for part in [own] + got]).astype(bf16)

    slot_two_grad = jnp.zeros((slots, home_rows), f32)
    for k in range(slots):
        rows = jnp.sum(
            jnp.where(packs[k], back_packed[k][:, :, width].astype(f32)[:, :, None], 0.0), axis=1
        )
        slot_two_grad = lax.dynamic_update_index_in_dim(
            slot_two_grad, rows.reshape(home_rows), col ^ k, 0
        )
    hidden_two_grad = unpack([part[..., :width] for part in back_packed], gates_two)
    logit_two_grad = gate_back(slot_two_grad.T, gate_vals_two, matches_two, chosen_two).astype(bf16)
    hidden_two_grad = hidden_two_grad + dot_t(logit_two_grad, ffn_router)
    router_two_grad = t_dot(logit_two_grad, hidden_two)
    gain_two_grad = jnp.sum(hidden_two_grad * normed_two, axis=0)
    resid_grad = dy_home + norm_back(hidden_two_grad * gain_two, normed_two, scale_two)

    resid_grad_all = after(gather_rows(resid_grad.astype(bf16)), side_got)
    out_part = t_dot(resid_grad_all, gated_vals).astype(bf16)
    vals_grad = after(dot(resid_grad_all, out_full), out_part)
    side_own = after((own_grads[0], side_got), vals_grad)
    vals_grad, side_sum = lax.optimization_barrier((vals_grad, total(*side_own)))
    other_sum = swap(side_sum, "dp", 2)
    ffn_packed = return_packed(after(ffn_sum, vals_grad))
    out_home = (resid + unpack(ffn_packed, gates_two)).astype(bf16)
    query_grad, key_grad, value_grad, slot_part_one = attention_backward(
        lens, query_rot, key_rot, kv_part, attn_vals, vals_grad, tables, gates_wide, log_total,
        own_heads, group_rows,
    )
    query_grad, key_grad, value_grad, slot_part_one = lax.optimization_barrier(
        (query_grad, key_grad, value_grad, slot_part_one, ffn_packed, keep_got[0])
    )[:4]
    kv_grad = jnp.concatenate([key_grad, value_grad], axis=1)
    hidden_one_part = dot_t(query_grad, query_full) + dot_t(kv_grad, kv_full)
    hidden_one_part = hidden_one_part.astype(bf16)
    joint_part_grad = t_dot(
        after(hidden_one, hidden_one_part), jnp.concatenate([query_grad, kv_grad], axis=1)
    ).astype(bf16)
    back_one = scatter_rows(
        jnp.concatenate([hidden_one_part, slot_part_one.astype(bf16)], axis=1)
    )
    back_one, keep_got = lax.optimization_barrier((back_one, keep_got, joint_part_grad))[:2]
    hidden_one_grad, slot_one_grad = back_one[:, :width], back_one[:, width : width + slots]

    def own(value):
        shaped = value.reshape((micro, group_rows) + value.shape[1:])
        part = lax.dynamic_slice_in_dim(shaped, col * tok_rows, tok_rows, 1)
        return part.reshape((home_rows,) + value.shape[1:])

    logit_one_grad = gate_back(
        slot_one_grad, own(gate_vals_one), own(matches_one), own(chosen_one)
    ).astype(bf16)
    hidden_one_grad = hidden_one_grad + dot_t(logit_one_grad, attn_router)
    router_one_grad = t_dot(logit_one_grad, hidden_one_home)
    gain_one_grad = jnp.sum(hidden_one_grad * normed_one, axis=0)
    in_home = resid_grad + norm_back(hidden_one_grad * gain_one, normed_one, scale_one)

    def reduced(value):
        return lax.psum_scatter(value, "dp", scatter_dimension=0, tiled=True)

    in_low = in_home.astype(bf16)
    out_grad = slots_of(after(reduced(out_part), in_low))
    joint_own = reduced(joint_part_grad)

    results = jnp.stack([out_home, in_low]).reshape(2, micro, tok_rows, width)
    results = jnp.einsum("mtr,bmtd->bmrd", deal, results, preferred_element_type=f32).astype(bf16)
    results = results.reshape(2 * micro, dp_count, piece_rows, width).transpose(1, 0, 2, 3)
    results = results.reshape(dp_count, 2 * micro * piece_rows, width)
    sent_back = results.shape[1]
    small = jnp.concatenate(
        [gain_one_grad[None], gain_two_grad[None], router_one_grad, router_two_grad], axis=0
    ).astype(bf16)
    sum_rows = small.shape[0]
    peak_count = own_heads * slots
    peak_parts, rest = [], peaks
    for _ in range(3):
        peak_parts.append(lax.reduce_precision(rest, 8, 7))
        rest = rest - peak_parts[-1]
    peak_row = jnp.concatenate(peak_parts).astype(bf16)
    small = jnp.pad(small, ((0, -sum_rows % 16 or 16), (0, 0)))
    small = lax.dynamic_update_slice(small, peak_row[None], (sum_rows, 0))
    small = jnp.broadcast_to(small[None], (dp_count,) + small.shape)
    results = jnp.concatenate([results, small], axis=1)
    results = lax.all_to_all(results, "dp", split_axis=0, concat_axis=0, tiled=True)
    results, keep_got, other_sum, out_grad, joint_own = lax.optimization_barrier(
        (results, keep_got, other_sum, out_grad, joint_own)
    )
    query_own, kv_own = joint_own[:, :query_width], joint_own[:, query_width:]
    small = results[:, sent_back:].astype(f32)
    results = results[:, :sent_back].reshape(dp_count, 2 * micro, piece_rows, width)
    results = results.transpose(1, 0, 2, 3).reshape(2, micro, tok_rows, width)
    peak_row = small[:, sum_rows, : 3 * peak_count].reshape(dp_count, 3, peak_count)
    peak_row = jnp.max((peak_row[:, 0] + peak_row[:, 1]) + peak_row[:, 2], axis=0)
    small = jnp.sum(small, axis=0)
    small = lax.dynamic_update_slice(small, peak_row[None], (sum_rows, 0))
    smalls = [swap(small, "expert", k) if k else small for k in range(slots)]
    peaks_all = jnp.zeros((slots, HEADS), f32)
    for k, part in enumerate(smalls):
        part = part[sum_rows, :peak_count].reshape(own_heads, slots).T
        peaks_all = lax.dynamic_update_slice(peaks_all, part, (0, (col ^ k) * own_heads))
    while len(smalls) > 1:
        smalls = [left + right for left, right in zip(smalls[::2], smalls[1::2])]
    sums = smalls[0][:sum_rows]

    keep_sums = [total(own_grads[1 + part], keep_got[part]) for part in range(2)]
    other_sums = other_sum.reshape(2, shard_rows, 3 * quarter)
    by_rows = [jnp.stack([keep_sums[part], other_sums[part]]) for part in range(2)]
    own_pair = jnp.where(core == 0, by_rows[0], by_rows[1])
    near_pair = swap(jnp.where(core == 0, by_rows[1], by_rows[0]), "dp", 1)
    by_core = [jnp.where(core == 0, own_pair, near_pair), jnp.where(core == 0, near_pair, own_pair)]
    by_side = [[jnp.where(side == s, part[0], part[1]) for part in by_core] for s in range(2)]
    blocks = [part for row in by_side for part in row]
    gate_up_grad = jnp.concatenate(
        [b[:, :quarter] for b in blocks] + [b[:, quarter : 2 * quarter] for b in blocks], axis=1
    ).astype(f32)
    down_grad = jnp.concatenate([b[:, 2 * quarter :] for b in blocks], axis=1).astype(f32)

    out_grad = out_grad.astype(f32)
    query_out = slots_of(query_own).astype(f32)
    key_part, value_part = kv_own[:, :own_width], kv_own[:, own_width:]
    first_back = lax.ppermute(
        jnp.where(even_col, key_part, value_part), "expert", [(b, a) for a, b in first_pairs]
    )
    second_back = lax.ppermute(
        jnp.where(even_col, value_part, key_part), "expert", [(b, a) for a, b in second_pairs]
    )
    kv_out = jnp.concatenate(
        [
            jnp.where(holds_keys, first_back, second_back),
            jnp.where(holds_keys, second_back, first_back),
        ],
        axis=1,
    ).astype(f32)

    limit = clip_limit[0].astype(f32)
    factor = limit / jnp.maximum(peaks_all, limit)
    query_scale = jnp.repeat(jnp.sqrt(take(factor, col)), HDIM)
    query_clipped = (query_weight.astype(f32) * query_scale[None, None, :]).astype(bf16)
    full_scale = jnp.concatenate(
        [jnp.repeat(jnp.sqrt(jnp.min(factor, axis=0)), HDIM), jnp.ones((query_width,), f32)]
    )
    piece_width = kv_weight.shape[1]
    piece_scale = lax.dynamic_slice_in_dim(full_scale, col * piece_width, piece_width)
    kv_clipped = (kv_weight.astype(f32) * piece_scale[None, :]).astype(bf16)
    return (
        results[0],
        results[1],
        sums[0],
        sums[1],
        sums[2 : 2 + slots].T,
        sums[2 + slots : sum_rows].T,
        query_out[None],
        out_grad[None],
        kv_out,
        gate_up_grad[None],
        down_grad[None],
        query_clipped,
        kv_clipped,
    )


def solution(mesh):
    placed = (
        P(None, ("dp", "expert"), None),
        P(None, ("dp", "expert"), None),
        P(),
        P(None, ("dp", "expert")),
        P(None, "dp", None),
        P(None, "dp", None),
        P(),
        P(),
        P(),
        P(),
        P(),
        P(),
        P("expert", "dp", None),
        P("expert", "dp", None),
        P("dp", "expert"),
        P("expert", "dp", None),
        P("expert", "dp", None),
    )
    return jax.shard_map(
        local,
        mesh=mesh,
        in_specs=placed,
        out_specs=(
            P(None, ("dp", "expert"), None),
            P(None, ("dp", "expert"), None),
            P(),
            P(),
            P(),
            P(),
            P("expert", "dp", None),
            P("expert", "dp", None),
            P("dp", "expert"),
            P("expert", "dp", None),
            P("expert", "dp", None),
            P("expert", "dp", None),
            P("dp", "expert"),
        ),
        check_vma=False,
    )
```

```python
import functools

import jax
import jax.numpy as jnp
from jax import lax
from jax.experimental import pallas as pl
from jax.experimental.pallas import tpu as pltpu
from jax.sharding import PartitionSpec as P

HEADS = 16
HDIM = 128
FF = 5632
TOP = 2

eps_norm = 1e-06
rope_base = 10000.0
very_low = -1e30

f32 = jnp.float32
bf16 = jnp.bfloat16


def dot(left, right):
    return jnp.dot(left, right, preferred_element_type=f32)


def dot_t(left, right):
    return lax.dot_general(left, right, (((1,), (1,)), ((), ())), preferred_element_type=f32)


def t_dot(left, right):
    return lax.dot_general(left, right, (((0,), (0,)), ((), ())), preferred_element_type=f32)


def swap(value, axis, step):
    count = lax.axis_size(axis)
    return lax.ppermute(value, axis, [(i, i ^ step) for i in range(count)])


def take(stacked, index):
    return lax.dynamic_index_in_dim(stacked, index, 0, keepdims=False)


def place(parts, positions):
    out = jnp.zeros((len(parts),) + parts[0].shape, parts[0].dtype)
    for part, position in zip(parts, positions):
        out = lax.dynamic_update_index_in_dim(out, part, position, 0)
    return out


def after(value, *others):
    return lax.optimization_barrier((value, others))[0]


def rotation_tables(places):
    half_dim = HDIM // 2
    frequency = rope_base ** (-jnp.arange(half_dim, dtype=f32) * 2.0 / HDIM)
    angles = places.astype(f32)[:, None] * frequency[None, :]
    cosine, sine = jnp.cos(angles), jnp.sin(angles)
    return (
        jnp.concatenate([cosine, cosine], axis=1),
        jnp.concatenate([-sine, sine], axis=1),
    )


def turn(values, cosine, sine):
    return values * cosine + pltpu.roll(values, HDIM // 2, 1) * sine


def lane_value(table, lane):
    lanes = lax.broadcasted_iota(jnp.int32, table.shape, 1)
    return jnp.sum(jnp.where(lanes == lane, table, 0.0), axis=1, keepdims=True)


def allowed_pairs(rows, first_len):
    query_at = lax.broadcasted_iota(jnp.int32, (rows, rows), 0)
    key_at = lax.broadcasted_iota(jnp.int32, (rows, rows), 1)
    return (key_at <= query_at) & ((key_at >= first_len) | (query_at < first_len))


def forward_kernel(
    lens, query, key, value, cosine, sine, gates, hits,
    vals_out, gated_out, query_out, key_out, total_out, peak_out,
):
    m, h = pl.program_id(0), pl.program_id(1)
    heads = pl.num_programs(1)
    rows = query.shape[0]
    slots = query.shape[1] // (heads * HDIM)

    @pl.when(h == 0)
    def _():
        total_out[...] = jnp.zeros_like(total_out)
        peak_out[...] = jnp.full_like(peak_out, very_low)

    cos_part, sin_part = cosine[...], sine[...]
    allowed = allowed_pairs(rows, lens[m])
    keys = turn(key[...].astype(f32), cos_part, sin_part).astype(bf16)
    key_out[...] = keys
    values = value[...]
    lanes = lax.broadcasted_iota(jnp.int32, total_out.shape, 1)
    peak_lanes = lax.broadcasted_iota(jnp.int32, peak_out.shape, 1)
    totals, peaks = total_out[...], peak_out[...]
    for s in range(slots):
        columns = pl.ds(pl.multiple_of((s * heads + h) * HDIM, HDIM), HDIM)
        turned = turn(query[:, columns], cos_part, sin_part).astype(bf16)
        query_out[:, columns] = turned
        scores = jnp.where(allowed, dot_t(turned, keys) * HDIM ** (-0.5), very_low)
        row_peak = jnp.max(scores, axis=1, keepdims=True)
        expo = jnp.exp(scores - row_peak)
        denom = jnp.sum(expo, axis=1, keepdims=True)
        probs = expo * (1.0 / denom)
        vals = dot(probs.astype(bf16), values).astype(bf16)
        vals_out[:, columns] = vals
        gated_out[:, columns] = (gates[:, s : s + 1] * vals.astype(f32)).astype(bf16)
        lane = h * slots + s
        totals = jnp.where(lanes == lane, row_peak + jnp.log(denom), totals)
        seen = jnp.where(hits[:, s : s + 1] > 0.0, row_peak, very_low)
        peaks = jnp.where(peak_lanes == lane, jnp.max(seen, axis=0, keepdims=True), peaks)
    total_out[...] = totals
    peak_out[...] = peaks


def backward_kernel(
    lens, query, key, value, vals, vals_grad, cosine, sine, gates, total,
    query_grad, key_grad, value_grad, gate_grad,
):
    m, h = pl.program_id(0), pl.program_id(1)
    heads = pl.num_programs(1)
    rows = query.shape[0]
    slots = query.shape[1] // (heads * HDIM)

    @pl.when(h == 0)
    def _():
        gate_grad[...] = jnp.zeros_like(gate_grad)

    allowed = allowed_pairs(rows, lens[m])
    cos_part, back_sine = cosine[...], -sine[...]
    keys, values, totals = key[...], value[...], total[...]
    lanes = lax.broadcasted_iota(jnp.int32, gate_grad.shape, 1)
    slot_sums = gate_grad[...]
    key_sum = jnp.zeros(key.shape, f32)
    value_sum = jnp.zeros(value.shape, f32)
    for s in range(slots):
        columns = pl.ds(pl.multiple_of((s * heads + h) * HDIM, HDIM), HDIM)
        full_grad = vals_grad[:, columns]
        slot_sum = jnp.sum(vals[:, columns].astype(f32) * full_grad, axis=1, keepdims=True)
        slot_sums += jnp.where(lanes == s, slot_sum, 0.0)
        gated_grad = (gates[:, s : s + 1] * full_grad).astype(bf16)
        queries = query[:, columns]
        scores = jnp.where(allowed, dot_t(queries, keys) * HDIM ** (-0.5), very_low)
        probs = jnp.exp(scores - lane_value(totals, h * slots + s))
        prob_grad = dot_t(gated_grad, values)
        inner = jnp.sum(probs * prob_grad, axis=1, keepdims=True)
        score_grad = (probs * (prob_grad - inner) * HDIM ** (-0.5)).astype(bf16)
        query_grad[:, columns] = turn(dot(score_grad, keys), cos_part, back_sine).astype(bf16)
        key_sum += t_dot(score_grad, queries)
        value_sum += t_dot(probs.astype(bf16), gated_grad)
    gate_grad[...] = slot_sums
    key_grad[...] = turn(key_sum, cos_part, back_sine).astype(bf16)
    value_grad[...] = value_sum.astype(bf16)


def attention_specs(own_heads, rows, width):
    def block(columns, index):
        return pl.BlockSpec((rows, columns), index)

    return {
        "query": block(width, lambda m, h, lens: (m, 0)),
        "key": block(HDIM, lambda m, h, lens: (m, h)),
        "value": block(HDIM, lambda m, h, lens: (m, own_heads + h)),
        "rows": block(HDIM, lambda m, h, lens: (m, 0)),
        "peak": pl.BlockSpec((8, HDIM), lambda m, h, lens: (m, 0)),
    }


def attention_forward(lens, query, joint_kv, tables, gates, hits, own_heads, rows):
    micro = lens.shape[0]
    at = attention_specs(own_heads, rows, query.shape[1])
    shape = jax.ShapeDtypeStruct
    total_rows = micro * rows
    return pl.pallas_call(
        forward_kernel,
        grid_spec=pltpu.PrefetchScalarGridSpec(
            num_scalar_prefetch=1,
            grid=(micro, own_heads),
            in_specs=[at["query"], at["key"], at["value"]] + [at["rows"]] * 4,
            out_specs=[at["query"]] * 3 + [at["key"], at["rows"], at["peak"]],
        ),
        out_shape=[shape(query.shape, bf16)] * 3
        + [
            shape((total_rows, own_heads * HDIM), bf16),
            shape((total_rows, HDIM), f32),
            shape((micro * 8, HDIM), f32),
        ],
        compiler_params=pltpu.CompilerParams(vmem_limit_bytes=48 * 2**20),
        cost_estimate=pl.CostEstimate(
            flops=4 * rows * rows * HDIM * micro * HEADS,
            bytes_accessed=14 * query.size,
            transcendentals=rows * rows * micro * HEADS,
        ),
        name="attention_forward",
    )(lens, query, joint_kv, joint_kv, tables[0], tables[1], gates, hits)


def attention_backward(
    lens, query, key, joint_kv, vals, vals_grad, tables, gates, total, own_heads, rows
):
    micro = lens.shape[0]
    at = attention_specs(own_heads, rows, query.shape[1])
    shape = jax.ShapeDtypeStruct
    total_rows = micro * rows
    return pl.pallas_call(
        backward_kernel,
        grid_spec=pltpu.PrefetchScalarGridSpec(
            num_scalar_prefetch=1,
            grid=(micro, own_heads),
            in_specs=[at["query"], at["key"], at["value"], at["query"], at["query"]]
            + [at["rows"]] * 4,
            out_specs=[at["query"], at["key"], at["key"], at["rows"]],
        ),
        out_shape=[shape(query.shape, bf16)]
        + [shape((total_rows, own_heads * HDIM), bf16)] * 2
        + [shape((total_rows, HDIM), f32)],
        compiler_params=pltpu.CompilerParams(vmem_limit_bytes=48 * 2**20),
        cost_estimate=pl.CostEstimate(
            flops=10 * rows * rows * HDIM * micro * HEADS,
            bytes_accessed=14 * query.size,
            transcendentals=rows * rows * micro * HEADS,
        ),
        name="attention_backward",
    )(lens, query, key, joint_kv, vals, vals_grad, tables[0], tables[1], gates, total)


def normalize(values):
    row_scale = lax.rsqrt(jnp.mean(values * values, axis=-1, keepdims=True) + eps_norm)
    return values * row_scale, row_scale


def norm_back(grad_hat, normed, row_scale):
    return row_scale * (grad_hat - normed * jnp.mean(grad_hat * normed, axis=-1, keepdims=True))


def route_gates(logits, routes, expert_table):
    expert_ids = jnp.arange(expert_table.shape[0], dtype=jnp.int32)
    matches = routes[:, :, None] == expert_ids[None, None, :]
    picked = jnp.sum(jnp.where(matches, logits[:, None, :], 0.0), axis=-1)
    gate_vals = jax.nn.softmax(picked, axis=-1)
    slot_ids = route_slots(routes, expert_table)
    chosen = slot_ids[:, :, None] == expert_ids[None, None, :]
    gates = jnp.sum(jnp.where(chosen, gate_vals[:, :, None], 0.0), axis=1)
    return gates, matches, chosen, gate_vals


def route_slots(routes, expert_table):
    expert_ids = jnp.arange(expert_table.shape[0], dtype=jnp.int32)
    matches = routes[..., None] == expert_ids
    return jnp.sum(jnp.where(matches, expert_table, 0), axis=-1)


def gate_back(slot_grad, gate_vals, matches, chosen):
    picked = jnp.sum(jnp.where(chosen, slot_grad[:, None, :], 0.0), axis=-1)
    inner_sum = jnp.sum(gate_vals * picked, axis=-1, keepdims=True)
    picked_grad = gate_vals * (picked - inner_sum)
    return jnp.sum(jnp.where(matches, picked_grad[:, :, None], 0.0), axis=1)


def unit_blocks(count):
    return [(start, min(512, count - start)) for start in range(0, count, 512)]


def expert_kernel(place_ref, hidden, grad, *refs):
    piece_count = (len(refs) - 6) // 2
    own_pieces, near_pieces = refs[:piece_count], refs[piece_count : 2 * piece_count]
    out, hidden_out, act_out, joint_out, weights, sems = refs[2 * piece_count :]
    core, chip = place_ref[0], place_ref[1]
    rows, columns = near_pieces[0].shape
    units = columns // 3
    width = grad.shape[1]

    @pl.when(pl.program_id(0) == 0)
    def _():
        copies = []
        for k in range(piece_count):
            base = (chip ^ k) * (2 * rows)
            for number, (piece, part) in enumerate(
                ((own_pieces[k], core), (near_pieces[k], 1 - core))
            ):
                start = pl.multiple_of(base + part * rows, 16)
                copies.append(
                    pltpu.make_async_copy(
                        piece, weights.at[pl.ds(start, rows)], sems.at[2 * k + number]
                    )
                )
        for copy in copies:
            copy.start()
        for copy in copies:
            copy.wait()

    slot_sum = jnp.zeros((hidden.shape[0], 1), f32)
    for start, size in unit_blocks(units):
        gate_pre = dot(hidden[:, :width], weights[:, start : start + size])
        up_pre = dot(hidden[:, :width], weights[:, units + start : units + start + size])
        act_grad = dot(grad[...], weights[:, 2 * units + start : 2 * units + start + size])
        sigma = 1.0 / (1.0 + jnp.exp(-gate_pre))
        silu_vals = gate_pre * sigma
        active = (silu_vals * up_pre).astype(bf16)
        act_out[:, start : start + size] = active
        slot_sum += jnp.sum(active.astype(f32) * act_grad, axis=1, keepdims=True)
        gate_grad = act_grad * up_pre * sigma * (1.0 + gate_pre * (1.0 - sigma))
        joint_out[:, start : start + size] = gate_grad.astype(bf16)
        joint_out[:, units + start : units + start + size] = (act_grad * silu_vals).astype(bf16)
    for start in range(0, width, 512):
        block = weights[start : start + 512, : 2 * units]
        hidden_out[:, start : start + 512] = dot_t(joint_out[...], block).astype(bf16)
        block = weights[start : start + 512, 2 * units :]
        out[:, start : start + 512] = dot_t(act_out[...], block).astype(bf16)
    lanes = lax.broadcasted_iota(jnp.int32, (hidden.shape[0], HDIM), 1)
    hidden_out[:, width:] = jnp.where(lanes == 0, slot_sum, 0.0).astype(bf16)


def expert_rows(position, hidden, grad, own_pieces, near_pieces):
    rows, width = grad.shape
    columns = near_pieces[0].shape[1]
    units = columns // 3
    tile = rows // 2
    shape = jax.ShapeDtypeStruct
    count = len(own_pieces)

    def tiled(size):
        return pl.BlockSpec((tile, size), lambda i, at: (i, 0))

    return pl.pallas_call(
        expert_kernel,
        grid_spec=pltpu.PrefetchScalarGridSpec(
            num_scalar_prefetch=1,
            grid=(rows // tile,),
            in_specs=[tiled(width + HDIM), tiled(width)]
            + [pl.BlockSpec(memory_space=pl.ANY)] * (2 * count),
            out_specs=[tiled(width), tiled(width + HDIM), tiled(units), tiled(2 * units)],
            scratch_shapes=[
                pltpu.VMEM((width, columns), bf16),
                pltpu.SemaphoreType.DMA((2 * count,)),
            ],
        ),
        out_shape=[
            shape((rows, width), bf16),
            shape((rows, width + HDIM), bf16),
            shape((rows, units), bf16),
            shape((rows, 2 * units), bf16),
        ],
        compiler_params=pltpu.CompilerParams(vmem_limit_bytes=56 * 2**20),
        cost_estimate=pl.CostEstimate(
            flops=4 * rows * width * columns,
            bytes_accessed=2 * (width * columns + 6 * rows * width),
            transcendentals=rows * units,
        ),
        name="expert_rows",
    )(position, hidden, grad, *own_pieces, *near_pieces)


def expert_grad_kernel(cuts, order, *refs):
    hidden, grad, gates, joint, active = [refs[2 * n : 2 * n + 2] for n in range(5)]
    outs = refs[10:]
    units = active[0].shape[1]

    def scaled(blocks):
        return [
            (block[...].astype(f32) * gate[:, :1].astype(f32)).astype(bf16)
            for block, gate in zip(blocks, gates)
        ]

    left, right = scaled(hidden), scaled(grad)
    step = pl.program_id(0)
    first = [0]
    for cut in cuts:
        first.append(first[-1] + cut)
    for out, start, cut in zip(outs, first, cuts):

        @pl.when((step >= start) & (step < start + cut))
        def _():
            for start, size in unit_blocks(2 * units):
                out[:, start : start + size] = sum(
                    t_dot(rows, part[:, start : start + size]) for rows, part in zip(left, joint)
                ).astype(bf16)
            for start, size in unit_blocks(units):
                out[:, 2 * units + start : 2 * units + start + size] = sum(
                    t_dot(rows, part[:, start : start + size]) for rows, part in zip(right, active)
                ).astype(bf16)


def expert_grads(chunks, cuts, chunk_rows, rows_of, joints, actives):
    hidden, grad = rows_of[:2], rows_of[2:]
    rows, units = actives[0].shape
    width = grad[0].shape[1]
    half = chunk_rows // 2
    count = len(chunks)
    order = jnp.stack([2 * chunk + part for chunk in chunks for part in range(2)]).astype(jnp.int32)

    def whole(size, column=0):
        return pl.BlockSpec(
            (rows, size), lambda i, at: (0, column), pipeline_mode=pl.Buffered(1)
        )

    column = pl.BlockSpec((rows, half), lambda i, at: (0, at[i]))
    return pl.pallas_call(
        functools.partial(expert_grad_kernel, cuts),
        grid_spec=pltpu.PrefetchScalarGridSpec(
            num_scalar_prefetch=1,
            grid=(2 * count,),
            in_specs=[column] * 4
            + [whole(HDIM, width // HDIM)] * 2
            + [whole(2 * units)] * 2
            + [whole(units)] * 2,
            out_specs=[
                pl.BlockSpec(
                    (half, 3 * units),
                    lambda i, at, start=sum(cuts[:n]), cut=cut: (jnp.clip(i - start, 0, cut - 1), 0),
                )
                for n, cut in enumerate(cuts)
            ],
        ),
        out_shape=[jax.ShapeDtypeStruct((cut * half, 3 * units), bf16) for cut in cuts],
        compiler_params=pltpu.CompilerParams(vmem_limit_bytes=56 * 2**20),
        cost_estimate=pl.CostEstimate(
            flops=4 * count * chunk_rows * rows * 3 * units,
            bytes_accessed=2 * (rows * 6 * units + count * chunk_rows * (4 * rows + 3 * units)),
            transcendentals=0,
        ),
        name="expert_grads",
    )(order, *hidden, *grad, *hidden, *joints, *actives)


def local(
    tokens,
    cotangent,
    seq_lengths,
    dealing,
    attn_routes,
    ffn_routes,
    expert_table,
    clip_limit,
    attn_gain,
    ffn_gain,
    attn_router,
    ffn_router,
    query_weight,
    attn_out_weight,
    kv_weight,
    gate_up_weight,
    down_weight,
):
    micro, tok_rows, width = tokens.shape
    dp_count = lax.axis_size("dp")
    slots = lax.axis_size("expert")
    col = lax.axis_index("expert")
    group = lax.axis_index("dp")
    piece_rows = tok_rows // dp_count
    cap = tok_rows * TOP * 3 // (2 * slots)
    group_rows = tok_rows * slots
    all_rows = micro * group_rows
    home_rows = micro * tok_rows
    query_width = HEADS * HDIM
    own_heads = HEADS // slots
    own_width = own_heads * HDIM
    shard_rows = query_weight.shape[1]
    score_scale = HDIM ** (-0.5)
    core = group % 2
    chip = group // 2
    side = chip % 2
    chips = dp_count // 2
    lines = chips // 2
    quarter = FF // 4
    chip_rows = 2 * shard_rows

    both = jnp.stack([tokens, cotangent]).reshape(2 * micro, dp_count, piece_rows, width)
    both = lax.all_to_all(both.transpose(1, 0, 2, 3), "dp", split_axis=0, concat_axis=0, tiled=True)
    def quarter_of(half, part):
        start = (2 * half + part) * quarter
        return jnp.concatenate(
            [
                lax.dynamic_slice_in_dim(gate_up_weight[0], start, quarter, 1),
                lax.dynamic_slice_in_dim(gate_up_weight[0], FF + start, quarter, 1),
                lax.dynamic_slice_in_dim(down_weight[0], start, quarter, 1),
            ],
            axis=1,
        )

    parts = (1 - core, core)
    keep_pair = [quarter_of(side, part) for part in parts]
    send_pair = [quarter_of(1 - side, part) for part in parts]
    both = both.transpose(1, 0, 2, 3).reshape(2, micro, tok_rows, width)
    deal = (dealing[:, :, None] == jnp.arange(tok_rows, dtype=jnp.int32)).astype(bf16)
    work = jnp.einsum("mtr,bmrd->bmtd", deal, both, preferred_element_type=f32)
    x_home = work[0].reshape(home_rows, width)
    dy_home = work[1].reshape(home_rows, width)

    def columns_of(*shards):
        pieces = [shard.reshape(shard_rows, slots, own_width) for shard in shards]
        out = jnp.zeros((shard_rows, len(shards) * query_width), shards[0].dtype)
        for k in range(slots):
            part = jnp.concatenate(
                [lax.dynamic_index_in_dim(piece, col ^ k, 1, keepdims=False) for piece in pieces],
                axis=1,
            )
            part = swap(part, "expert", k) if k else part
            for number in range(len(shards)):
                out = lax.dynamic_update_slice_in_dim(
                    out,
                    part[:, number * own_width : (number + 1) * own_width],
                    number * query_width + (col ^ k) * own_width,
                    1,
                )
        return out

    def slots_of(columns):
        pieces = columns.reshape(shard_rows, slots, own_width)
        out = jnp.zeros((shard_rows, query_width), columns.dtype)
        for k in range(slots):
            part = lax.dynamic_index_in_dim(pieces, col ^ k, 1, keepdims=False)
            part = swap(part, "expert", k) if k else part
            out = lax.dynamic_update_slice_in_dim(out, part, (col ^ k) * own_width, 1)
        return out

    half_slots = slots // 2
    first_pairs = [(c, 2 * c) for c in range(half_slots)]
    first_pairs += [(c, 2 * (c - half_slots) + 1) for c in range(half_slots, slots)]
    second_pairs = [(c, 2 * c + 1) for c in range(half_slots)]
    second_pairs += [(c, 2 * (c - half_slots)) for c in range(half_slots, slots)]
    holds_keys = col < half_slots
    even_col = col % 2 == 0
    low_kv, high_kv = kv_weight[:, :own_width], kv_weight[:, own_width:]
    first_got = lax.ppermute(jnp.where(holds_keys, low_kv, high_kv), "expert", first_pairs)
    second_got = lax.ppermute(jnp.where(holds_keys, high_kv, low_kv), "expert", second_pairs)
    own_kv = jnp.concatenate(
        [
            jnp.where(even_col, first_got, second_got),
            jnp.where(even_col, second_got, first_got),
        ],
        axis=1,
    )
    line_steps = [4 * line for line in range(1, lines)]
    side_first = swap(send_pair[0], "dp", 2)
    keep_first = [swap(keep_pair[0], "dp", step) for step in line_steps]
    joint_own = columns_of(query_weight[0], attn_out_weight[0])
    first_own = jnp.concatenate([joint_own[:, :query_width], own_kv], axis=1)
    first_own, second_own = lax.optimization_barrier(
        (first_own, joint_own[:, query_width:], side_first, keep_first)
    )[:2]
    joint_full = lax.all_gather(first_own, "dp", axis=0, tiled=True)
    out_full = lax.all_gather(second_own, "dp", axis=0, tiled=True)
    late_pair = after((keep_pair[1], send_pair[1], side_first), joint_full)
    keep_second = [swap(late_pair[0], "dp", step) for step in line_steps]
    side_second = swap(late_pair[1], "dp", 2)
    first_lines = [swap(late_pair[2], "dp", step) for step in line_steps]
    second_lines = [swap(side_second, "dp", step) for step in line_steps]
    firsts, seconds = [keep_pair[0], side_first], [keep_pair[1], side_second]
    for line in range(lines - 1):
        firsts += [keep_first[line], first_lines[line]]
        seconds += [keep_second[line], second_lines[line]]
    near_pieces = [swap(piece, "dp", 1) for piece in firsts]
    own_pieces = seconds
    query_full = joint_full[:, :query_width]
    kv_full = joint_full[:, query_width:]

    positions = jnp.arange(group_rows, dtype=jnp.int32)
    first_len = lax.dynamic_index_in_dim(seq_lengths[:, :, 0], group, 1, keepdims=True)
    in_second = positions[None, :] >= first_len
    places = positions[None, :] - jnp.where(in_second, first_len, 0)
    tables = rotation_tables(places.reshape(all_rows))

    def gather_rows(value):
        shaped = value.reshape(micro, tok_rows, -1)
        out = jnp.zeros((micro, group_rows, shaped.shape[-1]), value.dtype)
        for k in range(slots):
            part = swap(shaped, "expert", k) if k else shaped
            out = lax.dynamic_update_slice_in_dim(out, part, (col ^ k) * tok_rows, 1)
        return out.reshape(all_rows, -1)

    def scatter_rows(value):
        shaped = value.reshape(micro, group_rows, -1)
        total = None
        for k in range(slots):
            part = lax.dynamic_slice_in_dim(shaped, (col ^ k) * tok_rows, tok_rows, 1)
            if k:
                part = swap(part.astype(bf16), "expert", k)
            part = part.astype(f32)
            total = part if total is None else total + part
        return total.reshape(home_rows, -1)

    home_routes = lax.dynamic_slice_in_dim(ffn_routes, col * tok_rows, tok_rows, 1)
    home_slots = route_slots(home_routes, expert_table)
    packs = []
    before = jnp.tril(jnp.ones((tok_rows, tok_rows), bf16), -1)
    for k in range(slots):
        hits = jnp.any(home_slots == (col ^ k), axis=-1)
        rank = jnp.einsum("ts,ms->mt", before, hits.astype(bf16), preferred_element_type=f32)
        packs.append(
            hits[:, None, :]
            & (rank[:, None, :] == jnp.arange(cap, dtype=jnp.int32).astype(f32)[None, :, None])
        )
    packs = jnp.stack(packs)
    packs_low = packs.astype(bf16)
    pack_rows = micro * cap
    sent_rows = slots * pack_rows

    def send_packed(value, lane=None):
        packed = jnp.einsum(
            "kmct,mtd->kmcd", packs_low, value.reshape(micro, tok_rows, -1), preferred_element_type=f32
        ).astype(bf16)
        if lane is not None:
            lanes = jnp.pad(lane[..., None], ((0, 0), (0, 0), (0, 0), (0, HDIM - 1)))
            packed = jnp.concatenate([packed, lanes.astype(bf16)], axis=-1)
        parts = [swap(packed[k], "expert", k) if k else packed[k] for k in range(slots)]
        return jnp.stack(parts).reshape(sent_rows, -1)

    def near_rows(value):
        return jnp.concatenate([value, swap(value, "dp", 1)], axis=0)

    def quad_sums(value):
        (own, near), (far, across) = [jnp.split(half, 2, axis=0) for half in value]
        far_sum = far.astype(f32) + swap(across, "dp", 1).astype(f32)
        return own.astype(f32) + swap(near, "dp", 1).astype(f32), far_sum.astype(bf16)

    def return_packed(value, *others):
        shaped = value.astype(bf16).reshape(slots, micro, cap, -1)
        parts = [swap(shaped[k], "expert", k) if k else shaped[k] for k in range(slots)]
        return after(parts, *others)

    def unpack(packed, scale):
        total = None
        for k in range(slots):
            rows = jnp.einsum("mct,mcd->mtd", packs_low[k], packed[k], preferred_element_type=f32)
            rows = rows.reshape(home_rows, -1) * take(scale.T, col ^ k)[:, None]
            total = rows if total is None else total + rows
        return total

    gain_one = attn_gain.astype(f32)
    gain_two = ffn_gain.astype(f32)
    normed_one, scale_one = normalize(x_home)
    hidden_one_home = (normed_one * gain_one).astype(bf16)
    hidden_one_raw = gather_rows(after(hidden_one_home, near_pieces[:3]))
    hidden_one = hidden_one_raw
    grad_sent = send_packed(after(dy_home.astype(bf16), hidden_one))
    logits_one = dot(hidden_one, attn_router)
    gates_one, matches_one, chosen_one, gate_vals_one = route_gates(
        logits_one, attn_routes.reshape(all_rows, TOP), expert_table
    )
    hits_one = jnp.any(chosen_one, axis=1).astype(f32)

    def wide(value):
        return jnp.pad(value, ((0, 0), (0, HDIM - value.shape[1])))

    kv_part = dot(hidden_one, kv_full).astype(bf16)
    query_part = dot(hidden_one, query_full)
    lens = first_len[:, 0].astype(jnp.int32)
    gates_wide = wide(gates_one)
    attn_vals, gated_vals, query_rot, key_rot, log_total, peaks = attention_forward(
        lens, query_part, kv_part, tables, gates_wide, wide(hits_one), own_heads, group_rows
    )
    peaks = jnp.max(peaks, axis=0)[: own_heads * slots]
    attn_part = after(dot_t(gated_vals, out_full), keep_second, side_second)
    attn_home = after(scatter_rows(attn_part), first_lines)
    grad_sent = after(grad_sent, attn_home)
    grad_near, grad_far = near_rows(grad_sent), near_rows(swap(grad_sent, "dp", 2))

    resid = x_home + attn_home
    normed_two, scale_two = normalize(resid)
    hidden_two = (normed_two * gain_two).astype(bf16)
    logits_two = dot(hidden_two, ffn_router)
    gates_two, matches_two, chosen_two, gate_vals_two = route_gates(
        logits_two, home_routes.reshape(home_rows, TOP), expert_table
    )
    gates_by_slot = gates_two.reshape(micro, tok_rows, slots)
    gate_parts = []
    for k in range(slots):
        gate_col = lax.dynamic_index_in_dim(gates_by_slot, col ^ k, 2, keepdims=False)
        gate_parts.append(jnp.sum(jnp.where(packs[k], gate_col[:, None, :], 0.0), axis=-1))
    hidden_sent = after(
        send_packed(hidden_two, jnp.stack(gate_parts)), second_lines
    )
    hidden_near, hidden_far = near_rows(hidden_sent), swap(hidden_sent, "dp", 2)
    hidden_near = after(hidden_near, near_pieces, grad_near, grad_far)
    position = jnp.stack([core, chip]).astype(jnp.int32)
    near_results = expert_rows(
        position, hidden_near, after(grad_near, grad_far), own_pieces, near_pieces
    )
    hidden_far = near_rows(after(hidden_far, near_results))
    far_results = expert_rows(position, hidden_far, grad_far, own_pieces, near_pieces)
    ffn_parts, hidden_parts, actives, joint_grads = zip(near_results, far_results)

    def block_grads(steps, *others):
        rows = after((hidden_near, hidden_far, grad_near, grad_far), *others)
        cuts = (2,) * len(steps)
        return expert_grads([chip ^ k for k in steps], cuts, chip_rows, rows, joint_grads, actives)

    hidden_sum, hidden_far_sum = quad_sums(hidden_parts)
    ffn_sum, ffn_far_sum = quad_sums(ffn_parts)
    line_grads = block_grads([k ^ 1 for k in range(2, chips)], hidden_far_sum)
    side_got = [swap(line_grads[2 * line], "dp", step) for line, step in enumerate(line_steps)]
    blocks = after(line_grads[1::2], side_got)
    keep_got = [swap(block, "dp", step) for block, step in zip(blocks, line_steps)]
    hidden_got, ffn_far_sum, ffn_sum = lax.optimization_barrier(
        (swap(hidden_far_sum, "dp", 2), ffn_far_sum, ffn_sum, line_grads)
    )[:3]
    hidden_sum = hidden_sum + hidden_got.astype(f32)
    own_grads = block_grads([1, 0], hidden_sum)
    back_packed = return_packed(hidden_sum, *own_grads)
    ffn_sum = ffn_sum + swap(after(ffn_far_sum, hidden_got), "dp", 2).astype(f32)

    def total(own, got):
        return functools.reduce(jnp.add, [part.astype(f32) for part in [own] + got]).astype(bf16)

    slot_two_grad = jnp.zeros((slots, home_rows), f32)
    for k in range(slots):
        rows = jnp.sum(
            jnp.where(packs[k], back_packed[k][:, :, width].astype(f32)[:, :, None], 0.0), axis=1
        )
        slot_two_grad = lax.dynamic_update_index_in_dim(
            slot_two_grad, rows.reshape(home_rows), col ^ k, 0
        )
    hidden_two_grad = unpack([part[..., :width] for part in back_packed], gates_two)
    logit_two_grad = gate_back(slot_two_grad.T, gate_vals_two, matches_two, chosen_two).astype(bf16)
    hidden_two_grad = hidden_two_grad + dot_t(logit_two_grad, ffn_router)
    router_two_grad = t_dot(logit_two_grad, hidden_two)
    gain_two_grad = jnp.sum(hidden_two_grad * normed_two, axis=0)
    resid_grad = dy_home + norm_back(hidden_two_grad * gain_two, normed_two, scale_two)

    resid_grad_all, ffn_sum = lax.optimization_barrier(
        (gather_rows(resid_grad.astype(bf16)), ffn_sum, side_got)
    )[:2]
    out_part = t_dot(resid_grad_all, gated_vals).astype(bf16)
    vals_grad = after(dot(resid_grad_all, out_full), out_part)
    side_own = after((own_grads[0], side_got), vals_grad)
    vals_grad, side_sum = lax.optimization_barrier((vals_grad, total(*side_own)))
    other_sum = swap(side_sum, "dp", 2)
    ffn_packed = return_packed(after(ffn_sum, vals_grad))
    out_home = (resid + unpack(ffn_packed, gates_two)).astype(bf16)
    query_grad, key_grad, value_grad, slot_part_one = attention_backward(
        lens, query_rot, key_rot, kv_part, attn_vals, vals_grad, tables, gates_wide, log_total,
        own_heads, group_rows,
    )
    query_grad, key_grad, value_grad, slot_part_one = lax.optimization_barrier(
        (query_grad, key_grad, value_grad, slot_part_one, ffn_packed)
    )[:4]
    kv_grad = jnp.concatenate([key_grad, value_grad], axis=1)
    hidden_one_part = dot_t(query_grad, query_full) + dot_t(kv_grad, kv_full)
    hidden_one_part, keep_got = lax.optimization_barrier((hidden_one_part.astype(bf16), keep_got))
    joint_part_grad = t_dot(
        after(hidden_one, hidden_one_part), jnp.concatenate([query_grad, kv_grad], axis=1)
    ).astype(bf16)
    back_one = scatter_rows(
        jnp.concatenate([hidden_one_part, slot_part_one.astype(bf16)], axis=1)
    )
    back_one, other_sum = lax.optimization_barrier((back_one, other_sum, joint_part_grad))[:2]
    hidden_one_grad, slot_one_grad = back_one[:, :width], back_one[:, width : width + slots]

    def own(value):
        shaped = value.reshape((micro, group_rows) + value.shape[1:])
        part = lax.dynamic_slice_in_dim(shaped, col * tok_rows, tok_rows, 1)
        return part.reshape((home_rows,) + value.shape[1:])

    logit_one_grad = gate_back(
        slot_one_grad, own(gate_vals_one), own(matches_one), own(chosen_one)
    ).astype(bf16)
    hidden_one_grad = hidden_one_grad + dot_t(logit_one_grad, attn_router)
    router_one_grad = t_dot(logit_one_grad, hidden_one_home)
    gain_one_grad = jnp.sum(hidden_one_grad * normed_one, axis=0)
    in_home = resid_grad + norm_back(hidden_one_grad * gain_one, normed_one, scale_one)

    def reduced(value):
        return lax.psum_scatter(value, "dp", scatter_dimension=0, tiled=True)

    in_low, keep_got, other_sum = lax.optimization_barrier(
        (in_home.astype(bf16), keep_got, other_sum)
    )
    out_grad = slots_of(after(reduced(out_part), in_low))
    joint_own = reduced(joint_part_grad)

    results = jnp.stack([out_home, in_low]).reshape(2, micro, tok_rows, width)
    results = jnp.einsum("mtr,bmtd->bmrd", deal, results, preferred_element_type=f32).astype(bf16)
    results = results.reshape(2 * micro, dp_count, piece_rows, width).transpose(1, 0, 2, 3)
    results = results.reshape(dp_count, 2 * micro * piece_rows, width)
    sent_back = results.shape[1]
    small = jnp.concatenate(
        [gain_one_grad[None], gain_two_grad[None], router_one_grad, router_two_grad], axis=0
    ).astype(bf16)
    sum_rows = small.shape[0]
    peak_count = own_heads * slots
    peak_parts, rest = [], peaks
    for _ in range(3):
        peak_parts.append(lax.reduce_precision(rest, 8, 7))
        rest = rest - peak_parts[-1]
    peak_row = jnp.concatenate(peak_parts).astype(bf16)
    small = jnp.pad(small, ((0, -sum_rows % 16 or 16), (0, 0)))
    small = lax.dynamic_update_slice(small, peak_row[None], (sum_rows, 0))
    small = jnp.broadcast_to(small[None], (dp_count,) + small.shape)
    results = jnp.concatenate([results, small], axis=1)
    results = lax.all_to_all(results, "dp", split_axis=0, concat_axis=0, tiled=True)
    results, out_grad, joint_own = lax.optimization_barrier((results, out_grad, joint_own))
    query_own, kv_own = joint_own[:, :query_width], joint_own[:, query_width:]
    small = results[:, sent_back:].astype(f32)
    results = results[:, :sent_back].reshape(dp_count, 2 * micro, piece_rows, width)
    results = results.transpose(1, 0, 2, 3).reshape(2, micro, tok_rows, width)
    peak_row = small[:, sum_rows, : 3 * peak_count].reshape(dp_count, 3, peak_count)
    peak_row = jnp.max((peak_row[:, 0] + peak_row[:, 1]) + peak_row[:, 2], axis=0)
    small = jnp.sum(small, axis=0)
    small = lax.dynamic_update_slice(small, peak_row[None], (sum_rows, 0))
    smalls = [swap(small, "expert", k) if k else small for k in range(slots)]
    peaks_all = jnp.zeros((slots, HEADS), f32)
    for k, part in enumerate(smalls):
        part = part[sum_rows, :peak_count].reshape(own_heads, slots).T
        peaks_all = lax.dynamic_update_slice(peaks_all, part, (0, (col ^ k) * own_heads))
    while len(smalls) > 1:
        smalls = [left + right for left, right in zip(smalls[::2], smalls[1::2])]
    sums = smalls[0][:sum_rows]

    keep_sums = total(own_grads[1], keep_got).reshape(2, shard_rows, 3 * quarter)
    other_sums = other_sum.reshape(2, shard_rows, 3 * quarter)
    by_rows = [jnp.stack([keep_sums[part], other_sums[part]]) for part in range(2)]
    own_pair = jnp.where(core == 0, by_rows[0], by_rows[1])
    near_pair = swap(jnp.where(core == 0, by_rows[1], by_rows[0]), "dp", 1)
    by_core = [jnp.where(core == 0, own_pair, near_pair), jnp.where(core == 0, near_pair, own_pair)]
    by_side = [[jnp.where(side == s, part[0], part[1]) for part in by_core] for s in range(2)]
    blocks = [part for row in by_side for part in row]
    gate_up_grad = jnp.concatenate(
        [b[:, :quarter] for b in blocks] + [b[:, quarter : 2 * quarter] for b in blocks], axis=1
    ).astype(f32)
    down_grad = jnp.concatenate([b[:, 2 * quarter :] for b in blocks], axis=1).astype(f32)

    out_grad = out_grad.astype(f32)
    query_out = slots_of(query_own).astype(f32)
    key_part, value_part = kv_own[:, :own_width], kv_own[:, own_width:]
    first_back = lax.ppermute(
        jnp.where(even_col, key_part, value_part), "expert", [(b, a) for a, b in first_pairs]
    )
    second_back = lax.ppermute(
        jnp.where(even_col, value_part, key_part), "expert", [(b, a) for a, b in second_pairs]
    )
    kv_out = jnp.concatenate(
        [
            jnp.where(holds_keys, first_back, second_back),
            jnp.where(holds_keys, second_back, first_back),
        ],
        axis=1,
    ).astype(f32)

    limit = clip_limit[0].astype(f32)
    factor = limit / jnp.maximum(peaks_all, limit)
    query_scale = jnp.repeat(jnp.sqrt(take(factor, col)), HDIM)
    query_clipped = (query_weight.astype(f32) * query_scale[None, None, :]).astype(bf16)
    full_scale = jnp.concatenate(
        [jnp.repeat(jnp.sqrt(jnp.min(factor, axis=0)), HDIM), jnp.ones((query_width,), f32)]
    )
    piece_width = kv_weight.shape[1]
    piece_scale = lax.dynamic_slice_in_dim(full_scale, col * piece_width, piece_width)
    kv_clipped = (kv_weight.astype(f32) * piece_scale[None, :]).astype(bf16)
    return (
        results[0],
        results[1],
        sums[0],
        sums[1],
        sums[2 : 2 + slots].T,
        sums[2 + slots : sum_rows].T,
        query_out[None],
        out_grad[None],
        kv_out,
        gate_up_grad[None],
        down_grad[None],
        query_clipped,
        kv_clipped,
    )


def solution(mesh):
    placed = (
        P(None, ("dp", "expert"), None),
        P(None, ("dp", "expert"), None),
        P(),
        P(None, ("dp", "expert")),
        P(None, "dp", None),
        P(None, "dp", None),
        P(),
        P(),
        P(),
        P(),
        P(),
        P(),
        P("expert", "dp", None),
        P("expert", "dp", None),
        P("dp", "expert"),
        P("expert", "dp", None),
        P("expert", "dp", None),
    )
    return jax.shard_map(
        local,
        mesh=mesh,
        in_specs=placed,
        out_specs=(
            P(None, ("dp", "expert"), None),
            P(None, ("dp", "expert"), None),
            P(),
            P(),
            P(),
            P(),
            P("expert", "dp", None),
            P("expert", "dp", None),
            P("dp", "expert"),
            P("expert", "dp", None),
            P("expert", "dp", None),
            P("expert", "dp", None),
            P("dp", "expert"),
        ),
        check_vma=False,
    )
```

```python
import functools

import jax
import jax.numpy as jnp
from jax import lax
from jax.experimental import pallas as pl
from jax.experimental.pallas import tpu as pltpu
from jax.sharding import PartitionSpec as P

HEADS = 16
HDIM = 128
FF = 5632
TOP = 2

eps_norm = 1e-06
rope_base = 10000.0
very_low = -1e30

f32 = jnp.float32
bf16 = jnp.bfloat16


def dot(left, right):
    return jnp.dot(left, right, preferred_element_type=f32)


def dot_t(left, right):
    return lax.dot_general(left, right, (((1,), (1,)), ((), ())), preferred_element_type=f32)


def t_dot(left, right):
    return lax.dot_general(left, right, (((0,), (0,)), ((), ())), preferred_element_type=f32)


def swap(value, axis, step):
    count = lax.axis_size(axis)
    return lax.ppermute(value, axis, [(i, i ^ step) for i in range(count)])


def take(stacked, index):
    return lax.dynamic_index_in_dim(stacked, index, 0, keepdims=False)


def place(parts, positions):
    out = jnp.zeros((len(parts),) + parts[0].shape, parts[0].dtype)
    for part, position in zip(parts, positions):
        out = lax.dynamic_update_index_in_dim(out, part, position, 0)
    return out


def after(value, *others):
    return lax.optimization_barrier((value, others))[0]


def rotation_tables(places):
    half_dim = HDIM // 2
    frequency = rope_base ** (-jnp.arange(half_dim, dtype=f32) * 2.0 / HDIM)
    angles = places.astype(f32)[:, None] * frequency[None, :]
    cosine, sine = jnp.cos(angles), jnp.sin(angles)
    return (
        jnp.concatenate([cosine, cosine], axis=1),
        jnp.concatenate([-sine, sine], axis=1),
    )


def turn(values, cosine, sine):
    return values * cosine + pltpu.roll(values, HDIM // 2, 1) * sine


def lane_value(table, lane):
    lanes = lax.broadcasted_iota(jnp.int32, table.shape, 1)
    return jnp.sum(jnp.where(lanes == lane, table, 0.0), axis=1, keepdims=True)


def allowed_pairs(rows, first_len):
    query_at = lax.broadcasted_iota(jnp.int32, (rows, rows), 0)
    key_at = lax.broadcasted_iota(jnp.int32, (rows, rows), 1)
    return (key_at <= query_at) & ((key_at >= first_len) | (query_at < first_len))


def forward_kernel(
    lens, query, key, value, cosine, sine, gates, hits,
    vals_out, gated_out, query_out, key_out, total_out, peak_out,
):
    m, h = pl.program_id(0), pl.program_id(1)
    heads = pl.num_programs(1)
    rows = query.shape[0]
    slots = query.shape[1] // (heads * HDIM)

    @pl.when(h == 0)
    def _():
        total_out[...] = jnp.zeros_like(total_out)
        peak_out[...] = jnp.full_like(peak_out, very_low)

    cos_part, sin_part = cosine[...], sine[...]
    allowed = allowed_pairs(rows, lens[m])
    keys = turn(key[...].astype(f32), cos_part, sin_part).astype(bf16)
    key_out[...] = keys
    values = value[...]
    lanes = lax.broadcasted_iota(jnp.int32, total_out.shape, 1)
    peak_lanes = lax.broadcasted_iota(jnp.int32, peak_out.shape, 1)
    totals, peaks = total_out[...], peak_out[...]
    for s in range(slots):
        columns = pl.ds(pl.multiple_of((s * heads + h) * HDIM, HDIM), HDIM)
        turned = turn(query[:, columns], cos_part, sin_part).astype(bf16)
        query_out[:, columns] = turned
        scores = jnp.where(allowed, dot_t(turned, keys) * HDIM ** (-0.5), very_low)
        row_peak = jnp.max(scores, axis=1, keepdims=True)
        expo = jnp.exp(scores - row_peak)
        denom = jnp.sum(expo, axis=1, keepdims=True)
        probs = expo * (1.0 / denom)
        vals = dot(probs.astype(bf16), values).astype(bf16)
        vals_out[:, columns] = vals
        gated_out[:, columns] = (gates[:, s : s + 1] * vals.astype(f32)).astype(bf16)
        lane = h * slots + s
        totals = jnp.where(lanes == lane, row_peak + jnp.log(denom), totals)
        seen = jnp.where(hits[:, s : s + 1] > 0.0, row_peak, very_low)
        peaks = jnp.where(peak_lanes == lane, jnp.max(seen, axis=0, keepdims=True), peaks)
    total_out[...] = totals
    peak_out[...] = peaks


def backward_kernel(
    lens, query, key, value, vals, vals_grad, cosine, sine, gates, total,
    query_grad, key_grad, value_grad, gate_grad,
):
    m, h = pl.program_id(0), pl.program_id(1)
    heads = pl.num_programs(1)
    rows = query.shape[0]
    slots = query.shape[1] // (heads * HDIM)

    @pl.when(h == 0)
    def _():
        gate_grad[...] = jnp.zeros_like(gate_grad)

    allowed = allowed_pairs(rows, lens[m])
    cos_part, back_sine = cosine[...], -sine[...]
    keys, values, totals = key[...], value[...], total[...]
    lanes = lax.broadcasted_iota(jnp.int32, gate_grad.shape, 1)
    slot_sums = gate_grad[...]
    key_sum = jnp.zeros(key.shape, f32)
    value_sum = jnp.zeros(value.shape, f32)
    for s in range(slots):
        columns = pl.ds(pl.multiple_of((s * heads + h) * HDIM, HDIM), HDIM)
        full_grad = vals_grad[:, columns]
        slot_sum = jnp.sum(vals[:, columns].astype(f32) * full_grad, axis=1, keepdims=True)
        slot_sums += jnp.where(lanes == s, slot_sum, 0.0)
        gated_grad = (gates[:, s : s + 1] * full_grad).astype(bf16)
        queries = query[:, columns]
        scores = jnp.where(allowed, dot_t(queries, keys) * HDIM ** (-0.5), very_low)
        probs = jnp.exp(scores - lane_value(totals, h * slots + s))
        prob_grad = dot_t(gated_grad, values)
        inner = jnp.sum(probs * prob_grad, axis=1, keepdims=True)
        score_grad = (probs * (prob_grad - inner) * HDIM ** (-0.5)).astype(bf16)
        query_grad[:, columns] = turn(dot(score_grad, keys), cos_part, back_sine).astype(bf16)
        key_sum += t_dot(score_grad, queries)
        value_sum += t_dot(probs.astype(bf16), gated_grad)
    gate_grad[...] = slot_sums
    key_grad[...] = turn(key_sum, cos_part, back_sine).astype(bf16)
    value_grad[...] = value_sum.astype(bf16)


def attention_specs(own_heads, rows, width):
    def block(columns, index):
        return pl.BlockSpec((rows, columns), index)

    return {
        "query": block(width, lambda m, h, lens: (m, 0)),
        "key": block(HDIM, lambda m, h, lens: (m, h)),
        "value": block(HDIM, lambda m, h, lens: (m, own_heads + h)),
        "rows": block(HDIM, lambda m, h, lens: (m, 0)),
        "peak": pl.BlockSpec((8, HDIM), lambda m, h, lens: (m, 0)),
    }


def attention_forward(lens, query, joint_kv, tables, gates, hits, own_heads, rows):
    micro = lens.shape[0]
    at = attention_specs(own_heads, rows, query.shape[1])
    shape = jax.ShapeDtypeStruct
    total_rows = micro * rows
    return pl.pallas_call(
        forward_kernel,
        grid_spec=pltpu.PrefetchScalarGridSpec(
            num_scalar_prefetch=1,
            grid=(micro, own_heads),
            in_specs=[at["query"], at["key"], at["value"]] + [at["rows"]] * 4,
            out_specs=[at["query"]] * 3 + [at["key"], at["rows"], at["peak"]],
        ),
        out_shape=[shape(query.shape, bf16)] * 3
        + [
            shape((total_rows, own_heads * HDIM), bf16),
            shape((total_rows, HDIM), f32),
            shape((micro * 8, HDIM), f32),
        ],
        compiler_params=pltpu.CompilerParams(vmem_limit_bytes=48 * 2**20),
        cost_estimate=pl.CostEstimate(
            flops=4 * rows * rows * HDIM * micro * HEADS,
            bytes_accessed=14 * query.size,
            transcendentals=rows * rows * micro * HEADS,
        ),
        name="attention_forward",
    )(lens, query, joint_kv, joint_kv, tables[0], tables[1], gates, hits)


def attention_backward(
    lens, query, key, joint_kv, vals, vals_grad, tables, gates, total, own_heads, rows
):
    micro = lens.shape[0]
    at = attention_specs(own_heads, rows, query.shape[1])
    shape = jax.ShapeDtypeStruct
    total_rows = micro * rows
    return pl.pallas_call(
        backward_kernel,
        grid_spec=pltpu.PrefetchScalarGridSpec(
            num_scalar_prefetch=1,
            grid=(micro, own_heads),
            in_specs=[at["query"], at["key"], at["value"], at["query"], at["query"]]
            + [at["rows"]] * 4,
            out_specs=[at["query"], at["key"], at["key"], at["rows"]],
        ),
        out_shape=[shape(query.shape, bf16)]
        + [shape((total_rows, own_heads * HDIM), bf16)] * 2
        + [shape((total_rows, HDIM), f32)],
        compiler_params=pltpu.CompilerParams(vmem_limit_bytes=48 * 2**20),
        cost_estimate=pl.CostEstimate(
            flops=10 * rows * rows * HDIM * micro * HEADS,
            bytes_accessed=14 * query.size,
            transcendentals=rows * rows * micro * HEADS,
        ),
        name="attention_backward",
    )(lens, query, key, joint_kv, vals, vals_grad, tables[0], tables[1], gates, total)


def normalize(values):
    row_scale = lax.rsqrt(jnp.mean(values * values, axis=-1, keepdims=True) + eps_norm)
    return values * row_scale, row_scale


def norm_back(grad_hat, normed, row_scale):
    return row_scale * (grad_hat - normed * jnp.mean(grad_hat * normed, axis=-1, keepdims=True))


def route_gates(logits, routes, expert_table):
    expert_ids = jnp.arange(expert_table.shape[0], dtype=jnp.int32)
    matches = routes[:, :, None] == expert_ids[None, None, :]
    picked = jnp.sum(jnp.where(matches, logits[:, None, :], 0.0), axis=-1)
    gate_vals = jax.nn.softmax(picked, axis=-1)
    slot_ids = route_slots(routes, expert_table)
    chosen = slot_ids[:, :, None] == expert_ids[None, None, :]
    gates = jnp.sum(jnp.where(chosen, gate_vals[:, :, None], 0.0), axis=1)
    return gates, matches, chosen, gate_vals


def route_slots(routes, expert_table):
    expert_ids = jnp.arange(expert_table.shape[0], dtype=jnp.int32)
    matches = routes[..., None] == expert_ids
    return jnp.sum(jnp.where(matches, expert_table, 0), axis=-1)


def gate_back(slot_grad, gate_vals, matches, chosen):
    picked = jnp.sum(jnp.where(chosen, slot_grad[:, None, :], 0.0), axis=-1)
    inner_sum = jnp.sum(gate_vals * picked, axis=-1, keepdims=True)
    picked_grad = gate_vals * (picked - inner_sum)
    return jnp.sum(jnp.where(matches, picked_grad[:, :, None], 0.0), axis=1)


def unit_blocks(count):
    return [(start, min(512, count - start)) for start in range(0, count, 512)]


def expert_kernel(place_ref, hidden, grad, *refs):
    piece_count = (len(refs) - 6) // 2
    own_pieces, near_pieces = refs[:piece_count], refs[piece_count : 2 * piece_count]
    out, hidden_out, act_out, joint_out, weights, sems = refs[2 * piece_count :]
    core, chip = place_ref[0], place_ref[1]
    rows, columns = near_pieces[0].shape
    units = columns // 3
    width = grad.shape[1]

    @pl.when(pl.program_id(0) == 0)
    def _():
        copies = []
        for k in range(piece_count):
            base = (chip ^ k) * (2 * rows)
            for number, (piece, part) in enumerate(
                ((own_pieces[k], core), (near_pieces[k], 1 - core))
            ):
                start = pl.multiple_of(base + part * rows, 16)
                copies.append(
                    pltpu.make_async_copy(
                        piece, weights.at[pl.ds(start, rows)], sems.at[2 * k + number]
                    )
                )
        for copy in copies:
            copy.start()
        for copy in copies:
            copy.wait()

    slot_sum = jnp.zeros((hidden.shape[0], 1), f32)
    for start, size in unit_blocks(units):
        gate_pre = dot(hidden[:, :width], weights[:, start : start + size])
        up_pre = dot(hidden[:, :width], weights[:, units + start : units + start + size])
        act_grad = dot(grad[...], weights[:, 2 * units + start : 2 * units + start + size])
        sigma = 1.0 / (1.0 + jnp.exp(-gate_pre))
        silu_vals = gate_pre * sigma
        active = (silu_vals * up_pre).astype(bf16)
        act_out[:, start : start + size] = active
        slot_sum += jnp.sum(active.astype(f32) * act_grad, axis=1, keepdims=True)
        gate_grad = act_grad * up_pre * sigma * (1.0 + gate_pre * (1.0 - sigma))
        joint_out[:, start : start + size] = gate_grad.astype(bf16)
        joint_out[:, units + start : units + start + size] = (act_grad * silu_vals).astype(bf16)
    for start in range(0, width, 512):
        block = weights[start : start + 512, : 2 * units]
        hidden_out[:, start : start + 512] = dot_t(joint_out[...], block).astype(bf16)
        block = weights[start : start + 512, 2 * units :]
        out[:, start : start + 512] = dot_t(act_out[...], block).astype(bf16)
    lanes = lax.broadcasted_iota(jnp.int32, (hidden.shape[0], HDIM), 1)
    hidden_out[:, width:] = jnp.where(lanes == 0, slot_sum, 0.0).astype(bf16)


def expert_rows(position, hidden, grad, own_pieces, near_pieces):
    rows, width = grad.shape
    columns = near_pieces[0].shape[1]
    units = columns // 3
    tile = rows // 2
    shape = jax.ShapeDtypeStruct
    count = len(own_pieces)

    def tiled(size):
        return pl.BlockSpec((tile, size), lambda i, at: (i, 0))

    return pl.pallas_call(
        expert_kernel,
        grid_spec=pltpu.PrefetchScalarGridSpec(
            num_scalar_prefetch=1,
            grid=(rows // tile,),
            in_specs=[tiled(width + HDIM), tiled(width)]
            + [pl.BlockSpec(memory_space=pl.ANY)] * (2 * count),
            out_specs=[tiled(width), tiled(width + HDIM), tiled(units), tiled(2 * units)],
            scratch_shapes=[
                pltpu.VMEM((width, columns), bf16),
                pltpu.SemaphoreType.DMA((2 * count,)),
            ],
        ),
        out_shape=[
            shape((rows, width), bf16),
            shape((rows, width + HDIM), bf16),
            shape((rows, units), bf16),
            shape((rows, 2 * units), bf16),
        ],
        compiler_params=pltpu.CompilerParams(vmem_limit_bytes=56 * 2**20),
        cost_estimate=pl.CostEstimate(
            flops=4 * rows * width * columns,
            bytes_accessed=2 * (width * columns + 6 * rows * width),
            transcendentals=rows * units,
        ),
        name="expert_rows",
    )(position, hidden, grad, *own_pieces, *near_pieces)


def expert_grad_kernel(cuts, order, *refs):
    hidden, grad, gates, joint, active = [refs[2 * n : 2 * n + 2] for n in range(5)]
    outs = refs[10:]
    units = active[0].shape[1]

    def scaled(blocks):
        return [
            (block[...].astype(f32) * gate[:, :1].astype(f32)).astype(bf16)
            for block, gate in zip(blocks, gates)
        ]

    left, right = scaled(hidden), scaled(grad)
    step = pl.program_id(0)
    first = [0]
    for cut in cuts:
        first.append(first[-1] + cut)
    for out, start, cut in zip(outs, first, cuts):

        @pl.when((step >= start) & (step < start + cut))
        def _():
            for start, size in unit_blocks(2 * units):
                out[:, start : start + size] = sum(
                    t_dot(rows, part[:, start : start + size]) for rows, part in zip(left, joint)
                ).astype(bf16)
            for start, size in unit_blocks(units):
                out[:, 2 * units + start : 2 * units + start + size] = sum(
                    t_dot(rows, part[:, start : start + size]) for rows, part in zip(right, active)
                ).astype(bf16)


def expert_grads(chunks, cuts, chunk_rows, rows_of, joints, actives):
    hidden, grad = rows_of[:2], rows_of[2:]
    rows, units = actives[0].shape
    width = grad[0].shape[1]
    half = chunk_rows // 2
    count = len(chunks)
    order = jnp.stack([2 * chunk + part for chunk in chunks for part in range(2)]).astype(jnp.int32)

    def whole(size, column=0):
        return pl.BlockSpec(
            (rows, size), lambda i, at: (0, column), pipeline_mode=pl.Buffered(1)
        )

    column = pl.BlockSpec((rows, half), lambda i, at: (0, at[i]))
    return pl.pallas_call(
        functools.partial(expert_grad_kernel, cuts),
        grid_spec=pltpu.PrefetchScalarGridSpec(
            num_scalar_prefetch=1,
            grid=(2 * count,),
            in_specs=[column] * 4
            + [whole(HDIM, width // HDIM)] * 2
            + [whole(2 * units)] * 2
            + [whole(units)] * 2,
            out_specs=[
                pl.BlockSpec(
                    (half, 3 * units),
                    lambda i, at, start=sum(cuts[:n]), cut=cut: (jnp.clip(i - start, 0, cut - 1), 0),
                )
                for n, cut in enumerate(cuts)
            ],
        ),
        out_shape=[jax.ShapeDtypeStruct((cut * half, 3 * units), bf16) for cut in cuts],
        compiler_params=pltpu.CompilerParams(vmem_limit_bytes=56 * 2**20),
        cost_estimate=pl.CostEstimate(
            flops=4 * count * chunk_rows * rows * 3 * units,
            bytes_accessed=2 * (rows * 6 * units + count * chunk_rows * (4 * rows + 3 * units)),
            transcendentals=0,
        ),
        name="expert_grads",
    )(order, *hidden, *grad, *hidden, *joints, *actives)


def local(
    tokens,
    cotangent,
    seq_lengths,
    dealing,
    attn_routes,
    ffn_routes,
    expert_table,
    clip_limit,
    attn_gain,
    ffn_gain,
    attn_router,
    ffn_router,
    query_weight,
    attn_out_weight,
    kv_weight,
    gate_up_weight,
    down_weight,
):
    micro, tok_rows, width = tokens.shape
    dp_count = lax.axis_size("dp")
    slots = lax.axis_size("expert")
    col = lax.axis_index("expert")
    group = lax.axis_index("dp")
    piece_rows = tok_rows // dp_count
    cap = tok_rows * TOP * 3 // (2 * slots)
    group_rows = tok_rows * slots
    all_rows = micro * group_rows
    home_rows = micro * tok_rows
    query_width = HEADS * HDIM
    own_heads = HEADS // slots
    own_width = own_heads * HDIM
    shard_rows = query_weight.shape[1]
    score_scale = HDIM ** (-0.5)
    core = group % 2
    chip = group // 2
    side = chip % 2
    chips = dp_count // 2
    lines = chips // 2
    quarter = FF // 4
    chip_rows = 2 * shard_rows

    both = jnp.stack([tokens, cotangent]).reshape(2 * micro, dp_count, piece_rows, width)
    both = lax.all_to_all(both.transpose(1, 0, 2, 3), "dp", split_axis=0, concat_axis=0, tiled=True)
    def quarter_of(half, part):
        start = (2 * half + part) * quarter
        return jnp.concatenate(
            [
                lax.dynamic_slice_in_dim(gate_up_weight[0], start, quarter, 1),
                lax.dynamic_slice_in_dim(gate_up_weight[0], FF + start, quarter, 1),
                lax.dynamic_slice_in_dim(down_weight[0], start, quarter, 1),
            ],
            axis=1,
        )

    parts = (1 - core, core)
    keep_pair = [quarter_of(side, part) for part in parts]
    send_pair = [quarter_of(1 - side, part) for part in parts]
    kv_in, query_in, out_in = after(
        (kv_weight, query_weight[0], attn_out_weight[0]), keep_pair[0], send_pair[0]
    )
    both = both.transpose(1, 0, 2, 3).reshape(2, micro, tok_rows, width)
    deal = (dealing[:, :, None] == jnp.arange(tok_rows, dtype=jnp.int32)).astype(bf16)
    work = jnp.einsum("mtr,bmrd->bmtd", deal, both, preferred_element_type=f32)
    x_home = work[0].reshape(home_rows, width)
    dy_home = work[1].reshape(home_rows, width)

    def columns_of(*shards):
        pieces = [shard.reshape(shard_rows, slots, own_width) for shard in shards]
        out = jnp.zeros((shard_rows, len(shards) * query_width), shards[0].dtype)
        for k in range(slots):
            part = jnp.concatenate(
                [lax.dynamic_index_in_dim(piece, col ^ k, 1, keepdims=False) for piece in pieces],
                axis=1,
            )
            part = swap(part, "expert", k) if k else part
            for number in range(len(shards)):
                out = lax.dynamic_update_slice_in_dim(
                    out,
                    part[:, number * own_width : (number + 1) * own_width],
                    number * query_width + (col ^ k) * own_width,
                    1,
                )
        return out

    def slots_of(columns):
        pieces = columns.reshape(shard_rows, slots, own_width)
        out = jnp.zeros((shard_rows, query_width), columns.dtype)
        for k in range(slots):
            part = lax.dynamic_index_in_dim(pieces, col ^ k, 1, keepdims=False)
            part = swap(part, "expert", k) if k else part
            out = lax.dynamic_update_slice_in_dim(out, part, (col ^ k) * own_width, 1)
        return out

    half_slots = slots // 2
    first_pairs = [(c, 2 * c) for c in range(half_slots)]
    first_pairs += [(c, 2 * (c - half_slots) + 1) for c in range(half_slots, slots)]
    second_pairs = [(c, 2 * c + 1) for c in range(half_slots)]
    second_pairs += [(c, 2 * (c - half_slots)) for c in range(half_slots, slots)]
    holds_keys = col < half_slots
    even_col = col % 2 == 0
    low_kv, high_kv = kv_in[:, :own_width], kv_in[:, own_width:]
    first_got = lax.ppermute(jnp.where(holds_keys, low_kv, high_kv), "expert", first_pairs)
    second_got = lax.ppermute(jnp.where(holds_keys, high_kv, low_kv), "expert", second_pairs)
    own_kv = jnp.concatenate(
        [
            jnp.where(even_col, first_got, second_got),
            jnp.where(even_col, second_got, first_got),
        ],
        axis=1,
    )
    line_steps = [4 * line for line in range(1, lines)]
    side_first = swap(send_pair[0], "dp", 2)
    keep_first = [swap(keep_pair[0], "dp", step) for step in line_steps]
    joint_own = columns_of(query_in, out_in)
    first_own = jnp.concatenate([joint_own[:, :query_width], own_kv], axis=1)
    first_own, second_own = lax.optimization_barrier(
        (first_own, joint_own[:, query_width:], side_first, keep_first)
    )[:2]
    joint_full = lax.all_gather(first_own, "dp", axis=0, tiled=True)
    out_full = lax.all_gather(second_own, "dp", axis=0, tiled=True)
    late_pair = after((keep_pair[1], send_pair[1], side_first), joint_full)
    keep_second = [swap(late_pair[0], "dp", step) for step in line_steps]
    side_second = swap(late_pair[1], "dp", 2)
    first_lines = [swap(late_pair[2], "dp", step) for step in line_steps]
    second_lines = [swap(side_second, "dp", step) for step in line_steps]
    firsts, seconds = [keep_pair[0], side_first], [keep_pair[1], side_second]
    for line in range(lines - 1):
        firsts += [keep_first[line], first_lines[line]]
        seconds += [keep_second[line], second_lines[line]]
    near_pieces = [swap(piece, "dp", 1) for piece in firsts]
    own_pieces = seconds
    query_full = joint_full[:, :query_width]
    kv_full = joint_full[:, query_width:]

    positions = jnp.arange(group_rows, dtype=jnp.int32)
    first_len = lax.dynamic_index_in_dim(seq_lengths[:, :, 0], group, 1, keepdims=True)
    in_second = positions[None, :] >= first_len
    places = positions[None, :] - jnp.where(in_second, first_len, 0)
    tables = rotation_tables(places.reshape(all_rows))

    def gather_rows(value):
        shaped = value.reshape(micro, tok_rows, -1)
        out = jnp.zeros((micro, group_rows, shaped.shape[-1]), value.dtype)
        for k in range(slots):
            part = swap(shaped, "expert", k) if k else shaped
            out = lax.dynamic_update_slice_in_dim(out, part, (col ^ k) * tok_rows, 1)
        return out.reshape(all_rows, -1)

    def scatter_rows(value):
        shaped = value.reshape(micro, group_rows, -1)
        total = None
        for k in range(slots):
            part = lax.dynamic_slice_in_dim(shaped, (col ^ k) * tok_rows, tok_rows, 1)
            if k:
                part = swap(part.astype(bf16), "expert", k)
            part = part.astype(f32)
            total = part if total is None else total + part
        return total.reshape(home_rows, -1)

    home_routes = lax.dynamic_slice_in_dim(ffn_routes, col * tok_rows, tok_rows, 1)
    home_slots = route_slots(home_routes, expert_table)
    packs = []
    before = jnp.tril(jnp.ones((tok_rows, tok_rows), bf16), -1)
    for k in range(slots):
        hits = jnp.any(home_slots == (col ^ k), axis=-1)
        rank = jnp.einsum("ts,ms->mt", before, hits.astype(bf16), preferred_element_type=f32)
        packs.append(
            hits[:, None, :]
            & (rank[:, None, :] == jnp.arange(cap, dtype=jnp.int32).astype(f32)[None, :, None])
        )
    packs = jnp.stack(packs)
    packs_low = packs.astype(bf16)
    pack_rows = micro * cap
    sent_rows = slots * pack_rows

    def send_packed(value, lane=None):
        packed = jnp.einsum(
            "kmct,mtd->kmcd", packs_low, value.reshape(micro, tok_rows, -1), preferred_element_type=f32
        ).astype(bf16)
        if lane is not None:
            lanes = jnp.pad(lane[..., None], ((0, 0), (0, 0), (0, 0), (0, HDIM - 1)))
            packed = jnp.concatenate([packed, lanes.astype(bf16)], axis=-1)
        parts = [swap(packed[k], "expert", k) if k else packed[k] for k in range(slots)]
        return jnp.stack(parts).reshape(sent_rows, -1)

    def near_rows(value):
        return jnp.concatenate([value, swap(value, "dp", 1)], axis=0)

    def quad_sums(value):
        (own, near), (far, across) = [jnp.split(half, 2, axis=0) for half in value]
        far_sum = far.astype(f32) + swap(across, "dp", 1).astype(f32)
        return own.astype(f32) + swap(near, "dp", 1).astype(f32), far_sum.astype(bf16)

    def return_packed(value, *others):
        shaped = value.astype(bf16).reshape(slots, micro, cap, -1)
        parts = [swap(shaped[k], "expert", k) if k else shaped[k] for k in range(slots)]
        return after(parts, *others)

    def unpack(packed, scale):
        total = None
        for k in range(slots):
            rows = jnp.einsum("mct,mcd->mtd", packs_low[k], packed[k], preferred_element_type=f32)
            rows = rows.reshape(home_rows, -1) * take(scale.T, col ^ k)[:, None]
            total = rows if total is None else total + rows
        return total

    gain_one = attn_gain.astype(f32)
    gain_two = ffn_gain.astype(f32)
    normed_one, scale_one = normalize(x_home)
    hidden_one_home = (normed_one * gain_one).astype(bf16)
    hidden_one_raw = gather_rows(after(hidden_one_home, near_pieces[:3]))
    grad_sent = send_packed(dy_home.astype(bf16))
    hidden_one = after(hidden_one_raw, grad_sent)
    logits_one = dot(hidden_one, attn_router)
    gates_one, matches_one, chosen_one, gate_vals_one = route_gates(
        logits_one, attn_routes.reshape(all_rows, TOP), expert_table
    )
    hits_one = jnp.any(chosen_one, axis=1).astype(f32)

    def wide(value):
        return jnp.pad(value, ((0, 0), (0, HDIM - value.shape[1])))

    kv_part = dot(hidden_one, kv_full).astype(bf16)
    query_part = dot(hidden_one, query_full)
    lens = first_len[:, 0].astype(jnp.int32)
    gates_wide = wide(gates_one)
    attn_vals, gated_vals, query_rot, key_rot, log_total, peaks = attention_forward(
        lens, query_part, kv_part, tables, gates_wide, wide(hits_one), own_heads, group_rows
    )
    peaks = jnp.max(peaks, axis=0)[: own_heads * slots]
    attn_part = after(dot_t(gated_vals, out_full), keep_second, side_second)
    attn_home = after(scatter_rows(attn_part), first_lines)
    grad_sent = after(grad_sent, attn_home)
    grad_near, grad_far = near_rows(grad_sent), near_rows(swap(grad_sent, "dp", 2))

    resid = x_home + attn_home
    normed_two, scale_two = normalize(resid)
    hidden_two = (normed_two * gain_two).astype(bf16)
    logits_two = dot(hidden_two, ffn_router)
    gates_two, matches_two, chosen_two, gate_vals_two = route_gates(
        logits_two, home_routes.reshape(home_rows, TOP), expert_table
    )
    gates_by_slot = gates_two.reshape(micro, tok_rows, slots)
    gate_parts = []
    for k in range(slots):
        gate_col = lax.dynamic_index_in_dim(gates_by_slot, col ^ k, 2, keepdims=False)
        gate_parts.append(jnp.sum(jnp.where(packs[k], gate_col[:, None, :], 0.0), axis=-1))
    hidden_sent = after(
        send_packed(hidden_two, jnp.stack(gate_parts)), second_lines
    )
    hidden_near, hidden_far = near_rows(hidden_sent), swap(hidden_sent, "dp", 2)
    hidden_near = after(hidden_near, near_pieces, grad_near, grad_far)
    position = jnp.stack([core, chip]).astype(jnp.int32)
    near_results = expert_rows(
        position, hidden_near, after(grad_near, grad_far), own_pieces, near_pieces
    )
    hidden_far = near_rows(after(hidden_far, near_results))
    far_results = expert_rows(position, hidden_far, grad_far, own_pieces, near_pieces)
    ffn_parts, hidden_parts, actives, joint_grads = zip(near_results, far_results)

    def block_grads(steps, *others):
        rows = after((hidden_near, hidden_far, grad_near, grad_far), *others)
        cuts = (2,) * len(steps)
        return expert_grads([chip ^ k for k in steps], cuts, chip_rows, rows, joint_grads, actives)

    hidden_sum, hidden_far_sum = quad_sums(hidden_parts)
    ffn_sum, ffn_far_sum = quad_sums(after(ffn_parts, hidden_far_sum))
    line_grads = block_grads([k ^ 1 for k in range(2, chips)], hidden_far_sum)
    side_got = [swap(line_grads[2 * line], "dp", step) for line, step in enumerate(line_steps)]
    blocks = after(line_grads[1::2], side_got)
    keep_got = [swap(block, "dp", step) for block, step in zip(blocks, line_steps)]
    hidden_got, ffn_far_sum, ffn_sum = lax.optimization_barrier(
        (swap(hidden_far_sum, "dp", 2), ffn_far_sum, ffn_sum, line_grads)
    )[:3]
    hidden_sum = hidden_sum + hidden_got.astype(f32)
    own_grads = block_grads([1, 0], hidden_sum)
    back_packed = return_packed(hidden_sum, *own_grads)
    ffn_sum = ffn_sum + swap(after(ffn_far_sum, hidden_got), "dp", 2).astype(f32)

    def total(own, got):
        return functools.reduce(jnp.add, [part.astype(f32) for part in [own] + got]).astype(bf16)

    slot_two_grad = jnp.zeros((slots, home_rows), f32)
    for k in range(slots):
        rows = jnp.sum(
            jnp.where(packs[k], back_packed[k][:, :, width].astype(f32)[:, :, None], 0.0), axis=1
        )
        slot_two_grad = lax.dynamic_update_index_in_dim(
            slot_two_grad, rows.reshape(home_rows), col ^ k, 0
        )
    hidden_two_grad = unpack([part[..., :width] for part in back_packed], gates_two)
    logit_two_grad = gate_back(slot_two_grad.T, gate_vals_two, matches_two, chosen_two).astype(bf16)
    hidden_two_grad = hidden_two_grad + dot_t(logit_two_grad, ffn_router)
    router_two_grad = t_dot(logit_two_grad, hidden_two)
    gain_two_grad = jnp.sum(hidden_two_grad * normed_two, axis=0)
    resid_grad = dy_home + norm_back(hidden_two_grad * gain_two, normed_two, scale_two)

    resid_grad_all, ffn_sum = lax.optimization_barrier(
        (gather_rows(resid_grad.astype(bf16)), ffn_sum, side_got)
    )[:2]
    out_part = t_dot(resid_grad_all, gated_vals).astype(bf16)
    vals_grad = after(dot(resid_grad_all, out_full), out_part)
    side_own = after((own_grads[0], side_got), vals_grad)
    vals_grad, side_sum = lax.optimization_barrier((vals_grad, total(*side_own)))
    other_sum = swap(side_sum, "dp", 2)
    ffn_packed = return_packed(after(ffn_sum, vals_grad))
    out_home = (resid + unpack(ffn_packed, gates_two)).astype(bf16)
    query_grad, key_grad, value_grad, slot_part_one = attention_backward(
        lens, query_rot, key_rot, kv_part, attn_vals, vals_grad, tables, gates_wide, log_total,
        own_heads, group_rows,
    )
    query_grad, key_grad, value_grad, slot_part_one = lax.optimization_barrier(
        (query_grad, key_grad, value_grad, slot_part_one, ffn_packed)
    )[:4]
    kv_grad = jnp.concatenate([key_grad, value_grad], axis=1)
    hidden_one_part = dot_t(query_grad, query_full) + dot_t(kv_grad, kv_full)
    hidden_one_part = hidden_one_part.astype(bf16)
    joint_part_grad = t_dot(
        after(hidden_one, hidden_one_part), jnp.concatenate([query_grad, kv_grad], axis=1)
    ).astype(bf16)
    back_one = scatter_rows(
        jnp.concatenate([hidden_one_part, slot_part_one.astype(bf16)], axis=1)
    )
    back_one, other_sum, keep_got = lax.optimization_barrier(
        (back_one, other_sum, keep_got, joint_part_grad)
    )[:3]
    hidden_one_grad, slot_one_grad = back_one[:, :width], back_one[:, width : width + slots]

    def own(value):
        shaped = value.reshape((micro, group_rows) + value.shape[1:])
        part = lax.dynamic_slice_in_dim(shaped, col * tok_rows, tok_rows, 1)
        return part.reshape((home_rows,) + value.shape[1:])

    logit_one_grad = gate_back(
        slot_one_grad, own(gate_vals_one), own(matches_one), own(chosen_one)
    ).astype(bf16)
    hidden_one_grad = hidden_one_grad + dot_t(logit_one_grad, attn_router)
    router_one_grad = t_dot(logit_one_grad, hidden_one_home)
    gain_one_grad = jnp.sum(hidden_one_grad * normed_one, axis=0)
    in_home = resid_grad + norm_back(hidden_one_grad * gain_one, normed_one, scale_one)

    def reduced(value):
        return lax.psum_scatter(value, "dp", scatter_dimension=0, tiled=True)

    in_low, keep_got, other_sum = lax.optimization_barrier(
        (in_home.astype(bf16), keep_got, other_sum)
    )
    out_grad = slots_of(after(reduced(out_part), back_one))
    joint_own = reduced(joint_part_grad)

    results = jnp.stack([out_home, in_low]).reshape(2, micro, tok_rows, width)
    results = jnp.einsum("mtr,bmtd->bmrd", deal, results, preferred_element_type=f32).astype(bf16)
    results = results.reshape(2 * micro, dp_count, piece_rows, width).transpose(1, 0, 2, 3)
    results = results.reshape(dp_count, 2 * micro * piece_rows, width)
    sent_back = results.shape[1]
    small = jnp.concatenate(
        [gain_one_grad[None], gain_two_grad[None], router_one_grad, router_two_grad], axis=0
    ).astype(bf16)
    sum_rows = small.shape[0]
    peak_count = own_heads * slots
    peak_parts, rest = [], peaks
    for _ in range(3):
        peak_parts.append(lax.reduce_precision(rest, 8, 7))
        rest = rest - peak_parts[-1]
    peak_row = jnp.concatenate(peak_parts).astype(bf16)
    small = jnp.pad(small, ((0, -sum_rows % 16 or 16), (0, 0)))
    small = lax.dynamic_update_slice(small, peak_row[None], (sum_rows, 0))
    small = jnp.broadcast_to(small[None], (dp_count,) + small.shape)
    results = jnp.concatenate([results, small], axis=1)
    results = lax.all_to_all(results, "dp", split_axis=0, concat_axis=0, tiled=True)
    results, out_grad, joint_own = lax.optimization_barrier((results, out_grad, joint_own))
    query_own, kv_own = joint_own[:, :query_width], joint_own[:, query_width:]
    small = results[:, sent_back:].astype(f32)
    results = results[:, :sent_back].reshape(dp_count, 2 * micro, piece_rows, width)
    results = results.transpose(1, 0, 2, 3).reshape(2, micro, tok_rows, width)
    peak_row = small[:, sum_rows, : 3 * peak_count].reshape(dp_count, 3, peak_count)
    peak_row = jnp.max((peak_row[:, 0] + peak_row[:, 1]) + peak_row[:, 2], axis=0)
    small = jnp.sum(small, axis=0)
    small = lax.dynamic_update_slice(small, peak_row[None], (sum_rows, 0))
    smalls = [swap(small, "expert", k) if k else small for k in range(slots)]
    peaks_all = jnp.zeros((slots, HEADS), f32)
    for k, part in enumerate(smalls):
        part = part[sum_rows, :peak_count].reshape(own_heads, slots).T
        peaks_all = lax.dynamic_update_slice(peaks_all, part, (0, (col ^ k) * own_heads))
    while len(smalls) > 1:
        smalls = [left + right for left, right in zip(smalls[::2], smalls[1::2])]
    sums = smalls[0][:sum_rows]

    keep_sums = total(own_grads[1], keep_got).reshape(2, shard_rows, 3 * quarter)
    other_sums = other_sum.reshape(2, shard_rows, 3 * quarter)
    by_rows = [jnp.stack([keep_sums[part], other_sums[part]]) for part in range(2)]
    own_pair = jnp.where(core == 0, by_rows[0], by_rows[1])
    near_pair = swap(jnp.where(core == 0, by_rows[1], by_rows[0]), "dp", 1)
    by_core = [jnp.where(core == 0, own_pair, near_pair), jnp.where(core == 0, near_pair, own_pair)]
    by_side = [[jnp.where(side == s, part[0], part[1]) for part in by_core] for s in range(2)]
    blocks = [part for row in by_side for part in row]
    gate_up_grad = jnp.concatenate(
        [b[:, :quarter] for b in blocks] + [b[:, quarter : 2 * quarter] for b in blocks], axis=1
    ).astype(f32)
    down_grad = jnp.concatenate([b[:, 2 * quarter :] for b in blocks], axis=1).astype(f32)

    out_grad = out_grad.astype(f32)
    query_out = slots_of(query_own).astype(f32)
    key_part, value_part = kv_own[:, :own_width], kv_own[:, own_width:]
    first_back = lax.ppermute(
        jnp.where(even_col, key_part, value_part), "expert", [(b, a) for a, b in first_pairs]
    )
    second_back = lax.ppermute(
        jnp.where(even_col, value_part, key_part), "expert", [(b, a) for a, b in second_pairs]
    )
    kv_out = jnp.concatenate(
        [
            jnp.where(holds_keys, first_back, second_back),
            jnp.where(holds_keys, second_back, first_back),
        ],
        axis=1,
    ).astype(f32)

    limit = clip_limit[0].astype(f32)
    factor = limit / jnp.maximum(peaks_all, limit)
    query_scale = jnp.repeat(jnp.sqrt(take(factor, col)), HDIM)
    query_clipped = (query_weight.astype(f32) * query_scale[None, None, :]).astype(bf16)
    full_scale = jnp.concatenate(
        [jnp.repeat(jnp.sqrt(jnp.min(factor, axis=0)), HDIM), jnp.ones((query_width,), f32)]
    )
    piece_width = kv_weight.shape[1]
    piece_scale = lax.dynamic_slice_in_dim(full_scale, col * piece_width, piece_width)
    kv_clipped = (kv_weight.astype(f32) * piece_scale[None, :]).astype(bf16)
    return (
        results[0],
        results[1],
        sums[0],
        sums[1],
        sums[2 : 2 + slots].T,
        sums[2 + slots : sum_rows].T,
        query_out[None],
        out_grad[None],
        kv_out,
        gate_up_grad[None],
        down_grad[None],
        query_clipped,
        kv_clipped,
    )


def solution(mesh):
    placed = (
        P(None, ("dp", "expert"), None),
        P(None, ("dp", "expert"), None),
        P(),
        P(None, ("dp", "expert")),
        P(None, "dp", None),
        P(None, "dp", None),
        P(),
        P(),
        P(),
        P(),
        P(),
        P(),
        P("expert", "dp", None),
        P("expert", "dp", None),
        P("dp", "expert"),
        P("expert", "dp", None),
        P("expert", "dp", None),
    )
    return jax.shard_map(
        local,
        mesh=mesh,
        in_specs=placed,
        out_specs=(
            P(None, ("dp", "expert"), None),
            P(None, ("dp", "expert"), None),
            P(),
            P(),
            P(),
            P(),
            P("expert", "dp", None),
            P("expert", "dp", None),
            P("dp", "expert"),
            P("expert", "dp", None),
            P("expert", "dp", None),
            P("expert", "dp", None),
            P("dp", "expert"),
        ),
        check_vma=False,
    )
```

```python
import functools

import jax
import jax.numpy as jnp
from jax import lax
from jax.experimental import pallas as pl
from jax.experimental.pallas import tpu as pltpu
from jax.sharding import PartitionSpec as P

HEADS = 16
HDIM = 128
FF = 5632
TOP = 2

eps_norm = 1e-06
rope_base = 10000.0
very_low = -1e30

f32 = jnp.float32
bf16 = jnp.bfloat16


def dot(left, right):
    return jnp.dot(left, right, preferred_element_type=f32)


def dot_t(left, right):
    return lax.dot_general(left, right, (((1,), (1,)), ((), ())), preferred_element_type=f32)


def t_dot(left, right):
    return lax.dot_general(left, right, (((0,), (0,)), ((), ())), preferred_element_type=f32)


def swap(value, axis, step):
    count = lax.axis_size(axis)
    return lax.ppermute(value, axis, [(i, i ^ step) for i in range(count)])


def take(stacked, index):
    return lax.dynamic_index_in_dim(stacked, index, 0, keepdims=False)


def place(parts, positions):
    out = jnp.zeros((len(parts),) + parts[0].shape, parts[0].dtype)
    for part, position in zip(parts, positions):
        out = lax.dynamic_update_index_in_dim(out, part, position, 0)
    return out


def after(value, *others):
    return lax.optimization_barrier((value, others))[0]


def rotation_tables(places):
    half_dim = HDIM // 2
    frequency = rope_base ** (-jnp.arange(half_dim, dtype=f32) * 2.0 / HDIM)
    angles = places.astype(f32)[:, None] * frequency[None, :]
    cosine, sine = jnp.cos(angles), jnp.sin(angles)
    return (
        jnp.concatenate([cosine, cosine], axis=1),
        jnp.concatenate([-sine, sine], axis=1),
    )


def turn(values, cosine, sine):
    return values * cosine + pltpu.roll(values, HDIM // 2, 1) * sine


def lane_value(table, lane):
    lanes = lax.broadcasted_iota(jnp.int32, table.shape, 1)
    return jnp.sum(jnp.where(lanes == lane, table, 0.0), axis=1, keepdims=True)


def allowed_pairs(rows, first_len):
    query_at = lax.broadcasted_iota(jnp.int32, (rows, rows), 0)
    key_at = lax.broadcasted_iota(jnp.int32, (rows, rows), 1)
    return (key_at <= query_at) & ((key_at >= first_len) | (query_at < first_len))


def forward_kernel(
    lens, query, key, value, cosine, sine, gates, hits,
    vals_out, gated_out, query_out, key_out, total_out, peak_out,
):
    m, h = pl.program_id(0), pl.program_id(1)
    heads = pl.num_programs(1)
    rows = query.shape[0]
    slots = query.shape[1] // (heads * HDIM)

    @pl.when(h == 0)
    def _():
        total_out[...] = jnp.zeros_like(total_out)
        peak_out[...] = jnp.full_like(peak_out, very_low)

    cos_part, sin_part = cosine[...], sine[...]
    allowed = allowed_pairs(rows, lens[m])
    keys = turn(key[...].astype(f32), cos_part, sin_part).astype(bf16)
    key_out[...] = keys
    values = value[...]
    lanes = lax.broadcasted_iota(jnp.int32, total_out.shape, 1)
    peak_lanes = lax.broadcasted_iota(jnp.int32, peak_out.shape, 1)
    totals, peaks = total_out[...], peak_out[...]
    for s in range(slots):
        columns = pl.ds(pl.multiple_of((s * heads + h) * HDIM, HDIM), HDIM)
        turned = turn(query[:, columns], cos_part, sin_part).astype(bf16)
        query_out[:, columns] = turned
        scores = jnp.where(allowed, dot_t(turned, keys) * HDIM ** (-0.5), very_low)
        row_peak = jnp.max(scores, axis=1, keepdims=True)
        expo = jnp.exp(scores - row_peak)
        denom = jnp.sum(expo, axis=1, keepdims=True)
        probs = expo * (1.0 / denom)
        vals = dot(probs.astype(bf16), values).astype(bf16)
        vals_out[:, columns] = vals
        gated_out[:, columns] = (gates[:, s : s + 1] * vals.astype(f32)).astype(bf16)
        lane = h * slots + s
        totals = jnp.where(lanes == lane, row_peak + jnp.log(denom), totals)
        seen = jnp.where(hits[:, s : s + 1] > 0.0, row_peak, very_low)
        peaks = jnp.where(peak_lanes == lane, jnp.max(seen, axis=0, keepdims=True), peaks)
    total_out[...] = totals
    peak_out[...] = peaks


def backward_kernel(
    lens, query, key, value, vals, vals_grad, cosine, sine, gates, total,
    query_grad, key_grad, value_grad, gate_grad,
):
    m, h = pl.program_id(0), pl.program_id(1)
    heads = pl.num_programs(1)
    rows = query.shape[0]
    slots = query.shape[1] // (heads * HDIM)

    @pl.when(h == 0)
    def _():
        gate_grad[...] = jnp.zeros_like(gate_grad)

    allowed = allowed_pairs(rows, lens[m])
    cos_part, back_sine = cosine[...], -sine[...]
    keys, values, totals = key[...], value[...], total[...]
    lanes = lax.broadcasted_iota(jnp.int32, gate_grad.shape, 1)
    slot_sums = gate_grad[...]
    key_sum = jnp.zeros(key.shape, f32)
    value_sum = jnp.zeros(value.shape, f32)
    for s in range(slots):
        columns = pl.ds(pl.multiple_of((s * heads + h) * HDIM, HDIM), HDIM)
        full_grad = vals_grad[:, columns]
        slot_sum = jnp.sum(vals[:, columns].astype(f32) * full_grad, axis=1, keepdims=True)
        slot_sums += jnp.where(lanes == s, slot_sum, 0.0)
        gated_grad = (gates[:, s : s + 1] * full_grad).astype(bf16)
        queries = query[:, columns]
        scores = jnp.where(allowed, dot_t(queries, keys) * HDIM ** (-0.5), very_low)
        probs = jnp.exp(scores - lane_value(totals, h * slots + s))
        prob_grad = dot_t(gated_grad, values)
        inner = jnp.sum(probs * prob_grad, axis=1, keepdims=True)
        score_grad = (probs * (prob_grad - inner) * HDIM ** (-0.5)).astype(bf16)
        query_grad[:, columns] = turn(dot(score_grad, keys), cos_part, back_sine).astype(bf16)
        key_sum += t_dot(score_grad, queries)
        value_sum += t_dot(probs.astype(bf16), gated_grad)
    gate_grad[...] = slot_sums
    key_grad[...] = turn(key_sum, cos_part, back_sine).astype(bf16)
    value_grad[...] = value_sum.astype(bf16)


def attention_specs(own_heads, rows, width):
    def block(columns, index):
        return pl.BlockSpec((rows, columns), index)

    return {
        "query": block(width, lambda m, h, lens: (m, 0)),
        "key": block(HDIM, lambda m, h, lens: (m, h)),
        "value": block(HDIM, lambda m, h, lens: (m, own_heads + h)),
        "rows": block(HDIM, lambda m, h, lens: (m, 0)),
        "peak": pl.BlockSpec((8, HDIM), lambda m, h, lens: (m, 0)),
    }


def attention_forward(lens, query, joint_kv, tables, gates, hits, own_heads, rows):
    micro = lens.shape[0]
    at = attention_specs(own_heads, rows, query.shape[1])
    shape = jax.ShapeDtypeStruct
    total_rows = micro * rows
    return pl.pallas_call(
        forward_kernel,
        grid_spec=pltpu.PrefetchScalarGridSpec(
            num_scalar_prefetch=1,
            grid=(micro, own_heads),
            in_specs=[at["query"], at["key"], at["value"]] + [at["rows"]] * 4,
            out_specs=[at["query"]] * 3 + [at["key"], at["rows"], at["peak"]],
        ),
        out_shape=[shape(query.shape, bf16)] * 3
        + [
            shape((total_rows, own_heads * HDIM), bf16),
            shape((total_rows, HDIM), f32),
            shape((micro * 8, HDIM), f32),
        ],
        compiler_params=pltpu.CompilerParams(vmem_limit_bytes=48 * 2**20),
        cost_estimate=pl.CostEstimate(
            flops=4 * rows * rows * HDIM * micro * HEADS,
            bytes_accessed=14 * query.size,
            transcendentals=rows * rows * micro * HEADS,
        ),
        name="attention_forward",
    )(lens, query, joint_kv, joint_kv, tables[0], tables[1], gates, hits)


def attention_backward(
    lens, query, key, joint_kv, vals, vals_grad, tables, gates, total, own_heads, rows
):
    micro = lens.shape[0]
    at = attention_specs(own_heads, rows, query.shape[1])
    shape = jax.ShapeDtypeStruct
    total_rows = micro * rows
    return pl.pallas_call(
        backward_kernel,
        grid_spec=pltpu.PrefetchScalarGridSpec(
            num_scalar_prefetch=1,
            grid=(micro, own_heads),
            in_specs=[at["query"], at["key"], at["value"], at["query"], at["query"]]
            + [at["rows"]] * 4,
            out_specs=[at["query"], at["key"], at["key"], at["rows"]],
        ),
        out_shape=[shape(query.shape, bf16)]
        + [shape((total_rows, own_heads * HDIM), bf16)] * 2
        + [shape((total_rows, HDIM), f32)],
        compiler_params=pltpu.CompilerParams(vmem_limit_bytes=48 * 2**20),
        cost_estimate=pl.CostEstimate(
            flops=10 * rows * rows * HDIM * micro * HEADS,
            bytes_accessed=14 * query.size,
            transcendentals=rows * rows * micro * HEADS,
        ),
        name="attention_backward",
    )(lens, query, key, joint_kv, vals, vals_grad, tables[0], tables[1], gates, total)


def normalize(values):
    row_scale = lax.rsqrt(jnp.mean(values * values, axis=-1, keepdims=True) + eps_norm)
    return values * row_scale, row_scale


def norm_back(grad_hat, normed, row_scale):
    return row_scale * (grad_hat - normed * jnp.mean(grad_hat * normed, axis=-1, keepdims=True))


def route_gates(logits, routes, expert_table):
    expert_ids = jnp.arange(expert_table.shape[0], dtype=jnp.int32)
    matches = routes[:, :, None] == expert_ids[None, None, :]
    picked = jnp.sum(jnp.where(matches, logits[:, None, :], 0.0), axis=-1)
    gate_vals = jax.nn.softmax(picked, axis=-1)
    slot_ids = route_slots(routes, expert_table)
    chosen = slot_ids[:, :, None] == expert_ids[None, None, :]
    gates = jnp.sum(jnp.where(chosen, gate_vals[:, :, None], 0.0), axis=1)
    return gates, matches, chosen, gate_vals


def route_slots(routes, expert_table):
    expert_ids = jnp.arange(expert_table.shape[0], dtype=jnp.int32)
    matches = routes[..., None] == expert_ids
    return jnp.sum(jnp.where(matches, expert_table, 0), axis=-1)


def gate_back(slot_grad, gate_vals, matches, chosen):
    picked = jnp.sum(jnp.where(chosen, slot_grad[:, None, :], 0.0), axis=-1)
    inner_sum = jnp.sum(gate_vals * picked, axis=-1, keepdims=True)
    picked_grad = gate_vals * (picked - inner_sum)
    return jnp.sum(jnp.where(matches, picked_grad[:, :, None], 0.0), axis=1)


def unit_blocks(count):
    return [(start, min(512, count - start)) for start in range(0, count, 512)]


def expert_kernel(place_ref, hidden, grad, *refs):
    piece_count = (len(refs) - 6) // 2
    own_pieces, near_pieces = refs[:piece_count], refs[piece_count : 2 * piece_count]
    out, hidden_out, act_out, joint_out, weights, sems = refs[2 * piece_count :]
    core, chip = place_ref[0], place_ref[1]
    rows, columns = near_pieces[0].shape
    units = columns // 3
    width = grad.shape[1]

    @pl.when(pl.program_id(0) == 0)
    def _():
        copies = []
        for k in range(piece_count):
            base = (chip ^ k) * (2 * rows)
            for number, (piece, part) in enumerate(
                ((own_pieces[k], core), (near_pieces[k], 1 - core))
            ):
                start = pl.multiple_of(base + part * rows, 16)
                copies.append(
                    pltpu.make_async_copy(
                        piece, weights.at[pl.ds(start, rows)], sems.at[2 * k + number]
                    )
                )
        for copy in copies:
            copy.start()
        for copy in copies:
            copy.wait()

    slot_sum = jnp.zeros((hidden.shape[0], 1), f32)
    for start, size in unit_blocks(units):
        gate_pre = dot(hidden[:, :width], weights[:, start : start + size])
        up_pre = dot(hidden[:, :width], weights[:, units + start : units + start + size])
        act_grad = dot(grad[...], weights[:, 2 * units + start : 2 * units + start + size])
        sigma = 1.0 / (1.0 + jnp.exp(-gate_pre))
        silu_vals = gate_pre * sigma
        active = (silu_vals * up_pre).astype(bf16)
        act_out[:, start : start + size] = active
        slot_sum += jnp.sum(active.astype(f32) * act_grad, axis=1, keepdims=True)
        gate_grad = act_grad * up_pre * sigma * (1.0 + gate_pre * (1.0 - sigma))
        joint_out[:, start : start + size] = gate_grad.astype(bf16)
        joint_out[:, units + start : units + start + size] = (act_grad * silu_vals).astype(bf16)
    for start in range(0, width, 512):
        block = weights[start : start + 512, : 2 * units]
        hidden_out[:, start : start + 512] = dot_t(joint_out[...], block).astype(bf16)
        block = weights[start : start + 512, 2 * units :]
        out[:, start : start + 512] = dot_t(act_out[...], block).astype(bf16)
    lanes = lax.broadcasted_iota(jnp.int32, (hidden.shape[0], HDIM), 1)
    hidden_out[:, width:] = jnp.where(lanes == 0, slot_sum, 0.0).astype(bf16)


def expert_rows(position, hidden, grad, own_pieces, near_pieces):
    rows, width = grad.shape
    columns = near_pieces[0].shape[1]
    units = columns // 3
    tile = rows // 2
    shape = jax.ShapeDtypeStruct
    count = len(own_pieces)

    def tiled(size):
        return pl.BlockSpec((tile, size), lambda i, at: (i, 0))

    return pl.pallas_call(
        expert_kernel,
        grid_spec=pltpu.PrefetchScalarGridSpec(
            num_scalar_prefetch=1,
            grid=(rows // tile,),
            in_specs=[tiled(width + HDIM), tiled(width)]
            + [pl.BlockSpec(memory_space=pl.ANY)] * (2 * count),
            out_specs=[tiled(width), tiled(width + HDIM), tiled(units), tiled(2 * units)],
            scratch_shapes=[
                pltpu.VMEM((width, columns), bf16),
                pltpu.SemaphoreType.DMA((2 * count,)),
            ],
        ),
        out_shape=[
            shape((rows, width), bf16),
            shape((rows, width + HDIM), bf16),
            shape((rows, units), bf16),
            shape((rows, 2 * units), bf16),
        ],
        compiler_params=pltpu.CompilerParams(vmem_limit_bytes=56 * 2**20),
        cost_estimate=pl.CostEstimate(
            flops=4 * rows * width * columns,
            bytes_accessed=2 * (width * columns + 6 * rows * width),
            transcendentals=rows * units,
        ),
        name="expert_rows",
    )(position, hidden, grad, *own_pieces, *near_pieces)


def expert_grad_kernel(cuts, order, *refs):
    hidden, grad, gates, joint, active = [refs[2 * n : 2 * n + 2] for n in range(5)]
    outs = refs[10:]
    units = active[0].shape[1]

    def scaled(blocks):
        return [
            (block[...].astype(f32) * gate[:, :1].astype(f32)).astype(bf16)
            for block, gate in zip(blocks, gates)
        ]

    left, right = scaled(hidden), scaled(grad)
    step = pl.program_id(0)
    first = [0]
    for cut in cuts:
        first.append(first[-1] + cut)
    for out, start, cut in zip(outs, first, cuts):

        @pl.when((step >= start) & (step < start + cut))
        def _():
            for start, size in unit_blocks(2 * units):
                out[:, start : start + size] = sum(
                    t_dot(rows, part[:, start : start + size]) for rows, part in zip(left, joint)
                ).astype(bf16)
            for start, size in unit_blocks(units):
                out[:, 2 * units + start : 2 * units + start + size] = sum(
                    t_dot(rows, part[:, start : start + size]) for rows, part in zip(right, active)
                ).astype(bf16)


def expert_grads(chunks, cuts, chunk_rows, rows_of, joints, actives):
    hidden, grad = rows_of[:2], rows_of[2:]
    rows, units = actives[0].shape
    width = grad[0].shape[1]
    half = chunk_rows // 2
    count = len(chunks)
    order = jnp.stack([2 * chunk + part for chunk in chunks for part in range(2)]).astype(jnp.int32)

    def whole(size, column=0):
        return pl.BlockSpec(
            (rows, size), lambda i, at: (0, column), pipeline_mode=pl.Buffered(1)
        )

    column = pl.BlockSpec((rows, half), lambda i, at: (0, at[i]))
    return pl.pallas_call(
        functools.partial(expert_grad_kernel, cuts),
        grid_spec=pltpu.PrefetchScalarGridSpec(
            num_scalar_prefetch=1,
            grid=(2 * count,),
            in_specs=[column] * 4
            + [whole(HDIM, width // HDIM)] * 2
            + [whole(2 * units)] * 2
            + [whole(units)] * 2,
            out_specs=[
                pl.BlockSpec(
                    (half, 3 * units),
                    lambda i, at, start=sum(cuts[:n]), cut=cut: (jnp.clip(i - start, 0, cut - 1), 0),
                )
                for n, cut in enumerate(cuts)
            ],
        ),
        out_shape=[jax.ShapeDtypeStruct((cut * half, 3 * units), bf16) for cut in cuts],
        compiler_params=pltpu.CompilerParams(vmem_limit_bytes=56 * 2**20),
        cost_estimate=pl.CostEstimate(
            flops=4 * count * chunk_rows * rows * 3 * units,
            bytes_accessed=2 * (rows * 6 * units + count * chunk_rows * (4 * rows + 3 * units)),
            transcendentals=0,
        ),
        name="expert_grads",
    )(order, *hidden, *grad, *hidden, *joints, *actives)


def local(
    tokens,
    cotangent,
    seq_lengths,
    dealing,
    attn_routes,
    ffn_routes,
    expert_table,
    clip_limit,
    attn_gain,
    ffn_gain,
    attn_router,
    ffn_router,
    query_weight,
    attn_out_weight,
    kv_weight,
    gate_up_weight,
    down_weight,
):
    micro, tok_rows, width = tokens.shape
    dp_count = lax.axis_size("dp")
    slots = lax.axis_size("expert")
    col = lax.axis_index("expert")
    group = lax.axis_index("dp")
    piece_rows = tok_rows // dp_count
    cap = tok_rows * TOP * 3 // (2 * slots)
    group_rows = tok_rows * slots
    all_rows = micro * group_rows
    home_rows = micro * tok_rows
    query_width = HEADS * HDIM
    own_heads = HEADS // slots
    own_width = own_heads * HDIM
    shard_rows = query_weight.shape[1]
    score_scale = HDIM ** (-0.5)
    core = group % 2
    chip = group // 2
    side = chip % 2
    chips = dp_count // 2
    lines = chips // 2
    quarter = FF // 4
    chip_rows = 2 * shard_rows

    both = jnp.stack([tokens, cotangent]).reshape(2 * micro, dp_count, piece_rows, width)
    both = lax.all_to_all(both.transpose(1, 0, 2, 3), "dp", split_axis=0, concat_axis=0, tiled=True)
    def quarter_of(half, part):
        start = (2 * half + part) * quarter
        return jnp.concatenate(
            [
                lax.dynamic_slice_in_dim(gate_up_weight[0], start, quarter, 1),
                lax.dynamic_slice_in_dim(gate_up_weight[0], FF + start, quarter, 1),
                lax.dynamic_slice_in_dim(down_weight[0], start, quarter, 1),
            ],
            axis=1,
        )

    parts = (1 - core, core)
    keep_pair = [quarter_of(side, part) for part in parts]
    send_pair = [quarter_of(1 - side, part) for part in parts]
    kv_in, query_in, out_in = after(
        (kv_weight, query_weight[0], attn_out_weight[0]), keep_pair[0], send_pair[0]
    )
    both = both.transpose(1, 0, 2, 3).reshape(2, micro, tok_rows, width)
    deal = (dealing[:, :, None] == jnp.arange(tok_rows, dtype=jnp.int32)).astype(bf16)
    work = jnp.einsum("mtr,bmrd->bmtd", deal, both, preferred_element_type=f32)
    x_home = work[0].reshape(home_rows, width)
    dy_home = work[1].reshape(home_rows, width)

    def columns_of(*shards):
        pieces = [shard.reshape(shard_rows, slots, own_width) for shard in shards]
        out = jnp.zeros((shard_rows, len(shards) * query_width), shards[0].dtype)
        for k in range(slots):
            part = jnp.concatenate(
                [lax.dynamic_index_in_dim(piece, col ^ k, 1, keepdims=False) for piece in pieces],
                axis=1,
            )
            part = swap(part, "expert", k) if k else part
            for number in range(len(shards)):
                out = lax.dynamic_update_slice_in_dim(
                    out,
                    part[:, number * own_width : (number + 1) * own_width],
                    number * query_width + (col ^ k) * own_width,
                    1,
                )
        return out

    def slots_of(columns):
        pieces = columns.reshape(shard_rows, slots, own_width)
        out = jnp.zeros((shard_rows, query_width), columns.dtype)
        for k in range(slots):
            part = lax.dynamic_index_in_dim(pieces, col ^ k, 1, keepdims=False)
            part = swap(part, "expert", k) if k else part
            out = lax.dynamic_update_slice_in_dim(out, part, (col ^ k) * own_width, 1)
        return out

    half_slots = slots // 2
    first_pairs = [(c, 2 * c) for c in range(half_slots)]
    first_pairs += [(c, 2 * (c - half_slots) + 1) for c in range(half_slots, slots)]
    second_pairs = [(c, 2 * c + 1) for c in range(half_slots)]
    second_pairs += [(c, 2 * (c - half_slots)) for c in range(half_slots, slots)]
    holds_keys = col < half_slots
    even_col = col % 2 == 0
    low_kv, high_kv = kv_in[:, :own_width], kv_in[:, own_width:]
    first_got = lax.ppermute(jnp.where(holds_keys, low_kv, high_kv), "expert", first_pairs)
    second_got = lax.ppermute(jnp.where(holds_keys, high_kv, low_kv), "expert", second_pairs)
    own_kv = jnp.concatenate(
        [
            jnp.where(even_col, first_got, second_got),
            jnp.where(even_col, second_got, first_got),
        ],
        axis=1,
    )
    line_steps = [4 * line for line in range(1, lines)]
    side_first = swap(send_pair[0], "dp", 2)
    keep_first = [swap(keep_pair[0], "dp", step) for step in line_steps]
    joint_own = columns_of(query_in, out_in)
    first_own = jnp.concatenate([joint_own[:, :query_width], own_kv], axis=1)
    first_own, second_own = lax.optimization_barrier(
        (first_own, joint_own[:, query_width:], side_first, keep_first)
    )[:2]
    joint_full = lax.all_gather(first_own, "dp", axis=0, tiled=True)
    out_full = lax.all_gather(second_own, "dp", axis=0, tiled=True)
    late_pair = after((keep_pair[1], send_pair[1], side_first), joint_full)
    keep_second = [swap(late_pair[0], "dp", step) for step in line_steps]
    side_second = swap(late_pair[1], "dp", 2)
    first_lines = [swap(late_pair[2], "dp", step) for step in line_steps]
    second_lines = [swap(side_second, "dp", step) for step in line_steps]
    firsts, seconds = [keep_pair[0], side_first], [keep_pair[1], side_second]
    for line in range(lines - 1):
        firsts += [keep_first[line], first_lines[line]]
        seconds += [keep_second[line], second_lines[line]]
    near_pieces = [swap(piece, "dp", 1) for piece in firsts]
    own_pieces = seconds
    query_full = joint_full[:, :query_width]
    kv_full = joint_full[:, query_width:]

    positions = jnp.arange(group_rows, dtype=jnp.int32)
    first_len = lax.dynamic_index_in_dim(seq_lengths[:, :, 0], group, 1, keepdims=True)
    in_second = positions[None, :] >= first_len
    places = positions[None, :] - jnp.where(in_second, first_len, 0)
    tables = rotation_tables(places.reshape(all_rows))

    def gather_rows(value):
        shaped = value.reshape(micro, tok_rows, -1)
        out = jnp.zeros((micro, group_rows, shaped.shape[-1]), value.dtype)
        for k in range(slots):
            part = swap(shaped, "expert", k) if k else shaped
            out = lax.dynamic_update_slice_in_dim(out, part, (col ^ k) * tok_rows, 1)
        return out.reshape(all_rows, -1)

    def scatter_rows(value):
        shaped = value.reshape(micro, group_rows, -1)
        total = None
        for k in range(slots):
            part = lax.dynamic_slice_in_dim(shaped, (col ^ k) * tok_rows, tok_rows, 1)
            if k:
                part = swap(part.astype(bf16), "expert", k)
            part = part.astype(f32)
            total = part if total is None else total + part
        return total.reshape(home_rows, -1)

    home_routes = lax.dynamic_slice_in_dim(ffn_routes, col * tok_rows, tok_rows, 1)
    home_slots = route_slots(home_routes, expert_table)
    packs = []
    before = jnp.tril(jnp.ones((tok_rows, tok_rows), bf16), -1)
    for k in range(slots):
        hits = jnp.any(home_slots == (col ^ k), axis=-1)
        rank = jnp.einsum("ts,ms->mt", before, hits.astype(bf16), preferred_element_type=f32)
        packs.append(
            hits[:, None, :]
            & (rank[:, None, :] == jnp.arange(cap, dtype=jnp.int32).astype(f32)[None, :, None])
        )
    packs = jnp.stack(packs)
    packs_low = packs.astype(bf16)
    pack_rows = micro * cap
    sent_rows = slots * pack_rows

    def send_packed(value, lane=None):
        packed = jnp.einsum(
            "kmct,mtd->kmcd", packs_low, value.reshape(micro, tok_rows, -1), preferred_element_type=f32
        ).astype(bf16)
        if lane is not None:
            lanes = jnp.pad(lane[..., None], ((0, 0), (0, 0), (0, 0), (0, HDIM - 1)))
            packed = jnp.concatenate([packed, lanes.astype(bf16)], axis=-1)
        parts = [swap(packed[k], "expert", k) if k else packed[k] for k in range(slots)]
        return jnp.stack(parts).reshape(sent_rows, -1)

    def near_rows(value):
        return jnp.concatenate([value, swap(value, "dp", 1)], axis=0)

    def quad_sums(value):
        (own, near), (far, across) = [jnp.split(half, 2, axis=0) for half in value]
        far_sum = far.astype(f32) + swap(across, "dp", 1).astype(f32)
        return own.astype(f32) + swap(near, "dp", 1).astype(f32), far_sum.astype(bf16)

    def return_packed(value, *others):
        shaped = value.astype(bf16).reshape(slots, micro, cap, -1)
        parts = [swap(shaped[k], "expert", k) if k else shaped[k] for k in range(slots)]
        return after(parts, *others)

    def unpack(packed, scale):
        total = None
        for k in range(slots):
            rows = jnp.einsum("mct,mcd->mtd", packs_low[k], packed[k], preferred_element_type=f32)
            rows = rows.reshape(home_rows, -1) * take(scale.T, col ^ k)[:, None]
            total = rows if total is None else total + rows
        return total

    gain_one = attn_gain.astype(f32)
    gain_two = ffn_gain.astype(f32)
    normed_one, scale_one = normalize(x_home)
    hidden_one_home = (normed_one * gain_one).astype(bf16)
    hidden_one_raw = gather_rows(after(hidden_one_home, near_pieces[:3]))
    grad_sent = send_packed(dy_home.astype(bf16))
    hidden_one = after(hidden_one_raw, grad_sent)
    logits_one = dot(hidden_one, attn_router)
    gates_one, matches_one, chosen_one, gate_vals_one = route_gates(
        logits_one, attn_routes.reshape(all_rows, TOP), expert_table
    )
    hits_one = jnp.any(chosen_one, axis=1).astype(f32)

    def wide(value):
        return jnp.pad(value, ((0, 0), (0, HDIM - value.shape[1])))

    kv_part = dot(hidden_one, kv_full).astype(bf16)
    query_part = dot(hidden_one, query_full)
    lens = first_len[:, 0].astype(jnp.int32)
    gates_wide = wide(gates_one)
    attn_vals, gated_vals, query_rot, key_rot, log_total, peaks = attention_forward(
        lens, query_part, kv_part, tables, gates_wide, wide(hits_one), own_heads, group_rows
    )
    peaks = jnp.max(peaks, axis=0)[: own_heads * slots]
    attn_part = after(dot_t(gated_vals, out_full), keep_second, side_second)
    attn_home = after(scatter_rows(attn_part), first_lines)
    grad_sent = after(grad_sent, attn_home)
    grad_near, grad_far = near_rows(grad_sent), near_rows(swap(grad_sent, "dp", 2))

    resid = x_home + attn_home
    normed_two, scale_two = normalize(resid)
    hidden_two = (normed_two * gain_two).astype(bf16)
    logits_two = dot(hidden_two, ffn_router)
    gates_two, matches_two, chosen_two, gate_vals_two = route_gates(
        logits_two, home_routes.reshape(home_rows, TOP), expert_table
    )
    gates_by_slot = gates_two.reshape(micro, tok_rows, slots)
    gate_parts = []
    for k in range(slots):
        gate_col = lax.dynamic_index_in_dim(gates_by_slot, col ^ k, 2, keepdims=False)
        gate_parts.append(jnp.sum(jnp.where(packs[k], gate_col[:, None, :], 0.0), axis=-1))
    hidden_sent = after(
        send_packed(hidden_two, jnp.stack(gate_parts)), second_lines
    )
    hidden_near, hidden_far = near_rows(hidden_sent), swap(hidden_sent, "dp", 2)
    hidden_near = after(hidden_near, near_pieces, grad_near, grad_far)
    position = jnp.stack([core, chip]).astype(jnp.int32)
    near_results = expert_rows(
        position, hidden_near, after(grad_near, grad_far), own_pieces, near_pieces
    )
    hidden_far = near_rows(after(hidden_far, near_results))
    far_results = expert_rows(position, hidden_far, grad_far, own_pieces, near_pieces)
    ffn_parts, hidden_parts, actives, joint_grads = zip(near_results, far_results)

    def block_grads(steps, *others):
        rows = after((hidden_near, hidden_far, grad_near, grad_far), *others)
        cuts = (2,) * len(steps)
        return expert_grads([chip ^ k for k in steps], cuts, chip_rows, rows, joint_grads, actives)

    hidden_sum, hidden_far_sum = quad_sums(hidden_parts)
    ffn_sum, ffn_far_sum = quad_sums(after(ffn_parts, hidden_far_sum))
    line_grads = block_grads([k ^ 1 for k in range(2, chips)], hidden_far_sum)
    side_got = [swap(line_grads[2 * line], "dp", step) for line, step in enumerate(line_steps)]
    blocks = after(line_grads[1::2], side_got)
    keep_got = [swap(block, "dp", step) for block, step in zip(blocks, line_steps)]
    hidden_got, ffn_far_sum, ffn_sum = lax.optimization_barrier(
        (swap(hidden_far_sum, "dp", 2), ffn_far_sum, ffn_sum, line_grads)
    )[:3]
    hidden_sum = hidden_sum + hidden_got.astype(f32)
    own_grads = block_grads([1, 0], hidden_sum)
    back_packed = return_packed(hidden_sum, *own_grads)
    ffn_sum = ffn_sum + swap(after(ffn_far_sum, hidden_got), "dp", 2).astype(f32)

    def total(own, got):
        return functools.reduce(jnp.add, [part.astype(f32) for part in [own] + got]).astype(bf16)

    slot_two_grad = jnp.zeros((slots, home_rows), f32)
    for k in range(slots):
        rows = jnp.sum(
            jnp.where(packs[k], back_packed[k][:, :, width].astype(f32)[:, :, None], 0.0), axis=1
        )
        slot_two_grad = lax.dynamic_update_index_in_dim(
            slot_two_grad, rows.reshape(home_rows), col ^ k, 0
        )
    hidden_two_grad = unpack([part[..., :width] for part in back_packed], gates_two)
    logit_two_grad = gate_back(slot_two_grad.T, gate_vals_two, matches_two, chosen_two).astype(bf16)
    hidden_two_grad = hidden_two_grad + dot_t(logit_two_grad, ffn_router)
    router_two_grad = t_dot(logit_two_grad, hidden_two)
    gain_two_grad = jnp.sum(hidden_two_grad * normed_two, axis=0)
    resid_grad = dy_home + norm_back(hidden_two_grad * gain_two, normed_two, scale_two)

    resid_grad_all, ffn_sum = lax.optimization_barrier(
        (gather_rows(resid_grad.astype(bf16)), ffn_sum, side_got)
    )[:2]
    out_part = t_dot(resid_grad_all, gated_vals).astype(bf16)
    vals_grad = after(dot(resid_grad_all, out_full), out_part)
    side_own = after((own_grads[0], side_got), vals_grad)
    vals_grad, side_sum = lax.optimization_barrier((vals_grad, total(*side_own)))
    other_sum = swap(side_sum, "dp", 2)
    ffn_packed = return_packed(after(ffn_sum, vals_grad))
    out_home = (resid + unpack(ffn_packed, gates_two)).astype(bf16)
    query_grad, key_grad, value_grad, slot_part_one = attention_backward(
        lens, query_rot, key_rot, kv_part, attn_vals, vals_grad, tables, gates_wide, log_total,
        own_heads, group_rows,
    )
    query_grad, key_grad, value_grad, slot_part_one = lax.optimization_barrier(
        (query_grad, key_grad, value_grad, slot_part_one, ffn_packed)
    )[:4]
    kv_grad = jnp.concatenate([key_grad, value_grad], axis=1)
    hidden_one_part = dot_t(query_grad, query_full) + dot_t(kv_grad, kv_full)
    hidden_one_part = hidden_one_part.astype(bf16)
    joint_part_grad = t_dot(
        after(hidden_one, hidden_one_part), jnp.concatenate([query_grad, kv_grad], axis=1)
    ).astype(bf16)
    back_one = scatter_rows(
        jnp.concatenate([hidden_one_part, slot_part_one.astype(bf16)], axis=1)
    )
    back_one, other_sum, keep_got = lax.optimization_barrier(
        (back_one, other_sum, keep_got, joint_part_grad)
    )[:3]
    out_own = lax.psum_scatter(out_part, "dp", scatter_dimension=0, tiled=True)
    out_grad = slots_of(after(out_own, back_one))
    back_one, out_grad = lax.optimization_barrier((back_one, out_grad))
    hidden_one_grad, slot_one_grad = back_one[:, :width], back_one[:, width : width + slots]

    def own(value):
        shaped = value.reshape((micro, group_rows) + value.shape[1:])
        part = lax.dynamic_slice_in_dim(shaped, col * tok_rows, tok_rows, 1)
        return part.reshape((home_rows,) + value.shape[1:])

    logit_one_grad = gate_back(
        slot_one_grad, own(gate_vals_one), own(matches_one), own(chosen_one)
    ).astype(bf16)
    hidden_one_grad = hidden_one_grad + dot_t(logit_one_grad, attn_router)
    router_one_grad = t_dot(logit_one_grad, hidden_one_home)
    gain_one_grad = jnp.sum(hidden_one_grad * normed_one, axis=0)
    in_home = resid_grad + norm_back(hidden_one_grad * gain_one, normed_one, scale_one)

    def reduced(value):
        return lax.psum_scatter(value, "dp", scatter_dimension=0, tiled=True)

    in_low, keep_got, other_sum = lax.optimization_barrier(
        (in_home.astype(bf16), keep_got, other_sum)
    )
    joint_own = reduced(joint_part_grad)

    results = jnp.stack([out_home, in_low]).reshape(2, micro, tok_rows, width)
    results = jnp.einsum("mtr,bmtd->bmrd", deal, results, preferred_element_type=f32).astype(bf16)
    results = results.reshape(2 * micro, dp_count, piece_rows, width).transpose(1, 0, 2, 3)
    results = results.reshape(dp_count, 2 * micro * piece_rows, width)
    sent_back = results.shape[1]
    small = jnp.concatenate(
        [gain_one_grad[None], gain_two_grad[None], router_one_grad, router_two_grad], axis=0
    ).astype(bf16)
    sum_rows = small.shape[0]
    peak_count = own_heads * slots
    peak_parts, rest = [], peaks
    for _ in range(3):
        peak_parts.append(lax.reduce_precision(rest, 8, 7))
        rest = rest - peak_parts[-1]
    peak_row = jnp.concatenate(peak_parts).astype(bf16)
    small = jnp.pad(small, ((0, -sum_rows % 16 or 16), (0, 0)))
    small = lax.dynamic_update_slice(small, peak_row[None], (sum_rows, 0))
    small = jnp.broadcast_to(small[None], (dp_count,) + small.shape)
    results = jnp.concatenate([results, small], axis=1)
    results = lax.all_to_all(results, "dp", split_axis=0, concat_axis=0, tiled=True)
    results, joint_own = lax.optimization_barrier((results, joint_own))
    query_own, kv_own = joint_own[:, :query_width], joint_own[:, query_width:]
    small = results[:, sent_back:].astype(f32)
    results = results[:, :sent_back].reshape(dp_count, 2 * micro, piece_rows, width)
    results = results.transpose(1, 0, 2, 3).reshape(2, micro, tok_rows, width)
    peak_row = small[:, sum_rows, : 3 * peak_count].reshape(dp_count, 3, peak_count)
    peak_row = jnp.max((peak_row[:, 0] + peak_row[:, 1]) + peak_row[:, 2], axis=0)
    small = jnp.sum(small, axis=0)
    small = lax.dynamic_update_slice(small, peak_row[None], (sum_rows, 0))
    smalls = [swap(small, "expert", k) if k else small for k in range(slots)]
    peaks_all = jnp.zeros((slots, HEADS), f32)
    for k, part in enumerate(smalls):
        part = part[sum_rows, :peak_count].reshape(own_heads, slots).T
        peaks_all = lax.dynamic_update_slice(peaks_all, part, (0, (col ^ k) * own_heads))
    while len(smalls) > 1:
        smalls = [left + right for left, right in zip(smalls[::2], smalls[1::2])]
    sums = smalls[0][:sum_rows]

    keep_sums = total(own_grads[1], keep_got).reshape(2, shard_rows, 3 * quarter)
    other_sums = other_sum.reshape(2, shard_rows, 3 * quarter)
    by_rows = [jnp.stack([keep_sums[part], other_sums[part]]) for part in range(2)]
    own_pair = jnp.where(core == 0, by_rows[0], by_rows[1])
    near_pair = swap(jnp.where(core == 0, by_rows[1], by_rows[0]), "dp", 1)
    by_core = [jnp.where(core == 0, own_pair, near_pair), jnp.where(core == 0, near_pair, own_pair)]
    by_side = [[jnp.where(side == s, part[0], part[1]) for part in by_core] for s in range(2)]
    blocks = [part for row in by_side for part in row]
    gate_up_grad = jnp.concatenate(
        [b[:, :quarter] for b in blocks] + [b[:, quarter : 2 * quarter] for b in blocks], axis=1
    ).astype(f32)
    down_grad = jnp.concatenate([b[:, 2 * quarter :] for b in blocks], axis=1).astype(f32)

    out_grad = out_grad.astype(f32)
    query_out = slots_of(query_own).astype(f32)
    key_part, value_part = kv_own[:, :own_width], kv_own[:, own_width:]
    first_back = lax.ppermute(
        jnp.where(even_col, key_part, value_part), "expert", [(b, a) for a, b in first_pairs]
    )
    second_back = lax.ppermute(
        jnp.where(even_col, value_part, key_part), "expert", [(b, a) for a, b in second_pairs]
    )
    kv_out = jnp.concatenate(
        [
            jnp.where(holds_keys, first_back, second_back),
            jnp.where(holds_keys, second_back, first_back),
        ],
        axis=1,
    ).astype(f32)

    limit = clip_limit[0].astype(f32)
    factor = limit / jnp.maximum(peaks_all, limit)
    query_scale = jnp.repeat(jnp.sqrt(take(factor, col)), HDIM)
    query_clipped = (query_weight.astype(f32) * query_scale[None, None, :]).astype(bf16)
    full_scale = jnp.concatenate(
        [jnp.repeat(jnp.sqrt(jnp.min(factor, axis=0)), HDIM), jnp.ones((query_width,), f32)]
    )
    piece_width = kv_weight.shape[1]
    piece_scale = lax.dynamic_slice_in_dim(full_scale, col * piece_width, piece_width)
    kv_clipped = (kv_weight.astype(f32) * piece_scale[None, :]).astype(bf16)
    return (
        results[0],
        results[1],
        sums[0],
        sums[1],
        sums[2 : 2 + slots].T,
        sums[2 + slots : sum_rows].T,
        query_out[None],
        out_grad[None],
        kv_out,
        gate_up_grad[None],
        down_grad[None],
        query_clipped,
        kv_clipped,
    )


def solution(mesh):
    placed = (
        P(None, ("dp", "expert"), None),
        P(None, ("dp", "expert"), None),
        P(),
        P(None, ("dp", "expert")),
        P(None, "dp", None),
        P(None, "dp", None),
        P(),
        P(),
        P(),
        P(),
        P(),
        P(),
        P("expert", "dp", None),
        P("expert", "dp", None),
        P("dp", "expert"),
        P("expert", "dp", None),
        P("expert", "dp", None),
    )
    return jax.shard_map(
        local,
        mesh=mesh,
        in_specs=placed,
        out_specs=(
            P(None, ("dp", "expert"), None),
            P(None, ("dp", "expert"), None),
            P(),
            P(),
            P(),
            P(),
            P("expert", "dp", None),
            P("expert", "dp", None),
            P("dp", "expert"),
            P("expert", "dp", None),
            P("expert", "dp", None),
            P("expert", "dp", None),
            P("dp", "expert"),
        ),
        check_vma=False,
    )
```

```python
import functools

import jax
import jax.numpy as jnp
from jax import lax
from jax.experimental import pallas as pl
from jax.experimental.pallas import tpu as pltpu
from jax.sharding import PartitionSpec as P

HEADS = 16
HDIM = 128
FF = 5632
TOP = 2

eps_norm = 1e-06
rope_base = 10000.0
very_low = -1e30

f32 = jnp.float32
bf16 = jnp.bfloat16


def dot(left, right):
    return jnp.dot(left, right, preferred_element_type=f32)


def dot_t(left, right):
    return lax.dot_general(left, right, (((1,), (1,)), ((), ())), preferred_element_type=f32)


def t_dot(left, right):
    return lax.dot_general(left, right, (((0,), (0,)), ((), ())), preferred_element_type=f32)


def swap(value, axis, step):
    count = lax.axis_size(axis)
    return lax.ppermute(value, axis, [(i, i ^ step) for i in range(count)])


def take(stacked, index):
    return lax.dynamic_index_in_dim(stacked, index, 0, keepdims=False)


def place(parts, positions):
    out = jnp.zeros((len(parts),) + parts[0].shape, parts[0].dtype)
    for part, position in zip(parts, positions):
        out = lax.dynamic_update_index_in_dim(out, part, position, 0)
    return out


def after(value, *others):
    return lax.optimization_barrier((value, others))[0]


def rotation_tables(places):
    half_dim = HDIM // 2
    frequency = rope_base ** (-jnp.arange(half_dim, dtype=f32) * 2.0 / HDIM)
    angles = places.astype(f32)[:, None] * frequency[None, :]
    cosine, sine = jnp.cos(angles), jnp.sin(angles)
    return (
        jnp.concatenate([cosine, cosine], axis=1),
        jnp.concatenate([-sine, sine], axis=1),
    )


def turn(values, cosine, sine):
    return values * cosine + pltpu.roll(values, HDIM // 2, 1) * sine


def lane_value(table, lane):
    lanes = lax.broadcasted_iota(jnp.int32, table.shape, 1)
    return jnp.sum(jnp.where(lanes == lane, table, 0.0), axis=1, keepdims=True)


def allowed_pairs(rows, first_len):
    query_at = lax.broadcasted_iota(jnp.int32, (rows, rows), 0)
    key_at = lax.broadcasted_iota(jnp.int32, (rows, rows), 1)
    return (key_at <= query_at) & ((key_at >= first_len) | (query_at < first_len))


def forward_kernel(
    lens, query, key, value, cosine, sine, gates, hits,
    vals_out, gated_out, query_out, key_out, total_out, peak_out,
):
    m, h = pl.program_id(0), pl.program_id(1)
    heads = pl.num_programs(1)
    rows = query.shape[0]
    slots = query.shape[1] // (heads * HDIM)

    @pl.when(h == 0)
    def _():
        total_out[...] = jnp.zeros_like(total_out)
        peak_out[...] = jnp.full_like(peak_out, very_low)

    cos_part, sin_part = cosine[...], sine[...]
    allowed = allowed_pairs(rows, lens[m])
    keys = turn(key[...].astype(f32), cos_part, sin_part).astype(bf16)
    key_out[...] = keys
    values = value[...]
    lanes = lax.broadcasted_iota(jnp.int32, total_out.shape, 1)
    peak_lanes = lax.broadcasted_iota(jnp.int32, peak_out.shape, 1)
    totals, peaks = total_out[...], peak_out[...]
    for s in range(slots):
        columns = pl.ds(pl.multiple_of((s * heads + h) * HDIM, HDIM), HDIM)
        turned = turn(query[:, columns], cos_part, sin_part).astype(bf16)
        query_out[:, columns] = turned
        scores = jnp.where(allowed, dot_t(turned, keys) * HDIM ** (-0.5), very_low)
        row_peak = jnp.max(scores, axis=1, keepdims=True)
        expo = jnp.exp(scores - row_peak)
        denom = jnp.sum(expo, axis=1, keepdims=True)
        probs = expo * (1.0 / denom)
        vals = dot(probs.astype(bf16), values).astype(bf16)
        vals_out[:, columns] = vals
        gated_out[:, columns] = (gates[:, s : s + 1] * vals.astype(f32)).astype(bf16)
        lane = h * slots + s
        totals = jnp.where(lanes == lane, row_peak + jnp.log(denom), totals)
        seen = jnp.where(hits[:, s : s + 1] > 0.0, row_peak, very_low)
        peaks = jnp.where(peak_lanes == lane, jnp.max(seen, axis=0, keepdims=True), peaks)
    total_out[...] = totals
    peak_out[...] = peaks


def backward_kernel(
    lens, query, key, value, vals, vals_grad, cosine, sine, gates, total,
    query_grad, key_grad, value_grad, gate_grad,
):
    m, h = pl.program_id(0), pl.program_id(1)
    heads = pl.num_programs(1)
    rows = query.shape[0]
    slots = query.shape[1] // (heads * HDIM)

    @pl.when(h == 0)
    def _():
        gate_grad[...] = jnp.zeros_like(gate_grad)

    allowed = allowed_pairs(rows, lens[m])
    cos_part, back_sine = cosine[...], -sine[...]
    keys, values, totals = key[...], value[...], total[...]
    lanes = lax.broadcasted_iota(jnp.int32, gate_grad.shape, 1)
    slot_sums = gate_grad[...]
    key_sum = jnp.zeros(key.shape, f32)
    value_sum = jnp.zeros(value.shape, f32)
    for s in range(slots):
        columns = pl.ds(pl.multiple_of((s * heads + h) * HDIM, HDIM), HDIM)
        full_grad = vals_grad[:, columns]
        slot_sum = jnp.sum(vals[:, columns].astype(f32) * full_grad, axis=1, keepdims=True)
        slot_sums += jnp.where(lanes == s, slot_sum, 0.0)
        gated_grad = (gates[:, s : s + 1] * full_grad).astype(bf16)
        queries = query[:, columns]
        scores = jnp.where(allowed, dot_t(queries, keys) * HDIM ** (-0.5), very_low)
        probs = jnp.exp(scores - lane_value(totals, h * slots + s))
        prob_grad = dot_t(gated_grad, values)
        inner = jnp.sum(probs * prob_grad, axis=1, keepdims=True)
        score_grad = (probs * (prob_grad - inner) * HDIM ** (-0.5)).astype(bf16)
        query_grad[:, columns] = turn(dot(score_grad, keys), cos_part, back_sine).astype(bf16)
        key_sum += t_dot(score_grad, queries)
        value_sum += t_dot(probs.astype(bf16), gated_grad)
    gate_grad[...] = slot_sums
    key_grad[...] = turn(key_sum, cos_part, back_sine).astype(bf16)
    value_grad[...] = value_sum.astype(bf16)


def attention_specs(own_heads, rows, width):
    def block(columns, index):
        return pl.BlockSpec((rows, columns), index)

    return {
        "query": block(width, lambda m, h, lens: (m, 0)),
        "key": block(HDIM, lambda m, h, lens: (m, h)),
        "value": block(HDIM, lambda m, h, lens: (m, own_heads + h)),
        "rows": block(HDIM, lambda m, h, lens: (m, 0)),
        "peak": pl.BlockSpec((8, HDIM), lambda m, h, lens: (m, 0)),
    }


def attention_forward(lens, query, joint_kv, tables, gates, hits, own_heads, rows):
    micro = lens.shape[0]
    at = attention_specs(own_heads, rows, query.shape[1])
    shape = jax.ShapeDtypeStruct
    total_rows = micro * rows
    return pl.pallas_call(
        forward_kernel,
        grid_spec=pltpu.PrefetchScalarGridSpec(
            num_scalar_prefetch=1,
            grid=(micro, own_heads),
            in_specs=[at["query"], at["key"], at["value"]] + [at["rows"]] * 4,
            out_specs=[at["query"]] * 3 + [at["key"], at["rows"], at["peak"]],
        ),
        out_shape=[shape(query.shape, bf16)] * 3
        + [
            shape((total_rows, own_heads * HDIM), bf16),
            shape((total_rows, HDIM), f32),
            shape((micro * 8, HDIM), f32),
        ],
        compiler_params=pltpu.CompilerParams(vmem_limit_bytes=48 * 2**20),
        cost_estimate=pl.CostEstimate(
            flops=4 * rows * rows * HDIM * micro * HEADS,
            bytes_accessed=14 * query.size,
            transcendentals=rows * rows * micro * HEADS,
        ),
        name="attention_forward",
    )(lens, query, joint_kv, joint_kv, tables[0], tables[1], gates, hits)


def attention_backward(
    lens, query, key, joint_kv, vals, vals_grad, tables, gates, total, own_heads, rows
):
    micro = lens.shape[0]
    at = attention_specs(own_heads, rows, query.shape[1])
    shape = jax.ShapeDtypeStruct
    total_rows = micro * rows
    return pl.pallas_call(
        backward_kernel,
        grid_spec=pltpu.PrefetchScalarGridSpec(
            num_scalar_prefetch=1,
            grid=(micro, own_heads),
            in_specs=[at["query"], at["key"], at["value"], at["query"], at["query"]]
            + [at["rows"]] * 4,
            out_specs=[at["query"], at["key"], at["key"], at["rows"]],
        ),
        out_shape=[shape(query.shape, bf16)]
        + [shape((total_rows, own_heads * HDIM), bf16)] * 2
        + [shape((total_rows, HDIM), f32)],
        compiler_params=pltpu.CompilerParams(vmem_limit_bytes=48 * 2**20),
        cost_estimate=pl.CostEstimate(
            flops=10 * rows * rows * HDIM * micro * HEADS,
            bytes_accessed=14 * query.size,
            transcendentals=rows * rows * micro * HEADS,
        ),
        name="attention_backward",
    )(lens, query, key, joint_kv, vals, vals_grad, tables[0], tables[1], gates, total)


def normalize(values):
    row_scale = lax.rsqrt(jnp.mean(values * values, axis=-1, keepdims=True) + eps_norm)
    return values * row_scale, row_scale


def norm_back(grad_hat, normed, row_scale):
    return row_scale * (grad_hat - normed * jnp.mean(grad_hat * normed, axis=-1, keepdims=True))


def route_gates(logits, routes, expert_table):
    expert_ids = jnp.arange(expert_table.shape[0], dtype=jnp.int32)
    matches = routes[:, :, None] == expert_ids[None, None, :]
    picked = jnp.sum(jnp.where(matches, logits[:, None, :], 0.0), axis=-1)
    gate_vals = jax.nn.softmax(picked, axis=-1)
    slot_ids = route_slots(routes, expert_table)
    chosen = slot_ids[:, :, None] == expert_ids[None, None, :]
    gates = jnp.sum(jnp.where(chosen, gate_vals[:, :, None], 0.0), axis=1)
    return gates, matches, chosen, gate_vals


def route_slots(routes, expert_table):
    expert_ids = jnp.arange(expert_table.shape[0], dtype=jnp.int32)
    matches = routes[..., None] == expert_ids
    return jnp.sum(jnp.where(matches, expert_table, 0), axis=-1)


def gate_back(slot_grad, gate_vals, matches, chosen):
    picked = jnp.sum(jnp.where(chosen, slot_grad[:, None, :], 0.0), axis=-1)
    inner_sum = jnp.sum(gate_vals * picked, axis=-1, keepdims=True)
    picked_grad = gate_vals * (picked - inner_sum)
    return jnp.sum(jnp.where(matches, picked_grad[:, :, None], 0.0), axis=1)


def unit_blocks(count):
    return [(start, min(512, count - start)) for start in range(0, count, 512)]


def expert_kernel(place_ref, hidden, grad, *refs):
    piece_count = (len(refs) - 6) // 2
    own_pieces, near_pieces = refs[:piece_count], refs[piece_count : 2 * piece_count]
    out, hidden_out, act_out, joint_out, weights, sems = refs[2 * piece_count :]
    core, chip = place_ref[0], place_ref[1]
    rows, columns = near_pieces[0].shape
    units = columns // 3
    width = grad.shape[1]

    @pl.when(pl.program_id(0) == 0)
    def _():
        copies = []
        for k in range(piece_count):
            base = (chip ^ k) * (2 * rows)
            for number, (piece, part) in enumerate(
                ((own_pieces[k], core), (near_pieces[k], 1 - core))
            ):
                start = pl.multiple_of(base + part * rows, 16)
                copies.append(
                    pltpu.make_async_copy(
                        piece, weights.at[pl.ds(start, rows)], sems.at[2 * k + number]
                    )
                )
        for copy in copies:
            copy.start()
        for copy in copies:
            copy.wait()

    slot_sum = jnp.zeros((hidden.shape[0], 1), f32)
    for start, size in unit_blocks(units):
        gate_pre = dot(hidden[:, :width], weights[:, start : start + size])
        up_pre = dot(hidden[:, :width], weights[:, units + start : units + start + size])
        act_grad = dot(grad[...], weights[:, 2 * units + start : 2 * units + start + size])
        sigma = 1.0 / (1.0 + jnp.exp(-gate_pre))
        silu_vals = gate_pre * sigma
        active = (silu_vals * up_pre).astype(bf16)
        act_out[:, start : start + size] = active
        slot_sum += jnp.sum(active.astype(f32) * act_grad, axis=1, keepdims=True)
        gate_grad = act_grad * up_pre * sigma * (1.0 + gate_pre * (1.0 - sigma))
        joint_out[:, start : start + size] = gate_grad.astype(bf16)
        joint_out[:, units + start : units + start + size] = (act_grad * silu_vals).astype(bf16)
    for start in range(0, width, 512):
        block = weights[start : start + 512, : 2 * units]
        hidden_out[:, start : start + 512] = dot_t(joint_out[...], block).astype(bf16)
        block = weights[start : start + 512, 2 * units :]
        out[:, start : start + 512] = dot_t(act_out[...], block).astype(bf16)
    lanes = lax.broadcasted_iota(jnp.int32, (hidden.shape[0], HDIM), 1)
    hidden_out[:, width:] = jnp.where(lanes == 0, slot_sum, 0.0).astype(bf16)


def expert_rows(position, hidden, grad, own_pieces, near_pieces):
    rows, width = grad.shape
    columns = near_pieces[0].shape[1]
    units = columns // 3
    tile = rows // 2
    shape = jax.ShapeDtypeStruct
    count = len(own_pieces)

    def tiled(size):
        return pl.BlockSpec((tile, size), lambda i, at: (i, 0))

    return pl.pallas_call(
        expert_kernel,
        grid_spec=pltpu.PrefetchScalarGridSpec(
            num_scalar_prefetch=1,
            grid=(rows // tile,),
            in_specs=[tiled(width + HDIM), tiled(width)]
            + [pl.BlockSpec(memory_space=pl.ANY)] * (2 * count),
            out_specs=[tiled(width), tiled(width + HDIM), tiled(units), tiled(2 * units)],
            scratch_shapes=[
                pltpu.VMEM((width, columns), bf16),
                pltpu.SemaphoreType.DMA((2 * count,)),
            ],
        ),
        out_shape=[
            shape((rows, width), bf16),
            shape((rows, width + HDIM), bf16),
            shape((rows, units), bf16),
            shape((rows, 2 * units), bf16),
        ],
        compiler_params=pltpu.CompilerParams(vmem_limit_bytes=56 * 2**20),
        cost_estimate=pl.CostEstimate(
            flops=4 * rows * width * columns,
            bytes_accessed=2 * (width * columns + 6 * rows * width),
            transcendentals=rows * units,
        ),
        name="expert_rows",
    )(position, hidden, grad, *own_pieces, *near_pieces)


def expert_grad_kernel(cuts, order, *refs):
    hidden, grad, gates, joint, active = [refs[2 * n : 2 * n + 2] for n in range(5)]
    outs = refs[10:]
    units = active[0].shape[1]

    def scaled(blocks):
        return [
            (block[...].astype(f32) * gate[:, :1].astype(f32)).astype(bf16)
            for block, gate in zip(blocks, gates)
        ]

    left, right = scaled(hidden), scaled(grad)
    step = pl.program_id(0)
    first = [0]
    for cut in cuts:
        first.append(first[-1] + cut)
    for out, start, cut in zip(outs, first, cuts):

        @pl.when((step >= start) & (step < start + cut))
        def _():
            for start, size in unit_blocks(2 * units):
                out[:, start : start + size] = sum(
                    t_dot(rows, part[:, start : start + size]) for rows, part in zip(left, joint)
                ).astype(bf16)
            for start, size in unit_blocks(units):
                out[:, 2 * units + start : 2 * units + start + size] = sum(
                    t_dot(rows, part[:, start : start + size]) for rows, part in zip(right, active)
                ).astype(bf16)


def expert_grads(chunks, cuts, chunk_rows, rows_of, joints, actives):
    hidden, grad = rows_of[:2], rows_of[2:]
    rows, units = actives[0].shape
    width = grad[0].shape[1]
    half = chunk_rows // 2
    count = len(chunks)
    order = jnp.stack([2 * chunk + part for chunk in chunks for part in range(2)]).astype(jnp.int32)

    def whole(size, column=0):
        return pl.BlockSpec(
            (rows, size), lambda i, at: (0, column), pipeline_mode=pl.Buffered(1)
        )

    column = pl.BlockSpec((rows, half), lambda i, at: (0, at[i]))
    return pl.pallas_call(
        functools.partial(expert_grad_kernel, cuts),
        grid_spec=pltpu.PrefetchScalarGridSpec(
            num_scalar_prefetch=1,
            grid=(2 * count,),
            in_specs=[column] * 4
            + [whole(HDIM, width // HDIM)] * 2
            + [whole(2 * units)] * 2
            + [whole(units)] * 2,
            out_specs=[
                pl.BlockSpec(
                    (half, 3 * units),
                    lambda i, at, start=sum(cuts[:n]), cut=cut: (jnp.clip(i - start, 0, cut - 1), 0),
                )
                for n, cut in enumerate(cuts)
            ],
        ),
        out_shape=[jax.ShapeDtypeStruct((cut * half, 3 * units), bf16) for cut in cuts],
        compiler_params=pltpu.CompilerParams(vmem_limit_bytes=56 * 2**20),
        cost_estimate=pl.CostEstimate(
            flops=4 * count * chunk_rows * rows * 3 * units,
            bytes_accessed=2 * (rows * 6 * units + count * chunk_rows * (4 * rows + 3 * units)),
            transcendentals=0,
        ),
        name="expert_grads",
    )(order, *hidden, *grad, *hidden, *joints, *actives)


def local(
    tokens,
    cotangent,
    seq_lengths,
    dealing,
    attn_routes,
    ffn_routes,
    expert_table,
    clip_limit,
    attn_gain,
    ffn_gain,
    attn_router,
    ffn_router,
    query_weight,
    attn_out_weight,
    kv_weight,
    gate_up_weight,
    down_weight,
):
    micro, tok_rows, width = tokens.shape
    dp_count = lax.axis_size("dp")
    slots = lax.axis_size("expert")
    col = lax.axis_index("expert")
    group = lax.axis_index("dp")
    piece_rows = tok_rows // dp_count
    cap = tok_rows * TOP * 3 // (2 * slots)
    group_rows = tok_rows * slots
    all_rows = micro * group_rows
    home_rows = micro * tok_rows
    query_width = HEADS * HDIM
    own_heads = HEADS // slots
    own_width = own_heads * HDIM
    shard_rows = query_weight.shape[1]
    score_scale = HDIM ** (-0.5)
    core = group % 2
    chip = group // 2
    side = chip % 2
    chips = dp_count // 2
    lines = chips // 2
    quarter = FF // 4
    chip_rows = 2 * shard_rows

    both = jnp.stack([tokens, cotangent]).reshape(2 * micro, dp_count, piece_rows, width)
    both = lax.all_to_all(both.transpose(1, 0, 2, 3), "dp", split_axis=0, concat_axis=0, tiled=True)
    def quarter_of(half, part):
        start = (2 * half + part) * quarter
        return jnp.concatenate(
            [
                lax.dynamic_slice_in_dim(gate_up_weight[0], start, quarter, 1),
                lax.dynamic_slice_in_dim(gate_up_weight[0], FF + start, quarter, 1),
                lax.dynamic_slice_in_dim(down_weight[0], start, quarter, 1),
            ],
            axis=1,
        )

    parts = (1 - core, core)
    keep_pair = [quarter_of(side, part) for part in parts]
    send_pair = [quarter_of(1 - side, part) for part in parts]
    kv_in, query_in, out_in = after(
        (kv_weight, query_weight[0], attn_out_weight[0]), keep_pair[0], send_pair[0]
    )
    both = both.transpose(1, 0, 2, 3).reshape(2, micro, tok_rows, width)
    deal = (dealing[:, :, None] == jnp.arange(tok_rows, dtype=jnp.int32)).astype(bf16)
    work = jnp.einsum("mtr,bmrd->bmtd", deal, both, preferred_element_type=f32)
    x_home = work[0].reshape(home_rows, width)
    dy_home = work[1].reshape(home_rows, width)

    def columns_of(*shards):
        pieces = [shard.reshape(shard_rows, slots, own_width) for shard in shards]
        out = jnp.zeros((shard_rows, len(shards) * query_width), shards[0].dtype)
        for k in range(slots):
            part = jnp.concatenate(
                [lax.dynamic_index_in_dim(piece, col ^ k, 1, keepdims=False) for piece in pieces],
                axis=1,
            )
            part = swap(part, "expert", k) if k else part
            for number in range(len(shards)):
                out = lax.dynamic_update_slice_in_dim(
                    out,
                    part[:, number * own_width : (number + 1) * own_width],
                    number * query_width + (col ^ k) * own_width,
                    1,
                )
        return out

    def slots_of(columns):
        pieces = columns.reshape(shard_rows, slots, own_width)
        out = jnp.zeros((shard_rows, query_width), columns.dtype)
        for k in range(slots):
            part = lax.dynamic_index_in_dim(pieces, col ^ k, 1, keepdims=False)
            part = swap(part, "expert", k) if k else part
            out = lax.dynamic_update_slice_in_dim(out, part, (col ^ k) * own_width, 1)
        return out

    half_slots = slots // 2
    first_pairs = [(c, 2 * c) for c in range(half_slots)]
    first_pairs += [(c, 2 * (c - half_slots) + 1) for c in range(half_slots, slots)]
    second_pairs = [(c, 2 * c + 1) for c in range(half_slots)]
    second_pairs += [(c, 2 * (c - half_slots)) for c in range(half_slots, slots)]
    holds_keys = col < half_slots
    even_col = col % 2 == 0
    low_kv, high_kv = kv_in[:, :own_width], kv_in[:, own_width:]
    first_got = lax.ppermute(jnp.where(holds_keys, low_kv, high_kv), "expert", first_pairs)
    second_got = lax.ppermute(jnp.where(holds_keys, high_kv, low_kv), "expert", second_pairs)
    own_kv = jnp.concatenate(
        [
            jnp.where(even_col, first_got, second_got),
            jnp.where(even_col, second_got, first_got),
        ],
        axis=1,
    )
    line_steps = [4 * line for line in range(1, lines)]
    side_first = swap(send_pair[0], "dp", 2)
    keep_first = [swap(keep_pair[0], "dp", step) for step in line_steps]
    joint_own = columns_of(query_in, out_in)
    first_own = jnp.concatenate([joint_own[:, :query_width], own_kv], axis=1)
    first_own, second_own = lax.optimization_barrier(
        (first_own, joint_own[:, query_width:], side_first, keep_first)
    )[:2]
    joint_full = lax.all_gather(first_own, "dp", axis=0, tiled=True)
    out_full = lax.all_gather(second_own, "dp", axis=0, tiled=True)
    late_pair = after((keep_pair[1], send_pair[1], side_first), joint_full)
    keep_second = [swap(late_pair[0], "dp", step) for step in line_steps]
    side_second = swap(late_pair[1], "dp", 2)
    first_lines = [swap(late_pair[2], "dp", step) for step in line_steps]
    second_lines = [swap(side_second, "dp", step) for step in line_steps]
    firsts, seconds = [keep_pair[0], side_first], [keep_pair[1], side_second]
    for line in range(lines - 1):
        firsts += [keep_first[line], first_lines[line]]
        seconds += [keep_second[line], second_lines[line]]
    near_pieces = [swap(piece, "dp", 1) for piece in firsts]
    own_pieces = seconds
    query_full = joint_full[:, :query_width]
    kv_full = joint_full[:, query_width:]

    positions = jnp.arange(group_rows, dtype=jnp.int32)
    first_len = lax.dynamic_index_in_dim(seq_lengths[:, :, 0], group, 1, keepdims=True)
    in_second = positions[None, :] >= first_len
    places = positions[None, :] - jnp.where(in_second, first_len, 0)
    tables = rotation_tables(places.reshape(all_rows))

    def gather_rows(value):
        shaped = value.reshape(micro, tok_rows, -1)
        out = jnp.zeros((micro, group_rows, shaped.shape[-1]), value.dtype)
        for k in range(slots):
            part = swap(shaped, "expert", k) if k else shaped
            out = lax.dynamic_update_slice_in_dim(out, part, (col ^ k) * tok_rows, 1)
        return out.reshape(all_rows, -1)

    def scatter_rows(value):
        shaped = value.reshape(micro, group_rows, -1)
        total = None
        for k in range(slots):
            part = lax.dynamic_slice_in_dim(shaped, (col ^ k) * tok_rows, tok_rows, 1)
            if k:
                part = swap(part.astype(bf16), "expert", k)
            part = part.astype(f32)
            total = part if total is None else total + part
        return total.reshape(home_rows, -1)

    home_routes = lax.dynamic_slice_in_dim(ffn_routes, col * tok_rows, tok_rows, 1)
    home_slots = route_slots(home_routes, expert_table)
    packs = []
    before = jnp.tril(jnp.ones((tok_rows, tok_rows), bf16), -1)
    for k in range(slots):
        hits = jnp.any(home_slots == (col ^ k), axis=-1)
        rank = jnp.einsum("ts,ms->mt", before, hits.astype(bf16), preferred_element_type=f32)
        packs.append(
            hits[:, None, :]
            & (rank[:, None, :] == jnp.arange(cap, dtype=jnp.int32).astype(f32)[None, :, None])
        )
    packs = jnp.stack(packs)
    packs_low = packs.astype(bf16)
    pack_rows = micro * cap
    sent_rows = slots * pack_rows

    def send_packed(value, lane=None):
        packed = jnp.einsum(
            "kmct,mtd->kmcd", packs_low, value.reshape(micro, tok_rows, -1), preferred_element_type=f32
        ).astype(bf16)
        if lane is not None:
            lanes = jnp.pad(lane[..., None], ((0, 0), (0, 0), (0, 0), (0, HDIM - 1)))
            packed = jnp.concatenate([packed, lanes.astype(bf16)], axis=-1)
        parts = [swap(packed[k], "expert", k) if k else packed[k] for k in range(slots)]
        return jnp.stack(parts).reshape(sent_rows, -1)

    def near_rows(value):
        return jnp.concatenate([value, swap(value, "dp", 1)], axis=0)

    def quad_sums(value):
        (own, near), (far, across) = [jnp.split(half, 2, axis=0) for half in value]
        far_sum = far.astype(f32) + swap(across, "dp", 1).astype(f32)
        return own.astype(f32) + swap(near, "dp", 1).astype(f32), far_sum.astype(bf16)

    def return_packed(value, *others):
        shaped = value.astype(bf16).reshape(slots, micro, cap, -1)
        parts = [swap(shaped[k], "expert", k) if k else shaped[k] for k in range(slots)]
        return after(parts, *others)

    def unpack(packed, scale):
        total = None
        for k in range(slots):
            rows = jnp.einsum("mct,mcd->mtd", packs_low[k], packed[k], preferred_element_type=f32)
            rows = rows.reshape(home_rows, -1) * take(scale.T, col ^ k)[:, None]
            total = rows if total is None else total + rows
        return total

    gain_one = attn_gain.astype(f32)
    gain_two = ffn_gain.astype(f32)
    normed_one, scale_one = normalize(x_home)
    hidden_one_home = (normed_one * gain_one).astype(bf16)
    hidden_one_raw = gather_rows(after(hidden_one_home, near_pieces[:3]))
    grad_sent = send_packed(dy_home.astype(bf16))
    hidden_one = after(hidden_one_raw, grad_sent)
    logits_one = dot(hidden_one, attn_router)
    gates_one, matches_one, chosen_one, gate_vals_one = route_gates(
        logits_one, attn_routes.reshape(all_rows, TOP), expert_table
    )
    hits_one = jnp.any(chosen_one, axis=1).astype(f32)

    def wide(value):
        return jnp.pad(value, ((0, 0), (0, HDIM - value.shape[1])))

    kv_part = dot(hidden_one, kv_full).astype(bf16)
    query_part = dot(hidden_one, query_full)
    lens = first_len[:, 0].astype(jnp.int32)
    gates_wide = wide(gates_one)
    attn_vals, gated_vals, query_rot, key_rot, log_total, peaks = attention_forward(
        lens, query_part, kv_part, tables, gates_wide, wide(hits_one), own_heads, group_rows
    )
    peaks = jnp.max(peaks, axis=0)[: own_heads * slots]
    attn_part = after(dot_t(gated_vals, out_full), keep_second, side_second)
    attn_home = after(scatter_rows(attn_part), first_lines)
    grad_sent = after(grad_sent, attn_home)
    grad_near, grad_far = near_rows(grad_sent), near_rows(swap(grad_sent, "dp", 2))

    resid = x_home + attn_home
    normed_two, scale_two = normalize(resid)
    hidden_two = (normed_two * gain_two).astype(bf16)
    logits_two = dot(hidden_two, ffn_router)
    gates_two, matches_two, chosen_two, gate_vals_two = route_gates(
        logits_two, home_routes.reshape(home_rows, TOP), expert_table
    )
    gates_by_slot = gates_two.reshape(micro, tok_rows, slots)
    gate_parts = []
    for k in range(slots):
        gate_col = lax.dynamic_index_in_dim(gates_by_slot, col ^ k, 2, keepdims=False)
        gate_parts.append(jnp.sum(jnp.where(packs[k], gate_col[:, None, :], 0.0), axis=-1))
    hidden_sent = after(
        send_packed(hidden_two, jnp.stack(gate_parts)), second_lines
    )
    hidden_near, hidden_far = near_rows(hidden_sent), swap(hidden_sent, "dp", 2)
    hidden_near = after(hidden_near, near_pieces, grad_near, grad_far)
    position = jnp.stack([core, chip]).astype(jnp.int32)
    near_results = expert_rows(
        position, hidden_near, after(grad_near, grad_far), own_pieces, near_pieces
    )
    hidden_far = near_rows(after(hidden_far, near_results))
    far_results = expert_rows(position, hidden_far, grad_far, own_pieces, near_pieces)
    ffn_parts, hidden_parts, actives, joint_grads = zip(near_results, far_results)

    def block_grads(steps, *others):
        rows = after((hidden_near, hidden_far, grad_near, grad_far), *others)
        cuts = (2,) * len(steps)
        return expert_grads([chip ^ k for k in steps], cuts, chip_rows, rows, joint_grads, actives)

    hidden_sum, hidden_far_sum = quad_sums(hidden_parts)
    ffn_sum, ffn_far_sum = quad_sums(after(ffn_parts, hidden_far_sum))
    line_grads = block_grads([k ^ 1 for k in range(2, chips)], hidden_far_sum)
    side_got = [swap(line_grads[2 * line], "dp", step) for line, step in enumerate(line_steps)]
    blocks = after(line_grads[1::2], side_got)
    keep_got = [swap(block, "dp", step) for block, step in zip(blocks, line_steps)]
    hidden_got, ffn_far_sum, ffn_sum = lax.optimization_barrier(
        (swap(hidden_far_sum, "dp", 2), ffn_far_sum, ffn_sum, line_grads)
    )[:3]
    hidden_sum = hidden_sum + hidden_got.astype(f32)
    own_grads = block_grads([1, 0], hidden_sum)
    back_packed = return_packed(hidden_sum, *own_grads)
    ffn_sum = ffn_sum + swap(after(ffn_far_sum, hidden_got), "dp", 2).astype(f32)

    def total(own, got):
        return functools.reduce(jnp.add, [part.astype(f32) for part in [own] + got]).astype(bf16)

    slot_two_grad = jnp.zeros((slots, home_rows), f32)
    for k in range(slots):
        rows = jnp.sum(
            jnp.where(packs[k], back_packed[k][:, :, width].astype(f32)[:, :, None], 0.0), axis=1
        )
        slot_two_grad = lax.dynamic_update_index_in_dim(
            slot_two_grad, rows.reshape(home_rows), col ^ k, 0
        )
    hidden_two_grad = unpack([part[..., :width] for part in back_packed], gates_two)
    logit_two_grad = gate_back(slot_two_grad.T, gate_vals_two, matches_two, chosen_two).astype(bf16)
    hidden_two_grad = hidden_two_grad + dot_t(logit_two_grad, ffn_router)
    router_two_grad = t_dot(logit_two_grad, hidden_two)
    gain_two_grad = jnp.sum(hidden_two_grad * normed_two, axis=0)
    resid_grad = dy_home + norm_back(hidden_two_grad * gain_two, normed_two, scale_two)

    resid_grad_all, ffn_sum = lax.optimization_barrier(
        (gather_rows(resid_grad.astype(bf16)), ffn_sum, side_got)
    )[:2]
    out_part = t_dot(resid_grad_all, gated_vals).astype(bf16)
    vals_grad = after(dot(resid_grad_all, out_full), out_part)
    side_own = after((own_grads[0], side_got), vals_grad)
    vals_grad, side_sum = lax.optimization_barrier((vals_grad, total(*side_own)))
    other_sum = swap(side_sum, "dp", 2)
    ffn_packed = return_packed(after(ffn_sum, vals_grad))
    out_home = (resid + unpack(ffn_packed, gates_two)).astype(bf16)
    query_grad, key_grad, value_grad, slot_part_one = attention_backward(
        lens, query_rot, key_rot, kv_part, attn_vals, vals_grad, tables, gates_wide, log_total,
        own_heads, group_rows,
    )
    query_grad, key_grad, value_grad, slot_part_one = lax.optimization_barrier(
        (query_grad, key_grad, value_grad, slot_part_one, ffn_packed)
    )[:4]
    kv_grad = jnp.concatenate([key_grad, value_grad], axis=1)
    hidden_one_part = dot_t(query_grad, query_full) + dot_t(kv_grad, kv_full)
    hidden_one_part = hidden_one_part.astype(bf16)
    joint_part_grad = t_dot(
        after(hidden_one, hidden_one_part), jnp.concatenate([query_grad, kv_grad], axis=1)
    ).astype(bf16)
    back_one = scatter_rows(
        jnp.concatenate([hidden_one_part, slot_part_one.astype(bf16)], axis=1)
    )
    joint_part_grad, other_sum, keep_got = lax.optimization_barrier(
        (joint_part_grad, other_sum, keep_got)
    )
    out_own = lax.psum_scatter(out_part, "dp", scatter_dimension=0, tiled=True)
    out_grad = slots_of(after(out_own, back_one))
    hidden_one_grad, slot_one_grad = back_one[:, :width], back_one[:, width : width + slots]

    def own(value):
        shaped = value.reshape((micro, group_rows) + value.shape[1:])
        part = lax.dynamic_slice_in_dim(shaped, col * tok_rows, tok_rows, 1)
        return part.reshape((home_rows,) + value.shape[1:])

    logit_one_grad = gate_back(
        slot_one_grad, own(gate_vals_one), own(matches_one), own(chosen_one)
    ).astype(bf16)
    hidden_one_grad = hidden_one_grad + dot_t(logit_one_grad, attn_router)
    router_one_grad = t_dot(logit_one_grad, hidden_one_home)
    gain_one_grad = jnp.sum(hidden_one_grad * normed_one, axis=0)
    in_home = resid_grad + norm_back(hidden_one_grad * gain_one, normed_one, scale_one)

    def reduced(value):
        return lax.psum_scatter(value, "dp", scatter_dimension=0, tiled=True)

    in_low = in_home.astype(bf16)
    joint_own = reduced(joint_part_grad)

    results = jnp.stack([out_home, in_low]).reshape(2, micro, tok_rows, width)
    results = jnp.einsum("mtr,bmtd->bmrd", deal, results, preferred_element_type=f32).astype(bf16)
    results = results.reshape(2 * micro, dp_count, piece_rows, width).transpose(1, 0, 2, 3)
    results = results.reshape(dp_count, 2 * micro * piece_rows, width)
    sent_back = results.shape[1]
    small = jnp.concatenate(
        [gain_one_grad[None], gain_two_grad[None], router_one_grad, router_two_grad], axis=0
    ).astype(bf16)
    sum_rows = small.shape[0]
    peak_count = own_heads * slots
    peak_parts, rest = [], peaks
    for _ in range(3):
        peak_parts.append(lax.reduce_precision(rest, 8, 7))
        rest = rest - peak_parts[-1]
    peak_row = jnp.concatenate(peak_parts).astype(bf16)
    small = jnp.pad(small, ((0, -sum_rows % 16 or 16), (0, 0)))
    small = lax.dynamic_update_slice(small, peak_row[None], (sum_rows, 0))
    small = jnp.broadcast_to(small[None], (dp_count,) + small.shape)
    results = jnp.concatenate([results, small], axis=1)
    results = lax.all_to_all(results, "dp", split_axis=0, concat_axis=0, tiled=True)
    query_own, kv_own = joint_own[:, :query_width], joint_own[:, query_width:]
    small = results[:, sent_back:].astype(f32)
    results = results[:, :sent_back].reshape(dp_count, 2 * micro, piece_rows, width)
    results = results.transpose(1, 0, 2, 3).reshape(2, micro, tok_rows, width)
    peak_row = small[:, sum_rows, : 3 * peak_count].reshape(dp_count, 3, peak_count)
    peak_row = jnp.max((peak_row[:, 0] + peak_row[:, 1]) + peak_row[:, 2], axis=0)
    small = jnp.sum(small, axis=0)
    small = lax.dynamic_update_slice(small, peak_row[None], (sum_rows, 0))
    smalls = [swap(small, "expert", k) if k else small for k in range(slots)]
    peaks_all = jnp.zeros((slots, HEADS), f32)
    for k, part in enumerate(smalls):
        part = part[sum_rows, :peak_count].reshape(own_heads, slots).T
        peaks_all = lax.dynamic_update_slice(peaks_all, part, (0, (col ^ k) * own_heads))
    while len(smalls) > 1:
        smalls = [left + right for left, right in zip(smalls[::2], smalls[1::2])]
    sums = smalls[0][:sum_rows]

    keep_sums = total(own_grads[1], keep_got).reshape(2, shard_rows, 3 * quarter)
    other_sums = other_sum.reshape(2, shard_rows, 3 * quarter)
    by_rows = [jnp.stack([keep_sums[part], other_sums[part]]) for part in range(2)]
    own_pair = jnp.where(core == 0, by_rows[0], by_rows[1])
    near_pair = swap(jnp.where(core == 0, by_rows[1], by_rows[0]), "dp", 1)
    by_core = [jnp.where(core == 0, own_pair, near_pair), jnp.where(core == 0, near_pair, own_pair)]
    by_side = [[jnp.where(side == s, part[0], part[1]) for part in by_core] for s in range(2)]
    blocks = [part for row in by_side for part in row]
    gate_up_grad = jnp.concatenate(
        [b[:, :quarter] for b in blocks] + [b[:, quarter : 2 * quarter] for b in blocks], axis=1
    ).astype(f32)
    down_grad = jnp.concatenate([b[:, 2 * quarter :] for b in blocks], axis=1).astype(f32)

    out_grad = out_grad.astype(f32)
    query_out = slots_of(query_own).astype(f32)
    key_part, value_part = kv_own[:, :own_width], kv_own[:, own_width:]
    first_back = lax.ppermute(
        jnp.where(even_col, key_part, value_part), "expert", [(b, a) for a, b in first_pairs]
    )
    second_back = lax.ppermute(
        jnp.where(even_col, value_part, key_part), "expert", [(b, a) for a, b in second_pairs]
    )
    kv_out = jnp.concatenate(
        [
            jnp.where(holds_keys, first_back, second_back),
            jnp.where(holds_keys, second_back, first_back),
        ],
        axis=1,
    ).astype(f32)

    limit = clip_limit[0].astype(f32)
    factor = limit / jnp.maximum(peaks_all, limit)
    query_scale = jnp.repeat(jnp.sqrt(take(factor, col)), HDIM)
    query_clipped = (query_weight.astype(f32) * query_scale[None, None, :]).astype(bf16)
    full_scale = jnp.concatenate(
        [jnp.repeat(jnp.sqrt(jnp.min(factor, axis=0)), HDIM), jnp.ones((query_width,), f32)]
    )
    piece_width = kv_weight.shape[1]
    piece_scale = lax.dynamic_slice_in_dim(full_scale, col * piece_width, piece_width)
    kv_clipped = (kv_weight.astype(f32) * piece_scale[None, :]).astype(bf16)
    return (
        results[0],
        results[1],
        sums[0],
        sums[1],
        sums[2 : 2 + slots].T,
        sums[2 + slots : sum_rows].T,
        query_out[None],
        out_grad[None],
        kv_out,
        gate_up_grad[None],
        down_grad[None],
        query_clipped,
        kv_clipped,
    )


def solution(mesh):
    placed = (
        P(None, ("dp", "expert"), None),
        P(None, ("dp", "expert"), None),
        P(),
        P(None, ("dp", "expert")),
        P(None, "dp", None),
        P(None, "dp", None),
        P(),
        P(),
        P(),
        P(),
        P(),
        P(),
        P("expert", "dp", None),
        P("expert", "dp", None),
        P("dp", "expert"),
        P("expert", "dp", None),
        P("expert", "dp", None),
    )
    return jax.shard_map(
        local,
        mesh=mesh,
        in_specs=placed,
        out_specs=(
            P(None, ("dp", "expert"), None),
            P(None, ("dp", "expert"), None),
            P(),
            P(),
            P(),
            P(),
            P("expert", "dp", None),
            P("expert", "dp", None),
            P("dp", "expert"),
            P("expert", "dp", None),
            P("expert", "dp", None),
            P("expert", "dp", None),
            P("dp", "expert"),
        ),
        check_vma=False,
    )
```

```python
import functools

import jax
import jax.numpy as jnp
from jax import lax
from jax.experimental import pallas as pl
from jax.experimental.pallas import tpu as pltpu
from jax.sharding import PartitionSpec as P

HEADS = 16
HDIM = 128
FF = 5632
TOP = 2

eps_norm = 1e-06
rope_base = 10000.0
very_low = -1e30

f32 = jnp.float32
bf16 = jnp.bfloat16


def dot(left, right):
    return jnp.dot(left, right, preferred_element_type=f32)


def dot_t(left, right):
    return lax.dot_general(left, right, (((1,), (1,)), ((), ())), preferred_element_type=f32)


def t_dot(left, right):
    return lax.dot_general(left, right, (((0,), (0,)), ((), ())), preferred_element_type=f32)


def swap(value, axis, step):
    count = lax.axis_size(axis)
    return lax.ppermute(value, axis, [(i, i ^ step) for i in range(count)])


def take(stacked, index):
    return lax.dynamic_index_in_dim(stacked, index, 0, keepdims=False)


def place(parts, positions):
    out = jnp.zeros((len(parts),) + parts[0].shape, parts[0].dtype)
    for part, position in zip(parts, positions):
        out = lax.dynamic_update_index_in_dim(out, part, position, 0)
    return out


def after(value, *others):
    return lax.optimization_barrier((value, others))[0]


def rotation_tables(places):
    half_dim = HDIM // 2
    frequency = rope_base ** (-jnp.arange(half_dim, dtype=f32) * 2.0 / HDIM)
    angles = places.astype(f32)[:, None] * frequency[None, :]
    cosine, sine = jnp.cos(angles), jnp.sin(angles)
    return (
        jnp.concatenate([cosine, cosine], axis=1),
        jnp.concatenate([-sine, sine], axis=1),
    )


def turn(values, cosine, sine):
    return values * cosine + pltpu.roll(values, HDIM // 2, 1) * sine


def lane_value(table, lane):
    lanes = lax.broadcasted_iota(jnp.int32, table.shape, 1)
    return jnp.sum(jnp.where(lanes == lane, table, 0.0), axis=1, keepdims=True)


def allowed_pairs(rows, first_len):
    query_at = lax.broadcasted_iota(jnp.int32, (rows, rows), 0)
    key_at = lax.broadcasted_iota(jnp.int32, (rows, rows), 1)
    return (key_at <= query_at) & ((key_at >= first_len) | (query_at < first_len))


def forward_kernel(
    lens, query, key, value, cosine, sine, gates, hits,
    vals_out, gated_out, query_out, key_out, total_out, peak_out,
):
    m, h = pl.program_id(0), pl.program_id(1)
    heads = pl.num_programs(1)
    rows = query.shape[0]
    slots = query.shape[1] // (heads * HDIM)

    @pl.when(h == 0)
    def _():
        total_out[...] = jnp.zeros_like(total_out)
        peak_out[...] = jnp.full_like(peak_out, very_low)

    cos_part, sin_part = cosine[...], sine[...]
    allowed = allowed_pairs(rows, lens[m])
    keys = turn(key[...].astype(f32), cos_part, sin_part).astype(bf16)
    key_out[...] = keys
    values = value[...]
    lanes = lax.broadcasted_iota(jnp.int32, total_out.shape, 1)
    peak_lanes = lax.broadcasted_iota(jnp.int32, peak_out.shape, 1)
    totals, peaks = total_out[...], peak_out[...]
    for s in range(slots):
        columns = pl.ds(pl.multiple_of((s * heads + h) * HDIM, HDIM), HDIM)
        turned = turn(query[:, columns], cos_part, sin_part).astype(bf16)
        query_out[:, columns] = turned
        scores = jnp.where(allowed, dot_t(turned, keys) * HDIM ** (-0.5), very_low)
        row_peak = jnp.max(scores, axis=1, keepdims=True)
        expo = jnp.exp(scores - row_peak)
        denom = jnp.sum(expo, axis=1, keepdims=True)
        probs = expo * (1.0 / denom)
        vals = dot(probs.astype(bf16), values).astype(bf16)
        vals_out[:, columns] = vals
        gated_out[:, columns] = (gates[:, s : s + 1] * vals.astype(f32)).astype(bf16)
        lane = h * slots + s
        totals = jnp.where(lanes == lane, row_peak + jnp.log(denom), totals)
        seen = jnp.where(hits[:, s : s + 1] > 0.0, row_peak, very_low)
        peaks = jnp.where(peak_lanes == lane, jnp.max(seen, axis=0, keepdims=True), peaks)
    total_out[...] = totals
    peak_out[...] = peaks


def backward_kernel(
    lens, query, key, value, vals, vals_grad, cosine, sine, gates, total,
    query_grad, key_grad, value_grad, gate_grad,
):
    m, h = pl.program_id(0), pl.program_id(1)
    heads = pl.num_programs(1)
    rows = query.shape[0]
    slots = query.shape[1] // (heads * HDIM)

    @pl.when(h == 0)
    def _():
        gate_grad[...] = jnp.zeros_like(gate_grad)

    allowed = allowed_pairs(rows, lens[m])
    cos_part, back_sine = cosine[...], -sine[...]
    keys, values, totals = key[...], value[...], total[...]
    lanes = lax.broadcasted_iota(jnp.int32, gate_grad.shape, 1)
    slot_sums = gate_grad[...]
    key_sum = jnp.zeros(key.shape, f32)
    value_sum = jnp.zeros(value.shape, f32)
    for s in range(slots):
        columns = pl.ds(pl.multiple_of((s * heads + h) * HDIM, HDIM), HDIM)
        full_grad = vals_grad[:, columns]
        slot_sum = jnp.sum(vals[:, columns].astype(f32) * full_grad, axis=1, keepdims=True)
        slot_sums += jnp.where(lanes == s, slot_sum, 0.0)
        gated_grad = (gates[:, s : s + 1] * full_grad).astype(bf16)
        queries = query[:, columns]
        scores = jnp.where(allowed, dot_t(queries, keys) * HDIM ** (-0.5), very_low)
        probs = jnp.exp(scores - lane_value(totals, h * slots + s))
        prob_grad = dot_t(gated_grad, values)
        inner = jnp.sum(probs * prob_grad, axis=1, keepdims=True)
        score_grad = (probs * (prob_grad - inner) * HDIM ** (-0.5)).astype(bf16)
        query_grad[:, columns] = turn(dot(score_grad, keys), cos_part, back_sine).astype(bf16)
        key_sum += t_dot(score_grad, queries)
        value_sum += t_dot(probs.astype(bf16), gated_grad)
    gate_grad[...] = slot_sums
    key_grad[...] = turn(key_sum, cos_part, back_sine).astype(bf16)
    value_grad[...] = value_sum.astype(bf16)


def attention_specs(own_heads, rows, width):
    def block(columns, index):
        return pl.BlockSpec((rows, columns), index)

    return {
        "query": block(width, lambda m, h, lens: (m, 0)),
        "key": block(HDIM, lambda m, h, lens: (m, h)),
        "value": block(HDIM, lambda m, h, lens: (m, own_heads + h)),
        "rows": block(HDIM, lambda m, h, lens: (m, 0)),
        "peak": pl.BlockSpec((8, HDIM), lambda m, h, lens: (m, 0)),
    }


def attention_forward(lens, query, joint_kv, tables, gates, hits, own_heads, rows):
    micro = lens.shape[0]
    at = attention_specs(own_heads, rows, query.shape[1])
    shape = jax.ShapeDtypeStruct
    total_rows = micro * rows
    return pl.pallas_call(
        forward_kernel,
        grid_spec=pltpu.PrefetchScalarGridSpec(
            num_scalar_prefetch=1,
            grid=(micro, own_heads),
            in_specs=[at["query"], at["key"], at["value"]] + [at["rows"]] * 4,
            out_specs=[at["query"]] * 3 + [at["key"], at["rows"], at["peak"]],
        ),
        out_shape=[shape(query.shape, bf16)] * 3
        + [
            shape((total_rows, own_heads * HDIM), bf16),
            shape((total_rows, HDIM), f32),
            shape((micro * 8, HDIM), f32),
        ],
        compiler_params=pltpu.CompilerParams(vmem_limit_bytes=48 * 2**20),
        cost_estimate=pl.CostEstimate(
            flops=4 * rows * rows * HDIM * micro * HEADS,
            bytes_accessed=14 * query.size,
            transcendentals=rows * rows * micro * HEADS,
        ),
        name="attention_forward",
    )(lens, query, joint_kv, joint_kv, tables[0], tables[1], gates, hits)


def attention_backward(
    lens, query, key, joint_kv, vals, vals_grad, tables, gates, total, own_heads, rows
):
    micro = lens.shape[0]
    at = attention_specs(own_heads, rows, query.shape[1])
    shape = jax.ShapeDtypeStruct
    total_rows = micro * rows
    return pl.pallas_call(
        backward_kernel,
        grid_spec=pltpu.PrefetchScalarGridSpec(
            num_scalar_prefetch=1,
            grid=(micro, own_heads),
            in_specs=[at["query"], at["key"], at["value"], at["query"], at["query"]]
            + [at["rows"]] * 4,
            out_specs=[at["query"], at["key"], at["key"], at["rows"]],
        ),
        out_shape=[shape(query.shape, bf16)]
        + [shape((total_rows, own_heads * HDIM), bf16)] * 2
        + [shape((total_rows, HDIM), f32)],
        compiler_params=pltpu.CompilerParams(vmem_limit_bytes=48 * 2**20),
        cost_estimate=pl.CostEstimate(
            flops=10 * rows * rows * HDIM * micro * HEADS,
            bytes_accessed=14 * query.size,
            transcendentals=rows * rows * micro * HEADS,
        ),
        name="attention_backward",
    )(lens, query, key, joint_kv, vals, vals_grad, tables[0], tables[1], gates, total)


def normalize(values):
    row_scale = lax.rsqrt(jnp.mean(values * values, axis=-1, keepdims=True) + eps_norm)
    return values * row_scale, row_scale


def norm_back(grad_hat, normed, row_scale):
    return row_scale * (grad_hat - normed * jnp.mean(grad_hat * normed, axis=-1, keepdims=True))


def route_gates(logits, routes, expert_table):
    expert_ids = jnp.arange(expert_table.shape[0], dtype=jnp.int32)
    matches = routes[:, :, None] == expert_ids[None, None, :]
    picked = jnp.sum(jnp.where(matches, logits[:, None, :], 0.0), axis=-1)
    gate_vals = jax.nn.softmax(picked, axis=-1)
    slot_ids = route_slots(routes, expert_table)
    chosen = slot_ids[:, :, None] == expert_ids[None, None, :]
    gates = jnp.sum(jnp.where(chosen, gate_vals[:, :, None], 0.0), axis=1)
    return gates, matches, chosen, gate_vals


def route_slots(routes, expert_table):
    expert_ids = jnp.arange(expert_table.shape[0], dtype=jnp.int32)
    matches = routes[..., None] == expert_ids
    return jnp.sum(jnp.where(matches, expert_table, 0), axis=-1)


def gate_back(slot_grad, gate_vals, matches, chosen):
    picked = jnp.sum(jnp.where(chosen, slot_grad[:, None, :], 0.0), axis=-1)
    inner_sum = jnp.sum(gate_vals * picked, axis=-1, keepdims=True)
    picked_grad = gate_vals * (picked - inner_sum)
    return jnp.sum(jnp.where(matches, picked_grad[:, :, None], 0.0), axis=1)


def unit_blocks(count):
    return [(start, min(512, count - start)) for start in range(0, count, 512)]


def expert_kernel(place_ref, hidden, grad, *refs):
    piece_count = (len(refs) - 6) // 2
    own_pieces, near_pieces = refs[:piece_count], refs[piece_count : 2 * piece_count]
    out, hidden_out, act_out, joint_out, weights, sems = refs[2 * piece_count :]
    core, chip = place_ref[0], place_ref[1]
    rows, columns = near_pieces[0].shape
    units = columns // 3
    width = grad.shape[1]

    @pl.when(pl.program_id(0) == 0)
    def _():
        copies = []
        for k in range(piece_count):
            base = (chip ^ k) * (2 * rows)
            for number, (piece, part) in enumerate(
                ((own_pieces[k], core), (near_pieces[k], 1 - core))
            ):
                start = pl.multiple_of(base + part * rows, 16)
                copies.append(
                    pltpu.make_async_copy(
                        piece, weights.at[pl.ds(start, rows)], sems.at[2 * k + number]
                    )
                )
        for copy in copies:
            copy.start()
        for copy in copies:
            copy.wait()

    slot_sum = jnp.zeros((hidden.shape[0], 1), f32)
    for start, size in unit_blocks(units):
        gate_pre = dot(hidden[:, :width], weights[:, start : start + size])
        up_pre = dot(hidden[:, :width], weights[:, units + start : units + start + size])
        act_grad = dot(grad[...], weights[:, 2 * units + start : 2 * units + start + size])
        sigma = 1.0 / (1.0 + jnp.exp(-gate_pre))
        silu_vals = gate_pre * sigma
        active = (silu_vals * up_pre).astype(bf16)
        act_out[:, start : start + size] = active
        slot_sum += jnp.sum(active.astype(f32) * act_grad, axis=1, keepdims=True)
        gate_grad = act_grad * up_pre * sigma * (1.0 + gate_pre * (1.0 - sigma))
        joint_out[:, start : start + size] = gate_grad.astype(bf16)
        joint_out[:, units + start : units + start + size] = (act_grad * silu_vals).astype(bf16)
    for start in range(0, width, 512):
        block = weights[start : start + 512, : 2 * units]
        hidden_out[:, start : start + 512] = dot_t(joint_out[...], block).astype(bf16)
        block = weights[start : start + 512, 2 * units :]
        out[:, start : start + 512] = dot_t(act_out[...], block).astype(bf16)
    lanes = lax.broadcasted_iota(jnp.int32, (hidden.shape[0], HDIM), 1)
    hidden_out[:, width:] = jnp.where(lanes == 0, slot_sum, 0.0).astype(bf16)


def expert_rows(position, hidden, grad, own_pieces, near_pieces):
    rows, width = grad.shape
    columns = near_pieces[0].shape[1]
    units = columns // 3
    tile = rows // 2
    shape = jax.ShapeDtypeStruct
    count = len(own_pieces)

    def tiled(size):
        return pl.BlockSpec((tile, size), lambda i, at: (i, 0))

    return pl.pallas_call(
        expert_kernel,
        grid_spec=pltpu.PrefetchScalarGridSpec(
            num_scalar_prefetch=1,
            grid=(rows // tile,),
            in_specs=[tiled(width + HDIM), tiled(width)]
            + [pl.BlockSpec(memory_space=pl.ANY)] * (2 * count),
            out_specs=[tiled(width), tiled(width + HDIM), tiled(units), tiled(2 * units)],
            scratch_shapes=[
                pltpu.VMEM((width, columns), bf16),
                pltpu.SemaphoreType.DMA((2 * count,)),
            ],
        ),
        out_shape=[
            shape((rows, width), bf16),
            shape((rows, width + HDIM), bf16),
            shape((rows, units), bf16),
            shape((rows, 2 * units), bf16),
        ],
        compiler_params=pltpu.CompilerParams(vmem_limit_bytes=56 * 2**20),
        cost_estimate=pl.CostEstimate(
            flops=4 * rows * width * columns,
            bytes_accessed=2 * (width * columns + 6 * rows * width),
            transcendentals=rows * units,
        ),
        name="expert_rows",
    )(position, hidden, grad, *own_pieces, *near_pieces)


def expert_grad_kernel(cuts, order, *refs):
    hidden, grad, gates, joint, active = [refs[2 * n : 2 * n + 2] for n in range(5)]
    outs = refs[10:]
    units = active[0].shape[1]

    def scaled(blocks):
        return [
            (block[...].astype(f32) * gate[:, :1].astype(f32)).astype(bf16)
            for block, gate in zip(blocks, gates)
        ]

    left, right = scaled(hidden), scaled(grad)
    step = pl.program_id(0)
    first = [0]
    for cut in cuts:
        first.append(first[-1] + cut)
    for out, start, cut in zip(outs, first, cuts):

        @pl.when((step >= start) & (step < start + cut))
        def _():
            for start, size in unit_blocks(2 * units):
                out[:, start : start + size] = sum(
                    t_dot(rows, part[:, start : start + size]) for rows, part in zip(left, joint)
                ).astype(bf16)
            for start, size in unit_blocks(units):
                out[:, 2 * units + start : 2 * units + start + size] = sum(
                    t_dot(rows, part[:, start : start + size]) for rows, part in zip(right, active)
                ).astype(bf16)


def expert_grads(chunks, cuts, chunk_rows, rows_of, joints, actives):
    hidden, grad = rows_of[:2], rows_of[2:]
    rows, units = actives[0].shape
    width = grad[0].shape[1]
    half = chunk_rows // 2
    count = len(chunks)
    order = jnp.stack([2 * chunk + part for chunk in chunks for part in range(2)]).astype(jnp.int32)

    def whole(size, column=0):
        return pl.BlockSpec(
            (rows, size), lambda i, at: (0, column), pipeline_mode=pl.Buffered(1)
        )

    column = pl.BlockSpec((rows, half), lambda i, at: (0, at[i]))
    return pl.pallas_call(
        functools.partial(expert_grad_kernel, cuts),
        grid_spec=pltpu.PrefetchScalarGridSpec(
            num_scalar_prefetch=1,
            grid=(2 * count,),
            in_specs=[column] * 4
            + [whole(HDIM, width // HDIM)] * 2
            + [whole(2 * units)] * 2
            + [whole(units)] * 2,
            out_specs=[
                pl.BlockSpec(
                    (half, 3 * units),
                    lambda i, at, start=sum(cuts[:n]), cut=cut: (jnp.clip(i - start, 0, cut - 1), 0),
                )
                for n, cut in enumerate(cuts)
            ],
        ),
        out_shape=[jax.ShapeDtypeStruct((cut * half, 3 * units), bf16) for cut in cuts],
        compiler_params=pltpu.CompilerParams(vmem_limit_bytes=56 * 2**20),
        cost_estimate=pl.CostEstimate(
            flops=4 * count * chunk_rows * rows * 3 * units,
            bytes_accessed=2 * (rows * 6 * units + count * chunk_rows * (4 * rows + 3 * units)),
            transcendentals=0,
        ),
        name="expert_grads",
    )(order, *hidden, *grad, *hidden, *joints, *actives)


def local(
    tokens,
    cotangent,
    seq_lengths,
    dealing,
    attn_routes,
    ffn_routes,
    expert_table,
    clip_limit,
    attn_gain,
    ffn_gain,
    attn_router,
    ffn_router,
    query_weight,
    attn_out_weight,
    kv_weight,
    gate_up_weight,
    down_weight,
):
    micro, tok_rows, width = tokens.shape
    dp_count = lax.axis_size("dp")
    slots = lax.axis_size("expert")
    col = lax.axis_index("expert")
    group = lax.axis_index("dp")
    piece_rows = tok_rows // dp_count
    cap = tok_rows * TOP * 3 // (2 * slots)
    group_rows = tok_rows * slots
    all_rows = micro * group_rows
    home_rows = micro * tok_rows
    query_width = HEADS * HDIM
    own_heads = HEADS // slots
    own_width = own_heads * HDIM
    shard_rows = query_weight.shape[1]
    score_scale = HDIM ** (-0.5)
    core = group % 2
    chip = group // 2
    side = chip % 2
    chips = dp_count // 2
    lines = chips // 2
    quarter = FF // 4
    chip_rows = 2 * shard_rows

    both = jnp.stack([tokens, cotangent]).reshape(2 * micro, dp_count, piece_rows, width)
    both = lax.all_to_all(both.transpose(1, 0, 2, 3), "dp", split_axis=0, concat_axis=0, tiled=True)
    def quarter_of(half, part):
        start = (2 * half + part) * quarter
        return jnp.concatenate(
            [
                lax.dynamic_slice_in_dim(gate_up_weight[0], start, quarter, 1),
                lax.dynamic_slice_in_dim(gate_up_weight[0], FF + start, quarter, 1),
                lax.dynamic_slice_in_dim(down_weight[0], start, quarter, 1),
            ],
            axis=1,
        )

    parts = (1 - core, core)
    keep_pair = [quarter_of(side, part) for part in parts]
    send_pair = [quarter_of(1 - side, part) for part in parts]
    kv_in, query_in, out_in = after(
        (kv_weight, query_weight[0], attn_out_weight[0]), keep_pair[0], send_pair[0]
    )
    both = both.transpose(1, 0, 2, 3).reshape(2, micro, tok_rows, width)
    deal = (dealing[:, :, None] == jnp.arange(tok_rows, dtype=jnp.int32)).astype(bf16)
    work = jnp.einsum("mtr,bmrd->bmtd", deal, both, preferred_element_type=f32)
    x_home = work[0].reshape(home_rows, width)
    dy_home = work[1].reshape(home_rows, width)

    def columns_of(*shards):
        pieces = [shard.reshape(shard_rows, slots, own_width) for shard in shards]
        out = jnp.zeros((shard_rows, len(shards) * query_width), shards[0].dtype)
        for k in range(slots):
            part = jnp.concatenate(
                [lax.dynamic_index_in_dim(piece, col ^ k, 1, keepdims=False) for piece in pieces],
                axis=1,
            )
            part = swap(part, "expert", k) if k else part
            for number in range(len(shards)):
                out = lax.dynamic_update_slice_in_dim(
                    out,
                    part[:, number * own_width : (number + 1) * own_width],
                    number * query_width + (col ^ k) * own_width,
                    1,
                )
        return out

    def slots_of(columns):
        pieces = columns.reshape(shard_rows, slots, own_width)
        out = jnp.zeros((shard_rows, query_width), columns.dtype)
        for k in range(slots):
            part = lax.dynamic_index_in_dim(pieces, col ^ k, 1, keepdims=False)
            part = swap(part, "expert", k) if k else part
            out = lax.dynamic_update_slice_in_dim(out, part, (col ^ k) * own_width, 1)
        return out

    half_slots = slots // 2
    first_pairs = [(c, 2 * c) for c in range(half_slots)]
    first_pairs += [(c, 2 * (c - half_slots) + 1) for c in range(half_slots, slots)]
    second_pairs = [(c, 2 * c + 1) for c in range(half_slots)]
    second_pairs += [(c, 2 * (c - half_slots)) for c in range(half_slots, slots)]
    holds_keys = col < half_slots
    even_col = col % 2 == 0
    low_kv, high_kv = kv_in[:, :own_width], kv_in[:, own_width:]
    first_got = lax.ppermute(jnp.where(holds_keys, low_kv, high_kv), "expert", first_pairs)
    second_got = lax.ppermute(jnp.where(holds_keys, high_kv, low_kv), "expert", second_pairs)
    own_kv = jnp.concatenate(
        [
            jnp.where(even_col, first_got, second_got),
            jnp.where(even_col, second_got, first_got),
        ],
        axis=1,
    )
    line_steps = [4 * line for line in range(1, lines)]
    side_first = swap(send_pair[0], "dp", 2)
    keep_first = [swap(keep_pair[0], "dp", step) for step in line_steps]
    joint_own = columns_of(query_in, out_in)
    first_own = jnp.concatenate([joint_own[:, :query_width], own_kv], axis=1)
    first_own, second_own = lax.optimization_barrier(
        (first_own, joint_own[:, query_width:], side_first, keep_first)
    )[:2]
    joint_full = lax.all_gather(first_own, "dp", axis=0, tiled=True)
    out_full = lax.all_gather(second_own, "dp", axis=0, tiled=True)
    late_pair = after((keep_pair[1], send_pair[1], side_first), joint_full)
    keep_second = [swap(late_pair[0], "dp", step) for step in line_steps]
    side_second = swap(late_pair[1], "dp", 2)
    first_lines = [swap(late_pair[2], "dp", step) for step in line_steps]
    second_lines = [swap(side_second, "dp", step) for step in line_steps]
    firsts, seconds = [keep_pair[0], side_first], [keep_pair[1], side_second]
    for line in range(lines - 1):
        firsts += [keep_first[line], first_lines[line]]
        seconds += [keep_second[line], second_lines[line]]
    near_pieces = [swap(piece, "dp", 1) for piece in firsts]
    own_pieces = seconds
    query_full = joint_full[:, :query_width]
    kv_full = joint_full[:, query_width:]

    positions = jnp.arange(group_rows, dtype=jnp.int32)
    first_len = lax.dynamic_index_in_dim(seq_lengths[:, :, 0], group, 1, keepdims=True)
    in_second = positions[None, :] >= first_len
    places = positions[None, :] - jnp.where(in_second, first_len, 0)
    tables = rotation_tables(places.reshape(all_rows))

    def gather_rows(value):
        shaped = value.reshape(micro, tok_rows, -1)
        out = jnp.zeros((micro, group_rows, shaped.shape[-1]), value.dtype)
        for k in range(slots):
            part = swap(shaped, "expert", k) if k else shaped
            out = lax.dynamic_update_slice_in_dim(out, part, (col ^ k) * tok_rows, 1)
        return out.reshape(all_rows, -1)

    def scatter_rows(value):
        shaped = value.reshape(micro, group_rows, -1)
        total = None
        for k in range(slots):
            part = lax.dynamic_slice_in_dim(shaped, (col ^ k) * tok_rows, tok_rows, 1)
            if k:
                part = swap(part.astype(bf16), "expert", k)
            part = part.astype(f32)
            total = part if total is None else total + part
        return total.reshape(home_rows, -1)

    home_routes = lax.dynamic_slice_in_dim(ffn_routes, col * tok_rows, tok_rows, 1)
    home_slots = route_slots(home_routes, expert_table)
    packs = []
    before = jnp.tril(jnp.ones((tok_rows, tok_rows), bf16), -1)
    for k in range(slots):
        hits = jnp.any(home_slots == (col ^ k), axis=-1)
        rank = jnp.einsum("ts,ms->mt", before, hits.astype(bf16), preferred_element_type=f32)
        packs.append(
            hits[:, None, :]
            & (rank[:, None, :] == jnp.arange(cap, dtype=jnp.int32).astype(f32)[None, :, None])
        )
    packs = jnp.stack(packs)
    packs_low = packs.astype(bf16)
    pack_rows = micro * cap
    sent_rows = slots * pack_rows

    def send_packed(value, lane=None):
        packed = jnp.einsum(
            "kmct,mtd->kmcd", packs_low, value.reshape(micro, tok_rows, -1), preferred_element_type=f32
        ).astype(bf16)
        if lane is not None:
            lanes = jnp.pad(lane[..., None], ((0, 0), (0, 0), (0, 0), (0, HDIM - 1)))
            packed = jnp.concatenate([packed, lanes.astype(bf16)], axis=-1)
        parts = [swap(packed[k], "expert", k) if k else packed[k] for k in range(slots)]
        return jnp.stack(parts).reshape(sent_rows, -1)

    def near_rows(value):
        return jnp.concatenate([value, swap(value, "dp", 1)], axis=0)

    def quad_sums(value):
        (own, near), (far, across) = [jnp.split(half, 2, axis=0) for half in value]
        far_sum = far.astype(f32) + swap(across, "dp", 1).astype(f32)
        return own.astype(f32) + swap(near, "dp", 1).astype(f32), far_sum.astype(bf16)

    def return_packed(value, *others):
        shaped = value.astype(bf16).reshape(slots, micro, cap, -1)
        parts = [swap(shaped[k], "expert", k) if k else shaped[k] for k in range(slots)]
        return after(parts, *others)

    def unpack(packed, scale):
        total = None
        for k in range(slots):
            rows = jnp.einsum("mct,mcd->mtd", packs_low[k], packed[k], preferred_element_type=f32)
            rows = rows.reshape(home_rows, -1) * take(scale.T, col ^ k)[:, None]
            total = rows if total is None else total + rows
        return total

    gain_one = attn_gain.astype(f32)
    gain_two = ffn_gain.astype(f32)
    normed_one, scale_one = normalize(x_home)
    hidden_one_home = (normed_one * gain_one).astype(bf16)
    hidden_one_raw = gather_rows(after(hidden_one_home, near_pieces[:3]))
    grad_sent = send_packed(dy_home.astype(bf16))
    hidden_one = after(hidden_one_raw, grad_sent)
    logits_one = dot(hidden_one, attn_router)
    gates_one, matches_one, chosen_one, gate_vals_one = route_gates(
        logits_one, attn_routes.reshape(all_rows, TOP), expert_table
    )
    hits_one = jnp.any(chosen_one, axis=1).astype(f32)

    def wide(value):
        return jnp.pad(value, ((0, 0), (0, HDIM - value.shape[1])))

    kv_part = dot(hidden_one, kv_full).astype(bf16)
    query_part = dot(hidden_one, query_full)
    lens = first_len[:, 0].astype(jnp.int32)
    gates_wide = wide(gates_one)
    attn_vals, gated_vals, query_rot, key_rot, log_total, peaks = attention_forward(
        lens, query_part, kv_part, tables, gates_wide, wide(hits_one), own_heads, group_rows
    )
    peaks = jnp.max(peaks, axis=0)[: own_heads * slots]
    attn_part = after(dot_t(gated_vals, out_full), keep_second, side_second)
    attn_home = after(scatter_rows(attn_part), first_lines)
    grad_sent = after(grad_sent, attn_home)
    grad_near, grad_far = near_rows(grad_sent), near_rows(swap(grad_sent, "dp", 2))

    resid = x_home + attn_home
    normed_two, scale_two = normalize(resid)
    hidden_two = (normed_two * gain_two).astype(bf16)
    logits_two = dot(hidden_two, ffn_router)
    gates_two, matches_two, chosen_two, gate_vals_two = route_gates(
        logits_two, home_routes.reshape(home_rows, TOP), expert_table
    )
    gates_by_slot = gates_two.reshape(micro, tok_rows, slots)
    gate_parts = []
    for k in range(slots):
        gate_col = lax.dynamic_index_in_dim(gates_by_slot, col ^ k, 2, keepdims=False)
        gate_parts.append(jnp.sum(jnp.where(packs[k], gate_col[:, None, :], 0.0), axis=-1))
    hidden_sent = after(
        send_packed(hidden_two, jnp.stack(gate_parts)), second_lines
    )
    hidden_near, hidden_far = near_rows(hidden_sent), swap(hidden_sent, "dp", 2)
    hidden_near = after(hidden_near, near_pieces, grad_near, grad_far)
    position = jnp.stack([core, chip]).astype(jnp.int32)
    near_results = expert_rows(
        position, hidden_near, after(grad_near, grad_far), own_pieces, near_pieces
    )
    hidden_far = near_rows(after(hidden_far, near_results))
    far_results = expert_rows(position, hidden_far, grad_far, own_pieces, near_pieces)
    ffn_parts, hidden_parts, actives, joint_grads = zip(near_results, far_results)

    def block_grads(steps, *others):
        rows = after((hidden_near, hidden_far, grad_near, grad_far), *others)
        cuts = (2,) * len(steps)
        return expert_grads([chip ^ k for k in steps], cuts, chip_rows, rows, joint_grads, actives)

    hidden_sum, hidden_far_sum = quad_sums(hidden_parts)
    ffn_sum, ffn_far_sum = quad_sums(after(ffn_parts, hidden_far_sum))
    line_grads = block_grads([k ^ 1 for k in range(2, chips)], hidden_far_sum)
    side_got = [swap(line_grads[2 * line], "dp", step) for line, step in enumerate(line_steps)]
    blocks = after(line_grads[1::2], side_got)
    keep_got = [swap(block, "dp", step) for block, step in zip(blocks, line_steps)]
    hidden_got, ffn_far_sum, ffn_sum = lax.optimization_barrier(
        (swap(hidden_far_sum, "dp", 2), ffn_far_sum, ffn_sum, line_grads)
    )[:3]
    hidden_sum = hidden_sum + hidden_got.astype(f32)
    own_grads = block_grads([1, 0], hidden_sum)
    back_packed = return_packed(hidden_sum, *own_grads)
    ffn_sum = ffn_sum + swap(after(ffn_far_sum, hidden_got), "dp", 2).astype(f32)

    def total(own, got):
        return functools.reduce(jnp.add, [part.astype(f32) for part in [own] + got]).astype(bf16)

    slot_two_grad = jnp.zeros((slots, home_rows), f32)
    for k in range(slots):
        rows = jnp.sum(
            jnp.where(packs[k], back_packed[k][:, :, width].astype(f32)[:, :, None], 0.0), axis=1
        )
        slot_two_grad = lax.dynamic_update_index_in_dim(
            slot_two_grad, rows.reshape(home_rows), col ^ k, 0
        )
    hidden_two_grad = unpack([part[..., :width] for part in back_packed], gates_two)
    logit_two_grad = gate_back(slot_two_grad.T, gate_vals_two, matches_two, chosen_two).astype(bf16)
    hidden_two_grad = hidden_two_grad + dot_t(logit_two_grad, ffn_router)
    router_two_grad = t_dot(logit_two_grad, hidden_two)
    gain_two_grad = jnp.sum(hidden_two_grad * normed_two, axis=0)
    resid_grad = dy_home + norm_back(hidden_two_grad * gain_two, normed_two, scale_two)

    resid_grad_all, ffn_sum = lax.optimization_barrier(
        (gather_rows(resid_grad.astype(bf16)), ffn_sum, side_got)
    )[:2]
    out_part = t_dot(resid_grad_all, gated_vals).astype(bf16)
    vals_grad = after(dot(resid_grad_all, out_full), out_part)
    side_own = after((own_grads[0], side_got), vals_grad)
    vals_grad, side_sum = lax.optimization_barrier((vals_grad, total(*side_own)))
    other_sum = swap(side_sum, "dp", 2)
    ffn_packed = return_packed(after(ffn_sum, vals_grad))
    out_home = (resid + unpack(ffn_packed, gates_two)).astype(bf16)
    query_grad, key_grad, value_grad, slot_part_one = attention_backward(
        lens, query_rot, key_rot, kv_part, attn_vals, vals_grad, tables, gates_wide, log_total,
        own_heads, group_rows,
    )
    query_grad, key_grad, value_grad, slot_part_one = lax.optimization_barrier(
        (query_grad, key_grad, value_grad, slot_part_one, ffn_packed)
    )[:4]
    kv_grad = jnp.concatenate([key_grad, value_grad], axis=1)
    hidden_one_part = dot_t(query_grad, query_full) + dot_t(kv_grad, kv_full)
    hidden_one_part = hidden_one_part.astype(bf16)
    joint_part_grad = t_dot(
        after(hidden_one, hidden_one_part), jnp.concatenate([query_grad, kv_grad], axis=1)
    ).astype(bf16)
    back_one = scatter_rows(
        jnp.concatenate([hidden_one_part, slot_part_one.astype(bf16)], axis=1)
    )
    back_one = after(back_one, joint_part_grad)
    out_own = lax.psum_scatter(out_part, "dp", scatter_dimension=0, tiled=True)
    out_grad = slots_of(after(out_own, back_one))
    hidden_one_grad, slot_one_grad = back_one[:, :width], back_one[:, width : width + slots]

    def own(value):
        shaped = value.reshape((micro, group_rows) + value.shape[1:])
        part = lax.dynamic_slice_in_dim(shaped, col * tok_rows, tok_rows, 1)
        return part.reshape((home_rows,) + value.shape[1:])

    logit_one_grad = gate_back(
        slot_one_grad, own(gate_vals_one), own(matches_one), own(chosen_one)
    ).astype(bf16)
    hidden_one_grad = hidden_one_grad + dot_t(logit_one_grad, attn_router)
    router_one_grad = t_dot(logit_one_grad, hidden_one_home)
    gain_one_grad = jnp.sum(hidden_one_grad * normed_one, axis=0)
    in_home = resid_grad + norm_back(hidden_one_grad * gain_one, normed_one, scale_one)

    def reduced(value):
        return lax.psum_scatter(value, "dp", scatter_dimension=0, tiled=True)

    in_low = in_home.astype(bf16)
    joint_own = reduced(joint_part_grad)

    results = jnp.stack([out_home, in_low]).reshape(2, micro, tok_rows, width)
    results = jnp.einsum("mtr,bmtd->bmrd", deal, results, preferred_element_type=f32).astype(bf16)
    results = results.reshape(2 * micro, dp_count, piece_rows, width).transpose(1, 0, 2, 3)
    results = results.reshape(dp_count, 2 * micro * piece_rows, width)
    sent_back = results.shape[1]
    small = jnp.concatenate(
        [gain_one_grad[None], gain_two_grad[None], router_one_grad, router_two_grad], axis=0
    ).astype(bf16)
    sum_rows = small.shape[0]
    peak_count = own_heads * slots
    peak_parts, rest = [], peaks
    for _ in range(3):
        peak_parts.append(lax.reduce_precision(rest, 8, 7))
        rest = rest - peak_parts[-1]
    peak_row = jnp.concatenate(peak_parts).astype(bf16)
    small = jnp.pad(small, ((0, -sum_rows % 16 or 16), (0, 0)))
    small = lax.dynamic_update_slice(small, peak_row[None], (sum_rows, 0))
    small = jnp.broadcast_to(small[None], (dp_count,) + small.shape)
    results = jnp.concatenate([results, small], axis=1)
    results = lax.all_to_all(results, "dp", split_axis=0, concat_axis=0, tiled=True)
    query_own, kv_own = joint_own[:, :query_width], joint_own[:, query_width:]
    results, other_sum, keep_got = lax.optimization_barrier((results, other_sum, keep_got))
    small = results[:, sent_back:].astype(f32)
    results = results[:, :sent_back].reshape(dp_count, 2 * micro, piece_rows, width)
    results = results.transpose(1, 0, 2, 3).reshape(2, micro, tok_rows, width)
    peak_row = small[:, sum_rows, : 3 * peak_count].reshape(dp_count, 3, peak_count)
    peak_row = jnp.max((peak_row[:, 0] + peak_row[:, 1]) + peak_row[:, 2], axis=0)
    small = jnp.sum(small, axis=0)
    small = lax.dynamic_update_slice(small, peak_row[None], (sum_rows, 0))
    smalls = [swap(small, "expert", k) if k else small for k in range(slots)]
    peaks_all = jnp.zeros((slots, HEADS), f32)
    for k, part in enumerate(smalls):
        part = part[sum_rows, :peak_count].reshape(own_heads, slots).T
        peaks_all = lax.dynamic_update_slice(peaks_all, part, (0, (col ^ k) * own_heads))
    while len(smalls) > 1:
        smalls = [left + right for left, right in zip(smalls[::2], smalls[1::2])]
    sums = smalls[0][:sum_rows]

    keep_sums = total(own_grads[1], keep_got).reshape(2, shard_rows, 3 * quarter)
    other_sums = other_sum.reshape(2, shard_rows, 3 * quarter)
    by_rows = [jnp.stack([keep_sums[part], other_sums[part]]) for part in range(2)]
    own_pair = jnp.where(core == 0, by_rows[0], by_rows[1])
    near_pair = swap(jnp.where(core == 0, by_rows[1], by_rows[0]), "dp", 1)
    by_core = [jnp.where(core == 0, own_pair, near_pair), jnp.where(core == 0, near_pair, own_pair)]
    by_side = [[jnp.where(side == s, part[0], part[1]) for part in by_core] for s in range(2)]
    blocks = [part for row in by_side for part in row]
    gate_up_grad = jnp.concatenate(
        [b[:, :quarter] for b in blocks] + [b[:, quarter : 2 * quarter] for b in blocks], axis=1
    ).astype(f32)
    down_grad = jnp.concatenate([b[:, 2 * quarter :] for b in blocks], axis=1).astype(f32)

    out_grad = out_grad.astype(f32)
    query_out = slots_of(query_own).astype(f32)
    key_part, value_part = kv_own[:, :own_width], kv_own[:, own_width:]
    first_back = lax.ppermute(
        jnp.where(even_col, key_part, value_part), "expert", [(b, a) for a, b in first_pairs]
    )
    second_back = lax.ppermute(
        jnp.where(even_col, value_part, key_part), "expert", [(b, a) for a, b in second_pairs]
    )
    kv_out = jnp.concatenate(
        [
            jnp.where(holds_keys, first_back, second_back),
            jnp.where(holds_keys, second_back, first_back),
        ],
        axis=1,
    ).astype(f32)

    limit = clip_limit[0].astype(f32)
    factor = limit / jnp.maximum(peaks_all, limit)
    query_scale = jnp.repeat(jnp.sqrt(take(factor, col)), HDIM)
    query_clipped = (query_weight.astype(f32) * query_scale[None, None, :]).astype(bf16)
    full_scale = jnp.concatenate(
        [jnp.repeat(jnp.sqrt(jnp.min(factor, axis=0)), HDIM), jnp.ones((query_width,), f32)]
    )
    piece_width = kv_weight.shape[1]
    piece_scale = lax.dynamic_slice_in_dim(full_scale, col * piece_width, piece_width)
    kv_clipped = (kv_weight.astype(f32) * piece_scale[None, :]).astype(bf16)
    return (
        results[0],
        results[1],
        sums[0],
        sums[1],
        sums[2 : 2 + slots].T,
        sums[2 + slots : sum_rows].T,
        query_out[None],
        out_grad[None],
        kv_out,
        gate_up_grad[None],
        down_grad[None],
        query_clipped,
        kv_clipped,
    )


def solution(mesh):
    placed = (
        P(None, ("dp", "expert"), None),
        P(None, ("dp", "expert"), None),
        P(),
        P(None, ("dp", "expert")),
        P(None, "dp", None),
        P(None, "dp", None),
        P(),
        P(),
        P(),
        P(),
        P(),
        P(),
        P("expert", "dp", None),
        P("expert", "dp", None),
        P("dp", "expert"),
        P("expert", "dp", None),
        P("expert", "dp", None),
    )
    return jax.shard_map(
        local,
        mesh=mesh,
        in_specs=placed,
        out_specs=(
            P(None, ("dp", "expert"), None),
            P(None, ("dp", "expert"), None),
            P(),
            P(),
            P(),
            P(),
            P("expert", "dp", None),
            P("expert", "dp", None),
            P("dp", "expert"),
            P("expert", "dp", None),
            P("expert", "dp", None),
            P("expert", "dp", None),
            P("dp", "expert"),
        ),
        check_vma=False,
    )
```

```python
import functools

import jax
import jax.numpy as jnp
from jax import lax
from jax.experimental import pallas as pl
from jax.experimental.pallas import tpu as pltpu
from jax.sharding import PartitionSpec as P

HEADS = 16
HDIM = 128
FF = 5632
TOP = 2

eps_norm = 1e-06
rope_base = 10000.0
very_low = -1e30

f32 = jnp.float32
bf16 = jnp.bfloat16


def dot(left, right):
    return jnp.dot(left, right, preferred_element_type=f32)


def dot_t(left, right):
    return lax.dot_general(left, right, (((1,), (1,)), ((), ())), preferred_element_type=f32)


def t_dot(left, right):
    return lax.dot_general(left, right, (((0,), (0,)), ((), ())), preferred_element_type=f32)


def swap(value, axis, step):
    count = lax.axis_size(axis)
    return lax.ppermute(value, axis, [(i, i ^ step) for i in range(count)])


def take(stacked, index):
    return lax.dynamic_index_in_dim(stacked, index, 0, keepdims=False)


def place(parts, positions):
    out = jnp.zeros((len(parts),) + parts[0].shape, parts[0].dtype)
    for part, position in zip(parts, positions):
        out = lax.dynamic_update_index_in_dim(out, part, position, 0)
    return out


def after(value, *others):
    return lax.optimization_barrier((value, others))[0]


def rotation_tables(places):
    half_dim = HDIM // 2
    frequency = rope_base ** (-jnp.arange(half_dim, dtype=f32) * 2.0 / HDIM)
    angles = places.astype(f32)[:, None] * frequency[None, :]
    cosine, sine = jnp.cos(angles), jnp.sin(angles)
    return (
        jnp.concatenate([cosine, cosine], axis=1),
        jnp.concatenate([-sine, sine], axis=1),
    )


def turn(values, cosine, sine):
    return values * cosine + pltpu.roll(values, HDIM // 2, 1) * sine


def lane_value(table, lane):
    lanes = lax.broadcasted_iota(jnp.int32, table.shape, 1)
    return jnp.sum(jnp.where(lanes == lane, table, 0.0), axis=1, keepdims=True)


def allowed_pairs(rows, first_len):
    query_at = lax.broadcasted_iota(jnp.int32, (rows, rows), 0)
    key_at = lax.broadcasted_iota(jnp.int32, (rows, rows), 1)
    return (key_at <= query_at) & ((key_at >= first_len) | (query_at < first_len))


def forward_kernel(
    lens, query, key, value, cosine, sine, gates, hits,
    vals_out, gated_out, query_out, key_out, total_out, peak_out,
):
    m, h = pl.program_id(0), pl.program_id(1)
    heads = pl.num_programs(1)
    rows = query.shape[0]
    slots = query.shape[1] // (heads * HDIM)

    @pl.when(h == 0)
    def _():
        total_out[...] = jnp.zeros_like(total_out)
        peak_out[...] = jnp.full_like(peak_out, very_low)

    cos_part, sin_part = cosine[...], sine[...]
    allowed = allowed_pairs(rows, lens[m])
    keys = turn(key[...].astype(f32), cos_part, sin_part).astype(bf16)
    key_out[...] = keys
    values = value[...]
    lanes = lax.broadcasted_iota(jnp.int32, total_out.shape, 1)
    peak_lanes = lax.broadcasted_iota(jnp.int32, peak_out.shape, 1)
    totals, peaks = total_out[...], peak_out[...]
    for s in range(slots):
        columns = pl.ds(pl.multiple_of((s * heads + h) * HDIM, HDIM), HDIM)
        turned = turn(query[:, columns], cos_part, sin_part).astype(bf16)
        query_out[:, columns] = turned
        scores = jnp.where(allowed, dot_t(turned, keys) * HDIM ** (-0.5), very_low)
        row_peak = jnp.max(scores, axis=1, keepdims=True)
        expo = jnp.exp(scores - row_peak)
        denom = jnp.sum(expo, axis=1, keepdims=True)
        probs = expo * (1.0 / denom)
        vals = dot(probs.astype(bf16), values).astype(bf16)
        vals_out[:, columns] = vals
        gated_out[:, columns] = (gates[:, s : s + 1] * vals.astype(f32)).astype(bf16)
        lane = h * slots + s
        totals = jnp.where(lanes == lane, row_peak + jnp.log(denom), totals)
        seen = jnp.where(hits[:, s : s + 1] > 0.0, row_peak, very_low)
        peaks = jnp.where(peak_lanes == lane, jnp.max(seen, axis=0, keepdims=True), peaks)
    total_out[...] = totals
    peak_out[...] = peaks


def backward_kernel(
    lens, query, key, value, vals, vals_grad, cosine, sine, gates, total,
    query_grad, key_grad, value_grad, gate_grad,
):
    m, h = pl.program_id(0), pl.program_id(1)
    heads = pl.num_programs(1)
    rows = query.shape[0]
    slots = query.shape[1] // (heads * HDIM)

    @pl.when(h == 0)
    def _():
        gate_grad[...] = jnp.zeros_like(gate_grad)

    allowed = allowed_pairs(rows, lens[m])
    cos_part, back_sine = cosine[...], -sine[...]
    keys, values, totals = key[...], value[...], total[...]
    lanes = lax.broadcasted_iota(jnp.int32, gate_grad.shape, 1)
    slot_sums = gate_grad[...]
    key_sum = jnp.zeros(key.shape, f32)
    value_sum = jnp.zeros(value.shape, f32)
    for s in range(slots):
        columns = pl.ds(pl.multiple_of((s * heads + h) * HDIM, HDIM), HDIM)
        full_grad = vals_grad[:, columns]
        slot_sum = jnp.sum(vals[:, columns].astype(f32) * full_grad, axis=1, keepdims=True)
        slot_sums += jnp.where(lanes == s, slot_sum, 0.0)
        gated_grad = (gates[:, s : s + 1] * full_grad).astype(bf16)
        queries = query[:, columns]
        scores = jnp.where(allowed, dot_t(queries, keys) * HDIM ** (-0.5), very_low)
        probs = jnp.exp(scores - lane_value(totals, h * slots + s))
        prob_grad = dot_t(gated_grad, values)
        inner = jnp.sum(probs * prob_grad, axis=1, keepdims=True)
        score_grad = (probs * (prob_grad - inner) * HDIM ** (-0.5)).astype(bf16)
        query_grad[:, columns] = turn(dot(score_grad, keys), cos_part, back_sine).astype(bf16)
        key_sum += t_dot(score_grad, queries)
        value_sum += t_dot(probs.astype(bf16), gated_grad)
    gate_grad[...] = slot_sums
    key_grad[...] = turn(key_sum, cos_part, back_sine).astype(bf16)
    value_grad[...] = value_sum.astype(bf16)


def attention_specs(own_heads, rows, width):
    def block(columns, index):
        return pl.BlockSpec((rows, columns), index)

    return {
        "query": block(width, lambda m, h, lens: (m, 0)),
        "key": block(HDIM, lambda m, h, lens: (m, h)),
        "value": block(HDIM, lambda m, h, lens: (m, own_heads + h)),
        "rows": block(HDIM, lambda m, h, lens: (m, 0)),
        "peak": pl.BlockSpec((8, HDIM), lambda m, h, lens: (m, 0)),
    }


def attention_forward(lens, query, joint_kv, tables, gates, hits, own_heads, rows):
    micro = lens.shape[0]
    at = attention_specs(own_heads, rows, query.shape[1])
    shape = jax.ShapeDtypeStruct
    total_rows = micro * rows
    return pl.pallas_call(
        forward_kernel,
        grid_spec=pltpu.PrefetchScalarGridSpec(
            num_scalar_prefetch=1,
            grid=(micro, own_heads),
            in_specs=[at["query"], at["key"], at["value"]] + [at["rows"]] * 4,
            out_specs=[at["query"]] * 3 + [at["key"], at["rows"], at["peak"]],
        ),
        out_shape=[shape(query.shape, bf16)] * 3
        + [
            shape((total_rows, own_heads * HDIM), bf16),
            shape((total_rows, HDIM), f32),
            shape((micro * 8, HDIM), f32),
        ],
        compiler_params=pltpu.CompilerParams(vmem_limit_bytes=48 * 2**20),
        cost_estimate=pl.CostEstimate(
            flops=4 * rows * rows * HDIM * micro * HEADS,
            bytes_accessed=14 * query.size,
            transcendentals=rows * rows * micro * HEADS,
        ),
        name="attention_forward",
    )(lens, query, joint_kv, joint_kv, tables[0], tables[1], gates, hits)


def attention_backward(
    lens, query, key, joint_kv, vals, vals_grad, tables, gates, total, own_heads, rows
):
    micro = lens.shape[0]
    at = attention_specs(own_heads, rows, query.shape[1])
    shape = jax.ShapeDtypeStruct
    total_rows = micro * rows
    return pl.pallas_call(
        backward_kernel,
        grid_spec=pltpu.PrefetchScalarGridSpec(
            num_scalar_prefetch=1,
            grid=(micro, own_heads),
            in_specs=[at["query"], at["key"], at["value"], at["query"], at["query"]]
            + [at["rows"]] * 4,
            out_specs=[at["query"], at["key"], at["key"], at["rows"]],
        ),
        out_shape=[shape(query.shape, bf16)]
        + [shape((total_rows, own_heads * HDIM), bf16)] * 2
        + [shape((total_rows, HDIM), f32)],
        compiler_params=pltpu.CompilerParams(vmem_limit_bytes=48 * 2**20),
        cost_estimate=pl.CostEstimate(
            flops=10 * rows * rows * HDIM * micro * HEADS,
            bytes_accessed=14 * query.size,
            transcendentals=rows * rows * micro * HEADS,
        ),
        name="attention_backward",
    )(lens, query, key, joint_kv, vals, vals_grad, tables[0], tables[1], gates, total)


def normalize(values):
    row_scale = lax.rsqrt(jnp.mean(values * values, axis=-1, keepdims=True) + eps_norm)
    return values * row_scale, row_scale


def norm_back(grad_hat, normed, row_scale):
    return row_scale * (grad_hat - normed * jnp.mean(grad_hat * normed, axis=-1, keepdims=True))


def route_gates(logits, routes, expert_table):
    expert_ids = jnp.arange(expert_table.shape[0], dtype=jnp.int32)
    matches = routes[:, :, None] == expert_ids[None, None, :]
    picked = jnp.sum(jnp.where(matches, logits[:, None, :], 0.0), axis=-1)
    gate_vals = jax.nn.softmax(picked, axis=-1)
    slot_ids = route_slots(routes, expert_table)
    chosen = slot_ids[:, :, None] == expert_ids[None, None, :]
    gates = jnp.sum(jnp.where(chosen, gate_vals[:, :, None], 0.0), axis=1)
    return gates, matches, chosen, gate_vals


def route_slots(routes, expert_table):
    expert_ids = jnp.arange(expert_table.shape[0], dtype=jnp.int32)
    matches = routes[..., None] == expert_ids
    return jnp.sum(jnp.where(matches, expert_table, 0), axis=-1)


def gate_back(slot_grad, gate_vals, matches, chosen):
    picked = jnp.sum(jnp.where(chosen, slot_grad[:, None, :], 0.0), axis=-1)
    inner_sum = jnp.sum(gate_vals * picked, axis=-1, keepdims=True)
    picked_grad = gate_vals * (picked - inner_sum)
    return jnp.sum(jnp.where(matches, picked_grad[:, :, None], 0.0), axis=1)


def unit_blocks(count):
    return [(start, min(512, count - start)) for start in range(0, count, 512)]


def expert_kernel(place_ref, hidden, grad, *refs):
    piece_count = (len(refs) - 6) // 2
    own_pieces, near_pieces = refs[:piece_count], refs[piece_count : 2 * piece_count]
    out, hidden_out, act_out, joint_out, weights, sems = refs[2 * piece_count :]
    core, chip = place_ref[0], place_ref[1]
    rows, columns = near_pieces[0].shape
    units = columns // 3
    width = grad.shape[1]

    @pl.when(pl.program_id(0) == 0)
    def _():
        copies = []
        for k in range(piece_count):
            base = (chip ^ k) * (2 * rows)
            for number, (piece, part) in enumerate(
                ((own_pieces[k], core), (near_pieces[k], 1 - core))
            ):
                start = pl.multiple_of(base + part * rows, 16)
                copies.append(
                    pltpu.make_async_copy(
                        piece, weights.at[pl.ds(start, rows)], sems.at[2 * k + number]
                    )
                )
        for copy in copies:
            copy.start()
        for copy in copies:
            copy.wait()

    slot_sum = jnp.zeros((hidden.shape[0], 1), f32)
    for start, size in unit_blocks(units):
        gate_pre = dot(hidden[:, :width], weights[:, start : start + size])
        up_pre = dot(hidden[:, :width], weights[:, units + start : units + start + size])
        act_grad = dot(grad[...], weights[:, 2 * units + start : 2 * units + start + size])
        sigma = 1.0 / (1.0 + jnp.exp(-gate_pre))
        silu_vals = gate_pre * sigma
        active = (silu_vals * up_pre).astype(bf16)
        act_out[:, start : start + size] = active
        slot_sum += jnp.sum(active.astype(f32) * act_grad, axis=1, keepdims=True)
        gate_grad = act_grad * up_pre * sigma * (1.0 + gate_pre * (1.0 - sigma))
        joint_out[:, start : start + size] = gate_grad.astype(bf16)
        joint_out[:, units + start : units + start + size] = (act_grad * silu_vals).astype(bf16)
    for start in range(0, width, 512):
        block = weights[start : start + 512, : 2 * units]
        hidden_out[:, start : start + 512] = dot_t(joint_out[...], block).astype(bf16)
        block = weights[start : start + 512, 2 * units :]
        out[:, start : start + 512] = dot_t(act_out[...], block).astype(bf16)
    lanes = lax.broadcasted_iota(jnp.int32, (hidden.shape[0], HDIM), 1)
    hidden_out[:, width:] = jnp.where(lanes == 0, slot_sum, 0.0).astype(bf16)


def expert_rows(position, hidden, grad, own_pieces, near_pieces):
    rows, width = grad.shape
    columns = near_pieces[0].shape[1]
    units = columns // 3
    tile = rows // 2
    shape = jax.ShapeDtypeStruct
    count = len(own_pieces)

    def tiled(size):
        return pl.BlockSpec((tile, size), lambda i, at: (i, 0))

    return pl.pallas_call(
        expert_kernel,
        grid_spec=pltpu.PrefetchScalarGridSpec(
            num_scalar_prefetch=1,
            grid=(rows // tile,),
            in_specs=[tiled(width + HDIM), tiled(width)]
            + [pl.BlockSpec(memory_space=pl.ANY)] * (2 * count),
            out_specs=[tiled(width), tiled(width + HDIM), tiled(units), tiled(2 * units)],
            scratch_shapes=[
                pltpu.VMEM((width, columns), bf16),
                pltpu.SemaphoreType.DMA((2 * count,)),
            ],
        ),
        out_shape=[
            shape((rows, width), bf16),
            shape((rows, width + HDIM), bf16),
            shape((rows, units), bf16),
            shape((rows, 2 * units), bf16),
        ],
        compiler_params=pltpu.CompilerParams(vmem_limit_bytes=56 * 2**20),
        cost_estimate=pl.CostEstimate(
            flops=4 * rows * width * columns,
            bytes_accessed=2 * (width * columns + 6 * rows * width),
            transcendentals=rows * units,
        ),
        name="expert_rows",
    )(position, hidden, grad, *own_pieces, *near_pieces)


def expert_grad_kernel(cuts, order, *refs):
    hidden, grad, gates, joint, active = [refs[2 * n : 2 * n + 2] for n in range(5)]
    outs = refs[10:]
    units = active[0].shape[1]

    def scaled(blocks):
        return [
            (block[...].astype(f32) * gate[:, :1].astype(f32)).astype(bf16)
            for block, gate in zip(blocks, gates)
        ]

    left, right = scaled(hidden), scaled(grad)
    step = pl.program_id(0)
    first = [0]
    for cut in cuts:
        first.append(first[-1] + cut)
    for out, start, cut in zip(outs, first, cuts):

        @pl.when((step >= start) & (step < start + cut))
        def _():
            for start, size in unit_blocks(2 * units):
                out[:, start : start + size] = sum(
                    t_dot(rows, part[:, start : start + size]) for rows, part in zip(left, joint)
                ).astype(bf16)
            for start, size in unit_blocks(units):
                out[:, 2 * units + start : 2 * units + start + size] = sum(
                    t_dot(rows, part[:, start : start + size]) for rows, part in zip(right, active)
                ).astype(bf16)


def expert_grads(chunks, cuts, chunk_rows, rows_of, joints, actives):
    hidden, grad = rows_of[:2], rows_of[2:]
    rows, units = actives[0].shape
    width = grad[0].shape[1]
    half = chunk_rows // 2
    count = len(chunks)
    order = jnp.stack([2 * chunk + part for chunk in chunks for part in range(2)]).astype(jnp.int32)

    def whole(size, column=0):
        return pl.BlockSpec(
            (rows, size), lambda i, at: (0, column), pipeline_mode=pl.Buffered(1)
        )

    column = pl.BlockSpec((rows, half), lambda i, at: (0, at[i]))
    return pl.pallas_call(
        functools.partial(expert_grad_kernel, cuts),
        grid_spec=pltpu.PrefetchScalarGridSpec(
            num_scalar_prefetch=1,
            grid=(2 * count,),
            in_specs=[column] * 4
            + [whole(HDIM, width // HDIM)] * 2
            + [whole(2 * units)] * 2
            + [whole(units)] * 2,
            out_specs=[
                pl.BlockSpec(
                    (half, 3 * units),
                    lambda i, at, start=sum(cuts[:n]), cut=cut: (jnp.clip(i - start, 0, cut - 1), 0),
                )
                for n, cut in enumerate(cuts)
            ],
        ),
        out_shape=[jax.ShapeDtypeStruct((cut * half, 3 * units), bf16) for cut in cuts],
        compiler_params=pltpu.CompilerParams(vmem_limit_bytes=56 * 2**20),
        cost_estimate=pl.CostEstimate(
            flops=4 * count * chunk_rows * rows * 3 * units,
            bytes_accessed=2 * (rows * 6 * units + count * chunk_rows * (4 * rows + 3 * units)),
            transcendentals=0,
        ),
        name="expert_grads",
    )(order, *hidden, *grad, *hidden, *joints, *actives)


def local(
    tokens,
    cotangent,
    seq_lengths,
    dealing,
    attn_routes,
    ffn_routes,
    expert_table,
    clip_limit,
    attn_gain,
    ffn_gain,
    attn_router,
    ffn_router,
    query_weight,
    attn_out_weight,
    kv_weight,
    gate_up_weight,
    down_weight,
):
    micro, tok_rows, width = tokens.shape
    dp_count = lax.axis_size("dp")
    slots = lax.axis_size("expert")
    col = lax.axis_index("expert")
    group = lax.axis_index("dp")
    piece_rows = tok_rows // dp_count
    cap = tok_rows * TOP * 3 // (2 * slots)
    group_rows = tok_rows * slots
    all_rows = micro * group_rows
    home_rows = micro * tok_rows
    query_width = HEADS * HDIM
    own_heads = HEADS // slots
    own_width = own_heads * HDIM
    shard_rows = query_weight.shape[1]
    score_scale = HDIM ** (-0.5)
    core = group % 2
    chip = group // 2
    side = chip % 2
    chips = dp_count // 2
    lines = chips // 2
    quarter = FF // 4
    chip_rows = 2 * shard_rows

    both = jnp.stack([tokens, cotangent]).reshape(2 * micro, dp_count, piece_rows, width)
    both = lax.all_to_all(both.transpose(1, 0, 2, 3), "dp", split_axis=0, concat_axis=0, tiled=True)
    def quarter_of(half, part):
        start = (2 * half + part) * quarter
        return jnp.concatenate(
            [
                lax.dynamic_slice_in_dim(gate_up_weight[0], start, quarter, 1),
                lax.dynamic_slice_in_dim(gate_up_weight[0], FF + start, quarter, 1),
                lax.dynamic_slice_in_dim(down_weight[0], start, quarter, 1),
            ],
            axis=1,
        )

    parts = (1 - core, core)
    keep_pair = [quarter_of(side, part) for part in parts]
    send_pair = [quarter_of(1 - side, part) for part in parts]
    kv_in, query_in, out_in = after(
        (kv_weight, query_weight[0], attn_out_weight[0]), keep_pair[0], send_pair[0]
    )
    both = both.transpose(1, 0, 2, 3).reshape(2, micro, tok_rows, width)
    deal = (dealing[:, :, None] == jnp.arange(tok_rows, dtype=jnp.int32)).astype(bf16)
    work = jnp.einsum("mtr,bmrd->bmtd", deal, both, preferred_element_type=f32)
    x_home = work[0].reshape(home_rows, width)
    dy_home = work[1].reshape(home_rows, width)

    def columns_of(*shards):
        pieces = [shard.reshape(shard_rows, slots, own_width) for shard in shards]
        out = jnp.zeros((shard_rows, len(shards) * query_width), shards[0].dtype)
        for k in range(slots):
            part = jnp.concatenate(
                [lax.dynamic_index_in_dim(piece, col ^ k, 1, keepdims=False) for piece in pieces],
                axis=1,
            )
            part = swap(part, "expert", k) if k else part
            for number in range(len(shards)):
                out = lax.dynamic_update_slice_in_dim(
                    out,
                    part[:, number * own_width : (number + 1) * own_width],
                    number * query_width + (col ^ k) * own_width,
                    1,
                )
        return out

    def slots_of(columns):
        pieces = columns.reshape(shard_rows, slots, own_width)
        out = jnp.zeros((shard_rows, query_width), columns.dtype)
        for k in range(slots):
            part = lax.dynamic_index_in_dim(pieces, col ^ k, 1, keepdims=False)
            part = swap(part, "expert", k) if k else part
            out = lax.dynamic_update_slice_in_dim(out, part, (col ^ k) * own_width, 1)
        return out

    half_slots = slots // 2
    first_pairs = [(c, 2 * c) for c in range(half_slots)]
    first_pairs += [(c, 2 * (c - half_slots) + 1) for c in range(half_slots, slots)]
    second_pairs = [(c, 2 * c + 1) for c in range(half_slots)]
    second_pairs += [(c, 2 * (c - half_slots)) for c in range(half_slots, slots)]
    holds_keys = col < half_slots
    even_col = col % 2 == 0
    low_kv, high_kv = kv_in[:, :own_width], kv_in[:, own_width:]
    first_got = lax.ppermute(jnp.where(holds_keys, low_kv, high_kv), "expert", first_pairs)
    second_got = lax.ppermute(jnp.where(holds_keys, high_kv, low_kv), "expert", second_pairs)
    own_kv = jnp.concatenate(
        [
            jnp.where(even_col, first_got, second_got),
            jnp.where(even_col, second_got, first_got),
        ],
        axis=1,
    )
    line_steps = [4 * line for line in range(1, lines)]
    side_first = swap(send_pair[0], "dp", 2)
    keep_first = [swap(keep_pair[0], "dp", step) for step in line_steps]
    joint_own = columns_of(query_in, out_in)
    first_own = jnp.concatenate([joint_own[:, :query_width], own_kv], axis=1)
    first_own, second_own = lax.optimization_barrier(
        (first_own, joint_own[:, query_width:], side_first, keep_first)
    )[:2]
    joint_full = lax.all_gather(first_own, "dp", axis=0, tiled=True)
    out_full = lax.all_gather(second_own, "dp", axis=0, tiled=True)
    late_pair = after((keep_pair[1], send_pair[1], side_first), joint_full)
    keep_second = [swap(late_pair[0], "dp", step) for step in line_steps]
    side_second = swap(late_pair[1], "dp", 2)
    first_lines = [swap(late_pair[2], "dp", step) for step in line_steps]
    second_lines = [swap(side_second, "dp", step) for step in line_steps]
    firsts, seconds = [keep_pair[0], side_first], [keep_pair[1], side_second]
    for line in range(lines - 1):
        firsts += [keep_first[line], first_lines[line]]
        seconds += [keep_second[line], second_lines[line]]
    near_pieces = [swap(piece, "dp", 1) for piece in firsts]
    own_pieces = seconds
    query_full = joint_full[:, :query_width]
    kv_full = joint_full[:, query_width:]

    positions = jnp.arange(group_rows, dtype=jnp.int32)
    first_len = lax.dynamic_index_in_dim(seq_lengths[:, :, 0], group, 1, keepdims=True)
    in_second = positions[None, :] >= first_len
    places = positions[None, :] - jnp.where(in_second, first_len, 0)
    tables = rotation_tables(places.reshape(all_rows))

    def gather_rows(value):
        shaped = value.reshape(micro, tok_rows, -1)
        out = jnp.zeros((micro, group_rows, shaped.shape[-1]), value.dtype)
        for k in range(slots):
            part = swap(shaped, "expert", k) if k else shaped
            out = lax.dynamic_update_slice_in_dim(out, part, (col ^ k) * tok_rows, 1)
        return out.reshape(all_rows, -1)

    def scatter_rows(value):
        shaped = value.reshape(micro, group_rows, -1)
        total = None
        for k in range(slots):
            part = lax.dynamic_slice_in_dim(shaped, (col ^ k) * tok_rows, tok_rows, 1)
            if k:
                part = swap(part.astype(bf16), "expert", k)
            part = part.astype(f32)
            total = part if total is None else total + part
        return total.reshape(home_rows, -1)

    home_routes = lax.dynamic_slice_in_dim(ffn_routes, col * tok_rows, tok_rows, 1)
    home_slots = route_slots(home_routes, expert_table)
    packs = []
    before = jnp.tril(jnp.ones((tok_rows, tok_rows), bf16), -1)
    for k in range(slots):
        hits = jnp.any(home_slots == (col ^ k), axis=-1)
        rank = jnp.einsum("ts,ms->mt", before, hits.astype(bf16), preferred_element_type=f32)
        packs.append(
            hits[:, None, :]
            & (rank[:, None, :] == jnp.arange(cap, dtype=jnp.int32).astype(f32)[None, :, None])
        )
    packs = jnp.stack(packs)
    packs_low = packs.astype(bf16)
    pack_rows = micro * cap
    sent_rows = slots * pack_rows

    def send_packed(value, lane=None):
        packed = jnp.einsum(
            "kmct,mtd->kmcd", packs_low, value.reshape(micro, tok_rows, -1), preferred_element_type=f32
        ).astype(bf16)
        if lane is not None:
            lanes = jnp.pad(lane[..., None], ((0, 0), (0, 0), (0, 0), (0, HDIM - 1)))
            packed = jnp.concatenate([packed, lanes.astype(bf16)], axis=-1)
        parts = [swap(packed[k], "expert", k) if k else packed[k] for k in range(slots)]
        return jnp.stack(parts).reshape(sent_rows, -1)

    def near_rows(value):
        return jnp.concatenate([value, swap(value, "dp", 1)], axis=0)

    def quad_sums(value):
        (own, near), (far, across) = [jnp.split(half, 2, axis=0) for half in value]
        far_sum = far.astype(f32) + swap(across, "dp", 1).astype(f32)
        return own.astype(f32) + swap(near, "dp", 1).astype(f32), far_sum.astype(bf16)

    def return_packed(value, *others):
        shaped = value.astype(bf16).reshape(slots, micro, cap, -1)
        parts = [swap(shaped[k], "expert", k) if k else shaped[k] for k in range(slots)]
        return after(parts, *others)

    def unpack(packed, scale):
        total = None
        for k in range(slots):
            rows = jnp.einsum("mct,mcd->mtd", packs_low[k], packed[k], preferred_element_type=f32)
            rows = rows.reshape(home_rows, -1) * take(scale.T, col ^ k)[:, None]
            total = rows if total is None else total + rows
        return total

    gain_one = attn_gain.astype(f32)
    gain_two = ffn_gain.astype(f32)
    normed_one, scale_one = normalize(x_home)
    hidden_one_home = (normed_one * gain_one).astype(bf16)
    hidden_one_raw = gather_rows(after(hidden_one_home, near_pieces[:3]))
    grad_sent = send_packed(dy_home.astype(bf16))
    hidden_one = after(hidden_one_raw, grad_sent)
    logits_one = dot(hidden_one, attn_router)
    gates_one, matches_one, chosen_one, gate_vals_one = route_gates(
        logits_one, attn_routes.reshape(all_rows, TOP), expert_table
    )
    hits_one = jnp.any(chosen_one, axis=1).astype(f32)

    def wide(value):
        return jnp.pad(value, ((0, 0), (0, HDIM - value.shape[1])))

    kv_part = dot(hidden_one, kv_full).astype(bf16)
    query_part = dot(hidden_one, query_full)
    lens = first_len[:, 0].astype(jnp.int32)
    gates_wide = wide(gates_one)
    attn_vals, gated_vals, query_rot, key_rot, log_total, peaks = attention_forward(
        lens, query_part, kv_part, tables, gates_wide, wide(hits_one), own_heads, group_rows
    )
    peaks = jnp.max(peaks, axis=0)[: own_heads * slots]
    attn_part = after(dot_t(gated_vals, out_full), keep_second, side_second)
    attn_home = after(scatter_rows(attn_part), first_lines)
    grad_sent = after(grad_sent, attn_home)
    grad_near, grad_far = near_rows(grad_sent), near_rows(swap(grad_sent, "dp", 2))

    resid = x_home + attn_home
    normed_two, scale_two = normalize(resid)
    hidden_two = (normed_two * gain_two).astype(bf16)
    logits_two = dot(hidden_two, ffn_router)
    gates_two, matches_two, chosen_two, gate_vals_two = route_gates(
        logits_two, home_routes.reshape(home_rows, TOP), expert_table
    )
    gates_by_slot = gates_two.reshape(micro, tok_rows, slots)
    gate_parts = []
    for k in range(slots):
        gate_col = lax.dynamic_index_in_dim(gates_by_slot, col ^ k, 2, keepdims=False)
        gate_parts.append(jnp.sum(jnp.where(packs[k], gate_col[:, None, :], 0.0), axis=-1))
    hidden_sent = after(
        send_packed(hidden_two, jnp.stack(gate_parts)), second_lines
    )
    hidden_near, hidden_far = near_rows(hidden_sent), swap(hidden_sent, "dp", 2)
    hidden_near = after(hidden_near, near_pieces, grad_near, grad_far)
    position = jnp.stack([core, chip]).astype(jnp.int32)
    near_results = expert_rows(
        position, hidden_near, after(grad_near, grad_far), own_pieces, near_pieces
    )
    hidden_far = near_rows(after(hidden_far, near_results))
    far_results = expert_rows(position, hidden_far, grad_far, own_pieces, near_pieces)
    ffn_parts, hidden_parts, actives, joint_grads = zip(near_results, far_results)

    def block_grads(steps, *others):
        rows = after((hidden_near, hidden_far, grad_near, grad_far), *others)
        cuts = (2,) * len(steps)
        return expert_grads([chip ^ k for k in steps], cuts, chip_rows, rows, joint_grads, actives)

    hidden_sum, hidden_far_sum = quad_sums(hidden_parts)
    ffn_sum, ffn_far_sum = quad_sums(after(ffn_parts, hidden_far_sum))
    line_grads = block_grads([k ^ 1 for k in range(2, chips)], hidden_far_sum)
    side_got = [swap(line_grads[2 * line], "dp", step) for line, step in enumerate(line_steps)]
    blocks = after(line_grads[1::2], side_got)
    keep_got = [swap(block, "dp", step) for block, step in zip(blocks, line_steps)]
    hidden_got, ffn_far_sum, ffn_sum = lax.optimization_barrier(
        (swap(hidden_far_sum, "dp", 2), ffn_far_sum, ffn_sum, line_grads)
    )[:3]
    hidden_sum = hidden_sum + hidden_got.astype(f32)
    own_grads = block_grads([1, 0], hidden_sum)
    back_packed = return_packed(hidden_sum, *own_grads)
    ffn_sum = ffn_sum + swap(after(ffn_far_sum, hidden_got), "dp", 2).astype(f32)

    def total(own, got):
        return functools.reduce(jnp.add, [part.astype(f32) for part in [own] + got]).astype(bf16)

    slot_two_grad = jnp.zeros((slots, home_rows), f32)
    for k in range(slots):
        rows = jnp.sum(
            jnp.where(packs[k], back_packed[k][:, :, width].astype(f32)[:, :, None], 0.0), axis=1
        )
        slot_two_grad = lax.dynamic_update_index_in_dim(
            slot_two_grad, rows.reshape(home_rows), col ^ k, 0
        )
    hidden_two_grad = unpack([part[..., :width] for part in back_packed], gates_two)
    logit_two_grad = gate_back(slot_two_grad.T, gate_vals_two, matches_two, chosen_two).astype(bf16)
    hidden_two_grad = hidden_two_grad + dot_t(logit_two_grad, ffn_router)
    router_two_grad = t_dot(logit_two_grad, hidden_two)
    gain_two_grad = jnp.sum(hidden_two_grad * normed_two, axis=0)
    resid_grad = dy_home + norm_back(hidden_two_grad * gain_two, normed_two, scale_two)

    resid_grad_all, ffn_sum = lax.optimization_barrier(
        (gather_rows(resid_grad.astype(bf16)), ffn_sum, side_got)
    )[:2]
    out_part = t_dot(resid_grad_all, gated_vals).astype(bf16)
    vals_grad = after(dot(resid_grad_all, out_full), out_part)
    side_own = after((own_grads[0], side_got), vals_grad)
    vals_grad, side_sum = lax.optimization_barrier((vals_grad, total(*side_own)))
    other_sum = swap(side_sum, "dp", 2)
    ffn_packed = return_packed(after(ffn_sum, vals_grad))
    out_home = (resid + unpack(ffn_packed, gates_two)).astype(bf16)
    query_grad, key_grad, value_grad, slot_part_one = attention_backward(
        lens, query_rot, key_rot, kv_part, attn_vals, vals_grad, tables, gates_wide, log_total,
        own_heads, group_rows,
    )
    query_grad, key_grad, value_grad, slot_part_one = lax.optimization_barrier(
        (query_grad, key_grad, value_grad, slot_part_one, ffn_packed)
    )[:4]
    kv_grad = jnp.concatenate([key_grad, value_grad], axis=1)
    hidden_one_part = dot_t(query_grad, query_full) + dot_t(kv_grad, kv_full)
    hidden_one_part = hidden_one_part.astype(bf16)
    joint_part_grad = t_dot(
        after(hidden_one, hidden_one_part), jnp.concatenate([query_grad, kv_grad], axis=1)
    ).astype(bf16)
    back_one = scatter_rows(
        jnp.concatenate([hidden_one_part, slot_part_one.astype(bf16)], axis=1)
    )
    back_one = after(back_one, joint_part_grad)
    out_own = lax.psum_scatter(out_part, "dp", scatter_dimension=0, tiled=True)
    out_grad = slots_of(after(out_own, back_one))
    hidden_one_grad, slot_one_grad = back_one[:, :width], back_one[:, width : width + slots]

    def own(value):
        shaped = value.reshape((micro, group_rows) + value.shape[1:])
        part = lax.dynamic_slice_in_dim(shaped, col * tok_rows, tok_rows, 1)
        return part.reshape((home_rows,) + value.shape[1:])

    logit_one_grad = gate_back(
        slot_one_grad, own(gate_vals_one), own(matches_one), own(chosen_one)
    ).astype(bf16)
    hidden_one_grad = hidden_one_grad + dot_t(logit_one_grad, attn_router)
    router_one_grad = t_dot(logit_one_grad, hidden_one_home)
    gain_one_grad = jnp.sum(hidden_one_grad * normed_one, axis=0)
    in_home = resid_grad + norm_back(hidden_one_grad * gain_one, normed_one, scale_one)

    def reduced(value):
        return lax.psum_scatter(value, "dp", scatter_dimension=0, tiled=True)

    in_low = in_home.astype(bf16)
    joint_own = reduced(joint_part_grad)

    results = jnp.stack([out_home, in_low]).reshape(2, micro, tok_rows, width)
    results = jnp.einsum("mtr,bmtd->bmrd", deal, results, preferred_element_type=f32).astype(bf16)
    results = results.reshape(2 * micro, dp_count, piece_rows, width).transpose(1, 0, 2, 3)
    results = results.reshape(dp_count, 2 * micro * piece_rows, width)
    sent_back = results.shape[1]
    small = jnp.concatenate(
        [gain_one_grad[None], gain_two_grad[None], router_one_grad, router_two_grad], axis=0
    ).astype(bf16)
    sum_rows = small.shape[0]
    peak_count = own_heads * slots
    peak_parts, rest = [], peaks
    for _ in range(3):
        peak_parts.append(lax.reduce_precision(rest, 8, 7))
        rest = rest - peak_parts[-1]
    peak_row = jnp.concatenate(peak_parts).astype(bf16)
    small = jnp.pad(small, ((0, -sum_rows % 16 or 16), (0, 0)))
    small = lax.dynamic_update_slice(small, peak_row[None], (sum_rows, 0))
    small = jnp.broadcast_to(small[None], (dp_count,) + small.shape)
    results = jnp.concatenate([results, small], axis=1)
    results = lax.all_to_all(results, "dp", split_axis=0, concat_axis=0, tiled=True)
    query_own, kv_own = joint_own[:, :query_width], joint_own[:, query_width:]
    results, out_grad = lax.optimization_barrier((results, out_grad))
    results, other_sum, keep_got = lax.optimization_barrier((results, other_sum, keep_got))
    small = results[:, sent_back:].astype(f32)
    results = results[:, :sent_back].reshape(dp_count, 2 * micro, piece_rows, width)
    results = results.transpose(1, 0, 2, 3).reshape(2, micro, tok_rows, width)
    peak_row = small[:, sum_rows, : 3 * peak_count].reshape(dp_count, 3, peak_count)
    peak_row = jnp.max((peak_row[:, 0] + peak_row[:, 1]) + peak_row[:, 2], axis=0)
    small = jnp.sum(small, axis=0)
    small = lax.dynamic_update_slice(small, peak_row[None], (sum_rows, 0))
    smalls = jnp.broadcast_to(small[None], (slots,) + small.shape)
    smalls = lax.all_to_all(smalls, "expert", split_axis=0, concat_axis=0, tiled=True)
    peaks_all = smalls[:, sum_rows, :peak_count].reshape(slots, own_heads, slots)
    peaks_all = peaks_all.transpose(2, 0, 1).reshape(slots, HEADS)
    sums = functools.reduce(jnp.add, [smalls[k, :sum_rows] for k in range(slots)])

    keep_sums = total(own_grads[1], keep_got).reshape(2, shard_rows, 3 * quarter)
    other_sums = other_sum.reshape(2, shard_rows, 3 * quarter)
    by_rows = [jnp.stack([keep_sums[part], other_sums[part]]) for part in range(2)]
    own_pair = jnp.where(core == 0, by_rows[0], by_rows[1])
    near_pair = swap(jnp.where(core == 0, by_rows[1], by_rows[0]), "dp", 1)
    by_core = [jnp.where(core == 0, own_pair, near_pair), jnp.where(core == 0, near_pair, own_pair)]
    by_side = [[jnp.where(side == s, part[0], part[1]) for part in by_core] for s in range(2)]
    blocks = [part for row in by_side for part in row]
    gate_up_grad = jnp.concatenate(
        [b[:, :quarter] for b in blocks] + [b[:, quarter : 2 * quarter] for b in blocks], axis=1
    ).astype(f32)
    down_grad = jnp.concatenate([b[:, 2 * quarter :] for b in blocks], axis=1).astype(f32)

    out_grad = out_grad.astype(f32)
    query_out = slots_of(query_own).astype(f32)
    key_part, value_part = kv_own[:, :own_width], kv_own[:, own_width:]
    first_back = lax.ppermute(
        jnp.where(even_col, key_part, value_part), "expert", [(b, a) for a, b in first_pairs]
    )
    second_back = lax.ppermute(
        jnp.where(even_col, value_part, key_part), "expert", [(b, a) for a, b in second_pairs]
    )
    kv_out = jnp.concatenate(
        [
            jnp.where(holds_keys, first_back, second_back),
            jnp.where(holds_keys, second_back, first_back),
        ],
        axis=1,
    ).astype(f32)

    limit = clip_limit[0].astype(f32)
    factor = limit / jnp.maximum(peaks_all, limit)
    query_scale = jnp.repeat(jnp.sqrt(take(factor, col)), HDIM)
    query_clipped = (query_weight.astype(f32) * query_scale[None, None, :]).astype(bf16)
    full_scale = jnp.concatenate(
        [jnp.repeat(jnp.sqrt(jnp.min(factor, axis=0)), HDIM), jnp.ones((query_width,), f32)]
    )
    piece_width = kv_weight.shape[1]
    piece_scale = lax.dynamic_slice_in_dim(full_scale, col * piece_width, piece_width)
    kv_clipped = (kv_weight.astype(f32) * piece_scale[None, :]).astype(bf16)
    return (
        results[0],
        results[1],
        sums[0],
        sums[1],
        sums[2 : 2 + slots].T,
        sums[2 + slots : sum_rows].T,
        query_out[None],
        out_grad[None],
        kv_out,
        gate_up_grad[None],
        down_grad[None],
        query_clipped,
        kv_clipped,
    )


def solution(mesh):
    placed = (
        P(None, ("dp", "expert"), None),
        P(None, ("dp", "expert"), None),
        P(),
        P(None, ("dp", "expert")),
        P(None, "dp", None),
        P(None, "dp", None),
        P(),
        P(),
        P(),
        P(),
        P(),
        P(),
        P("expert", "dp", None),
        P("expert", "dp", None),
        P("dp", "expert"),
        P("expert", "dp", None),
        P("expert", "dp", None),
    )
    return jax.shard_map(
        local,
        mesh=mesh,
        in_specs=placed,
        out_specs=(
            P(None, ("dp", "expert"), None),
            P(None, ("dp", "expert"), None),
            P(),
            P(),
            P(),
            P(),
            P("expert", "dp", None),
            P("expert", "dp", None),
            P("dp", "expert"),
            P("expert", "dp", None),
            P("expert", "dp", None),
            P("expert", "dp", None),
            P("dp", "expert"),
        ),
        check_vma=False,
    )
```

```python
import functools

import jax
import jax.numpy as jnp
from jax import lax
from jax.experimental import pallas as pl
from jax.experimental.pallas import tpu as pltpu
from jax.sharding import PartitionSpec as P

HEADS = 16
HDIM = 128
FF = 5632
TOP = 2

eps_norm = 1e-06
rope_base = 10000.0
very_low = -1e30

f32 = jnp.float32
bf16 = jnp.bfloat16


def dot(left, right):
    return jnp.dot(left, right, preferred_element_type=f32)


def dot_t(left, right):
    return lax.dot_general(left, right, (((1,), (1,)), ((), ())), preferred_element_type=f32)


def t_dot(left, right):
    return lax.dot_general(left, right, (((0,), (0,)), ((), ())), preferred_element_type=f32)


def swap(value, axis, step):
    count = lax.axis_size(axis)
    return lax.ppermute(value, axis, [(i, i ^ step) for i in range(count)])


def take(stacked, index):
    return lax.dynamic_index_in_dim(stacked, index, 0, keepdims=False)


def place(parts, positions):
    out = jnp.zeros((len(parts),) + parts[0].shape, parts[0].dtype)
    for part, position in zip(parts, positions):
        out = lax.dynamic_update_index_in_dim(out, part, position, 0)
    return out


def after(value, *others):
    return lax.optimization_barrier((value, others))[0]


def rotation_tables(places):
    half_dim = HDIM // 2
    frequency = rope_base ** (-jnp.arange(half_dim, dtype=f32) * 2.0 / HDIM)
    angles = places.astype(f32)[:, None] * frequency[None, :]
    cosine, sine = jnp.cos(angles), jnp.sin(angles)
    return (
        jnp.concatenate([cosine, cosine], axis=1),
        jnp.concatenate([-sine, sine], axis=1),
    )


def turn(values, cosine, sine):
    return values * cosine + pltpu.roll(values, HDIM // 2, 1) * sine


def lane_value(table, lane):
    lanes = lax.broadcasted_iota(jnp.int32, table.shape, 1)
    return jnp.sum(jnp.where(lanes == lane, table, 0.0), axis=1, keepdims=True)


def allowed_pairs(rows, first_len):
    query_at = lax.broadcasted_iota(jnp.int32, (rows, rows), 0)
    key_at = lax.broadcasted_iota(jnp.int32, (rows, rows), 1)
    return (key_at <= query_at) & ((key_at >= first_len) | (query_at < first_len))


def forward_kernel(
    lens, query, key, value, cosine, sine, gates, hits,
    vals_out, gated_out, query_out, key_out, total_out, peak_out,
):
    m, h = pl.program_id(0), pl.program_id(1)
    heads = pl.num_programs(1)
    rows = query.shape[0]
    slots = query.shape[1] // (heads * HDIM)

    @pl.when(h == 0)
    def _():
        total_out[...] = jnp.zeros_like(total_out)
        peak_out[...] = jnp.full_like(peak_out, very_low)

    cos_part, sin_part = cosine[...], sine[...]
    allowed = allowed_pairs(rows, lens[m])
    keys = turn(key[...].astype(f32), cos_part, sin_part).astype(bf16)
    key_out[...] = keys
    values = value[...]
    lanes = lax.broadcasted_iota(jnp.int32, total_out.shape, 1)
    peak_lanes = lax.broadcasted_iota(jnp.int32, peak_out.shape, 1)
    totals, peaks = total_out[...], peak_out[...]
    for s in range(slots):
        columns = pl.ds(pl.multiple_of((s * heads + h) * HDIM, HDIM), HDIM)
        turned = turn(query[:, columns], cos_part, sin_part).astype(bf16)
        query_out[:, columns] = turned
        scores = jnp.where(allowed, dot_t(turned, keys) * HDIM ** (-0.5), very_low)
        row_peak = jnp.max(scores, axis=1, keepdims=True)
        expo = jnp.exp(scores - row_peak)
        denom = jnp.sum(expo, axis=1, keepdims=True)
        probs = expo * (1.0 / denom)
        vals = dot(probs.astype(bf16), values).astype(bf16)
        vals_out[:, columns] = vals
        gated_out[:, columns] = (gates[:, s : s + 1] * vals.astype(f32)).astype(bf16)
        lane = h * slots + s
        totals = jnp.where(lanes == lane, row_peak + jnp.log(denom), totals)
        seen = jnp.where(hits[:, s : s + 1] > 0.0, row_peak, very_low)
        peaks = jnp.where(peak_lanes == lane, jnp.max(seen, axis=0, keepdims=True), peaks)
    total_out[...] = totals
    peak_out[...] = peaks


def backward_kernel(
    lens, query, key, value, vals, vals_grad, cosine, sine, gates, total,
    query_grad, key_grad, value_grad, gate_grad,
):
    m, h = pl.program_id(0), pl.program_id(1)
    heads = pl.num_programs(1)
    rows = query.shape[0]
    slots = query.shape[1] // (heads * HDIM)

    @pl.when(h == 0)
    def _():
        gate_grad[...] = jnp.zeros_like(gate_grad)

    allowed = allowed_pairs(rows, lens[m])
    cos_part, back_sine = cosine[...], -sine[...]
    keys, values, totals = key[...], value[...], total[...]
    lanes = lax.broadcasted_iota(jnp.int32, gate_grad.shape, 1)
    slot_sums = gate_grad[...]
    key_sum = jnp.zeros(key.shape, f32)
    value_sum = jnp.zeros(value.shape, f32)
    for s in range(slots):
        columns = pl.ds(pl.multiple_of((s * heads + h) * HDIM, HDIM), HDIM)
        full_grad = vals_grad[:, columns]
        slot_sum = jnp.sum(vals[:, columns].astype(f32) * full_grad, axis=1, keepdims=True)
        slot_sums += jnp.where(lanes == s, slot_sum, 0.0)
        gated_grad = (gates[:, s : s + 1] * full_grad).astype(bf16)
        queries = query[:, columns]
        scores = jnp.where(allowed, dot_t(queries, keys) * HDIM ** (-0.5), very_low)
        probs = jnp.exp(scores - lane_value(totals, h * slots + s))
        prob_grad = dot_t(gated_grad, values)
        inner = jnp.sum(probs * prob_grad, axis=1, keepdims=True)
        score_grad = (probs * (prob_grad - inner) * HDIM ** (-0.5)).astype(bf16)
        query_grad[:, columns] = turn(dot(score_grad, keys), cos_part, back_sine).astype(bf16)
        key_sum += t_dot(score_grad, queries)
        value_sum += t_dot(probs.astype(bf16), gated_grad)
    gate_grad[...] = slot_sums
    key_grad[...] = turn(key_sum, cos_part, back_sine).astype(bf16)
    value_grad[...] = value_sum.astype(bf16)


def attention_specs(own_heads, rows, width):
    def block(columns, index):
        return pl.BlockSpec((rows, columns), index)

    return {
        "query": block(width, lambda m, h, lens: (m, 0)),
        "key": block(HDIM, lambda m, h, lens: (m, h)),
        "value": block(HDIM, lambda m, h, lens: (m, own_heads + h)),
        "rows": block(HDIM, lambda m, h, lens: (m, 0)),
        "peak": pl.BlockSpec((8, HDIM), lambda m, h, lens: (m, 0)),
    }


def attention_forward(lens, query, joint_kv, tables, gates, hits, own_heads, rows):
    micro = lens.shape[0]
    at = attention_specs(own_heads, rows, query.shape[1])
    shape = jax.ShapeDtypeStruct
    total_rows = micro * rows
    return pl.pallas_call(
        forward_kernel,
        grid_spec=pltpu.PrefetchScalarGridSpec(
            num_scalar_prefetch=1,
            grid=(micro, own_heads),
            in_specs=[at["query"], at["key"], at["value"]] + [at["rows"]] * 4,
            out_specs=[at["query"]] * 3 + [at["key"], at["rows"], at["peak"]],
        ),
        out_shape=[shape(query.shape, bf16)] * 3
        + [
            shape((total_rows, own_heads * HDIM), bf16),
            shape((total_rows, HDIM), f32),
            shape((micro * 8, HDIM), f32),
        ],
        compiler_params=pltpu.CompilerParams(vmem_limit_bytes=48 * 2**20),
        cost_estimate=pl.CostEstimate(
            flops=4 * rows * rows * HDIM * micro * HEADS,
            bytes_accessed=14 * query.size,
            transcendentals=rows * rows * micro * HEADS,
        ),
        name="attention_forward",
    )(lens, query, joint_kv, joint_kv, tables[0], tables[1], gates, hits)


def attention_backward(
    lens, query, key, joint_kv, vals, vals_grad, tables, gates, total, own_heads, rows
):
    micro = lens.shape[0]
    at = attention_specs(own_heads, rows, query.shape[1])
    shape = jax.ShapeDtypeStruct
    total_rows = micro * rows
    return pl.pallas_call(
        backward_kernel,
        grid_spec=pltpu.PrefetchScalarGridSpec(
            num_scalar_prefetch=1,
            grid=(micro, own_heads),
            in_specs=[at["query"], at["key"], at["value"], at["query"], at["query"]]
            + [at["rows"]] * 4,
            out_specs=[at["query"], at["key"], at["key"], at["rows"]],
        ),
        out_shape=[shape(query.shape, bf16)]
        + [shape((total_rows, own_heads * HDIM), bf16)] * 2
        + [shape((total_rows, HDIM), f32)],
        compiler_params=pltpu.CompilerParams(vmem_limit_bytes=48 * 2**20),
        cost_estimate=pl.CostEstimate(
            flops=10 * rows * rows * HDIM * micro * HEADS,
            bytes_accessed=14 * query.size,
            transcendentals=rows * rows * micro * HEADS,
        ),
        name="attention_backward",
    )(lens, query, key, joint_kv, vals, vals_grad, tables[0], tables[1], gates, total)


def normalize(values):
    row_scale = lax.rsqrt(jnp.mean(values * values, axis=-1, keepdims=True) + eps_norm)
    return values * row_scale, row_scale


def norm_back(grad_hat, normed, row_scale):
    return row_scale * (grad_hat - normed * jnp.mean(grad_hat * normed, axis=-1, keepdims=True))


def route_gates(logits, routes, expert_table):
    expert_ids = jnp.arange(expert_table.shape[0], dtype=jnp.int32)
    matches = routes[:, :, None] == expert_ids[None, None, :]
    picked = jnp.sum(jnp.where(matches, logits[:, None, :], 0.0), axis=-1)
    gate_vals = jax.nn.softmax(picked, axis=-1)
    slot_ids = route_slots(routes, expert_table)
    chosen = slot_ids[:, :, None] == expert_ids[None, None, :]
    gates = jnp.sum(jnp.where(chosen, gate_vals[:, :, None], 0.0), axis=1)
    return gates, matches, chosen, gate_vals


def route_slots(routes, expert_table):
    expert_ids = jnp.arange(expert_table.shape[0], dtype=jnp.int32)
    matches = routes[..., None] == expert_ids
    return jnp.sum(jnp.where(matches, expert_table, 0), axis=-1)


def gate_back(slot_grad, gate_vals, matches, chosen):
    picked = jnp.sum(jnp.where(chosen, slot_grad[:, None, :], 0.0), axis=-1)
    inner_sum = jnp.sum(gate_vals * picked, axis=-1, keepdims=True)
    picked_grad = gate_vals * (picked - inner_sum)
    return jnp.sum(jnp.where(matches, picked_grad[:, :, None], 0.0), axis=1)


def unit_blocks(count):
    return [(start, min(512, count - start)) for start in range(0, count, 512)]


def expert_kernel(place_ref, hidden, grad, *refs):
    piece_count = (len(refs) - 6) // 2
    own_pieces, near_pieces = refs[:piece_count], refs[piece_count : 2 * piece_count]
    out, hidden_out, act_out, joint_out, weights, sems = refs[2 * piece_count :]
    core, chip = place_ref[0], place_ref[1]
    rows, columns = near_pieces[0].shape
    units = columns // 3
    width = grad.shape[1]

    first = pl.program_id(0) == 0
    blocks = unit_blocks(units)
    copies = [[] for _ in blocks]
    for k in range(piece_count):
        base = (chip ^ k) * (2 * rows)
        for piece, part in ((own_pieces[k], core), (near_pieces[k], 1 - core)):
            held = weights.at[pl.ds(pl.multiple_of(base + part * rows, 16), rows)]
            for group, (start, size) in zip(copies, blocks):
                for offset in range(start, 3 * units, units):
                    number = len(blocks) * len(group) + blocks.index((start, size))
                    group.append(
                        pltpu.make_async_copy(
                            piece.at[:, pl.ds(offset, size)],
                            held.at[:, pl.ds(offset, size)],
                            sems.at[number],
                        )
                    )

    @pl.when(first)
    def _():
        for group in copies:
            for copy in group:
                copy.start()

    slot_sum = jnp.zeros((hidden.shape[0], 1), f32)
    for group, (start, size) in zip(copies, blocks):

        @pl.when(first)
        def _():
            for copy in group:
                copy.wait()

        gate_pre = dot(hidden[:, :width], weights[:, start : start + size])
        up_pre = dot(hidden[:, :width], weights[:, units + start : units + start + size])
        act_grad = dot(grad[...], weights[:, 2 * units + start : 2 * units + start + size])
        sigma = 1.0 / (1.0 + jnp.exp(-gate_pre))
        silu_vals = gate_pre * sigma
        active = (silu_vals * up_pre).astype(bf16)
        act_out[:, start : start + size] = active
        slot_sum += jnp.sum(active.astype(f32) * act_grad, axis=1, keepdims=True)
        gate_grad = act_grad * up_pre * sigma * (1.0 + gate_pre * (1.0 - sigma))
        joint_out[:, start : start + size] = gate_grad.astype(bf16)
        joint_out[:, units + start : units + start + size] = (act_grad * silu_vals).astype(bf16)
    for start in range(0, width, 512):
        block = weights[start : start + 512, : 2 * units]
        hidden_out[:, start : start + 512] = dot_t(joint_out[...], block).astype(bf16)
        block = weights[start : start + 512, 2 * units :]
        out[:, start : start + 512] = dot_t(act_out[...], block).astype(bf16)
    lanes = lax.broadcasted_iota(jnp.int32, (hidden.shape[0], HDIM), 1)
    hidden_out[:, width:] = jnp.where(lanes == 0, slot_sum, 0.0).astype(bf16)


def expert_rows(position, hidden, grad, own_pieces, near_pieces):
    rows, width = grad.shape
    columns = near_pieces[0].shape[1]
    units = columns // 3
    tile = rows // 2
    shape = jax.ShapeDtypeStruct
    count = len(own_pieces)

    def tiled(size):
        return pl.BlockSpec((tile, size), lambda i, at: (i, 0))

    return pl.pallas_call(
        expert_kernel,
        grid_spec=pltpu.PrefetchScalarGridSpec(
            num_scalar_prefetch=1,
            grid=(rows // tile,),
            in_specs=[tiled(width + HDIM), tiled(width)]
            + [pl.BlockSpec(memory_space=pl.ANY)] * (2 * count),
            out_specs=[tiled(width), tiled(width + HDIM), tiled(units), tiled(2 * units)],
            scratch_shapes=[
                pltpu.VMEM((width, columns), bf16),
                pltpu.SemaphoreType.DMA((6 * count * len(unit_blocks(units)),)),
            ],
        ),
        out_shape=[
            shape((rows, width), bf16),
            shape((rows, width + HDIM), bf16),
            shape((rows, units), bf16),
            shape((rows, 2 * units), bf16),
        ],
        compiler_params=pltpu.CompilerParams(vmem_limit_bytes=56 * 2**20),
        cost_estimate=pl.CostEstimate(
            flops=4 * rows * width * columns,
            bytes_accessed=2 * (width * columns + 6 * rows * width),
            transcendentals=rows * units,
        ),
        name="expert_rows",
    )(position, hidden, grad, *own_pieces, *near_pieces)


def expert_grad_kernel(cuts, order, *refs):
    hidden, grad, gates, joint, active = [refs[2 * n : 2 * n + 2] for n in range(5)]
    outs = refs[10:]
    units = active[0].shape[1]

    def scaled(blocks):
        return [
            (block[...].astype(f32) * gate[:, :1].astype(f32)).astype(bf16)
            for block, gate in zip(blocks, gates)
        ]

    left, right = scaled(hidden), scaled(grad)
    step = pl.program_id(0)
    first = [0]
    for cut in cuts:
        first.append(first[-1] + cut)
    for out, start, cut in zip(outs, first, cuts):

        @pl.when((step >= start) & (step < start + cut))
        def _():
            for start, size in unit_blocks(2 * units):
                out[:, start : start + size] = sum(
                    t_dot(rows, part[:, start : start + size]) for rows, part in zip(left, joint)
                ).astype(bf16)
            for start, size in unit_blocks(units):
                out[:, 2 * units + start : 2 * units + start + size] = sum(
                    t_dot(rows, part[:, start : start + size]) for rows, part in zip(right, active)
                ).astype(bf16)


def expert_grads(chunks, cuts, chunk_rows, rows_of, joints, actives):
    hidden, grad = rows_of[:2], rows_of[2:]
    rows, units = actives[0].shape
    width = grad[0].shape[1]
    half = chunk_rows // 2
    count = len(chunks)
    order = jnp.stack([2 * chunk + part for chunk in chunks for part in range(2)]).astype(jnp.int32)

    def whole(size, column=0):
        return pl.BlockSpec(
            (rows, size), lambda i, at: (0, column), pipeline_mode=pl.Buffered(1)
        )

    column = pl.BlockSpec((rows, half), lambda i, at: (0, at[i]))
    return pl.pallas_call(
        functools.partial(expert_grad_kernel, cuts),
        grid_spec=pltpu.PrefetchScalarGridSpec(
            num_scalar_prefetch=1,
            grid=(2 * count,),
            in_specs=[column] * 4
            + [whole(HDIM, width // HDIM)] * 2
            + [whole(2 * units)] * 2
            + [whole(units)] * 2,
            out_specs=[
                pl.BlockSpec(
                    (half, 3 * units),
                    lambda i, at, start=sum(cuts[:n]), cut=cut: (jnp.clip(i - start, 0, cut - 1), 0),
                )
                for n, cut in enumerate(cuts)
            ],
        ),
        out_shape=[jax.ShapeDtypeStruct((cut * half, 3 * units), bf16) for cut in cuts],
        compiler_params=pltpu.CompilerParams(vmem_limit_bytes=56 * 2**20),
        cost_estimate=pl.CostEstimate(
            flops=4 * count * chunk_rows * rows * 3 * units,
            bytes_accessed=2 * (rows * 6 * units + count * chunk_rows * (4 * rows + 3 * units)),
            transcendentals=0,
        ),
        name="expert_grads",
    )(order, *hidden, *grad, *hidden, *joints, *actives)


def local(
    tokens,
    cotangent,
    seq_lengths,
    dealing,
    attn_routes,
    ffn_routes,
    expert_table,
    clip_limit,
    attn_gain,
    ffn_gain,
    attn_router,
    ffn_router,
    query_weight,
    attn_out_weight,
    kv_weight,
    gate_up_weight,
    down_weight,
):
    micro, tok_rows, width = tokens.shape
    dp_count = lax.axis_size("dp")
    slots = lax.axis_size("expert")
    col = lax.axis_index("expert")
    group = lax.axis_index("dp")
    piece_rows = tok_rows // dp_count
    cap = tok_rows * TOP * 3 // (2 * slots)
    group_rows = tok_rows * slots
    all_rows = micro * group_rows
    home_rows = micro * tok_rows
    query_width = HEADS * HDIM
    own_heads = HEADS // slots
    own_width = own_heads * HDIM
    shard_rows = query_weight.shape[1]
    score_scale = HDIM ** (-0.5)
    core = group % 2
    chip = group // 2
    side = chip % 2
    chips = dp_count // 2
    lines = chips // 2
    quarter = FF // 4
    chip_rows = 2 * shard_rows

    both = jnp.stack([tokens, cotangent]).reshape(2 * micro, dp_count, piece_rows, width)
    both = lax.all_to_all(both.transpose(1, 0, 2, 3), "dp", split_axis=0, concat_axis=0, tiled=True)
    def quarter_of(half, part):
        start = (2 * half + part) * quarter
        return jnp.concatenate(
            [
                lax.dynamic_slice_in_dim(gate_up_weight[0], start, quarter, 1),
                lax.dynamic_slice_in_dim(gate_up_weight[0], FF + start, quarter, 1),
                lax.dynamic_slice_in_dim(down_weight[0], start, quarter, 1),
            ],
            axis=1,
        )

    parts = (1 - core, core)
    keep_pair = [quarter_of(side, part) for part in parts]
    send_pair = [quarter_of(1 - side, part) for part in parts]
    kv_in, query_in, out_in = after(
        (kv_weight, query_weight[0], attn_out_weight[0]), keep_pair[0], send_pair[0]
    )
    both = both.transpose(1, 0, 2, 3).reshape(2, micro, tok_rows, width)
    deal = (dealing[:, :, None] == jnp.arange(tok_rows, dtype=jnp.int32)).astype(bf16)
    work = jnp.einsum("mtr,bmrd->bmtd", deal, both, preferred_element_type=f32)
    x_home = work[0].reshape(home_rows, width)
    dy_home = work[1].reshape(home_rows, width)

    def columns_of(*shards):
        pieces = [shard.reshape(shard_rows, slots, own_width) for shard in shards]
        out = jnp.zeros((shard_rows, len(shards) * query_width), shards[0].dtype)
        for k in range(slots):
            part = jnp.concatenate(
                [lax.dynamic_index_in_dim(piece, col ^ k, 1, keepdims=False) for piece in pieces],
                axis=1,
            )
            part = swap(part, "expert", k) if k else part
            for number in range(len(shards)):
                out = lax.dynamic_update_slice_in_dim(
                    out,
                    part[:, number * own_width : (number + 1) * own_width],
                    number * query_width + (col ^ k) * own_width,
                    1,
                )
        return out

    def slots_of(columns):
        pieces = columns.reshape(shard_rows, slots, own_width)
        out = jnp.zeros((shard_rows, query_width), columns.dtype)
        for k in range(slots):
            part = lax.dynamic_index_in_dim(pieces, col ^ k, 1, keepdims=False)
            part = swap(part, "expert", k) if k else part
            out = lax.dynamic_update_slice_in_dim(out, part, (col ^ k) * own_width, 1)
        return out

    half_slots = slots // 2
    first_pairs = [(c, 2 * c) for c in range(half_slots)]
    first_pairs += [(c, 2 * (c - half_slots) + 1) for c in range(half_slots, slots)]
    second_pairs = [(c, 2 * c + 1) for c in range(half_slots)]
    second_pairs += [(c, 2 * (c - half_slots)) for c in range(half_slots, slots)]
    holds_keys = col < half_slots
    even_col = col % 2 == 0
    low_kv, high_kv = kv_in[:, :own_width], kv_in[:, own_width:]
    first_got = lax.ppermute(jnp.where(holds_keys, low_kv, high_kv), "expert", first_pairs)
    second_got = lax.ppermute(jnp.where(holds_keys, high_kv, low_kv), "expert", second_pairs)
    own_kv = jnp.concatenate(
        [
            jnp.where(even_col, first_got, second_got),
            jnp.where(even_col, second_got, first_got),
        ],
        axis=1,
    )
    line_steps = [4 * line for line in range(1, lines)]
    side_first = swap(send_pair[0], "dp", 2)
    keep_first = [swap(keep_pair[0], "dp", step) for step in line_steps]
    joint_own = columns_of(query_in, out_in)
    first_own = jnp.concatenate([joint_own[:, :query_width], own_kv], axis=1)
    first_own, second_own = lax.optimization_barrier(
        (first_own, joint_own[:, query_width:], side_first, keep_first)
    )[:2]
    joint_full = lax.all_gather(first_own, "dp", axis=0, tiled=True)
    out_full = lax.all_gather(second_own, "dp", axis=0, tiled=True)
    late_pair = after((keep_pair[1], send_pair[1], side_first), joint_full)
    keep_second = [swap(late_pair[0], "dp", step) for step in line_steps]
    side_second = swap(late_pair[1], "dp", 2)
    first_lines = [swap(late_pair[2], "dp", step) for step in line_steps]
    second_lines = [swap(side_second, "dp", step) for step in line_steps]
    firsts, seconds = [keep_pair[0], side_first], [keep_pair[1], side_second]
    for line in range(lines - 1):
        firsts += [keep_first[line], first_lines[line]]
        seconds += [keep_second[line], second_lines[line]]
    near_pieces = [swap(piece, "dp", 1) for piece in firsts]
    own_pieces = seconds
    query_full = joint_full[:, :query_width]
    kv_full = joint_full[:, query_width:]

    positions = jnp.arange(group_rows, dtype=jnp.int32)
    first_len = lax.dynamic_index_in_dim(seq_lengths[:, :, 0], group, 1, keepdims=True)
    in_second = positions[None, :] >= first_len
    places = positions[None, :] - jnp.where(in_second, first_len, 0)
    tables = rotation_tables(places.reshape(all_rows))

    def gather_rows(value):
        shaped = value.reshape(micro, tok_rows, -1)
        out = jnp.zeros((micro, group_rows, shaped.shape[-1]), value.dtype)
        for k in range(slots):
            part = swap(shaped, "expert", k) if k else shaped
            out = lax.dynamic_update_slice_in_dim(out, part, (col ^ k) * tok_rows, 1)
        return out.reshape(all_rows, -1)

    def scatter_rows(value):
        shaped = value.reshape(micro, group_rows, -1)
        total = None
        for k in range(slots):
            part = lax.dynamic_slice_in_dim(shaped, (col ^ k) * tok_rows, tok_rows, 1)
            if k:
                part = swap(part.astype(bf16), "expert", k)
            part = part.astype(f32)
            total = part if total is None else total + part
        return total.reshape(home_rows, -1)

    home_routes = lax.dynamic_slice_in_dim(ffn_routes, col * tok_rows, tok_rows, 1)
    home_slots = route_slots(home_routes, expert_table)
    packs = []
    before = jnp.tril(jnp.ones((tok_rows, tok_rows), bf16), -1)
    for k in range(slots):
        hits = jnp.any(home_slots == (col ^ k), axis=-1)
        rank = jnp.einsum("ts,ms->mt", before, hits.astype(bf16), preferred_element_type=f32)
        packs.append(
            hits[:, None, :]
            & (rank[:, None, :] == jnp.arange(cap, dtype=jnp.int32).astype(f32)[None, :, None])
        )
    packs = jnp.stack(packs)
    packs_low = packs.astype(bf16)
    pack_rows = micro * cap
    sent_rows = slots * pack_rows

    def send_packed(value, lane=None):
        packed = jnp.einsum(
            "kmct,mtd->kmcd", packs_low, value.reshape(micro, tok_rows, -1), preferred_element_type=f32
        ).astype(bf16)
        if lane is not None:
            lanes = jnp.pad(lane[..., None], ((0, 0), (0, 0), (0, 0), (0, HDIM - 1)))
            packed = jnp.concatenate([packed, lanes.astype(bf16)], axis=-1)
        parts = [swap(packed[k], "expert", k) if k else packed[k] for k in range(slots)]
        return jnp.stack(parts).reshape(sent_rows, -1)

    def near_rows(value):
        return jnp.concatenate([value, swap(value, "dp", 1)], axis=0)

    def quad_sums(value):
        (own, near), (far, across) = [jnp.split(half, 2, axis=0) for half in value]
        far_sum = far.astype(f32) + swap(across, "dp", 1).astype(f32)
        return own.astype(f32) + swap(near, "dp", 1).astype(f32), far_sum.astype(bf16)

    def return_packed(value, *others):
        shaped = value.astype(bf16).reshape(slots, micro, cap, -1)
        parts = [swap(shaped[k], "expert", k) if k else shaped[k] for k in range(slots)]
        return after(parts, *others)

    def unpack(packed, scale):
        total = None
        for k in range(slots):
            rows = jnp.einsum("mct,mcd->mtd", packs_low[k], packed[k], preferred_element_type=f32)
            rows = rows.reshape(home_rows, -1) * take(scale.T, col ^ k)[:, None]
            total = rows if total is None else total + rows
        return total

    gain_one = attn_gain.astype(f32)
    gain_two = ffn_gain.astype(f32)
    normed_one, scale_one = normalize(x_home)
    hidden_one_home = (normed_one * gain_one).astype(bf16)
    hidden_one_raw = gather_rows(after(hidden_one_home, near_pieces[:3]))
    grad_sent = send_packed(dy_home.astype(bf16))
    hidden_one = after(hidden_one_raw, grad_sent)
    logits_one = dot(hidden_one, attn_router)
    gates_one, matches_one, chosen_one, gate_vals_one = route_gates(
        logits_one, attn_routes.reshape(all_rows, TOP), expert_table
    )
    hits_one = jnp.any(chosen_one, axis=1).astype(f32)

    def wide(value):
        return jnp.pad(value, ((0, 0), (0, HDIM - value.shape[1])))

    kv_part = dot(hidden_one, kv_full).astype(bf16)
    query_part = dot(hidden_one, query_full)
    lens = first_len[:, 0].astype(jnp.int32)
    gates_wide = wide(gates_one)
    attn_vals, gated_vals, query_rot, key_rot, log_total, peaks = attention_forward(
        lens, query_part, kv_part, tables, gates_wide, wide(hits_one), own_heads, group_rows
    )
    peaks = jnp.max(peaks, axis=0)[: own_heads * slots]
    attn_part = after(dot_t(gated_vals, out_full), keep_second, side_second)
    attn_home = after(scatter_rows(attn_part), first_lines)
    grad_sent = after(grad_sent, attn_home)
    grad_near, grad_far = near_rows(grad_sent), near_rows(swap(grad_sent, "dp", 2))

    resid = x_home + attn_home
    normed_two, scale_two = normalize(resid)
    hidden_two = (normed_two * gain_two).astype(bf16)
    logits_two = dot(hidden_two, ffn_router)
    gates_two, matches_two, chosen_two, gate_vals_two = route_gates(
        logits_two, home_routes.reshape(home_rows, TOP), expert_table
    )
    gates_by_slot = gates_two.reshape(micro, tok_rows, slots)
    gate_parts = []
    for k in range(slots):
        gate_col = lax.dynamic_index_in_dim(gates_by_slot, col ^ k, 2, keepdims=False)
        gate_parts.append(jnp.sum(jnp.where(packs[k], gate_col[:, None, :], 0.0), axis=-1))
    hidden_sent = after(
        send_packed(hidden_two, jnp.stack(gate_parts)), second_lines
    )
    hidden_near, hidden_far = near_rows(hidden_sent), swap(hidden_sent, "dp", 2)
    hidden_near = after(hidden_near, near_pieces, grad_near, grad_far)
    position = jnp.stack([core, chip]).astype(jnp.int32)
    near_results = expert_rows(
        position, hidden_near, after(grad_near, grad_far), own_pieces, near_pieces
    )
    hidden_far = near_rows(after(hidden_far, near_results))
    far_results = expert_rows(position, hidden_far, grad_far, own_pieces, near_pieces)
    ffn_parts, hidden_parts, actives, joint_grads = zip(near_results, far_results)

    def block_grads(steps, *others):
        rows = after((hidden_near, hidden_far, grad_near, grad_far), *others)
        cuts = (2,) * len(steps)
        return expert_grads([chip ^ k for k in steps], cuts, chip_rows, rows, joint_grads, actives)

    hidden_sum, hidden_far_sum = quad_sums(hidden_parts)
    ffn_sum, ffn_far_sum = quad_sums(after(ffn_parts, hidden_far_sum))
    line_grads = block_grads([k ^ 1 for k in range(2, chips)], hidden_far_sum)
    side_got = [swap(line_grads[2 * line], "dp", step) for line, step in enumerate(line_steps)]
    blocks = after(line_grads[1::2], side_got)
    keep_got = [swap(block, "dp", step) for block, step in zip(blocks, line_steps)]
    hidden_got, ffn_far_sum, ffn_sum = lax.optimization_barrier(
        (swap(hidden_far_sum, "dp", 2), ffn_far_sum, ffn_sum, line_grads)
    )[:3]
    hidden_sum = hidden_sum + hidden_got.astype(f32)
    own_grads = block_grads([1, 0], hidden_sum)
    back_packed = return_packed(hidden_sum, *own_grads)
    ffn_sum = ffn_sum + swap(after(ffn_far_sum, hidden_got), "dp", 2).astype(f32)

    def total(own, got):
        return functools.reduce(jnp.add, [part.astype(f32) for part in [own] + got]).astype(bf16)

    slot_two_grad = jnp.zeros((slots, home_rows), f32)
    for k in range(slots):
        rows = jnp.sum(
            jnp.where(packs[k], back_packed[k][:, :, width].astype(f32)[:, :, None], 0.0), axis=1
        )
        slot_two_grad = lax.dynamic_update_index_in_dim(
            slot_two_grad, rows.reshape(home_rows), col ^ k, 0
        )
    hidden_two_grad = unpack([part[..., :width] for part in back_packed], gates_two)
    logit_two_grad = gate_back(slot_two_grad.T, gate_vals_two, matches_two, chosen_two).astype(bf16)
    hidden_two_grad = hidden_two_grad + dot_t(logit_two_grad, ffn_router)
    router_two_grad = t_dot(logit_two_grad, hidden_two)
    gain_two_grad = jnp.sum(hidden_two_grad * normed_two, axis=0)
    resid_grad = dy_home + norm_back(hidden_two_grad * gain_two, normed_two, scale_two)

    resid_grad_all, ffn_sum = lax.optimization_barrier(
        (gather_rows(resid_grad.astype(bf16)), ffn_sum, side_got)
    )[:2]
    out_part = t_dot(resid_grad_all, gated_vals).astype(bf16)
    vals_grad = after(dot(resid_grad_all, out_full), out_part)
    side_own = after((own_grads[0], side_got), vals_grad)
    vals_grad, side_sum = lax.optimization_barrier((vals_grad, total(*side_own)))
    other_sum = swap(side_sum, "dp", 2)
    ffn_packed = return_packed(after(ffn_sum, vals_grad))
    out_home = (resid + unpack(ffn_packed, gates_two)).astype(bf16)
    query_grad, key_grad, value_grad, slot_part_one = attention_backward(
        lens, query_rot, key_rot, kv_part, attn_vals, vals_grad, tables, gates_wide, log_total,
        own_heads, group_rows,
    )
    query_grad, key_grad, value_grad, slot_part_one = lax.optimization_barrier(
        (query_grad, key_grad, value_grad, slot_part_one, ffn_packed)
    )[:4]
    kv_grad = jnp.concatenate([key_grad, value_grad], axis=1)
    hidden_one_part = dot_t(query_grad, query_full) + dot_t(kv_grad, kv_full)
    hidden_one_part = hidden_one_part.astype(bf16)
    joint_part_grad = t_dot(
        after(hidden_one, hidden_one_part), jnp.concatenate([query_grad, kv_grad], axis=1)
    ).astype(bf16)
    back_one = scatter_rows(
        jnp.concatenate([hidden_one_part, slot_part_one.astype(bf16)], axis=1)
    )
    back_one = after(back_one, joint_part_grad)
    out_own = lax.psum_scatter(out_part, "dp", scatter_dimension=0, tiled=True)
    out_grad = slots_of(after(out_own, back_one))
    hidden_one_grad, slot_one_grad = back_one[:, :width], back_one[:, width : width + slots]

    def own(value):
        shaped = value.reshape((micro, group_rows) + value.shape[1:])
        part = lax.dynamic_slice_in_dim(shaped, col * tok_rows, tok_rows, 1)
        return part.reshape((home_rows,) + value.shape[1:])

    logit_one_grad = gate_back(
        slot_one_grad, own(gate_vals_one), own(matches_one), own(chosen_one)
    ).astype(bf16)
    hidden_one_grad = hidden_one_grad + dot_t(logit_one_grad, attn_router)
    router_one_grad = t_dot(logit_one_grad, hidden_one_home)
    gain_one_grad = jnp.sum(hidden_one_grad * normed_one, axis=0)
    in_home = resid_grad + norm_back(hidden_one_grad * gain_one, normed_one, scale_one)

    def reduced(value):
        return lax.psum_scatter(value, "dp", scatter_dimension=0, tiled=True)

    in_low = in_home.astype(bf16)
    joint_own = reduced(joint_part_grad)

    results = jnp.stack([out_home, in_low]).reshape(2, micro, tok_rows, width)
    results = jnp.einsum("mtr,bmtd->bmrd", deal, results, preferred_element_type=f32).astype(bf16)
    results = results.reshape(2 * micro, dp_count, piece_rows, width).transpose(1, 0, 2, 3)
    results = results.reshape(dp_count, 2 * micro * piece_rows, width)
    sent_back = results.shape[1]
    small = jnp.concatenate(
        [gain_one_grad[None], gain_two_grad[None], router_one_grad, router_two_grad], axis=0
    ).astype(bf16)
    sum_rows = small.shape[0]
    peak_count = own_heads * slots
    peak_parts, rest = [], peaks
    for _ in range(3):
        peak_parts.append(lax.reduce_precision(rest, 8, 7))
        rest = rest - peak_parts[-1]
    peak_row = jnp.concatenate(peak_parts).astype(bf16)
    small = jnp.pad(small, ((0, -sum_rows % 16 or 16), (0, 0)))
    small = lax.dynamic_update_slice(small, peak_row[None], (sum_rows, 0))
    small = jnp.broadcast_to(small[None], (dp_count,) + small.shape)
    results = jnp.concatenate([results, small], axis=1)
    results = lax.all_to_all(results, "dp", split_axis=0, concat_axis=0, tiled=True)
    query_own, kv_own = joint_own[:, :query_width], joint_own[:, query_width:]
    results, out_grad = lax.optimization_barrier((results, out_grad))
    results, other_sum, keep_got = lax.optimization_barrier((results, other_sum, keep_got))
    small = results[:, sent_back:].astype(f32)
    results = results[:, :sent_back].reshape(dp_count, 2 * micro, piece_rows, width)
    results = results.transpose(1, 0, 2, 3).reshape(2, micro, tok_rows, width)
    peak_row = small[:, sum_rows, : 3 * peak_count].reshape(dp_count, 3, peak_count)
    peak_row = jnp.max((peak_row[:, 0] + peak_row[:, 1]) + peak_row[:, 2], axis=0)
    small = jnp.sum(small, axis=0)
    small = lax.dynamic_update_slice(small, peak_row[None], (sum_rows, 0))
    smalls = jnp.broadcast_to(small[None], (slots,) + small.shape)
    smalls = lax.all_to_all(smalls, "expert", split_axis=0, concat_axis=0, tiled=True)
    peaks_all = smalls[:, sum_rows, :peak_count].reshape(slots, own_heads, slots)
    peaks_all = peaks_all.transpose(2, 0, 1).reshape(slots, HEADS)
    sums = functools.reduce(jnp.add, [smalls[k, :sum_rows] for k in range(slots)])

    keep_sums = total(own_grads[1], keep_got).reshape(2, shard_rows, 3 * quarter)
    other_sums = other_sum.reshape(2, shard_rows, 3 * quarter)
    by_rows = [jnp.stack([keep_sums[part], other_sums[part]]) for part in range(2)]
    own_pair = jnp.where(core == 0, by_rows[0], by_rows[1])
    near_pair = swap(jnp.where(core == 0, by_rows[1], by_rows[0]), "dp", 1)
    by_core = [jnp.where(core == 0, own_pair, near_pair), jnp.where(core == 0, near_pair, own_pair)]
    by_side = [[jnp.where(side == s, part[0], part[1]) for part in by_core] for s in range(2)]
    blocks = [part for row in by_side for part in row]
    gate_up_grad = jnp.concatenate(
        [b[:, :quarter] for b in blocks] + [b[:, quarter : 2 * quarter] for b in blocks], axis=1
    ).astype(f32)
    down_grad = jnp.concatenate([b[:, 2 * quarter :] for b in blocks], axis=1).astype(f32)

    out_grad = out_grad.astype(f32)
    query_out = slots_of(query_own).astype(f32)
    key_part, value_part = kv_own[:, :own_width], kv_own[:, own_width:]
    first_back = lax.ppermute(
        jnp.where(even_col, key_part, value_part), "expert", [(b, a) for a, b in first_pairs]
    )
    second_back = lax.ppermute(
        jnp.where(even_col, value_part, key_part), "expert", [(b, a) for a, b in second_pairs]
    )
    kv_out = jnp.concatenate(
        [
            jnp.where(holds_keys, first_back, second_back),
            jnp.where(holds_keys, second_back, first_back),
        ],
        axis=1,
    ).astype(f32)

    limit = clip_limit[0].astype(f32)
    factor = limit / jnp.maximum(peaks_all, limit)
    query_scale = jnp.repeat(jnp.sqrt(take(factor, col)), HDIM)
    query_clipped = (query_weight.astype(f32) * query_scale[None, None, :]).astype(bf16)
    full_scale = jnp.concatenate(
        [jnp.repeat(jnp.sqrt(jnp.min(factor, axis=0)), HDIM), jnp.ones((query_width,), f32)]
    )
    piece_width = kv_weight.shape[1]
    piece_scale = lax.dynamic_slice_in_dim(full_scale, col * piece_width, piece_width)
    kv_clipped = (kv_weight.astype(f32) * piece_scale[None, :]).astype(bf16)
    return (
        results[0],
        results[1],
        sums[0],
        sums[1],
        sums[2 : 2 + slots].T,
        sums[2 + slots : sum_rows].T,
        query_out[None],
        out_grad[None],
        kv_out,
        gate_up_grad[None],
        down_grad[None],
        query_clipped,
        kv_clipped,
    )


def solution(mesh):
    placed = (
        P(None, ("dp", "expert"), None),
        P(None, ("dp", "expert"), None),
        P(),
        P(None, ("dp", "expert")),
        P(None, "dp", None),
        P(None, "dp", None),
        P(),
        P(),
        P(),
        P(),
        P(),
        P(),
        P("expert", "dp", None),
        P("expert", "dp", None),
        P("dp", "expert"),
        P("expert", "dp", None),
        P("expert", "dp", None),
    )
    return jax.shard_map(
        local,
        mesh=mesh,
        in_specs=placed,
        out_specs=(
            P(None, ("dp", "expert"), None),
            P(None, ("dp", "expert"), None),
            P(),
            P(),
            P(),
            P(),
            P("expert", "dp", None),
            P("expert", "dp", None),
            P("dp", "expert"),
            P("expert", "dp", None),
            P("expert", "dp", None),
            P("expert", "dp", None),
            P("dp", "expert"),
        ),
        check_vma=False,
    )
```
